32 devices in a mesh: seq: 4 (over z), tp: 4 (over x, core), dp: 2 (over y).
Axes of the slice: x: 2, y: 2, z: 4, core: 2. Of those that a mesh axis runs over, the one named last changes fastest.
Arguments:
- query_gate: bfloat16 [2, 1024, 4096], P('dp', 'seq', 'tp'), may hold values from -6 to 6
- key_gate: bfloat16 [2, 1024, 4096], P('dp', 'seq', 'tp'), may hold values from -6 to 6
- value_input: bfloat16 [2, 1024, 4096], P('dp', 'seq', 'tp'), may hold values from -6 to 6
- filter_taps: bfloat16 [4096, 128], P('tp'), may hold values from -0.5 to 0.5
- skip_gain: float32 [4096], P('tp'), may hold values from -1 to 1
- out_weight: bfloat16 [4096, 4096], P('tp', 'dp'), may hold values from -0.09375 to 0.09375
- cotangent: bfloat16 [2, 1024, 4096], P('dp', 'seq', 'tp'), may hold values from -6 to 6
Outputs:
- grad_query: bfloat16 [2, 1024, 4096], P('dp', 'seq', 'tp')
- grad_key: bfloat16 [2, 1024, 4096], P('dp', 'seq', 'tp')
- grad_value: bfloat16 [2, 1024, 4096], P('dp', 'seq', 'tp')
- grad_filter: float32 [4096, 128], P('tp')
- grad_skip: float32 [4096], P('tp')
- grad_weight: float32 [4096, 4096], P(('seq', 'dp'), 'tp')
The draws below stay inside these ranges and needn't reach their ends.
All inputs are finite; a program needn't handle non-finite values.
Results may differ from the reference program's by a relative error of at most 0.0095.
Values may be sent and summed in bfloat16 or wider, within the bound.
No kernel may reach another device: no remote copies, remote signals or barrier semaphores. Data moves between devices by JAX's collectives and lax.ppermute only.
A program may use at most 192 MiB of HBM per device.

```python
import math
import jax
import jax.numpy as jnp
from jax import lax

D = 4096
TAPS = 128
LENGTH = 1024
SEQS = 2


def draw_cotangent(key, part):
    position = jnp.arange(LENGTH, dtype=jnp.float32) / LENGTH
    values = jax.random.normal(key, (SEQS, LENGTH, D), jnp.float32) * (0.5 + position)[None, :, None]
    return jnp.clip(values, -6.0, 6.0).astype(jnp.bfloat16)


def block_levels(stream_key, extent, cuts, smallest, largest):
    factor_of, own = 1.0, jax.random.fold_in(stream_key, 6)
    for dim, shards_of in cuts:
        heights = jnp.exp(jax.random.uniform(jax.random.fold_in(own, dim), (shards_of,), jnp.float32, smallest / len(cuts), largest / len(cuts)))
        factor_of = factor_of * jnp.repeat(heights, extent[dim] // shards_of).reshape([-1 if axis == dim else 1 for axis in range(len(extent))])
    return factor_of


def centred(own_key, dims, deviation, limit, cuts=(), held_as=jnp.bfloat16):
    factor_of = block_levels(own_key, dims, cuts, -0.22, 0.18) if cuts else 1.0
    drawn = jax.random.normal(own_key, dims, jnp.float32) * deviation * factor_of
    return jnp.minimum(jnp.maximum(drawn, -limit), limit).astype(held_as)


def setup_inputs(seed: int = 0) -> dict:
    keys = jax.random.split(jax.random.key(seed), 8)
    query_gate = centred(keys[0], (SEQS, LENGTH, D), 1.0, 6.0, ((0, 2), (1, 4), (2, 4)))
    key_gate = centred(keys[1], (SEQS, LENGTH, D), 1.0, 6.0, ((0, 2), (1, 4), (2, 4)))
    value_input = centred(keys[2], (SEQS, LENGTH, D), 1.0, 6.0, ((0, 2), (1, 4), (2, 4)))
    filter_taps = centred(keys[3], (D, TAPS), TAPS ** -0.5, 0.5, ((0, 4),))
    skip_gain = jnp.clip(jax.random.uniform(keys[4], (D,), jnp.float32, -1.0, 1.0) * block_levels(keys[4], (D,), ((0, 4),), -0.4, 0.0), -1.0, 1.0)
    out_weight = centred(keys[5], (D, D), D ** -0.5, 0.09375, ((0, 4), (1, 2)))
    cotangent = draw_cotangent(jax.random.fold_in(keys[7], 71), 0)
    return {"query_gate": query_gate, "key_gate": key_gate, "value_input": value_input, "filter_taps": filter_taps, "skip_gain": skip_gain, "out_weight": out_weight, "cotangent": cotangent}


block_rows = 32
highest = lax.Precision.HIGHEST

def taps_matrix(vector, row_count, col_count):
    channels, width_all = vector.shape
    tiled = jnp.tile(vector, (1, row_count + 1))
    skewed = tiled[:, :row_count * (width_all - 1)].reshape(channels, row_count, width_all - 1)
    return skewed[:, :, row_count - 1:row_count - 1 + col_count]

def forward_table(filter_taps):
    channels, tap_count = filter_taps.shape
    padding = jnp.zeros((channels, block_rows), filter_taps.dtype)
    vector = jnp.concatenate([padding, filter_taps[:, ::-1], padding], axis=1)
    return taps_matrix(vector, block_rows, tap_count + block_rows)

def backward_table(filter_taps):
    channels, tap_count = filter_taps.shape
    before = jnp.zeros((channels, block_rows - 1), filter_taps.dtype)
    after = jnp.zeros((channels, block_rows + 1), filter_taps.dtype)
    vector = jnp.concatenate([before, filter_taps, after], axis=1)
    return taps_matrix(vector, block_rows, tap_count + block_rows)

def windows(extended, length, tap_count):
    pieces = []
    for shift_index in range(tap_count // block_rows + 1):
        lower = shift_index * block_rows
        pieces.append(extended[lower:lower + length].reshape(length // block_rows, block_rows, extended.shape[1]))
    return jnp.concatenate(pieces, axis=1)

def lag_sums(blocks, tap_count):
    channels, row_count, col_count = blocks.shape
    flattened = blocks.reshape(channels, row_count * col_count)
    padded = jnp.concatenate([flattened, jnp.zeros((channels, row_count), blocks.dtype)], axis=1)
    diagonal = padded.reshape(channels, row_count, col_count + 1)[:, :, 1:tap_count + 1]
    return lax.optimization_barrier(jnp.sum(diagonal, axis=1))[:, ::-1]

def reference(query_gate, key_gate, value_input, filter_taps, skip_gain, out_weight, cotangent):
    norm_factor = 1.0 / math.sqrt(SEQS * LENGTH)
    band_width = min(D, 512)
    fwd_table = forward_table(filter_taps).astype(jnp.float32)
    bwd_table = backward_table(filter_taps).astype(jnp.float32)
    filter_total = jnp.zeros((D, TAPS), jnp.float32)
    skip_total = jnp.zeros((D,), jnp.float32)
    weight_total = jnp.zeros((D, D), jnp.float32)
    query_list, key_list, value_list = ([], [], [])
    for sequence in range(SEQS):
        queries = query_gate[sequence].astype(jnp.float32)
        key_rows = key_gate[sequence].astype(jnp.float32)
        value_rows = value_input[sequence].astype(jnp.float32)
        mixed = (key_rows * value_rows).astype(jnp.bfloat16)
        extended = jnp.concatenate([jnp.zeros((TAPS, D), jnp.bfloat16), mixed], axis=0).astype(jnp.float32)
        conv_parts = []
        for lower in range(0, D, band_width):
            wins = windows(extended[:, lower:lower + band_width], LENGTH, TAPS)
            conv = jnp.einsum('cab,ibc->iac', fwd_table[lower:lower + band_width], wins, precision=highest)
            conv_parts.append(conv.reshape(LENGTH, band_width))
        state = jnp.concatenate(conv_parts, axis=1) + skip_gain[None, :] * mixed.astype(jnp.float32)
        gated = (queries * state).astype(jnp.bfloat16)
        grad_gated = jnp.dot(cotangent[sequence], out_weight.T, preferred_element_type=jnp.float32)
        query_list.append((grad_gated * state).astype(jnp.bfloat16))
        signal = (grad_gated * queries).astype(jnp.bfloat16)
        signal_ext = jnp.concatenate([signal, jnp.zeros((TAPS, D), jnp.bfloat16)], axis=0).astype(jnp.float32)
        signal_blocks = signal.astype(jnp.float32).reshape(LENGTH // block_rows, block_rows, D)
        back_parts, lag_parts = ([], [])
        for lower in range(0, D, band_width):
            wins = windows(signal_ext[:, lower:lower + band_width], LENGTH, TAPS)
            back = jnp.einsum('cab,ibc->iac', bwd_table[lower:lower + band_width], wins, precision=highest)
            back_parts.append(back.reshape(LENGTH, band_width))
            fwins = windows(extended[:, lower:lower + band_width], LENGTH, TAPS)
            blocks = jnp.einsum('iac,ibc->cab', signal_blocks[:, :, lower:lower + band_width], fwins, precision=highest)
            lag_parts.append(lag_sums(blocks, TAPS))
        back = jnp.concatenate(back_parts, axis=1) + skip_gain[None, :] * signal.astype(jnp.float32)
        key_list.append((back * value_rows).astype(jnp.bfloat16))
        value_list.append((back * key_rows).astype(jnp.bfloat16))
        filter_total = filter_total + jnp.concatenate(lag_parts, axis=0)
        skip_total = skip_total + lax.optimization_barrier(jnp.sum(signal.astype(jnp.float32) * mixed.astype(jnp.float32), axis=0))
        weight_total = weight_total + jnp.dot(cotangent[sequence].T, gated, preferred_element_type=jnp.float32)
    return (jnp.stack(query_list), jnp.stack(key_list), jnp.stack(value_list), filter_total * norm_factor, skip_total * norm_factor, weight_total * norm_factor)
```

```python
import math

import jax
import jax.numpy as jnp
import numpy as np
from jax import lax
from jax.sharding import PartitionSpec as P

high = lax.Precision.HIGH


def analysis_table(size, positions):
    half = size // 2
    omega = 2.0 * np.pi * (np.arange(half) + 0.5) / size
    angle = omega[:, None] * np.asarray(positions)[None, :]
    return np.concatenate([np.cos(angle), -np.sin(angle)], axis=0).astype(np.float32)


def transform(table, rows):
    return jnp.dot(
        table, rows.astype(jnp.float32), precision=high, preferred_element_type=jnp.float32
    )


def spectrum_product(left, right, conjugate_right):
    half = left.shape[0] // 2
    left_re, left_im = left[:half], left[half:]
    right_re, right_im = right[:half], right[half:]
    if conjugate_right:
        right_im = -right_im
    return jnp.concatenate(
        [left_re * right_re - left_im * right_im, left_re * right_im + left_im * right_re], axis=0
    )


def swap_pairs(value, axis, distance):
    count = lax.axis_size(axis)
    return lax.ppermute(value, axis, [(i, i ^ distance) for i in range(count)])


def sum_over(value, axis):
    distance = 1
    while distance < lax.axis_size(axis):
        own = value.astype(jnp.bfloat16)
        other = swap_pairs(own, axis, distance)
        value = own.astype(jnp.float32) + other.astype(jnp.float32)
        distance *= 2
    return value


def per_device(query_gate, key_gate, value_input, filter_taps, skip_gain, out_weight, cotangent):
    f32, bf16 = jnp.float32, jnp.bfloat16
    queries, key_rows, value_rows, cot = (
        query_gate[0],
        key_gate[0],
        value_input[0],
        cotangent[0],
    )
    length, channels = queries.shape
    taps = filter_taps.shape[1]
    n_seq, n_tp, n_dp = lax.axis_size("seq"), lax.axis_size("tp"), lax.axis_size("dp")
    subs = n_tp // n_dp
    me_tp, me_dp = lax.axis_index("tp"), lax.axis_index("dp")
    me_half, me_sub = me_tp // subs, me_tp % subs
    size = length + taps
    norm_factor = 1.0 / math.sqrt(length * n_seq * n_dp)

    ext = analysis_table(size, np.arange(size))
    scale = 2.0 / size
    synth_fwd = np.ascontiguousarray(ext[:, taps:].T)
    synth_bwd = np.ascontiguousarray(ext[:, :length].T)
    synth_lag = np.ascontiguousarray(analysis_table(size, np.arange(taps) - taps).T)

    mixed = (key_rows.astype(f32) * value_rows.astype(f32)).astype(bf16)
    prior = lax.ppermute(mixed[length - taps :], "seq", [(i, i + 1) for i in range(n_seq - 1)])

    def tp_dp(half, sub, replica):
        return (half * subs + sub) * n_dp + replica

    rounds = []
    for turn in range(2):
        route = [
            (tp_dp(h, c, d), tp_dp(d ^ turn, c, h))
            for h in range(n_dp)
            for c in range(subs)
            for d in range(n_dp)
        ]
        rounds.append(lax.ppermute(cot, ("tp", "dp"), route))
    same = me_half == me_dp
    other_cot = jnp.where(same, rounds[1], rounds[0])
    own_cot = jnp.where(same, rounds[0], rounds[1])

    def project(pieces_of):
        total = None
        for shift in range(subs):
            if shift:
                route = [
                    (tp_dp(h, c, d), tp_dp(h, (c + shift) % subs, d))
                    for h in range(n_dp)
                    for c in range(subs)
                    for d in range(n_dp)
                ]
                piece = lax.ppermute(pieces_of, ("tp", "dp"), route)
            else:
                piece = pieces_of
            width = piece.shape[1]
            which = (me_sub - shift + subs) % subs
            block = lax.dynamic_slice_in_dim(out_weight, which * width, width, axis=1)
            part = lax.dot_general(
                piece, block, (((1,), (1,)), ((), ())), preferred_element_type=f32
            )
            total = part if total is None else total + part
        return total

    other_part = swap_pairs(project(other_cot).astype(bf16), "dp", 1)
    own_part = project(own_cot)

    filt = transform(analysis_table(size, np.arange(taps)), filter_taps.T)
    bias = jnp.concatenate(
        [
            jnp.broadcast_to(skip_gain[None], (size // 2, channels)),
            jnp.zeros((size // 2, channels), f32),
        ]
    )
    filt = (filt + bias) * scale
    mixed_spec = transform(ext, jnp.concatenate([prior, mixed], axis=0))
    state = transform(synth_fwd, spectrum_product(mixed_spec, filt, False))
    gated = (queries.astype(f32) * state).astype(bf16)
    gated_all = lax.all_gather(gated, "seq", axis=0, tiled=True)

    if n_seq == n_tp:
        moved = lax.ppermute(
            cot, ("seq", "tp"), [(s * n_tp + t, t * n_tp + s) for s in range(n_seq) for t in range(n_tp)]
        )
        cot_all = lax.all_gather(moved, "tp", axis=0, tiled=True)
    else:
        full = lax.all_gather(cot, "tp", axis=1, tiled=True)
        cot_all = lax.all_to_all(full, "seq", 1, 0, tiled=True)

    grad_gated = own_part + other_part.astype(f32)
    grad_query = (grad_gated * state).astype(bf16)
    signal = (grad_gated * queries.astype(f32)).astype(bf16)
    later = lax.ppermute(signal[:taps], "seq", [(i + 1, i) for i in range(n_seq - 1)])
    signal_spec = transform(ext[:, :length], signal)
    lags = transform(synth_lag, spectrum_product(signal_spec, mixed_spec, True))
    lags = sum_over(sum_over(lags, "dp"), "seq")
    grad_filter = lags.T * (norm_factor * scale)
    signal_spec = signal_spec + transform(ext[:, length:], later)
    back = transform(synth_bwd, spectrum_product(signal_spec, filt, True))
    grad_key = (back * value_rows.astype(f32)).astype(bf16)
    grad_value = (back * key_rows.astype(f32)).astype(bf16)

    rows = cot_all.shape[1] // n_dp

    def weight_part(replica):
        block = lax.dynamic_slice_in_dim(cot_all, replica * rows, rows, axis=1)
        return lax.dot_general(
            block, gated_all, (((0,), (0,)), ((), ())), preferred_element_type=f32
        )

    sent = swap_pairs(weight_part(1 - me_dp).astype(bf16), "dp", 1)
    grad_weight = (weight_part(me_dp) + sent.astype(f32)) * norm_factor
    return (
        grad_query[None],
        grad_key[None],
        grad_value[None],
        grad_filter,
        grad_filter[:, 0],
        grad_weight,
    )


def solution(mesh):
    tokens = P("dp", "seq", "tp")
    return jax.shard_map(
        per_device,
        mesh=mesh,
        in_specs=(tokens, tokens, tokens, P("tp", None), P("tp"), P("tp", "dp"), tokens),
        out_specs=(tokens, tokens, tokens, P("tp", None), P("tp"), P(("seq", "dp"), "tp")),
        check_vma=False,
    )
```

```python
import functools
import math

import jax
import jax.numpy as jnp
import ml_dtypes
import numpy as np
from jax import lax
from jax.experimental import pallas as pl
from jax.experimental.pallas import tpu as pltpu
from jax.sharding import PartitionSpec as P

f32, bf16 = jnp.float32, jnp.bfloat16
lanes = 256
vmem_bytes = 32 * 1024 * 1024


def analysis_table(size, positions):
    half = size // 2
    omega = 2.0 * np.pi * (np.arange(half) + 0.5) / size
    angle = omega[:, None] * np.asarray(positions)[None, :]
    return np.concatenate([np.cos(angle), -np.sin(angle)], axis=0)


def split_table(table):
    high = table.astype(ml_dtypes.bfloat16)
    low = (table - high.astype(np.float64)).astype(ml_dtypes.bfloat16)
    return np.stack([high, low])


def split_rows(rows):
    high = rows.astype(bf16)
    return high, (rows - high.astype(f32)).astype(bf16)


def dot(left, right):
    return jnp.dot(left, right, preferred_element_type=f32)


def dot_nt(left, right):
    return lax.dot_general(left, right, (((1,), (1,)), ((), ())), preferred_element_type=f32)


def forward_transform(table, rows):
    return dot(table[0], rows) + dot(table[1], rows)


def inverse_transform(table, spectrum):
    high, low = split_rows(spectrum)
    return dot(table[0], high) + dot(table[0], low) + dot(table[1], high)


def spectrum_product(left, right, conjugate_right):
    half = left.shape[0] // 2
    left_re, left_im = left[:half], left[half:]
    right_re, right_im = right[:half], right[half:]
    if conjugate_right:
        right_im = -right_im
    return jnp.concatenate(
        [left_re * right_re - left_im * right_im, left_re * right_im + left_im * right_re], axis=0
    )


def prepare_kernel(scale, own_table, tap_table, key_ref, value_ref, taps_ref, skip_ref, spec_ref, filt_ref):
    mixed = (key_ref[...].astype(f32) * value_ref[...].astype(f32)).astype(bf16)
    spec_ref[...] = forward_transform(own_table, mixed)
    filt = dot_nt(tap_table[0], taps_ref[...]) + dot_nt(tap_table[1], taps_ref[...])
    half = filt.shape[0] // 2
    filt_ref[:half] = (filt[:half] + skip_ref[...]) * scale
    filt_ref[half:] = filt[half:] * scale


def state_kernel(prior_table, synth, prior_ref, own_ref, filt_ref, query_ref, spec_ref, state_ref, gated_ref):
    spec = own_ref[...] + forward_transform(prior_table, prior_ref[...])
    spec_ref[...] = spec
    state = inverse_transform(synth, spectrum_product(spec, filt_ref[...], False))
    state_ref[...] = state
    gated_ref[...] = (query_ref[...].astype(f32) * state).astype(bf16)


def project_kernel(count, which_ref, *refs):
    total = None
    for piece_ref, weight_ref in zip(refs[:count], refs[count : 2 * count]):
        part = dot_nt(piece_ref[...], weight_ref[...])
        total = part if total is None else total + part
    refs[-1][...] = total.astype(refs[-1].dtype)


def lag_kernel(own_table, synth, signal_ref, spec_ref, signal_spec_ref, lag_ref):
    signal_spec = forward_transform(own_table, signal_ref[...])
    signal_spec_ref[...] = signal_spec
    lag_ref[...] = inverse_transform(synth, spectrum_product(signal_spec, spec_ref[...], True))


def back_kernel(late_table, synth, own_ref, later_ref, filt_ref, key_ref, value_ref, grad_key_ref, grad_value_ref):
    spec = own_ref[...] + forward_transform(late_table, later_ref[...])
    back = inverse_transform(synth, spectrum_product(spec, filt_ref[...], True))
    grad_key_ref[...] = (back * value_ref[...].astype(f32)).astype(bf16)
    grad_value_ref[...] = (back * key_ref[...].astype(f32)).astype(bf16)


def by_channel(kernel, tables, args, outs, channels, flops):
    count = len(tables)

    def body(*refs):
        kernel(*refs)

    def column_spec(shape, by_row):
        if by_row:
            return pl.BlockSpec((lanes, shape[1]), lambda i: (i, 0))
        return pl.BlockSpec((shape[0], lanes), lambda i: (0, i))

    specs = [pl.BlockSpec(t.shape, lambda i: (0, 0, 0)) for t in tables]
    specs += [column_spec(a.shape, a.shape[1] != channels) for a in args]
    moved = sum(a.size * a.dtype.itemsize for a in args) + sum(
        o.size * jnp.dtype(o.dtype).itemsize for o in outs
    )
    return pl.pallas_call(
        body,
        grid=(channels // lanes,),
        in_specs=specs,
        out_specs=[column_spec(o.shape, False) for o in outs],
        out_shape=outs,
        compiler_params=pltpu.CompilerParams(vmem_limit_bytes=vmem_bytes),
        cost_estimate=pl.CostEstimate(flops=flops // 64, bytes_accessed=moved // 64, transcendentals=0),
    )(*[jnp.asarray(t) for t in tables], *args)


def project(pieces, places, out_weight, dtype):
    count = len(pieces)
    length, width = pieces[0].shape
    channels = out_weight.shape[0]
    grid_spec = pltpu.PrefetchScalarGridSpec(
        num_scalar_prefetch=1,
        grid=(channels // lanes,),
        in_specs=[pl.BlockSpec((length, width), lambda i, w: (0, 0))] * count
        + [pl.BlockSpec((lanes, width), functools.partial(lambda n, i, w: (i, w[n]), n)) for n in range(count)],
        out_specs=pl.BlockSpec((length, lanes), lambda i, w: (0, i)),
    )
    return pl.pallas_call(
        functools.partial(project_kernel, count),
        grid_spec=grid_spec,
        out_shape=jax.ShapeDtypeStruct((length, channels), dtype),
        compiler_params=pltpu.CompilerParams(vmem_limit_bytes=vmem_bytes),
        cost_estimate=pl.CostEstimate(
            flops=2 * length * channels * out_weight.shape[1],
            bytes_accessed=out_weight.size * 2 + length * channels * 6,
            transcendentals=0,
        ),
    )(jnp.stack(places).astype(jnp.int32), *pieces, *([out_weight] * count))


def swap_pairs(value, axis, distance):
    count = lax.axis_size(axis)
    return lax.ppermute(value, axis, [(i, i ^ distance) for i in range(count)])


def after(value, *earlier):
    return lax.optimization_barrier((value, *earlier))[0]


def per_device(query_gate, key_gate, value_input, filter_taps, skip_gain, out_weight, cotangent):
    queries, key_rows, value_rows, cot = (
        query_gate[0],
        key_gate[0],
        value_input[0],
        cotangent[0],
    )
    length, channels = queries.shape
    taps = filter_taps.shape[1]
    n_seq, n_tp, n_dp = lax.axis_size("seq"), lax.axis_size("tp"), lax.axis_size("dp")
    subs = n_tp // n_dp
    me_tp, me_dp = lax.axis_index("tp"), lax.axis_index("dp")
    me_half, me_sub = me_tp // subs, me_tp % subs
    size = length + taps
    norm_factor = 1.0 / math.sqrt(length * n_seq * n_dp)

    whole = analysis_table(size, np.arange(size))
    scale = 2.0 / size
    own_table = split_table(whole[:, :length])
    tap_table = split_table(whole[:, :taps])
    late_table = split_table(whole[:, length:])
    shifted_table = split_table(whole[:, taps:])
    synth_fwd = np.ascontiguousarray(split_table(whole[:, taps:].T))
    synth_bwd = np.ascontiguousarray(split_table(whole[:, :length].T))
    synth_lag = np.ascontiguousarray(split_table(analysis_table(size, np.arange(taps) - taps).T))
    spectrum = jax.ShapeDtypeStruct((size, channels), f32)
    rows16 = jax.ShapeDtypeStruct((length, channels), bf16)
    rows32 = jax.ShapeDtypeStruct((length, channels), f32)
    unit = 2 * size * channels

    tail = (
        key_rows[length - taps :].astype(f32) * value_rows[length - taps :].astype(f32)
    ).astype(bf16)
    prior = lax.ppermute(tail, "seq", [(i, i + 1) for i in range(n_seq - 1)])

    def tp_dp(half, sub, replica):
        return (half * subs + sub) * n_dp + replica

    places = [(h, c, d) for h in range(n_dp) for c in range(subs) for d in range(n_dp)]
    rounds = []
    for turn in range(2):
        route = [(tp_dp(h, c, d), tp_dp(d ^ turn, c, h)) for h, c, d in places]
        rounds.append(lax.ppermute(cot, ("tp", "dp"), route))

    own_spec, filt = by_channel(
        functools.partial(prepare_kernel, scale),
        [shifted_table, tap_table],
        [key_rows, value_rows, filter_taps, skip_gain[None]],
        [spectrum, spectrum],
        channels,
        2 * unit * (length + taps),
    )
    mixed_spec, state, gated = by_channel(
        state_kernel,
        [tap_table, synth_fwd],
        [prior, own_spec, filt, queries],
        [spectrum, rows32, rows16],
        channels,
        unit * (2 * taps + 3 * length),
    )
    gated_all = lax.all_gather(gated, "seq", axis=0, tiled=True)

    same = me_half == me_dp
    other_cot = jnp.where(same, rounds[1], rounds[0])
    own_cot = jnp.where(same, rounds[0], rounds[1])

    def from_subs(piece):
        pieces = [piece]
        for shift in range(1, subs):
            route = [(tp_dp(h, c, d), tp_dp(h, (c + shift) % subs, d)) for h, c, d in places]
            pieces.append(lax.ppermute(piece, ("tp", "dp"), route))
        return pieces

    weight_places = [(me_sub - shift + subs) % subs for shift in range(subs)]
    other_sent = project(from_subs(other_cot), weight_places, out_weight, bf16)
    other_part = swap_pairs(other_sent, "dp", 1)
    own_part = project(from_subs(own_cot), weight_places, out_weight, f32)

    if n_seq == n_tp:
        moved = lax.ppermute(
            after(cot, other_cot),
            ("seq", "tp"),
            [(s * n_tp + t, t * n_tp + s) for s in range(n_seq) for t in range(n_tp)],
        )
        cot_all = lax.all_gather(moved, "tp", axis=0, tiled=True)
    else:
        full = lax.all_gather(cot, "tp", axis=1, tiled=True)
        cot_all = lax.all_to_all(full, "seq", 1, 0, tiled=True)

    grad_gated = own_part + other_part.astype(f32)
    grad_query = (grad_gated * state).astype(bf16)
    signal = (grad_gated * queries.astype(f32)).astype(bf16)
    later = lax.ppermute(signal[:taps], "seq", [(i + 1, i) for i in range(n_seq - 1)])
    signal_spec, lags = by_channel(
        lag_kernel,
        [own_table, synth_lag],
        [signal, mixed_spec],
        [spectrum, jax.ShapeDtypeStruct((taps, channels), f32)],
        channels,
        unit * (2 * length + 3 * taps),
    )
    grad_key, grad_value = by_channel(
        back_kernel,
        [late_table, synth_bwd],
        [signal_spec, later, filt, key_rows, value_rows],
        [rows16, rows16],
        channels,
        unit * (2 * taps + 3 * length),
    )

    share = taps // n_dp
    lag_sum = lax.dynamic_slice_in_dim(lags, me_dp * share, share, axis=0) + swap_pairs(
        lax.dynamic_slice_in_dim(lags, (1 - me_dp) * share, share, axis=0).astype(bf16), "dp", 1
    ).astype(f32)
    distance = 1
    while distance < n_seq:
        rounded = lag_sum.astype(bf16)
        lag_sum = rounded.astype(f32) + swap_pairs(rounded, "seq", distance).astype(f32)
        distance *= 2
    mine = lag_sum.astype(bf16)
    theirs = swap_pairs(mine, "dp", 1)
    first = me_dp == 0
    lag_sum = jnp.concatenate([jnp.where(first, mine, theirs), jnp.where(first, theirs, mine)], axis=0)
    grad_filter = lag_sum.astype(f32).T * (norm_factor * scale)

    rows = cot_all.shape[1] // n_dp

    def weight_part(replica):
        block = lax.dynamic_slice_in_dim(cot_all, replica * rows, rows, axis=1)
        return lax.dot_general(
            block, gated_all, (((0,), (0,)), ((), ())), preferred_element_type=f32
        )

    sent = swap_pairs(weight_part(1 - me_dp).astype(bf16), "dp", 1)
    grad_weight = (weight_part(me_dp) + sent.astype(f32)) * norm_factor
    return (
        grad_query[None],
        grad_key[None],
        grad_value[None],
        grad_filter,
        grad_filter[:, 0],
        grad_weight,
    )


def solution(mesh):
    tokens = P("dp", "seq", "tp")
    return jax.shard_map(
        per_device,
        mesh=mesh,
        in_specs=(tokens, tokens, tokens, P("tp", None), P("tp"), P("tp", "dp"), tokens),
        out_specs=(tokens, tokens, tokens, P("tp", None), P("tp"), P(("seq", "dp"), "tp")),
        check_vma=False,
    )
```

```python
import functools
import math

import jax
import jax.numpy as jnp
import ml_dtypes
import numpy as np
from jax import lax
from jax.experimental import pallas as pl
from jax.experimental.pallas import tpu as pltpu
from jax.sharding import PartitionSpec as P

f32, bf16 = jnp.float32, jnp.bfloat16
lanes = 256
vmem_bytes = 32 * 1024 * 1024


def analysis_table(size, positions):
    half = size // 2
    omega = 2.0 * np.pi * (np.arange(half) + 0.5) / size
    angle = omega[:, None] * np.asarray(positions)[None, :]
    return np.concatenate([np.cos(angle), -np.sin(angle)], axis=0)


def split_table(table):
    high = table.astype(ml_dtypes.bfloat16)
    low = (table - high.astype(np.float64)).astype(ml_dtypes.bfloat16)
    return np.stack([high, low])


def split_rows(rows):
    high = rows.astype(bf16)
    return high, (rows - high.astype(f32)).astype(bf16)


def dot(left, right):
    return jnp.dot(left, right, preferred_element_type=f32)


def dot_nt(left, right):
    return lax.dot_general(left, right, (((1,), (1,)), ((), ())), preferred_element_type=f32)


def forward_transform(table, rows):
    return dot(table[0], rows) + dot(table[1], rows)


def inverse_transform(table, spectrum):
    high, low = split_rows(spectrum)
    return dot(table[0], high) + dot(table[0], low) + dot(table[1], high)


def spectrum_product(left, right, conjugate_right):
    half = left.shape[0] // 2
    left_re, left_im = left[:half], left[half:]
    right_re, right_im = right[:half], right[half:]
    if conjugate_right:
        right_im = -right_im
    return jnp.concatenate(
        [left_re * right_re - left_im * right_im, left_re * right_im + left_im * right_re], axis=0
    )


def prepare_kernel(scale, own_table, tap_table, key_ref, value_ref, taps_ref, skip_ref, spec_ref, filt_ref):
    mixed = (key_ref[...].astype(f32) * value_ref[...].astype(f32)).astype(bf16)
    spec_ref[...] = forward_transform(own_table, mixed)
    filt = dot_nt(tap_table[0], taps_ref[...]) + dot_nt(tap_table[1], taps_ref[...])
    half = filt.shape[0] // 2
    filt_ref[:half] = (filt[:half] + skip_ref[...]) * scale
    filt_ref[half:] = filt[half:] * scale


def state_kernel(prior_table, synth, prior_ref, own_ref, filt_ref, query_ref, spec_ref, state_ref, gated_ref):
    spec = own_ref[...] + forward_transform(prior_table, prior_ref[...])
    spec_ref[...] = spec
    state = inverse_transform(synth, spectrum_product(spec, filt_ref[...], False))
    state_ref[...] = state
    gated_ref[0] = (query_ref[...].astype(f32) * state).astype(bf16)


def project_kernel(place_ref, first_mine, second_mine, first_theirs, second_theirs, weight_mine, weight_theirs, out_ref):
    def write(mine, theirs):
        total = dot_nt(mine[...], weight_mine[...]) + dot_nt(theirs[...], weight_theirs[...])
        out_ref[...] = total.astype(out_ref.dtype)

    pl.when(place_ref[0] == 0)(lambda: write(first_mine, first_theirs))
    pl.when(place_ref[0] != 0)(lambda: write(second_mine, second_theirs))


def weight_kernel(count, place_ref, *refs):
    total = None
    for cot_ref, gated_ref in zip(refs[:count], refs[count : 2 * count]):
        part = dot(cot_ref[0], gated_ref[0])
        total = part if total is None else total + part
    refs[-1][...] = total.astype(refs[-1].dtype)


def lag_kernel(own_table, synth, signal_ref, spec_ref, signal_spec_ref, lag_ref):
    signal_spec = forward_transform(own_table, signal_ref[...])
    signal_spec_ref[...] = signal_spec
    lag_ref[...] = inverse_transform(synth, spectrum_product(signal_spec, spec_ref[...], True))


def back_kernel(late_table, synth, own_ref, later_ref, filt_ref, key_ref, value_ref, grad_key_ref, grad_value_ref):
    spec = own_ref[...] + forward_transform(late_table, later_ref[...])
    back = inverse_transform(synth, spectrum_product(spec, filt_ref[...], True))
    grad_key_ref[...] = (back * value_ref[...].astype(f32)).astype(bf16)
    grad_value_ref[...] = (back * key_ref[...].astype(f32)).astype(bf16)


def estimate(flops, arrays):
    moved = sum(a.size * jnp.dtype(a.dtype).itemsize for a in arrays)
    return pl.CostEstimate(flops=flops // 64, bytes_accessed=moved // 64, transcendentals=0)


def by_channel(kernel, tables, args, outs, channels, flops):
    def column_spec(shape):
        if len(shape) == 3:
            per = shape[2] // lanes
            return pl.BlockSpec((1, shape[1], lanes), lambda i: (i // per, 0, i % per))
        if shape[1] != channels:
            return pl.BlockSpec((lanes, shape[1]), lambda i: (i, 0))
        return pl.BlockSpec((shape[0], lanes), lambda i: (0, i))

    return pl.pallas_call(
        kernel,
        grid=(channels // lanes,),
        in_specs=[pl.BlockSpec(t.shape, lambda i: (0, 0, 0)) for t in tables]
        + [column_spec(a.shape) for a in args],
        out_specs=[column_spec(o.shape) for o in outs],
        out_shape=outs,
        compiler_params=pltpu.CompilerParams(vmem_limit_bytes=vmem_bytes),
        cost_estimate=estimate(flops, [*args, *outs]),
    )(*[jnp.asarray(t) for t in tables], *args)


def project(places, firsts, seconds, out_weight, dtype):
    length, width = firsts[0].shape
    channels = out_weight.shape[0]
    out = jax.ShapeDtypeStruct((length, channels), dtype)
    pieces = [firsts[0], seconds[0], firsts[1], seconds[1]]
    grid_spec = pltpu.PrefetchScalarGridSpec(
        num_scalar_prefetch=1,
        grid=(channels // lanes,),
        in_specs=[pl.BlockSpec((length, width), lambda i, w: (0, 0))] * 4
        + [
            pl.BlockSpec((lanes, width), lambda i, w: (i, w[1])),
            pl.BlockSpec((lanes, width), lambda i, w: (i, w[2])),
        ],
        out_specs=pl.BlockSpec((length, lanes), lambda i, w: (0, i)),
    )
    return pl.pallas_call(
        project_kernel,
        grid_spec=grid_spec,
        out_shape=out,
        compiler_params=pltpu.CompilerParams(vmem_limit_bytes=vmem_bytes),
        cost_estimate=estimate(2 * length * out_weight.size, [*pieces, out_weight, out]),
    )(places, *pieces, out_weight, out_weight)


def weight_sum(places, cot_pieces, gated_pieces, half, rows, dtype):
    count = len(gated_pieces)
    _, length, width = gated_pieces[0].shape
    out = jax.ShapeDtypeStruct((rows, width), dtype)

    def cot_spec(n):
        return pl.BlockSpec((1, rows, length), lambda i, w: (w[n], w[count], 0))

    def gated_spec(piece):
        place = half if piece.shape[0] > 1 else 0
        return pl.BlockSpec((1, length, lanes), lambda i, w: (place, 0, i))

    grid_spec = pltpu.PrefetchScalarGridSpec(
        num_scalar_prefetch=1,
        grid=(width // lanes,),
        in_specs=[cot_spec(n) for n in range(count)]
        + [gated_spec(piece) for piece in gated_pieces],
        out_specs=pl.BlockSpec((rows, lanes), lambda i, w: (0, i)),
    )
    return pl.pallas_call(
        functools.partial(weight_kernel, count),
        grid_spec=grid_spec,
        out_shape=out,
        compiler_params=pltpu.CompilerParams(vmem_limit_bytes=vmem_bytes),
        cost_estimate=estimate(2 * count * length * rows * width, [cot_pieces, *gated_pieces, out]),
    )(places, *([cot_pieces] * count), *gated_pieces)


def swap_pairs(value, axis, distance):
    count = lax.axis_size(axis)
    return lax.ppermute(value, axis, [(i, i ^ distance) for i in range(count)])


def after(value, *earlier):
    return lax.optimization_barrier((value, *earlier))[0]


def per_device(query_gate, key_gate, value_input, filter_taps, skip_gain, out_weight, cotangent):
    queries, key_rows, value_rows, cot = (
        query_gate[0],
        key_gate[0],
        value_input[0],
        cotangent[0],
    )
    length, channels = queries.shape
    taps = filter_taps.shape[1]
    n_seq, n_tp, n_dp = lax.axis_size("seq"), lax.axis_size("tp"), lax.axis_size("dp")
    subs = n_tp // n_dp
    me_tp, me_dp = lax.axis_index("tp"), lax.axis_index("dp")
    me_half, me_sub = me_tp // subs, me_tp % subs
    size = length + taps
    norm_factor = 1.0 / math.sqrt(length * n_seq * n_dp)

    whole = analysis_table(size, np.arange(size))
    scale = 2.0 / size
    own_table = split_table(whole[:, :length])
    tap_table = split_table(whole[:, :taps])
    late_table = split_table(whole[:, length:])
    shifted_table = split_table(whole[:, taps:])
    synth_fwd = np.ascontiguousarray(split_table(whole[:, taps:].T))
    synth_bwd = np.ascontiguousarray(split_table(whole[:, :length].T))
    synth_lag = np.ascontiguousarray(split_table(analysis_table(size, np.arange(taps) - taps).T))
    spectrum = jax.ShapeDtypeStruct((size, channels), f32)
    rows16 = jax.ShapeDtypeStruct((length, channels), bf16)
    rows32 = jax.ShapeDtypeStruct((length, channels), f32)
    unit = 2 * size * channels

    tail = (
        key_rows[length - taps :].astype(f32) * value_rows[length - taps :].astype(f32)
    ).astype(bf16)
    prior = lax.ppermute(tail, "seq", [(i, i + 1) for i in range(n_seq - 1)])

    def tp_dp(half, sub, replica):
        return (half * subs + sub) * n_dp + replica

    places = [(h, c, d) for h in range(n_dp) for c in range(subs) for d in range(n_dp)]
    rounds = []
    for turn in range(2):
        route = [(tp_dp(h, c, d), tp_dp(d ^ turn, c, h)) for h, c, d in places]
        rounds.append(lax.ppermute(cot, ("tp", "dp"), route))
    square = n_seq == n_tp
    if square:
        holder = [(s % n_dp) * subs + s // n_dp for s in range(n_seq)]
        route = [(s * n_tp + t, t * n_tp + holder[s]) for s in range(n_seq) for t in range(n_tp)]
        moved = lax.ppermute(cot.T, ("seq", "tp"), route)
    else:
        moved = cot

    own_spec, filt = by_channel(
        functools.partial(prepare_kernel, scale),
        [shifted_table, tap_table],
        [key_rows, value_rows, filter_taps, skip_gain[None]],
        [spectrum, spectrum],
        channels,
        2 * unit * (length + taps),
    )
    prior, moved, own_spec, filt, *rounds = lax.optimization_barrier(
        (prior, moved, own_spec, filt, *rounds)
    )
    mixed_spec, state, gated = by_channel(
        state_kernel,
        [tap_table, synth_fwd],
        [prior, own_spec, filt, queries],
        [spectrum, rows32, jax.ShapeDtypeStruct((2, length, channels // 2), bf16)],
        channels,
        unit * (2 * taps + 3 * length),
    )

    route = [(tp_dp(h, c, d), tp_dp(h, (c + 1) % subs, d)) for h, c, d in places]
    theirs = [lax.ppermute(r, ("tp", "dp"), route) for r in rounds]
    gated, *theirs = lax.optimization_barrier((gated, *theirs))
    firsts, seconds = zip(rounds, theirs)
    same = (me_half == me_dp).astype(jnp.int32)
    subs_of = [me_sub, (me_sub + 1) % subs]
    other_sent = project(jnp.stack([same, *subs_of]).astype(jnp.int32), firsts, seconds, out_weight, bf16)
    other_part = swap_pairs(other_sent, "dp", 1)

    rows = n_tp * channels // (n_seq * n_dp)
    own_place = jnp.stack([1 - same, *subs_of]).astype(jnp.int32)
    if square:
        order = [*range(0, n_seq, 2), *reversed(range(1, n_seq, 2))]
        ring = [(order[k], order[(k + 1) % n_seq]) for k in range(n_seq)]
        pieces = [gated, lax.ppermute(gated, "seq", ring)]
        pieces[1], own_place = lax.optimization_barrier((pieces[1], own_place))
    own_part = project(own_place, firsts, seconds, out_weight, f32)

    if square:
        cot_pieces = lax.all_gather(moved, "tp", axis=0)
        table = np.zeros((n_seq, n_seq), np.int32)
        for k, s in enumerate(order):
            table[s] = [holder[order[k - r]] for r in range(n_seq)]
        sources = jnp.asarray(table)[lax.axis_index("seq")]
        for _ in range(n_seq - 3):
            pieces.append(lax.ppermute(pieces[-1], "seq", ring))

        def weight_half(half):
            held = [*pieces, lax.ppermute(pieces[-1][half : half + 1], "seq", ring)]

            def part(replica, dtype):
                where = jnp.concatenate([sources, replica[None].astype(jnp.int32)])
                return weight_sum(where, cot_pieces, held, half, rows, dtype)

            sent = swap_pairs(part(1 - me_dp, bf16), "dp", 1)
            return (part(me_dp, f32) + sent.astype(f32)) * norm_factor

        def weight_all():
            return jnp.concatenate([weight_half(0), weight_half(1)], axis=1)

    else:
        full = lax.all_gather(cot, "tp", axis=1, tiled=True)
        cot_all = lax.all_to_all(full, "seq", 1, 0, tiled=True)
        gated_all = lax.all_gather(gated, "seq", axis=1, tiled=True)

        def part(replica, piece):
            block = lax.dynamic_slice_in_dim(cot_all, replica * rows, rows, axis=1)
            return lax.dot_general(
                block, piece, (((0,), (0,)), ((), ())), preferred_element_type=f32
            )

        def weight_one(piece):
            sent = swap_pairs(part(1 - me_dp, piece).astype(bf16), "dp", 1)
            return (part(me_dp, piece) + sent.astype(f32)) * norm_factor

        def weight_all():
            return jnp.concatenate([weight_one(gated_all[0]), weight_one(gated_all[1])], axis=1)

    grad_gated = own_part + other_part.astype(f32)
    grad_query = (grad_gated * state).astype(bf16)
    signal = (grad_gated * queries.astype(f32)).astype(bf16)
    later = lax.ppermute(signal[:taps], "seq", [(i + 1, i) for i in range(n_seq - 1)])
    signal_spec, lags = by_channel(
        lag_kernel,
        [own_table, synth_lag],
        [signal, mixed_spec],
        [spectrum, jax.ShapeDtypeStruct((taps, channels), f32)],
        channels,
        unit * (2 * length + 3 * taps),
    )
    if square:
        later, *pieces = lax.optimization_barrier((later, *pieces))
    grad_key, grad_value = by_channel(
        back_kernel,
        [late_table, synth_bwd],
        [signal_spec, later, filt, key_rows, value_rows],
        [rows16, rows16],
        channels,
        unit * (2 * taps + 3 * length),
    )

    share = taps // n_dp
    lag_sum = lax.dynamic_slice_in_dim(lags, me_dp * share, share, axis=0) + swap_pairs(
        lax.dynamic_slice_in_dim(lags, (1 - me_dp) * share, share, axis=0).astype(bf16), "dp", 1
    ).astype(f32)
    lag_sum, grad_key, grad_value = lax.optimization_barrier((lag_sum, grad_key, grad_value))
    distance = 1
    while distance < n_seq:
        rounded = lag_sum.astype(bf16)
        lag_sum = rounded.astype(f32) + swap_pairs(rounded, "seq", distance).astype(f32)
        distance *= 2
    mine = lag_sum.astype(bf16)
    theirs = swap_pairs(mine, "dp", 1)
    first = me_dp == 0
    lag_sum = jnp.concatenate([jnp.where(first, mine, theirs), jnp.where(first, theirs, mine)], axis=0)
    grad_filter = lag_sum.astype(f32).T * (norm_factor * scale)

    grad_weight = weight_all()
    return (
        grad_query[None],
        grad_key[None],
        grad_value[None],
        grad_filter,
        grad_filter[:, 0],
        grad_weight,
    )


def solution(mesh):
    tokens = P("dp", "seq", "tp")
    return jax.shard_map(
        per_device,
        mesh=mesh,
        in_specs=(tokens, tokens, tokens, P("tp", None), P("tp"), P("tp", "dp"), tokens),
        out_specs=(tokens, tokens, tokens, P("tp", None), P("tp"), P(("seq", "dp"), "tp")),
        check_vma=False,
    )
```

```python
import functools
import math

import jax
import jax.numpy as jnp
import ml_dtypes
import numpy as np
from jax import lax
from jax.experimental import pallas as pl
from jax.experimental.pallas import tpu as pltpu
from jax.sharding import PartitionSpec as P

f32, bf16 = jnp.float32, jnp.bfloat16
lanes = 256
vmem_bytes = 58 * 1024 * 1024


def analysis_table(size, positions):
    half = size // 2
    omega = 2.0 * np.pi * (np.arange(half) + 0.5) / size
    angle = omega[:, None] * np.asarray(positions)[None, :]
    return np.concatenate([np.cos(angle), -np.sin(angle)], axis=0)


def split_table(table):
    high = table.astype(ml_dtypes.bfloat16)
    low = (table - high.astype(np.float64)).astype(ml_dtypes.bfloat16)
    return np.stack([high, low])


def split_rows(rows):
    high = rows.astype(bf16)
    return high, (rows - high.astype(f32)).astype(bf16)


def dot(left, right):
    return jnp.dot(left, right, preferred_element_type=f32)


def dot_nt(left, right):
    return lax.dot_general(left, right, (((1,), (1,)), ((), ())), preferred_element_type=f32)


def forward_transform(table, rows):
    return dot(table[0], rows) + dot(table[1], rows)


def inverse_transform(table, spectrum):
    high, low = split_rows(spectrum)
    return dot(table[0], high) + dot(table[0], low) + dot(table[1], high)


def spectrum_product(left, right, conjugate_right):
    half = left.shape[0] // 2
    left_re, left_im = left[:half], left[half:]
    right_re, right_im = right[:half], right[half:]
    if conjugate_right:
        right_im = -right_im
    return jnp.concatenate(
        [left_re * right_re - left_im * right_im, left_re * right_im + left_im * right_re], axis=0
    )


def prepare_kernel(scale, own_table, tap_table, key_ref, value_ref, taps_ref, skip_ref, spec_ref, filt_ref):
    mixed = (key_ref[...].astype(f32) * value_ref[...].astype(f32)).astype(bf16)
    spec_ref[...] = forward_transform(own_table, mixed)
    filt = dot_nt(tap_table[0], taps_ref[...]) + dot_nt(tap_table[1], taps_ref[...])
    half = filt.shape[0] // 2
    filt_ref[:half] = (filt[:half] + skip_ref[...]) * scale
    filt_ref[half:] = filt[half:] * scale


def state_kernel(prior_table, synth, prior_ref, own_ref, filt_ref, query_ref, spec_ref, state_ref, gated_ref):
    spec = own_ref[...] + forward_transform(prior_table, prior_ref[...])
    spec_ref[...] = spec
    state = inverse_transform(synth, spectrum_product(spec, filt_ref[...], False))
    state_ref[...] = state
    gated_ref[0] = (query_ref[...].astype(f32) * state).astype(bf16)


def project_kernel(place_ref, first_mine, second_mine, first_theirs, second_theirs, weight_mine, weight_theirs, out_ref):
    def write(mine, theirs):
        total = dot_nt(mine[...], weight_mine[...]) + dot_nt(theirs[...], weight_theirs[...])
        out_ref[...] = total.astype(out_ref.dtype)

    pl.when(place_ref[0] == 0)(lambda: write(first_mine, first_theirs))
    pl.when(place_ref[0] != 0)(lambda: write(second_mine, second_theirs))


def weight_kernel(count, place_ref, *refs):
    total = None
    for cot_ref, gated_ref in zip(refs[:count], refs[count : 2 * count]):
        part = dot(cot_ref[0], gated_ref[0])
        total = part if total is None else total + part
    refs[-1][...] = total.astype(refs[-1].dtype)


def lag_kernel(own_table, synth, signal_ref, spec_ref, signal_spec_ref, lag_ref):
    signal_spec = forward_transform(own_table, signal_ref[...])
    signal_spec_ref[...] = signal_spec
    lag_ref[...] = inverse_transform(synth, spectrum_product(signal_spec, spec_ref[...], True))


def back_kernel(late_table, synth, own_ref, later_ref, filt_ref, key_ref, value_ref, grad_key_ref, grad_value_ref):
    spec = own_ref[...] + forward_transform(late_table, later_ref[...])
    back = inverse_transform(synth, spectrum_product(spec, filt_ref[...], True))
    grad_key_ref[...] = (back * value_ref[...].astype(f32)).astype(bf16)
    grad_value_ref[...] = (back * key_ref[...].astype(f32)).astype(bf16)


def estimate(flops, arrays):
    moved = sum(a.size * jnp.dtype(a.dtype).itemsize for a in arrays)
    return pl.CostEstimate(flops=flops // 64, bytes_accessed=moved // 64, transcendentals=0)


def by_channel(kernel, tables, args, outs, channels, flops):
    def column_spec(shape):
        if len(shape) == 3:
            per = shape[2] // lanes
            return pl.BlockSpec((1, shape[1], lanes), lambda i: (i // per, 0, i % per))
        if shape[1] != channels:
            return pl.BlockSpec((lanes, shape[1]), lambda i: (i, 0))
        return pl.BlockSpec((shape[0], lanes), lambda i: (0, i))

    return pl.pallas_call(
        kernel,
        grid=(channels // lanes,),
        in_specs=[pl.BlockSpec(t.shape, lambda i: (0, 0, 0)) for t in tables]
        + [column_spec(a.shape) for a in args],
        out_specs=[column_spec(o.shape) for o in outs],
        out_shape=outs,
        compiler_params=pltpu.CompilerParams(vmem_limit_bytes=vmem_bytes),
        cost_estimate=estimate(flops, [*args, *outs]),
    )(*[jnp.asarray(t) for t in tables], *args)


def project(places, firsts, seconds, out_weight, dtype):
    length, width = firsts[0].shape
    channels = out_weight.shape[0]
    out = jax.ShapeDtypeStruct((length, channels), dtype)
    pieces = [firsts[0], seconds[0], firsts[1], seconds[1]]
    grid_spec = pltpu.PrefetchScalarGridSpec(
        num_scalar_prefetch=1,
        grid=(channels // lanes,),
        in_specs=[pl.BlockSpec((length, width), lambda i, w: (0, 0))] * 4
        + [
            pl.BlockSpec((lanes, width), lambda i, w: (i, w[1])),
            pl.BlockSpec((lanes, width), lambda i, w: (i, w[2])),
        ],
        out_specs=pl.BlockSpec((length, lanes), lambda i, w: (0, i)),
    )
    return pl.pallas_call(
        project_kernel,
        grid_spec=grid_spec,
        out_shape=out,
        compiler_params=pltpu.CompilerParams(vmem_limit_bytes=vmem_bytes),
        cost_estimate=estimate(2 * length * out_weight.size, [*pieces, out_weight, out]),
    )(places, *pieces, out_weight, out_weight)


def weight_sum(places, cot_pieces, gated_pieces, half, rows, dtype):
    count = len(gated_pieces)
    _, length, width = gated_pieces[0].shape
    out = jax.ShapeDtypeStruct((rows, width), dtype)

    def cot_spec(n):
        return pl.BlockSpec((1, rows, length), lambda i, w: (w[n], w[count], 0))

    def gated_spec(piece):
        place = half if piece.shape[0] > 1 else 0
        return pl.BlockSpec((1, length, lanes), lambda i, w: (place, 0, i))

    grid_spec = pltpu.PrefetchScalarGridSpec(
        num_scalar_prefetch=1,
        grid=(width // lanes,),
        in_specs=[cot_spec(n) for n in range(count)]
        + [gated_spec(piece) for piece in gated_pieces],
        out_specs=pl.BlockSpec((rows, lanes), lambda i, w: (0, i)),
    )
    return pl.pallas_call(
        functools.partial(weight_kernel, count),
        grid_spec=grid_spec,
        out_shape=out,
        compiler_params=pltpu.CompilerParams(vmem_limit_bytes=vmem_bytes),
        cost_estimate=estimate(2 * count * length * rows * width, [cot_pieces, *gated_pieces, out]),
    )(places, *([cot_pieces] * count), *gated_pieces)


def swap_pairs(value, axis, distance):
    count = lax.axis_size(axis)
    return lax.ppermute(value, axis, [(i, i ^ distance) for i in range(count)])


def after(value, *earlier):
    return lax.optimization_barrier((value, *earlier))[0]


def per_device(query_gate, key_gate, value_input, filter_taps, skip_gain, out_weight, cotangent):
    queries, key_rows, value_rows, cot = (
        query_gate[0],
        key_gate[0],
        value_input[0],
        cotangent[0],
    )
    length, channels = queries.shape
    taps = filter_taps.shape[1]
    n_seq, n_tp, n_dp = lax.axis_size("seq"), lax.axis_size("tp"), lax.axis_size("dp")
    subs = n_tp // n_dp
    me_tp, me_dp = lax.axis_index("tp"), lax.axis_index("dp")
    me_half, me_sub = me_tp // subs, me_tp % subs
    size = length + taps
    norm_factor = 1.0 / math.sqrt(length * n_seq * n_dp)

    whole = analysis_table(size, np.arange(size))
    scale = 2.0 / size
    own_table = split_table(whole[:, :length])
    tap_table = split_table(whole[:, :taps])
    late_table = split_table(whole[:, length:])
    shifted_table = split_table(whole[:, taps:])
    synth_fwd = np.ascontiguousarray(split_table(whole[:, taps:].T))
    synth_bwd = np.ascontiguousarray(split_table(whole[:, :length].T))
    synth_lag = np.ascontiguousarray(split_table(analysis_table(size, np.arange(taps) - taps).T))
    spectrum = jax.ShapeDtypeStruct((size, channels), f32)
    rows16 = jax.ShapeDtypeStruct((length, channels), bf16)
    rows32 = jax.ShapeDtypeStruct((length, channels), f32)
    unit = 2 * size * channels

    tail = (
        key_rows[length - taps :].astype(f32) * value_rows[length - taps :].astype(f32)
    ).astype(bf16)
    tail, cot = lax.optimization_barrier((tail, cot))
    prior = lax.ppermute(tail, "seq", [(i, i + 1) for i in range(n_seq - 1)])

    def tp_dp(half, sub, replica):
        return (half * subs + sub) * n_dp + replica

    places = [(h, c, d) for h in range(n_dp) for c in range(subs) for d in range(n_dp)]
    rounds = []
    for turn in range(2):
        route = [(tp_dp(h, c, d), tp_dp(d ^ turn, c, h)) for h, c, d in places]
        rounds.append(lax.ppermute(cot, ("tp", "dp"), route))
    square = n_seq == n_tp
    if square:
        holder = [(s % n_dp) * subs + s // n_dp for s in range(n_seq)]
        route = [(s * n_tp + t, t * n_tp + holder[s]) for s in range(n_seq) for t in range(n_tp)]
        moved = lax.ppermute(after(cot, prior).T, ("seq", "tp"), route)
    else:
        moved = cot

    own_spec, filt = by_channel(
        functools.partial(prepare_kernel, scale),
        [shifted_table, tap_table],
        [key_rows, value_rows, filter_taps, skip_gain[None]],
        [spectrum, spectrum],
        channels,
        2 * unit * (length + taps),
    )
    prior, own_spec, filt, *rounds = lax.optimization_barrier((prior, own_spec, filt, *rounds))
    mixed_spec, state, gated = by_channel(
        state_kernel,
        [tap_table, synth_fwd],
        [prior, own_spec, filt, queries],
        [spectrum, rows32, jax.ShapeDtypeStruct((2, length, channels // 2), bf16)],
        channels,
        unit * (2 * taps + 3 * length),
    )

    route = [(tp_dp(h, c, d), tp_dp(h, (c + 1) % subs, d)) for h, c, d in places]
    theirs = [lax.ppermute(r, ("tp", "dp"), route) for r in rounds]
    gated, moved, *theirs = lax.optimization_barrier((gated, moved, *theirs))
    firsts, seconds = zip(rounds, theirs)
    same = (me_half == me_dp).astype(jnp.int32)
    subs_of = [me_sub, (me_sub + 1) % subs]
    other_sent = project(jnp.stack([same, *subs_of]).astype(jnp.int32), firsts, seconds, out_weight, bf16)
    other_part = swap_pairs(other_sent, "dp", 1)

    rows = n_tp * channels // (n_seq * n_dp)
    own_place = jnp.stack([1 - same, *subs_of]).astype(jnp.int32)
    if square:
        order = [*range(0, n_seq, 2), *reversed(range(1, n_seq, 2))]
        ring = [(order[k], order[(k + 1) % n_seq]) for k in range(n_seq)]
        pieces = [gated, lax.ppermute(gated, "seq", ring)]
        pieces[1], own_place = lax.optimization_barrier((pieces[1], own_place))
    own_part = project(own_place, firsts, seconds, out_weight, f32)

    if square:
        cot_pieces = lax.all_gather(moved, "tp", axis=0)
        table = np.zeros((n_seq, n_seq), np.int32)
        for k, s in enumerate(order):
            table[s] = [holder[order[k - r]] for r in range(n_seq)]
        sources = jnp.asarray(table)[lax.axis_index("seq")]
        for _ in range(n_seq - 3):
            pieces.append(lax.ppermute(pieces[-1], "seq", ring))

        def weight_half(half):
            held = [*pieces, lax.ppermute(pieces[-1][half : half + 1], "seq", ring)]

            def part(replica, dtype):
                where = jnp.concatenate([sources, replica[None].astype(jnp.int32)])
                return weight_sum(where, cot_pieces, held, half, rows, dtype)

            sent = swap_pairs(part(1 - me_dp, bf16), "dp", 1)
            return (part(me_dp, f32) + sent.astype(f32)) * norm_factor

        def weight_all():
            return jnp.concatenate([weight_half(0), weight_half(1)], axis=1)

    else:
        full = lax.all_gather(cot, "tp", axis=1, tiled=True)
        cot_all = lax.all_to_all(full, "seq", 1, 0, tiled=True)
        gated_all = lax.all_gather(gated, "seq", axis=1, tiled=True)

        def part(replica, piece):
            block = lax.dynamic_slice_in_dim(cot_all, replica * rows, rows, axis=1)
            return lax.dot_general(
                block, piece, (((0,), (0,)), ((), ())), preferred_element_type=f32
            )

        def weight_one(piece):
            sent = swap_pairs(part(1 - me_dp, piece).astype(bf16), "dp", 1)
            return (part(me_dp, piece) + sent.astype(f32)) * norm_factor

        def weight_all():
            return jnp.concatenate([weight_one(gated_all[0]), weight_one(gated_all[1])], axis=1)

    grad_gated = own_part + other_part.astype(f32)
    grad_query = (grad_gated * state).astype(bf16)
    signal = (grad_gated * queries.astype(f32)).astype(bf16)
    later = lax.ppermute(signal[:taps], "seq", [(i + 1, i) for i in range(n_seq - 1)])
    signal_spec, lags = by_channel(
        lag_kernel,
        [own_table, synth_lag],
        [signal, mixed_spec],
        [spectrum, jax.ShapeDtypeStruct((taps, channels), f32)],
        channels,
        unit * (2 * length + 3 * taps),
    )
    grad_key, grad_value = by_channel(
        back_kernel,
        [late_table, synth_bwd],
        [signal_spec, later, filt, key_rows, value_rows],
        [rows16, rows16],
        channels,
        unit * (2 * taps + 3 * length),
    )

    share = taps // n_dp
    lag_sum = lax.dynamic_slice_in_dim(lags, me_dp * share, share, axis=0) + swap_pairs(
        lax.dynamic_slice_in_dim(lags, (1 - me_dp) * share, share, axis=0).astype(bf16), "dp", 1
    ).astype(f32)
    distance = 1
    while distance < n_seq:
        rounded = lag_sum.astype(bf16)
        lag_sum = rounded.astype(f32) + swap_pairs(rounded, "seq", distance).astype(f32)
        distance *= 2
    mine = lag_sum.astype(bf16)
    theirs = swap_pairs(mine, "dp", 1)
    first = me_dp == 0
    lag_sum = jnp.concatenate([jnp.where(first, mine, theirs), jnp.where(first, theirs, mine)], axis=0)
    grad_filter = lag_sum.astype(f32).T * (norm_factor * scale)

    grad_weight = weight_all()
    return (
        grad_query[None],
        grad_key[None],
        grad_value[None],
        grad_filter,
        grad_filter[:, 0],
        grad_weight,
    )


def solution(mesh):
    tokens = P("dp", "seq", "tp")
    return jax.shard_map(
        per_device,
        mesh=mesh,
        in_specs=(tokens, tokens, tokens, P("tp", None), P("tp"), P("tp", "dp"), tokens),
        out_specs=(tokens, tokens, tokens, P("tp", None), P("tp"), P(("seq", "dp"), "tp")),
        check_vma=False,
    )
```

```python
import functools
import math

import jax
import jax.numpy as jnp
import ml_dtypes
import numpy as np
from jax import lax
from jax.experimental import pallas as pl
from jax.experimental.pallas import tpu as pltpu
from jax.sharding import PartitionSpec as P

f32, bf16 = jnp.float32, jnp.bfloat16
lanes = 256
vmem_bytes = 32 * 1024 * 1024


def analysis_table(size, positions):
    half = size // 2
    omega = 2.0 * np.pi * (np.arange(half) + 0.5) / size
    angle = omega[:, None] * np.asarray(positions)[None, :]
    return np.concatenate([np.cos(angle), -np.sin(angle)], axis=0)


def split_table(table):
    high = table.astype(ml_dtypes.bfloat16)
    low = (table - high.astype(np.float64)).astype(ml_dtypes.bfloat16)
    return np.stack([high, low])


def split_rows(rows):
    high = rows.astype(bf16)
    return high, (rows - high.astype(f32)).astype(bf16)


def dot(left, right):
    return jnp.dot(left, right, preferred_element_type=f32)


def dot_nt(left, right):
    return lax.dot_general(left, right, (((1,), (1,)), ((), ())), preferred_element_type=f32)


def forward_transform(table, rows, start):
    columns = pl.ds(start, rows.shape[0])
    return dot(table[0, :, columns], rows) + dot(table[1, :, columns], rows)


def inverse_transform(table, spectrum, start, count):
    high, low = split_rows(spectrum)
    rows = pl.ds(start, count)
    upper = table[0, rows]
    return dot(upper, high) + dot(upper, low) + dot(table[1, rows], high)


def spectrum_product(left, right, conjugate_right):
    half = left.shape[0] // 2
    left_re, left_im = left[:half], left[half:]
    right_re, right_im = right[:half], right[half:]
    if conjugate_right:
        right_im = -right_im
    return jnp.concatenate(
        [left_re * right_re - left_im * right_im, left_re * right_im + left_im * right_re], axis=0
    )


def prepare_kernel(scale, table, key_ref, value_ref, taps_ref, skip_ref, spec_ref, filt_ref):
    mixed = (key_ref[...].astype(f32) * value_ref[...].astype(f32)).astype(bf16)
    taps = taps_ref.shape[1]
    spec_ref[...] = forward_transform(table, mixed, taps)
    filt = dot_nt(table[0, :, :taps], taps_ref[...]) + dot_nt(table[1, :, :taps], taps_ref[...])
    half = filt.shape[0] // 2
    filt_ref[:half] = (filt[:half] + skip_ref[...]) * scale
    filt_ref[half:] = filt[half:] * scale


def state_kernel(table, synth, prior_ref, own_ref, filt_ref, query_ref, spec_ref, state_ref, gated_ref):
    spec = own_ref[...] + forward_transform(table, prior_ref[...], 0)
    spec_ref[...] = spec
    product = spectrum_product(spec, filt_ref[...], False)
    state = inverse_transform(synth, product, prior_ref.shape[0], query_ref.shape[0])
    state_ref[...] = state
    gated_ref[0] = (query_ref[...].astype(f32) * state).astype(bf16)


def transpose_kernel(rows_ref, out_ref):
    out_ref[...] = rows_ref[...].T


def project_kernel(place_ref, first_mine, second_mine, first_theirs, second_theirs, weight_mine, weight_theirs, out_ref):
    def write(mine, theirs):
        total = dot_nt(mine[...], weight_mine[...]) + dot_nt(theirs[...], weight_theirs[...])
        out_ref[...] = total.astype(out_ref.dtype)

    pl.when(place_ref[0] == 0)(lambda: write(first_mine, first_theirs))
    pl.when(place_ref[0] != 0)(lambda: write(second_mine, second_theirs))


def weight_kernel(count, place_ref, *refs):
    total = None
    for cot_ref, gated_ref in zip(refs[:count], refs[count : 2 * count]):
        part = dot(cot_ref[0], gated_ref[0])
        total = part if total is None else total + part
    refs[-1][...] = total.astype(refs[-1].dtype)


def lag_kernel(table, synth, signal_ref, spec_ref, signal_spec_ref, lag_ref):
    length, taps = signal_ref.shape[0], lag_ref.shape[0]
    signal_spec = forward_transform(table, signal_ref[...], 0)
    signal_spec_ref[...] = signal_spec
    product = spectrum_product(signal_spec, spec_ref[...], True)
    lag_ref[...] = -inverse_transform(synth, product, length, taps)


def back_kernel(table, synth, own_ref, later_ref, filt_ref, key_ref, value_ref, grad_key_ref, grad_value_ref):
    length = key_ref.shape[0]
    spec = own_ref[...] + forward_transform(table, later_ref[...], length)
    back = inverse_transform(synth, spectrum_product(spec, filt_ref[...], True), 0, length)
    grad_key_ref[...] = (back * value_ref[...].astype(f32)).astype(bf16)
    grad_value_ref[...] = (back * key_ref[...].astype(f32)).astype(bf16)


def estimate(flops, arrays):
    moved = sum(a.size * jnp.dtype(a.dtype).itemsize for a in arrays)
    return pl.CostEstimate(flops=flops, bytes_accessed=moved, transcendentals=0)


def by_channel(kernel, tables, args, outs, channels, flops):
    def column_spec(shape):
        if len(shape) == 3:
            per = shape[2] // lanes
            return pl.BlockSpec((1, shape[1], lanes), lambda i: (i // per, 0, i % per))
        if shape[1] != channels:
            return pl.BlockSpec((lanes, shape[1]), lambda i: (i, 0))
        return pl.BlockSpec((shape[0], lanes), lambda i: (0, i))

    return pl.pallas_call(
        kernel,
        grid=(channels // lanes,),
        in_specs=[pl.BlockSpec(t.shape, lambda i: (0, 0, 0)) for t in tables]
        + [column_spec(a.shape) for a in args],
        out_specs=[column_spec(o.shape) for o in outs],
        out_shape=outs,
        compiler_params=pltpu.CompilerParams(vmem_limit_bytes=vmem_bytes),
        cost_estimate=estimate(flops, [*args, *outs]),
    )(*[jnp.asarray(t) for t in tables], *args)


def project(places, firsts, seconds, out_weight, dtype):
    length, width = firsts[0].shape
    channels = out_weight.shape[0]
    out = jax.ShapeDtypeStruct((length, channels), dtype)
    pieces = [firsts[0], seconds[0], firsts[1], seconds[1]]
    grid_spec = pltpu.PrefetchScalarGridSpec(
        num_scalar_prefetch=1,
        grid=(channels // lanes,),
        in_specs=[pl.BlockSpec((length, width), lambda i, w: (0, 0))] * 4
        + [
            pl.BlockSpec((lanes, width), lambda i, w: (i, w[1])),
            pl.BlockSpec((lanes, width), lambda i, w: (i, w[2])),
        ],
        out_specs=pl.BlockSpec((length, lanes), lambda i, w: (0, i)),
    )
    return pl.pallas_call(
        project_kernel,
        grid_spec=grid_spec,
        out_shape=out,
        compiler_params=pltpu.CompilerParams(vmem_limit_bytes=vmem_bytes),
        cost_estimate=estimate(2 * length * out_weight.size, [*pieces, out_weight, out]),
    )(places, *pieces, out_weight, out_weight)


def weight_sum(places, cot_pieces, gated_pieces, half, rows, dtype):
    count = len(gated_pieces)
    _, length, width = gated_pieces[0].shape
    out = jax.ShapeDtypeStruct((rows, width), dtype)

    def cot_spec(n):
        return pl.BlockSpec((1, rows, length), lambda i, w: (w[n], w[count], 0))

    def gated_spec(piece):
        place = half if piece.shape[0] > 1 else 0
        return pl.BlockSpec((1, length, lanes), lambda i, w: (place, 0, i))

    grid_spec = pltpu.PrefetchScalarGridSpec(
        num_scalar_prefetch=1,
        grid=(width // lanes,),
        in_specs=[cot_spec(n) for n in range(count)]
        + [gated_spec(piece) for piece in gated_pieces],
        out_specs=pl.BlockSpec((rows, lanes), lambda i, w: (0, i)),
    )
    return pl.pallas_call(
        functools.partial(weight_kernel, count),
        grid_spec=grid_spec,
        out_shape=out,
        compiler_params=pltpu.CompilerParams(vmem_limit_bytes=vmem_bytes),
        cost_estimate=estimate(2 * count * length * rows * width, [cot_pieces, *gated_pieces, out]),
    )(places, *([cot_pieces] * count), *gated_pieces)


def swap_pairs(value, axis, distance):
    count = lax.axis_size(axis)
    return lax.ppermute(value, axis, [(i, i ^ distance) for i in range(count)])


def after(value, *earlier):
    return lax.optimization_barrier((value, *earlier))[0]


def per_device(query_gate, key_gate, value_input, filter_taps, skip_gain, out_weight, cotangent):
    queries, key_rows, value_rows, cot = (
        query_gate[0],
        key_gate[0],
        value_input[0],
        cotangent[0],
    )
    length, channels = queries.shape
    taps = filter_taps.shape[1]
    n_seq, n_tp, n_dp = lax.axis_size("seq"), lax.axis_size("tp"), lax.axis_size("dp")
    subs = n_tp // n_dp
    me_tp, me_dp = lax.axis_index("tp"), lax.axis_index("dp")
    me_half, me_sub = me_tp // subs, me_tp % subs
    size = length + taps
    norm_factor = 1.0 / math.sqrt(length * n_seq * n_dp)

    whole = analysis_table(size, np.arange(size))
    scale = 2.0 / size
    tables = [split_table(whole), np.ascontiguousarray(split_table(whole.T))]
    spectrum = jax.ShapeDtypeStruct((size, channels), f32)
    rows16 = jax.ShapeDtypeStruct((length, channels), bf16)
    rows32 = jax.ShapeDtypeStruct((length, channels), f32)
    unit = 2 * size * channels

    tail = (
        key_rows[length - taps :].astype(f32) * value_rows[length - taps :].astype(f32)
    ).astype(bf16)
    tail, cot = lax.optimization_barrier((tail, cot))
    prior = lax.ppermute(tail, "seq", [(i, i + 1) for i in range(n_seq - 1)])

    def tp_dp(half, sub, replica):
        return (half * subs + sub) * n_dp + replica

    places = [(h, c, d) for h in range(n_dp) for c in range(subs) for d in range(n_dp)]
    rounds = []
    for turn in range(2):
        route = [(tp_dp(h, c, d), tp_dp(d ^ turn, c, h)) for h, c, d in places]
        rounds.append(lax.ppermute(cot, ("tp", "dp"), route))
    square = n_seq == n_tp == 4 and subs == 2
    if square:

        def holder(s, block):
            return (s + block) % 2 * subs + s // 2

        crossed = {0: (1, 2), 1: (0, 3)}
        route = [
            (s * n_tp + t, s * n_tp + sum(crossed[s % 2]) - t)
            for s in range(n_seq)
            for t in crossed[s % 2]
        ]
        cot_rows = pl.pallas_call(
            transpose_kernel,
            grid=(cot.shape[1] // lanes,),
            in_specs=[pl.BlockSpec((length, lanes), lambda i: (0, i))],
            out_specs=pl.BlockSpec((lanes, length), lambda i: (i, 0)),
            out_shape=jax.ShapeDtypeStruct(cot.shape[::-1], bf16),
            compiler_params=pltpu.CompilerParams(vmem_limit_bytes=vmem_bytes),
            cost_estimate=estimate(0, [cot, cot]),
        )(cot)
        swapped = lax.ppermute(cot_rows, ("seq", "tp"), route)
        moves_now = sum(
            jnp.logical_and(lax.axis_index("seq") % 2 == parity, me_tp == t)
            for parity in crossed
            for t in crossed[parity]
        )
        held = jnp.where(moves_now > 0, swapped, cot_rows)
        route = []
        for s in range(n_seq):
            for t in range(n_tp):
                block = sum(crossed[s % 2]) - t if t in crossed[s % 2] else t
                route.append((s * n_tp + t, block * n_tp + holder(s, block)))
        moved = lax.ppermute(held, ("seq", "tp"), route)
    else:
        moved = cot

    own_spec, filt = by_channel(
        functools.partial(prepare_kernel, scale),
        tables[:1],
        [key_rows, value_rows, filter_taps, skip_gain[None]],
        [spectrum, spectrum],
        channels,
        2 * unit * (length + taps),
    )
    prior, own_spec, filt, *rounds = lax.optimization_barrier((prior, own_spec, filt, *rounds))
    mixed_spec, state, gated = by_channel(
        state_kernel,
        tables,
        [prior, own_spec, filt, queries],
        [spectrum, rows32, jax.ShapeDtypeStruct((2, length, channels // 2), bf16)],
        channels,
        unit * (2 * taps + 3 * length),
    )

    route = [(tp_dp(h, c, d), tp_dp(h, (c + 1) % subs, d)) for h, c, d in places]
    theirs = [lax.ppermute(r, ("tp", "dp"), route) for r in rounds]
    gated, moved, *theirs = lax.optimization_barrier((gated, moved, *theirs))
    firsts, seconds = zip(rounds, theirs)
    same = (me_half == me_dp).astype(jnp.int32)
    subs_of = [me_sub, (me_sub + 1) % subs]
    other_sent = project(jnp.stack([same, *subs_of]).astype(jnp.int32), firsts, seconds, out_weight, bf16)
    other_part = swap_pairs(other_sent, "dp", 1)

    rows = n_tp * channels // (n_seq * n_dp)
    own_place = jnp.stack([1 - same, *subs_of]).astype(jnp.int32)
    if square:
        order = [*range(0, n_seq, 2), *reversed(range(1, n_seq, 2))]
        ring = [(order[k], order[(k + 1) % n_seq]) for k in range(n_seq)]
        pieces = [gated, lax.ppermute(gated, "seq", ring)]
        pieces[1], own_place = lax.optimization_barrier((pieces[1], own_place))
    own_part = project(own_place, firsts, seconds, out_weight, f32)

    if square:
        cot_pieces = lax.all_gather(moved, "tp", axis=0)
        table = np.zeros((n_seq, n_seq), np.int32)
        for k, s in enumerate(order):
            table[s] = [holder(order[k - r], s) for r in range(n_seq)]
        sources = jnp.asarray(table)[lax.axis_index("seq")]
        for _ in range(n_seq - 3):
            pieces.append(lax.ppermute(pieces[-1], "seq", ring))

        def weight_half(half):
            held = [*pieces, lax.ppermute(pieces[-1][half : half + 1], "seq", ring)]

            def part(replica, dtype):
                where = jnp.concatenate([sources, replica[None].astype(jnp.int32)])
                return weight_sum(where, cot_pieces, held, half, rows, dtype)

            sent = swap_pairs(part(1 - me_dp, bf16), "dp", 1)
            return (part(me_dp, f32) + sent.astype(f32)) * norm_factor

        def weight_all():
            return jnp.concatenate([weight_half(0), weight_half(1)], axis=1)

    else:
        full = lax.all_gather(cot, "tp", axis=1, tiled=True)
        cot_all = lax.all_to_all(full, "seq", 1, 0, tiled=True)
        gated_all = lax.all_gather(gated, "seq", axis=1, tiled=True)

        def part(replica, piece):
            block = lax.dynamic_slice_in_dim(cot_all, replica * rows, rows, axis=1)
            return lax.dot_general(
                block, piece, (((0,), (0,)), ((), ())), preferred_element_type=f32
            )

        def weight_one(piece):
            sent = swap_pairs(part(1 - me_dp, piece).astype(bf16), "dp", 1)
            return (part(me_dp, piece) + sent.astype(f32)) * norm_factor

        def weight_all():
            return jnp.concatenate([weight_one(gated_all[0]), weight_one(gated_all[1])], axis=1)

    grad_gated = own_part + other_part.astype(f32)
    grad_query = (grad_gated * state).astype(bf16)
    signal = (grad_gated * queries.astype(f32)).astype(bf16)
    later = lax.ppermute(signal[:taps], "seq", [(i + 1, i) for i in range(n_seq - 1)])
    signal_spec, lags = by_channel(
        lag_kernel,
        tables,
        [signal, mixed_spec],
        [spectrum, jax.ShapeDtypeStruct((taps, channels), f32)],
        channels,
        unit * (2 * length + 3 * taps),
    )
    grad_key, grad_value = by_channel(
        back_kernel,
        tables,
        [signal_spec, later, filt, key_rows, value_rows],
        [rows16, rows16],
        channels,
        unit * (2 * taps + 3 * length),
    )

    share = taps // n_dp
    lag_sum = lax.dynamic_slice_in_dim(lags, me_dp * share, share, axis=0) + swap_pairs(
        lax.dynamic_slice_in_dim(lags, (1 - me_dp) * share, share, axis=0).astype(bf16), "dp", 1
    ).astype(f32)
    if square:
        lag_sum, *pieces = lax.optimization_barrier((lag_sum, *pieces))
    distance = 1
    while distance < n_seq:
        rounded = lag_sum.astype(bf16)
        lag_sum = rounded.astype(f32) + swap_pairs(rounded, "seq", distance).astype(f32)
        distance *= 2
    mine = lag_sum.astype(bf16)
    theirs = swap_pairs(mine, "dp", 1)
    first = me_dp == 0
    lag_sum = jnp.concatenate([jnp.where(first, mine, theirs), jnp.where(first, theirs, mine)], axis=0)
    grad_filter = lag_sum.astype(f32).T * (norm_factor * scale)

    grad_weight = weight_all()
    return (
        grad_query[None],
        grad_key[None],
        grad_value[None],
        grad_filter,
        grad_filter[:, 0],
        grad_weight,
    )


def solution(mesh):
    tokens = P("dp", "seq", "tp")
    return jax.shard_map(
        per_device,
        mesh=mesh,
        in_specs=(tokens, tokens, tokens, P("tp", None), P("tp"), P("tp", "dp"), tokens),
        out_specs=(tokens, tokens, tokens, P("tp", None), P("tp"), P(("seq", "dp"), "tp")),
        check_vma=False,
    )
```

```python
import functools
import math

import jax
import jax.numpy as jnp
import ml_dtypes
import numpy as np
from jax import lax
from jax.experimental import pallas as pl
from jax.experimental.pallas import tpu as pltpu
from jax.sharding import PartitionSpec as P

f32, bf16 = jnp.float32, jnp.bfloat16
lanes = 256
vmem_bytes = 32 * 1024 * 1024


def analysis_table(size, positions):
    half = size // 2
    omega = 2.0 * np.pi * (np.arange(half) + 0.5) / size
    angle = omega[:, None] * np.asarray(positions)[None, :]
    return np.concatenate([np.cos(angle), -np.sin(angle)], axis=0)


def split_table(table):
    high = table.astype(ml_dtypes.bfloat16)
    low = (table - high.astype(np.float64)).astype(ml_dtypes.bfloat16)
    return np.stack([high, low])


def split_rows(rows):
    high = rows.astype(bf16)
    return high, (rows - high.astype(f32)).astype(bf16)


def dot(left, right):
    return jnp.dot(left, right, preferred_element_type=f32)


def dot_nt(left, right):
    return lax.dot_general(left, right, (((1,), (1,)), ((), ())), preferred_element_type=f32)


def forward_transform(table, rows, start):
    columns = pl.ds(start, rows.shape[0])
    return dot(table[0, :, columns], rows) + dot(table[1, :, columns], rows)


def inverse_transform(table, spectrum, start, count):
    high, low = split_rows(spectrum)
    rows = pl.ds(start, count)
    upper = table[0, rows]
    return dot(upper, high) + dot(upper, low) + dot(table[1, rows], high)


def spectrum_product(left, right, conjugate_right):
    half = left.shape[0] // 2
    left_re, left_im = left[:half], left[half:]
    right_re, right_im = right[:half], right[half:]
    if conjugate_right:
        right_im = -right_im
    return jnp.concatenate(
        [left_re * right_re - left_im * right_im, left_re * right_im + left_im * right_re], axis=0
    )


def mixed_spectrum(table, prior_ref, key_ref, value_ref):
    mixed = (key_ref[...].astype(f32) * value_ref[...].astype(f32)).astype(bf16)
    prior = prior_ref[...]
    return forward_transform(table, prior, 0) + forward_transform(table, mixed, prior.shape[0])


def filter_spectrum(scale, table, taps_ref, skip_ref):
    taps = taps_ref.shape[1]
    filt = dot_nt(table[0, :, :taps], taps_ref[...]) + dot_nt(table[1, :, :taps], taps_ref[...])
    half = filt.shape[0] // 2
    return jnp.concatenate([(filt[:half] + skip_ref[...]) * scale, filt[half:] * scale], axis=0)


def state_kernel(
    scale, table, synth, prior_ref, key_ref, value_ref, taps_ref, skip_ref, query_ref, state_ref, first_ref, second_ref
):
    spec = mixed_spectrum(table, prior_ref, key_ref, value_ref)
    product = spectrum_product(spec, filter_spectrum(scale, table, taps_ref, skip_ref), False)
    state = inverse_transform(synth, product, prior_ref.shape[0], query_ref.shape[0])
    state_ref[...] = state
    gated = (query_ref[...].astype(f32) * state).astype(bf16)
    in_first = pl.program_id(0) < pl.num_programs(0) // 2

    @pl.when(in_first)
    def _():
        first_ref[...] = gated

    @pl.when(jnp.logical_not(in_first))
    def _():
        second_ref[...] = gated


def transpose_kernel(rows_ref, out_ref):
    out_ref[...] = rows_ref[...].T


def project_kernel(place_ref, first_mine, second_mine, first_theirs, second_theirs, weight_mine, weight_theirs, out_ref):
    def write(mine, theirs):
        total = dot_nt(mine[...], weight_mine[...]) + dot_nt(theirs[...], weight_theirs[...])
        out_ref[...] = total.astype(out_ref.dtype)

    pl.when(place_ref[0] == 0)(lambda: write(first_mine, first_theirs))
    pl.when(place_ref[0] != 0)(lambda: write(second_mine, second_theirs))


def weight_kernel(count, place_ref, *refs):
    out_ref, held_ref = refs[2 * count :]
    for n, gated_ref in enumerate(refs[count : 2 * count]):
        held_ref[n] = gated_ref[...]
    total = None
    for n, cot_ref in enumerate(refs[:count]):
        part = dot(cot_ref[...], held_ref[place_ref[n]])
        total = part if total is None else total + part
    out_ref[...] = total.astype(out_ref.dtype)


def lag_kernel(
    table, synth, own_ref, other_ref, state_ref, query_ref, prior_ref, key_ref, value_ref, grad_ref, signal_ref, lag_ref
):
    length, taps = signal_ref.shape[0], lag_ref.shape[0]
    grad_gated = own_ref[...] + other_ref[...].astype(f32)
    grad_ref[...] = (grad_gated * state_ref[...]).astype(bf16)
    signal = (grad_gated * query_ref[...].astype(f32)).astype(bf16)
    signal_ref[...] = signal
    spec = mixed_spectrum(table, prior_ref, key_ref, value_ref)
    product = spectrum_product(forward_transform(table, signal, 0), spec, True)
    lag_ref[...] = -inverse_transform(synth, product, length, taps)


def back_kernel(
    scale, table, synth, signal_ref, later_ref, taps_ref, skip_ref, key_ref, value_ref, grad_key_ref, grad_value_ref
):
    length = key_ref.shape[0]
    spec = forward_transform(table, signal_ref[...], 0) + forward_transform(table, later_ref[...], length)
    product = spectrum_product(spec, filter_spectrum(scale, table, taps_ref, skip_ref), True)
    back = inverse_transform(synth, product, 0, length)
    grad_key_ref[...] = (back * value_ref[...].astype(f32)).astype(bf16)
    grad_value_ref[...] = (back * key_ref[...].astype(f32)).astype(bf16)


def estimate(flops, arrays):
    moved = sum(a.size * jnp.dtype(a.dtype).itemsize for a in arrays)
    return pl.CostEstimate(flops=flops, bytes_accessed=moved, transcendentals=0)


def by_channel(kernel, tables, args, outs, channels, flops):
    steps = channels // lanes

    def column_spec(shape, place=0):
        if shape[1] == channels // 2:
            shift = place % 2 * (steps // 2)
            return pl.BlockSpec(
                (shape[0], lanes), lambda i: (0, jnp.clip(i - shift, 0, steps // 2 - 1))
            )
        if shape[1] != channels:
            return pl.BlockSpec((lanes, shape[1]), lambda i: (i, 0))
        return pl.BlockSpec((shape[0], lanes), lambda i: (0, i))

    return pl.pallas_call(
        kernel,
        grid=(steps,),
        in_specs=[pl.BlockSpec(t.shape, lambda i: (0, 0, 0)) for t in tables]
        + [column_spec(a.shape) for a in args],
        out_specs=[column_spec(o.shape, n + 1) for n, o in enumerate(outs)],
        out_shape=outs,
        compiler_params=pltpu.CompilerParams(vmem_limit_bytes=vmem_bytes),
        cost_estimate=estimate(flops, [*args, *outs]),
    )(*[jnp.asarray(t) for t in tables], *args)


def project(places, firsts, seconds, out_weight, dtype):
    length, width = firsts[0].shape
    channels = out_weight.shape[0]
    out = jax.ShapeDtypeStruct((length, channels), dtype)
    pieces = [firsts[0], seconds[0], firsts[1], seconds[1]]
    grid_spec = pltpu.PrefetchScalarGridSpec(
        num_scalar_prefetch=1,
        grid=(channels // lanes,),
        in_specs=[pl.BlockSpec((length, width), lambda i, w: (0, 0))] * 4
        + [
            pl.BlockSpec((lanes, width), lambda i, w: (i, w[1])),
            pl.BlockSpec((lanes, width), lambda i, w: (i, w[2])),
        ],
        out_specs=pl.BlockSpec((length, lanes), lambda i, w: (0, i)),
    )
    return pl.pallas_call(
        project_kernel,
        grid_spec=grid_spec,
        out_shape=out,
        compiler_params=pltpu.CompilerParams(vmem_limit_bytes=vmem_bytes),
        cost_estimate=estimate(2 * length * out_weight.size, [*pieces, out_weight, out]),
    )(places, *pieces, out_weight, out_weight)


def weight_sum(places, cot_pieces, gated_pieces, rows, dtype):
    count = len(gated_pieces)
    length, width = gated_pieces[0].shape
    out = jax.ShapeDtypeStruct((rows, width), dtype)

    grid_spec = pltpu.PrefetchScalarGridSpec(
        num_scalar_prefetch=1,
        grid=(width // lanes,),
        in_specs=[pl.BlockSpec((rows, length), lambda i, w: (w[count], 0))] * count
        + [pl.BlockSpec((length, lanes), lambda i, w: (0, i))] * count,
        out_specs=pl.BlockSpec((rows, lanes), lambda i, w: (0, i)),
        scratch_shapes=[pltpu.VMEM((count, length, lanes), bf16)],
    )
    return pl.pallas_call(
        functools.partial(weight_kernel, count),
        grid_spec=grid_spec,
        out_shape=out,
        compiler_params=pltpu.CompilerParams(vmem_limit_bytes=vmem_bytes),
        cost_estimate=estimate(2 * count * length * rows * width, [*cot_pieces, *gated_pieces, out]),
    )(places, *cot_pieces, *gated_pieces)


def swap_pairs(value, axis, distance):
    count = lax.axis_size(axis)
    return lax.ppermute(value, axis, [(i, i ^ distance) for i in range(count)])


def after(value, *earlier):
    return lax.optimization_barrier((value, *earlier))[0]


def per_device(query_gate, key_gate, value_input, filter_taps, skip_gain, out_weight, cotangent):
    queries, key_rows, value_rows, cot = (
        query_gate[0],
        key_gate[0],
        value_input[0],
        cotangent[0],
    )
    length, channels = queries.shape
    taps = filter_taps.shape[1]
    n_seq, n_tp, n_dp = lax.axis_size("seq"), lax.axis_size("tp"), lax.axis_size("dp")
    subs = n_tp // n_dp
    me_tp, me_dp = lax.axis_index("tp"), lax.axis_index("dp")
    me_half, me_sub = me_tp // subs, me_tp % subs
    size = length + taps
    norm_factor = 1.0 / math.sqrt(length * n_seq * n_dp)

    whole = analysis_table(size, np.arange(size))
    scale = 2.0 / size
    tables = [split_table(whole), np.ascontiguousarray(split_table(whole.T))]
    rows16 = jax.ShapeDtypeStruct((length, channels), bf16)
    rows32 = jax.ShapeDtypeStruct((length, channels), f32)
    half16 = jax.ShapeDtypeStruct((length, channels // 2), bf16)
    unit = 2 * size * channels

    tail = (
        key_rows[length - taps :].astype(f32) * value_rows[length - taps :].astype(f32)
    ).astype(bf16)
    tail, cot = lax.optimization_barrier((tail, cot))
    prior = lax.ppermute(tail, "seq", [(i, i + 1) for i in range(n_seq - 1)])

    def tp_dp(half, sub, replica):
        return (half * subs + sub) * n_dp + replica

    places = [(h, c, d) for h in range(n_dp) for c in range(subs) for d in range(n_dp)]
    rounds = []
    for turn in range(2):
        route = [(tp_dp(h, c, d), tp_dp(d ^ turn, c, h)) for h, c, d in places]
        rounds.append(lax.ppermute(cot, ("tp", "dp"), route))
    square = n_seq == n_tp == 4 and subs == 2
    if square:

        def holder(s, block):
            return (s + block) % 2 * subs + s // 2

        crossed = {0: (1, 2), 1: (0, 3)}
        route = [
            (s * n_tp + t, s * n_tp + sum(crossed[s % 2]) - t)
            for s in range(n_seq)
            for t in crossed[s % 2]
        ]
        cot_rows = pl.pallas_call(
            transpose_kernel,
            grid=(cot.shape[1] // lanes,),
            in_specs=[pl.BlockSpec((length, lanes), lambda i: (0, i))],
            out_specs=pl.BlockSpec((lanes, length), lambda i: (i, 0)),
            out_shape=jax.ShapeDtypeStruct(cot.shape[::-1], bf16),
            compiler_params=pltpu.CompilerParams(vmem_limit_bytes=vmem_bytes),
            cost_estimate=estimate(0, [cot, cot]),
        )(cot)
        swapped = lax.ppermute(cot_rows, ("seq", "tp"), route)
        moves_now = sum(
            jnp.logical_and(lax.axis_index("seq") % 2 == parity, me_tp == t)
            for parity in crossed
            for t in crossed[parity]
        )
        held = jnp.where(moves_now > 0, swapped, cot_rows)
        route = []
        for s in range(n_seq):
            for t in range(n_tp):
                block = sum(crossed[s % 2]) - t if t in crossed[s % 2] else t
                route.append((s * n_tp + t, block * n_tp + holder(s, block)))
        moved = lax.ppermute(held, ("seq", "tp"), route)
    else:
        moved = cot

    state, *gated = by_channel(
        functools.partial(state_kernel, scale),
        tables,
        [prior, key_rows, value_rows, filter_taps, skip_gain[None], queries],
        [rows32, half16, half16],
        channels,
        unit * (4 * taps + 5 * length),
    )
    gated[0], gated[1], *rounds = lax.optimization_barrier((*gated, *rounds))

    route = [(tp_dp(h, c, d), tp_dp(h, (c + 1) % subs, d)) for h, c, d in places]
    theirs = [lax.ppermute(r, ("tp", "dp"), route) for r in rounds]
    firsts, seconds = zip(rounds, theirs)
    same = (me_half == me_dp).astype(jnp.int32)
    subs_of = [me_sub, (me_sub + 1) % subs]
    other_place = jnp.stack([same, *subs_of]).astype(jnp.int32)
    rows = n_tp * channels // (n_seq * n_dp)
    own_place = jnp.stack([1 - same, *subs_of]).astype(jnp.int32)
    if square:
        order = [*range(0, n_seq, 2), *reversed(range(1, n_seq, 2))]
        ring = [(order[k], order[(k + 1) % n_seq]) for k in range(n_seq)]
        halves = [[half] for half in gated]

        def ring_step(pieces):
            pieces.append(lax.ppermute(pieces[-1], "seq", ring))

        ring_step(halves[0])
        halves[0][1], other_place = lax.optimization_barrier((halves[0][1], other_place))
        ring_step(halves[0])
        halves[0][2], own_place = lax.optimization_barrier((halves[0][2], own_place))
        ring_step(halves[0])
        ring_step(halves[1])
    other_sent = project(other_place, firsts, seconds, out_weight, bf16)
    other_part = swap_pairs(other_sent, "dp", 1)
    own_part = project(own_place, firsts, seconds, out_weight, f32)

    if square:
        sent_by = lambda value, flip: lax.ppermute(value, "tp", [(t, t ^ flip) for t in range(n_tp)])
        across = sent_by(moved, subs)
        cot_pieces = [moved, sent_by(moved, 1), across, sent_by(across, 1)]
        table = np.zeros((n_seq, n_tp, n_tp), np.int32)
        for k, s in enumerate(order):
            for r in range(n_seq):
                for t in range(n_tp):
                    table[s, t, t ^ holder(order[k - r], s)] = r
        sources = jnp.asarray(table)[lax.axis_index("seq"), me_tp]
        halves[0][3], own_part = lax.optimization_barrier((halves[0][3], own_part))
        ring_step(halves[1])

        def weight_half(held):
            def part(replica, dtype):
                where = jnp.concatenate([sources, replica[None].astype(jnp.int32)])
                return weight_sum(where, cot_pieces, held, rows, dtype)

            return part

        def weight_all():
            sent = [first_sent, weight_half(halves[1])(1 - me_dp, bf16)]
            sent = [swap_pairs(value, "dp", 1) for value in sent]
            return jnp.concatenate(
                [
                    (weight_half(held)(me_dp, f32) + value.astype(f32)) * norm_factor
                    for held, value in zip(halves, sent)
                ],
                axis=1,
            )

    else:
        full = lax.all_gather(cot, "tp", axis=1, tiled=True)
        cot_all = lax.all_to_all(full, "seq", 1, 0, tiled=True)
        gated_all = [lax.all_gather(half, "seq", axis=0, tiled=True) for half in gated]

        def part(replica, piece):
            block = lax.dynamic_slice_in_dim(cot_all, replica * rows, rows, axis=1)
            return lax.dot_general(
                block, piece, (((0,), (0,)), ((), ())), preferred_element_type=f32
            )

        def weight_one(piece):
            sent = swap_pairs(part(1 - me_dp, piece).astype(bf16), "dp", 1)
            return (part(me_dp, piece) + sent.astype(f32)) * norm_factor

        def weight_all():
            return jnp.concatenate([weight_one(gated_all[0]), weight_one(gated_all[1])], axis=1)

    grad_query, signal, lags = by_channel(
        lag_kernel,
        tables,
        [own_part, other_part, state, queries, prior, key_rows, value_rows],
        [rows16, rows16, jax.ShapeDtypeStruct((taps, channels), f32)],
        channels,
        unit * (2 * taps + 4 * length + 3 * taps),
    )
    later = lax.ppermute(signal[:taps], "seq", [(i + 1, i) for i in range(n_seq - 1)])
    grad_key, grad_value = by_channel(
        functools.partial(back_kernel, scale),
        tables,
        [signal, later, filter_taps, skip_gain[None], key_rows, value_rows],
        [rows16, rows16],
        channels,
        unit * (4 * taps + 5 * length),
    )

    share = taps // n_dp
    lag_sum = lax.dynamic_slice_in_dim(lags, me_dp * share, share, axis=0) + swap_pairs(
        lax.dynamic_slice_in_dim(lags, (1 - me_dp) * share, share, axis=0).astype(bf16), "dp", 1
    ).astype(f32)
    if square:
        halves[1][2], lag_sum = lax.optimization_barrier((halves[1][2], lag_sum))
        ring_step(halves[1])
        first_sent = weight_half(halves[0])(1 - me_dp, bf16)
    distance = 1
    while distance < n_seq:
        rounded = lag_sum.astype(bf16)
        lag_sum = rounded.astype(f32) + swap_pairs(rounded, "seq", distance).astype(f32)
        if square and distance == 1:
            first_sent, lag_sum = lax.optimization_barrier((first_sent, lag_sum))
        distance *= 2
    mine = lag_sum.astype(bf16)
    theirs = swap_pairs(mine, "dp", 1)
    first = me_dp == 0
    lag_sum = jnp.concatenate([jnp.where(first, mine, theirs), jnp.where(first, theirs, mine)], axis=0)
    grad_filter = lag_sum.astype(f32).T * (norm_factor * scale)

    grad_weight = weight_all()
    return (
        grad_query[None],
        grad_key[None],
        grad_value[None],
        grad_filter,
        grad_filter[:, 0],
        grad_weight,
    )


def solution(mesh):
    tokens = P("dp", "seq", "tp")
    return jax.shard_map(
        per_device,
        mesh=mesh,
        in_specs=(tokens, tokens, tokens, P("tp", None), P("tp"), P("tp", "dp"), tokens),
        out_specs=(tokens, tokens, tokens, P("tp", None), P("tp"), P(("seq", "dp"), "tp")),
        check_vma=False,
    )
```

```python
import functools
import math

import jax
import jax.numpy as jnp
import ml_dtypes
import numpy as np
from jax import lax
from jax.experimental import pallas as pl
from jax.experimental.pallas import tpu as pltpu
from jax.sharding import PartitionSpec as P

f32, bf16 = jnp.float32, jnp.bfloat16
lanes = 256
vmem_bytes = 58 * 1024 * 1024


def analysis_table(size, positions):
    half = size // 2
    omega = 2.0 * np.pi * (np.arange(half) + 0.5) / size
    angle = omega[:, None] * np.asarray(positions)[None, :]
    return np.concatenate([np.cos(angle), -np.sin(angle)], axis=0)


def split_table(table):
    high = table.astype(ml_dtypes.bfloat16)
    low = (table - high.astype(np.float64)).astype(ml_dtypes.bfloat16)
    return np.stack([high, low])


def split_rows(rows):
    high = rows.astype(bf16)
    return high, (rows - high.astype(f32)).astype(bf16)


def dot(left, right):
    return jnp.dot(left, right, preferred_element_type=f32)


def dot_nt(left, right):
    return lax.dot_general(left, right, (((1,), (1,)), ((), ())), preferred_element_type=f32)


def forward_transform(table, rows, start):
    columns = pl.ds(start, rows.shape[0])
    return dot(table[0, :, columns], rows) + dot(table[1, :, columns], rows)


def inverse_transform(table, spectrum, start, count):
    high, low = split_rows(spectrum)
    rows = pl.ds(start, count)
    upper = table[0, rows]
    return dot(upper, high) + dot(upper, low) + dot(table[1, rows], high)


def spectrum_product(left, right, conjugate_right):
    half = left.shape[0] // 2
    left_re, left_im = left[:half], left[half:]
    right_re, right_im = right[:half], right[half:]
    if conjugate_right:
        right_im = -right_im
    return jnp.concatenate(
        [left_re * right_re - left_im * right_im, left_re * right_im + left_im * right_re], axis=0
    )


def mixed_spectrum(table, prior_ref, key_ref, value_ref):
    mixed = (key_ref[...].astype(f32) * value_ref[...].astype(f32)).astype(bf16)
    prior = prior_ref[...]
    return forward_transform(table, prior, 0) + forward_transform(table, mixed, prior.shape[0])


def filter_spectrum(scale, table, taps_ref, skip_ref):
    taps = taps_ref.shape[1]
    filt = dot_nt(table[0, :, :taps], taps_ref[...]) + dot_nt(table[1, :, :taps], taps_ref[...])
    half = filt.shape[0] // 2
    return jnp.concatenate([(filt[:half] + skip_ref[...]) * scale, filt[half:] * scale], axis=0)


def state_kernel(
    scale, table, synth, prior_ref, key_ref, value_ref, taps_ref, skip_ref, query_ref, state_ref, gated_ref
):
    spec = mixed_spectrum(table, prior_ref, key_ref, value_ref)
    product = spectrum_product(spec, filter_spectrum(scale, table, taps_ref, skip_ref), False)
    state = inverse_transform(synth, product, prior_ref.shape[0], query_ref.shape[0])
    state_ref[...] = state
    gated_ref[...] = (query_ref[...].astype(f32) * state).astype(bf16)


def transpose_kernel(rows_ref, out_ref):
    out_ref[...] = rows_ref[...].T


def project_kernel(
    place_ref, first_mine, second_mine, first_theirs, second_theirs, weight, out, pieces, blocks, totals, piece_sem, block_sem, out_sem
):
    steps, _, _, width = blocks.shape

    def piece_copy(n, source):
        return pltpu.make_async_copy(source, pieces.at[n], piece_sem.at[n])

    def block_copy(n, i):
        rows = pl.ds(pl.multiple_of(i * lanes, lanes), lanes)
        columns = pl.ds(pl.multiple_of(place_ref[1 + n] * width, width), width)
        return pltpu.make_async_copy(weight.at[rows, columns], blocks.at[i, n], block_sem.at[i, n])

    def out_copy(i):
        place = out.at[:, pl.ds(pl.multiple_of(i * lanes, lanes), lanes)]
        return pltpu.make_async_copy(totals.at[i], place, out_sem.at[i])

    @pl.when(place_ref[0] == 0)
    def _():
        piece_copy(0, first_mine).start()
        piece_copy(1, first_theirs).start()

    @pl.when(place_ref[0] != 0)
    def _():
        piece_copy(0, second_mine).start()
        piece_copy(1, second_theirs).start()

    for i in range(steps):
        for n in range(2):
            block_copy(n, i).start()
    for n in range(2):
        piece_copy(n, first_mine).wait()

    @pl.loop(0, steps)
    def _(i):
        for n in range(2):
            block_copy(n, i).wait()
        total = dot_nt(pieces[0], blocks[i, 0]) + dot_nt(pieces[1], blocks[i, 1])
        totals[i] = total.astype(totals.dtype)
        out_copy(i).start()

    for i in range(steps):
        out_copy(i).wait()


def weight_kernel(count, place_ref, *refs):
    out_ref, held_ref = refs[2 * count :]
    for n, gated_ref in enumerate(refs[count : 2 * count]):
        held_ref[n] = gated_ref[...]
    total = None
    for n, cot_ref in enumerate(refs[:count]):
        part = dot(cot_ref[...], held_ref[place_ref[n]])
        total = part if total is None else total + part
    out_ref[...] = total.astype(out_ref.dtype)


def lag_kernel(
    table, synth, own_ref, other_ref, state_ref, query_ref, prior_ref, key_ref, value_ref, grad_ref, signal_ref, lag_ref
):
    length, taps = signal_ref.shape[0], lag_ref.shape[0]
    grad_gated = own_ref[...] + other_ref[...].astype(f32)
    grad_ref[...] = (grad_gated * state_ref[...]).astype(bf16)
    signal = (grad_gated * query_ref[...].astype(f32)).astype(bf16)
    signal_ref[...] = signal
    spec = mixed_spectrum(table, prior_ref, key_ref, value_ref)
    product = spectrum_product(forward_transform(table, signal, 0), spec, True)
    lag_ref[...] = -inverse_transform(synth, product, length, taps)


def back_kernel(
    scale, table, synth, signal_ref, later_ref, taps_ref, skip_ref, key_ref, value_ref, grad_key_ref, grad_value_ref
):
    length = key_ref.shape[0]
    spec = forward_transform(table, signal_ref[...], 0) + forward_transform(table, later_ref[...], length)
    product = spectrum_product(spec, filter_spectrum(scale, table, taps_ref, skip_ref), True)
    back = inverse_transform(synth, product, 0, length)
    grad_key_ref[...] = (back * value_ref[...].astype(f32)).astype(bf16)
    grad_value_ref[...] = (back * key_ref[...].astype(f32)).astype(bf16)


def estimate(flops, arrays):
    moved = sum(a.size * jnp.dtype(a.dtype).itemsize for a in arrays)
    return pl.CostEstimate(flops=flops, bytes_accessed=moved, transcendentals=0)


def by_channel(body, tables, args, outs, channels, flops):
    steps = channels // lanes
    flat_outs = [o for group in outs for o in group]
    n_tables, n_args, n_outs = len(tables), len(args), len(outs)

    def part(ref, i, count):
        start = pl.multiple_of(i * lanes, lanes)
        if ref.shape[1] == count * lanes:
            return ref.at[:, pl.ds(start, lanes)]
        return ref.at[pl.ds(start, lanes), :]

    def kernel(*refs):
        refs = list(refs)
        take = lambda count: [refs.pop(0) for _ in range(count)]
        table_in, arg_in, outs_to = take(n_tables), take(n_args), take(len(flat_outs))
        table_held, arg_held, out_held = take(n_tables), take(n_args), take(n_outs)
        table_sem, arg_sem, out_sem = refs
        groups = [[outs_to.pop(0) for _ in group] for group in outs]

        def table_copy(k):
            return pltpu.make_async_copy(table_in[k], table_held[k], table_sem.at[k])

        def arg_copy(k, i):
            return pltpu.make_async_copy(part(arg_in[k], i, steps), arg_held[k].at[i], arg_sem.at[k, i])

        def out_copy(k, n, i):
            per = steps // len(groups[k])
            place = part(groups[k][n], i - n * per, per)
            return pltpu.make_async_copy(out_held[k].at[i], place, out_sem.at[k, i])

        for k in range(n_tables):
            table_copy(k).start()
        for i in range(steps):
            for k in range(n_args):
                arg_copy(k, i).start()
        for k in range(n_tables):
            table_copy(k).wait()

        for n in range(max(len(group) for group in groups)):
            per = steps // max(len(group) for group in groups)

            @pl.loop(n * per, (n + 1) * per)
            def _(i):
                for k in range(n_args):
                    arg_copy(k, i).wait()
                body(*table_held, *[held.at[i] for held in arg_held], *[held.at[i] for held in out_held])
                for k in range(n_outs):
                    out_copy(k, min(n, len(groups[k]) - 1), i).start()

        for i in range(steps):
            for k in range(n_outs):
                out_copy(k, i * len(groups[k]) // steps, i).wait()

    def held(value):
        if value.shape[1] in (channels, channels // 2):
            return pltpu.VMEM((steps, value.shape[0], lanes), value.dtype)
        return pltpu.VMEM((steps, lanes, value.shape[1]), value.dtype)

    return pl.pallas_call(
        kernel,
        in_specs=[pl.BlockSpec(memory_space=pl.ANY)] * (n_tables + n_args),
        out_specs=[pl.BlockSpec(memory_space=pl.ANY)] * len(flat_outs),
        out_shape=flat_outs,
        scratch_shapes=[
            *[pltpu.VMEM(t.shape, bf16) for t in tables],
            *[held(a) for a in args],
            *[held(group[0]) for group in outs],
            pltpu.SemaphoreType.DMA((n_tables,)),
            pltpu.SemaphoreType.DMA((n_args, steps)),
            pltpu.SemaphoreType.DMA((n_outs, steps)),
        ],
        compiler_params=pltpu.CompilerParams(vmem_limit_bytes=vmem_bytes),
        cost_estimate=estimate(flops, [*args, *flat_outs]),
    )(*[jnp.asarray(t) for t in tables], *args)


def project(places, firsts, seconds, out_weight, dtype):
    length, width = firsts[0].shape
    channels = out_weight.shape[0]
    steps = channels // lanes
    out = jax.ShapeDtypeStruct((length, channels), dtype)
    pieces = [firsts[0], seconds[0], firsts[1], seconds[1]]
    return pl.pallas_call(
        project_kernel,
        in_specs=[pl.BlockSpec(memory_space=pltpu.SMEM)] + [pl.BlockSpec(memory_space=pl.ANY)] * 5,
        out_specs=pl.BlockSpec(memory_space=pl.ANY),
        out_shape=out,
        scratch_shapes=[
            pltpu.VMEM((2, length, width), bf16),
            pltpu.VMEM((steps, 2, lanes, width), bf16),
            pltpu.VMEM((steps, length, lanes), dtype),
            pltpu.SemaphoreType.DMA((2,)),
            pltpu.SemaphoreType.DMA((steps, 2)),
            pltpu.SemaphoreType.DMA((steps,)),
        ],
        compiler_params=pltpu.CompilerParams(vmem_limit_bytes=vmem_bytes),
        cost_estimate=estimate(2 * length * out_weight.size, [*pieces, out_weight, out]),
    )(places, *pieces, out_weight)


def weight_sum(places, cot_pieces, gated_pieces, rows, dtype):
    count = len(gated_pieces)
    length, width = gated_pieces[0].shape
    out = jax.ShapeDtypeStruct((rows, width), dtype)

    grid_spec = pltpu.PrefetchScalarGridSpec(
        num_scalar_prefetch=1,
        grid=(width // lanes,),
        in_specs=[pl.BlockSpec((rows, length), lambda i, w: (w[count], 0), pipeline_mode=pl.Buffered(1))] * count
        + [pl.BlockSpec((length, lanes), lambda i, w: (0, i))] * count,
        out_specs=pl.BlockSpec((rows, lanes), lambda i, w: (0, i)),
        scratch_shapes=[pltpu.VMEM((count, length, lanes), bf16)],
    )
    return pl.pallas_call(
        functools.partial(weight_kernel, count),
        grid_spec=grid_spec,
        out_shape=out,
        compiler_params=pltpu.CompilerParams(vmem_limit_bytes=vmem_bytes),
        cost_estimate=estimate(2 * count * length * rows * width, [*cot_pieces, *gated_pieces, out]),
    )(places, *cot_pieces, *gated_pieces)


def swap_pairs(value, axis, distance):
    count = lax.axis_size(axis)
    return lax.ppermute(value, axis, [(i, i ^ distance) for i in range(count)])


def after(value, *earlier):
    return lax.optimization_barrier((value, *earlier))[0]


def per_device(query_gate, key_gate, value_input, filter_taps, skip_gain, out_weight, cotangent):
    queries, key_rows, value_rows, cot = (
        query_gate[0],
        key_gate[0],
        value_input[0],
        cotangent[0],
    )
    length, channels = queries.shape
    taps = filter_taps.shape[1]
    n_seq, n_tp, n_dp = lax.axis_size("seq"), lax.axis_size("tp"), lax.axis_size("dp")
    subs = n_tp // n_dp
    me_tp, me_dp = lax.axis_index("tp"), lax.axis_index("dp")
    me_half, me_sub = me_tp // subs, me_tp % subs
    size = length + taps
    norm_factor = 1.0 / math.sqrt(length * n_seq * n_dp)

    whole = analysis_table(size, np.arange(size))
    scale = 2.0 / size
    tables = [split_table(whole), np.ascontiguousarray(split_table(whole.T))]
    rows16 = jax.ShapeDtypeStruct((length, channels), bf16)
    rows32 = jax.ShapeDtypeStruct((length, channels), f32)
    half16 = jax.ShapeDtypeStruct((length, channels // 2), bf16)
    unit = 2 * size * channels

    tail = (
        key_rows[length - taps :].astype(f32) * value_rows[length - taps :].astype(f32)
    ).astype(bf16)
    tail, cot = lax.optimization_barrier((tail, cot))
    prior = lax.ppermute(tail, "seq", [(i, i + 1) for i in range(n_seq - 1)])

    def tp_dp(half, sub, replica):
        return (half * subs + sub) * n_dp + replica

    places = [(h, c, d) for h in range(n_dp) for c in range(subs) for d in range(n_dp)]
    rounds = []
    for turn in range(2):
        route = [(tp_dp(h, c, d), tp_dp(d ^ turn, c, h)) for h, c, d in places]
        rounds.append(lax.ppermute(cot, ("tp", "dp"), route))
    square = n_seq == n_tp == 4 and subs == 2
    if square:

        def holder(s, block):
            return (s + block) % 2 * subs + s // 2

        crossed = {0: (1, 2), 1: (0, 3)}
        route = [
            (s * n_tp + t, s * n_tp + sum(crossed[s % 2]) - t)
            for s in range(n_seq)
            for t in crossed[s % 2]
        ]
        cot_rows = pl.pallas_call(
            transpose_kernel,
            grid=(cot.shape[1] // lanes,),
            in_specs=[pl.BlockSpec((length, lanes), lambda i: (0, i))],
            out_specs=pl.BlockSpec((lanes, length), lambda i: (i, 0)),
            out_shape=jax.ShapeDtypeStruct(cot.shape[::-1], bf16),
            compiler_params=pltpu.CompilerParams(vmem_limit_bytes=vmem_bytes),
            cost_estimate=estimate(0, [cot, cot]),
        )(cot)
        swapped = lax.ppermute(cot_rows, ("seq", "tp"), route)
        moves_now = sum(
            jnp.logical_and(lax.axis_index("seq") % 2 == parity, me_tp == t)
            for parity in crossed
            for t in crossed[parity]
        )
        held = jnp.where(moves_now > 0, swapped, cot_rows)
        route = []
        for s in range(n_seq):
            for t in range(n_tp):
                block = sum(crossed[s % 2]) - t if t in crossed[s % 2] else t
                route.append((s * n_tp + t, block * n_tp + holder(s, block)))
        moved = lax.ppermute(after(held, prior), ("seq", "tp"), route)
    else:
        moved = cot

    state, *gated = by_channel(
        functools.partial(state_kernel, scale),
        tables,
        [prior, key_rows, value_rows, filter_taps, skip_gain[None], queries],
        [[rows32], [half16, half16]],
        channels,
        unit * (4 * taps + 5 * length),
    )
    gated[0], gated[1], moved, *rounds = lax.optimization_barrier((*gated, moved, *rounds))

    route = [(tp_dp(h, c, d), tp_dp(h, (c + 1) % subs, d)) for h, c, d in places]
    theirs = [lax.ppermute(r, ("tp", "dp"), route) for r in rounds]
    firsts, seconds = zip(rounds, theirs)
    same = (me_half == me_dp).astype(jnp.int32)
    subs_of = [me_sub, (me_sub + 1) % subs]
    other_place = jnp.stack([same, *subs_of]).astype(jnp.int32)
    rows = n_tp * channels // (n_seq * n_dp)
    own_place = jnp.stack([1 - same, *subs_of]).astype(jnp.int32)
    if square:
        order = [*range(0, n_seq, 2), *reversed(range(1, n_seq, 2))]
        ring = [(order[k], order[(k + 1) % n_seq]) for k in range(n_seq)]
        halves = [[half] for half in gated]

        def ring_step(pieces):
            pieces.append(lax.ppermute(pieces[-1], "seq", ring))

        ring_step(halves[0])
        halves[0][1], other_place = lax.optimization_barrier((halves[0][1], other_place))
        ring_step(halves[0])
        halves[0][2], own_place = lax.optimization_barrier((halves[0][2], own_place))
        ring_step(halves[0])
        ring_step(halves[1])
    other_sent = project(other_place, firsts, seconds, out_weight, bf16)
    other_part = swap_pairs(other_sent, "dp", 1)
    own_part = project(own_place, firsts, seconds, out_weight, f32)

    if square:
        sent_by = lambda value, flip: lax.ppermute(value, "tp", [(t, t ^ flip) for t in range(n_tp)])
        across = sent_by(moved, subs)
        cot_pieces = [moved, sent_by(moved, 1), across, sent_by(across, 1)]
        table = np.zeros((n_seq, n_tp, n_tp), np.int32)
        for k, s in enumerate(order):
            for r in range(n_seq):
                for t in range(n_tp):
                    table[s, t, t ^ holder(order[k - r], s)] = r
        sources = jnp.asarray(table)[lax.axis_index("seq"), me_tp]
        halves[0][3], own_part = lax.optimization_barrier((halves[0][3], own_part))
        ring_step(halves[1])

        def weight_half(held):
            def part(replica, dtype):
                where = jnp.concatenate([sources, replica[None].astype(jnp.int32)])
                return weight_sum(where, cot_pieces, held, rows, dtype)

            return part

        def weight_all():
            sent = [first_received, swap_pairs(weight_half(halves[1])(1 - me_dp, bf16), "dp", 1)]
            return jnp.concatenate(
                [
                    (weight_half(held)(me_dp, f32) + value.astype(f32)) * norm_factor
                    for held, value in zip(halves, sent)
                ],
                axis=1,
            )

    else:
        full = lax.all_gather(cot, "tp", axis=1, tiled=True)
        cot_all = lax.all_to_all(full, "seq", 1, 0, tiled=True)
        gated_all = [lax.all_gather(half, "seq", axis=0, tiled=True) for half in gated]

        def part(replica, piece):
            block = lax.dynamic_slice_in_dim(cot_all, replica * rows, rows, axis=1)
            return lax.dot_general(
                block, piece, (((0,), (0,)), ((), ())), preferred_element_type=f32
            )

        def weight_one(piece):
            sent = swap_pairs(part(1 - me_dp, piece).astype(bf16), "dp", 1)
            return (part(me_dp, piece) + sent.astype(f32)) * norm_factor

        def weight_all():
            return jnp.concatenate([weight_one(gated_all[0]), weight_one(gated_all[1])], axis=1)

    grad_query, signal, lags = by_channel(
        lag_kernel,
        tables,
        [own_part, other_part, state, queries, prior, key_rows, value_rows],
        [[rows16], [rows16], [jax.ShapeDtypeStruct((taps, channels), f32)]],
        channels,
        unit * (2 * taps + 4 * length + 3 * taps),
    )
    later = lax.ppermute(signal[:taps], "seq", [(i + 1, i) for i in range(n_seq - 1)])

    share = taps // n_dp
    lag_sum = lax.dynamic_slice_in_dim(lags, me_dp * share, share, axis=0) + swap_pairs(
        lax.dynamic_slice_in_dim(lags, (1 - me_dp) * share, share, axis=0).astype(bf16), "dp", 1
    ).astype(f32)
    if square:
        halves[1][2], lag_sum = lax.optimization_barrier((halves[1][2], lag_sum))
        ring_step(halves[1])
        first_sent = weight_half(halves[0])(1 - me_dp, bf16)
    distance = 1
    while distance < n_seq:
        rounded = lag_sum.astype(bf16)
        lag_sum = rounded.astype(f32) + swap_pairs(rounded, "seq", distance).astype(f32)
        if square and distance == 1:
            first_sent, lag_sum = lax.optimization_barrier((first_sent, lag_sum))
        distance *= 2
    mine = lag_sum.astype(bf16)
    theirs = swap_pairs(mine, "dp", 1)
    first = me_dp == 0
    lag_sum = jnp.concatenate([jnp.where(first, mine, theirs), jnp.where(first, theirs, mine)], axis=0)
    grad_filter = lag_sum.astype(f32).T * (norm_factor * scale)

    if square:
        first_received = swap_pairs(first_sent, "dp", 1)
        first_received, later = lax.optimization_barrier((first_received, later))
    grad_key, grad_value = by_channel(
        functools.partial(back_kernel, scale),
        tables,
        [signal, later, filter_taps, skip_gain[None], key_rows, value_rows],
        [[rows16], [rows16]],
        channels,
        unit * (4 * taps + 5 * length),
    )
    grad_weight = weight_all()
    return (
        grad_query[None],
        grad_key[None],
        grad_value[None],
        grad_filter,
        grad_filter[:, 0],
        grad_weight,
    )


def solution(mesh):
    tokens = P("dp", "seq", "tp")
    return jax.shard_map(
        per_device,
        mesh=mesh,
        in_specs=(tokens, tokens, tokens, P("tp", None), P("tp"), P("tp", "dp"), tokens),
        out_specs=(tokens, tokens, tokens, P("tp", None), P("tp"), P(("seq", "dp"), "tp")),
        check_vma=False,
    )
```

```python
import functools
import math

import jax
import jax.numpy as jnp
import ml_dtypes
import numpy as np
from jax import lax
from jax.experimental import pallas as pl
from jax.experimental.pallas import tpu as pltpu
from jax.sharding import PartitionSpec as P

f32, bf16 = jnp.float32, jnp.bfloat16
lanes = 256
vmem_bytes = 58 * 1024 * 1024


def analysis_table(size, positions):
    half = size // 2
    omega = 2.0 * np.pi * (np.arange(half) + 0.5) / size
    angle = omega[:, None] * np.asarray(positions)[None, :]
    return np.concatenate([np.cos(angle), -np.sin(angle)], axis=0)


def split_table(table):
    high = table.astype(ml_dtypes.bfloat16)
    low = (table - high.astype(np.float64)).astype(ml_dtypes.bfloat16)
    return np.stack([high, low])


def split_rows(rows):
    high = rows.astype(bf16)
    return high, (rows - high.astype(f32)).astype(bf16)


def dot(left, right):
    return jnp.dot(left, right, preferred_element_type=f32)


def dot_nt(left, right):
    return lax.dot_general(left, right, (((1,), (1,)), ((), ())), preferred_element_type=f32)


def forward_transform(table, rows, start):
    columns = pl.ds(start, rows.shape[0])
    return dot(table[0, :, columns], rows) + dot(table[1, :, columns], rows)


def inverse_transform(table, spectrum, start, count):
    high, low = split_rows(spectrum)
    rows = pl.ds(start, count)
    upper = table[0, rows]
    return dot(upper, high) + dot(upper, low) + dot(table[1, rows], high)


def spectrum_product(left, right, conjugate_right):
    half = left.shape[0] // 2
    left_re, left_im = left[:half], left[half:]
    right_re, right_im = right[:half], right[half:]
    if conjugate_right:
        right_im = -right_im
    return jnp.concatenate(
        [left_re * right_re - left_im * right_im, left_re * right_im + left_im * right_re], axis=0
    )


def mixed_spectrum(table, prior_ref, key_ref, value_ref):
    mixed = (key_ref[...].astype(f32) * value_ref[...].astype(f32)).astype(bf16)
    prior = prior_ref[...]
    return forward_transform(table, prior, 0) + forward_transform(table, mixed, prior.shape[0])


def filter_spectrum(scale, table, taps_ref, skip_ref):
    taps = taps_ref.shape[1]
    filt = dot_nt(table[0, :, :taps], taps_ref[...]) + dot_nt(table[1, :, :taps], taps_ref[...])
    half = filt.shape[0] // 2
    return jnp.concatenate([(filt[:half] + skip_ref[...]) * scale, filt[half:] * scale], axis=0)


def state_kernel(
    scale, table, synth, prior_ref, key_ref, value_ref, taps_ref, skip_ref, query_ref, state_ref, gated_ref
):
    spec = mixed_spectrum(table, prior_ref, key_ref, value_ref)
    product = spectrum_product(spec, filter_spectrum(scale, table, taps_ref, skip_ref), False)
    state = inverse_transform(synth, product, prior_ref.shape[0], query_ref.shape[0])
    state_ref[...] = state
    gated_ref[...] = (query_ref[...].astype(f32) * state).astype(bf16)


def project_kernel(
    place_ref, first_mine, second_mine, first_theirs, second_theirs, weight, other, own, pieces, blocks, others, owns, piece_sem, block_sem, out_sem
):
    steps, _, total_width = blocks.shape
    length, width = first_mine.shape

    def piece_copy(n, sub, source):
        rows = pl.ds(n * length, length)
        columns = pl.ds(pl.multiple_of(place_ref[1 + sub] * width, width), width)
        return pltpu.make_async_copy(source, pieces.at[rows, columns], piece_sem.at[n, sub])

    def block_copy(i):
        return pltpu.make_async_copy(weight.at[pl.ds(i * lanes, lanes)], blocks.at[i], block_sem.at[i])

    def out_copies(i):
        columns = pl.ds(pl.multiple_of(i * lanes, lanes), lanes)
        return [
            pltpu.make_async_copy(others.at[i], other.at[:, columns], out_sem.at[0, i]),
            pltpu.make_async_copy(owns.at[i], own.at[:, columns], out_sem.at[1, i]),
        ]

    for i in range(steps):
        block_copy(i).start()

    def fetch(own_first):
        for sub, (first, second) in enumerate([(first_mine, second_mine), (first_theirs, second_theirs)]):
            piece_copy(0, sub, second if own_first else first).start()
            piece_copy(1, sub, first if own_first else second).start()

    pl.when(place_ref[0] != 0)(lambda: fetch(True))
    pl.when(place_ref[0] == 0)(lambda: fetch(False))
    for n in range(2):
        for sub in range(2):
            piece_copy(n, sub, first_mine).wait()

    @pl.loop(0, steps)
    def _(i):
        block_copy(i).wait()
        total = dot_nt(pieces[...], blocks[i])
        others[i] = total[:length].astype(bf16)
        owns[i] = total[length:]
        for copy in out_copies(i):
            copy.start()

    for i in range(steps):
        for copy in out_copies(i):
            copy.wait()


def weight_kernel(count, place_ref, *refs):
    cot_in, gated_in = refs[:count], refs[count : 2 * count]
    other, own, cots, gateds, others, owns, in_sem, out_sem = refs[2 * count :]
    length = gateds.shape[1]
    rows = other.shape[0]
    block = min(rows, lanes)
    copies = [pltpu.make_async_copy(cot_in[n], cots.at[n], in_sem.at[0, n]) for n in range(count)]
    copies += [pltpu.make_async_copy(gated_in[n], gateds.at[n], in_sem.at[1, n]) for n in range(count)]
    for copy in copies:
        copy.start()
    for copy in copies:
        copy.wait()
    outs = [
        pltpu.make_async_copy(others, other, out_sem.at[0]),
        pltpu.make_async_copy(owns, own, out_sem.at[1]),
    ]

    def fill(replica, target):
        @pl.loop(0, rows // block)
        def _(i):
            start = pl.multiple_of(replica * rows + i * block, block)
            total = None
            for n in range(count):
                part = dot(cots[n, pl.ds(start, block), :], gateds[place_ref[n]])
                total = part if total is None else total + part
            target[pl.ds(pl.multiple_of(i * block, block), block), :] = total.astype(target.dtype)

    me = place_ref[count]
    fill(1 - me, others)
    outs[0].start()
    fill(me, owns)
    outs[1].start()
    for copy in outs:
        copy.wait()


def lag_kernel(
    table, synth, own_ref, other_ref, state_ref, query_ref, prior_ref, key_ref, value_ref, grad_ref, signal_ref, lag_ref
):
    length, taps = signal_ref.shape[0], lag_ref.shape[0]
    grad_gated = own_ref[...] + other_ref[...].astype(f32)
    grad_ref[...] = (grad_gated * state_ref[...]).astype(bf16)
    signal = (grad_gated * query_ref[...].astype(f32)).astype(bf16)
    signal_ref[...] = signal
    spec = mixed_spectrum(table, prior_ref, key_ref, value_ref)
    product = spectrum_product(forward_transform(table, signal, 0), spec, True)
    lag_ref[...] = -inverse_transform(synth, product, length, taps)


def back_kernel(
    scale, table, synth, signal_ref, later_ref, taps_ref, skip_ref, key_ref, value_ref, grad_key_ref, grad_value_ref
):
    length = key_ref.shape[0]
    spec = forward_transform(table, signal_ref[...], 0) + forward_transform(table, later_ref[...], length)
    product = spectrum_product(spec, filter_spectrum(scale, table, taps_ref, skip_ref), True)
    back = inverse_transform(synth, product, 0, length)
    grad_key_ref[...] = (back * value_ref[...].astype(f32)).astype(bf16)
    grad_value_ref[...] = (back * key_ref[...].astype(f32)).astype(bf16)


def estimate(flops, arrays):
    moved = sum(a.size * jnp.dtype(a.dtype).itemsize for a in arrays)
    return pl.CostEstimate(flops=flops, bytes_accessed=moved, transcendentals=0)


def by_channel(body, tables, args, outs, channels, flops):
    steps = channels // lanes
    flat_outs = [o for group in outs for o in group]
    n_tables, n_args, n_outs = len(tables), len(args), len(outs)

    def part(ref, i, count):
        start = pl.multiple_of(i * lanes, lanes)
        if ref.shape[1] == count * lanes:
            return ref.at[:, pl.ds(start, lanes)]
        return ref.at[pl.ds(start, lanes), :]

    def kernel(*refs):
        refs = list(refs)
        take = lambda count: [refs.pop(0) for _ in range(count)]
        table_in, arg_in, outs_to = take(n_tables), take(n_args), take(len(flat_outs))
        table_held, arg_held, out_held = take(n_tables), take(n_args), take(n_outs)
        table_sem, arg_sem, out_sem = refs
        groups = [[outs_to.pop(0) for _ in group] for group in outs]

        def table_copy(k):
            return pltpu.make_async_copy(table_in[k], table_held[k], table_sem.at[k])

        def arg_copy(k):
            return pltpu.make_async_copy(arg_in[k], arg_held[k], arg_sem.at[k])

        def out_copy(k, n, i):
            per = steps // len(groups[k])
            place = part(groups[k][n], i - n * per, per)
            return pltpu.make_async_copy(out_held[k].at[i], place, out_sem.at[k, i])

        for k in range(n_tables):
            table_copy(k).start()
        for k in range(n_args):
            arg_copy(k).start()
        for k in range(n_tables):
            table_copy(k).wait()
        for k in range(n_args):
            arg_copy(k).wait()

        for n in range(max(len(group) for group in groups)):
            per = steps // max(len(group) for group in groups)

            @pl.loop(n * per, (n + 1) * per)
            def _(i):
                body(*table_held, *[part(ref, i, steps) for ref in arg_held], *[held.at[i] for held in out_held])
                for k in range(n_outs):
                    out_copy(k, min(n, len(groups[k]) - 1), i).start()

        for i in range(steps):
            for k in range(n_outs):
                out_copy(k, i * len(groups[k]) // steps, i).wait()

    return pl.pallas_call(
        kernel,
        in_specs=[pl.BlockSpec(memory_space=pl.ANY)] * (n_tables + n_args),
        out_specs=[pl.BlockSpec(memory_space=pl.ANY)] * len(flat_outs),
        out_shape=flat_outs,
        scratch_shapes=[
            *[pltpu.VMEM(t.shape, bf16) for t in tables],
            *[pltpu.VMEM(a.shape, a.dtype) for a in args],
            *[pltpu.VMEM((steps, group[0].shape[0], lanes), group[0].dtype) for group in outs],
            pltpu.SemaphoreType.DMA((n_tables,)),
            pltpu.SemaphoreType.DMA((n_args,)),
            pltpu.SemaphoreType.DMA((n_outs, steps)),
        ],
        compiler_params=pltpu.CompilerParams(vmem_limit_bytes=vmem_bytes),
        cost_estimate=estimate(flops, [*args, *flat_outs]),
    )(*[jnp.asarray(t) for t in tables], *args)


def local_call(kernel, places, args, outs, scratch, flops):
    return pl.pallas_call(
        kernel,
        in_specs=[pl.BlockSpec(memory_space=pltpu.SMEM)] + [pl.BlockSpec(memory_space=pl.ANY)] * len(args),
        out_specs=[pl.BlockSpec(memory_space=pl.ANY)] * len(outs),
        out_shape=outs,
        scratch_shapes=scratch,
        compiler_params=pltpu.CompilerParams(vmem_limit_bytes=vmem_bytes),
        cost_estimate=estimate(flops, [*args, *outs]),
    )(places, *args)


def project(places, firsts, seconds, out_weight):
    length, width = firsts[0].shape
    channels, total_width = out_weight.shape
    steps = channels // lanes
    return local_call(
        project_kernel,
        places,
        [firsts[0], seconds[0], firsts[1], seconds[1], out_weight],
        [jax.ShapeDtypeStruct((length, channels), dtype) for dtype in (bf16, f32)],
        [
            pltpu.VMEM((2 * length, total_width), bf16),
            pltpu.VMEM((steps, lanes, total_width), bf16),
            pltpu.VMEM((steps, length, lanes), bf16),
            pltpu.VMEM((steps, length, lanes), f32),
            pltpu.SemaphoreType.DMA((2, 2)),
            pltpu.SemaphoreType.DMA((steps,)),
            pltpu.SemaphoreType.DMA((2, steps)),
        ],
        4 * length * out_weight.size,
    )


def weight_sum(places, cot_pieces, gated_pieces, rows):
    count = len(gated_pieces)
    length, width = gated_pieces[0].shape
    outs = [jax.ShapeDtypeStruct((rows, width), dtype) for dtype in (bf16, f32)]
    return local_call(
        functools.partial(weight_kernel, count),
        places,
        [*cot_pieces, *gated_pieces],
        outs,
        [
            pltpu.VMEM((count, *cot_pieces[0].shape), bf16),
            pltpu.VMEM((count, length, width), bf16),
            *[pltpu.VMEM(o.shape, o.dtype) for o in outs],
            pltpu.SemaphoreType.DMA((2, count)),
            pltpu.SemaphoreType.DMA((2,)),
        ],
        4 * count * length * rows * width,
    )


def transpose_kernel(rows_in, out, rows, turned, sems):
    copy = pltpu.make_async_copy(rows_in, rows, sems.at[0])
    copy.start()
    copy.wait()
    for i in range(rows.shape[1] // lanes):
        turned[pl.ds(i * lanes, lanes), :] = rows[:, pl.ds(i * lanes, lanes)].T
    copy = pltpu.make_async_copy(turned, out, sems.at[1])
    copy.start()
    copy.wait()


def transposed(rows):
    return pl.pallas_call(
        transpose_kernel,
        in_specs=[pl.BlockSpec(memory_space=pl.ANY)],
        out_specs=pl.BlockSpec(memory_space=pl.ANY),
        out_shape=jax.ShapeDtypeStruct(rows.shape[::-1], rows.dtype),
        scratch_shapes=[
            pltpu.VMEM(rows.shape, rows.dtype),
            pltpu.VMEM(rows.shape[::-1], rows.dtype),
            pltpu.SemaphoreType.DMA((2,)),
        ],
        compiler_params=pltpu.CompilerParams(vmem_limit_bytes=vmem_bytes),
        cost_estimate=estimate(0, [rows, rows]),
    )(rows)


def swap_pairs(value, axis, distance):
    count = lax.axis_size(axis)
    return lax.ppermute(value, axis, [(i, i ^ distance) for i in range(count)])


def after(value, *earlier):
    return lax.optimization_barrier((value, *earlier))[0]


def per_device(query_gate, key_gate, value_input, filter_taps, skip_gain, out_weight, cotangent):
    queries, key_rows, value_rows, cot = (
        query_gate[0],
        key_gate[0],
        value_input[0],
        cotangent[0],
    )
    length, channels = queries.shape
    taps = filter_taps.shape[1]
    n_seq, n_tp, n_dp = lax.axis_size("seq"), lax.axis_size("tp"), lax.axis_size("dp")
    subs = n_tp // n_dp
    me_tp, me_dp = lax.axis_index("tp"), lax.axis_index("dp")
    me_half, me_sub = me_tp // subs, me_tp % subs
    size = length + taps
    norm_factor = 1.0 / math.sqrt(length * n_seq * n_dp)

    whole = analysis_table(size, np.arange(size))
    scale = 2.0 / size
    tables = [split_table(whole), np.ascontiguousarray(split_table(whole.T))]
    rows16 = jax.ShapeDtypeStruct((length, channels), bf16)
    rows32 = jax.ShapeDtypeStruct((length, channels), f32)
    half16 = jax.ShapeDtypeStruct((length, channels // 2), bf16)
    unit = 2 * size * channels

    tail = (
        key_rows[length - taps :].astype(f32) * value_rows[length - taps :].astype(f32)
    ).astype(bf16)
    tail, cot = lax.optimization_barrier((tail, cot))
    prior = lax.ppermute(tail, "seq", [(i, i + 1) for i in range(n_seq - 1)])

    def tp_dp(half, sub, replica):
        return (half * subs + sub) * n_dp + replica

    places = [(h, c, d) for h in range(n_dp) for c in range(subs) for d in range(n_dp)]
    rounds = []
    for turn in range(2):
        route = [(tp_dp(h, c, d), tp_dp(d ^ turn, c, h)) for h, c, d in places]
        rounds.append(lax.ppermute(cot, ("tp", "dp"), route))
    square = n_seq == n_tp == 4 and subs == 2
    if square:

        def holder(s):
            return s % 2 * subs + s // 2

        route = [(s * n_tp + t, t * n_tp + holder(s)) for s in range(n_seq) for t in range(n_tp)]
        moved = lax.ppermute(cot, ("seq", "tp"), route)
    else:
        moved = cot

    state, *gated = by_channel(
        functools.partial(state_kernel, scale),
        tables,
        [prior, key_rows, value_rows, filter_taps, skip_gain[None], queries],
        [[rows32], [half16, half16]],
        channels,
        unit * (4 * taps + 5 * length),
    )
    gated[0], gated[1], *rounds = lax.optimization_barrier((*gated, *rounds))

    route = [(tp_dp(h, c, d), tp_dp(h, (c + 1) % subs, d)) for h, c, d in places]
    theirs = [lax.ppermute(r, ("tp", "dp"), route) for r in rounds]
    firsts, seconds = zip(rounds, theirs)
    same = (me_half == me_dp).astype(jnp.int32)
    subs_of = [me_sub, (me_sub + 1) % subs]
    place = jnp.stack([same, *subs_of]).astype(jnp.int32)
    rows = n_tp * channels // (n_seq * n_dp)
    if square:
        order = [*range(0, n_seq, 2), *reversed(range(1, n_seq, 2))]
        ring = [(order[k], order[(k + 1) % n_seq]) for k in range(n_seq)]
        halves = [[half] for half in gated]

        def ring_step(pieces):
            pieces.append(lax.ppermute(pieces[-1], "seq", ring))

        ring_step(halves[0])
        halves[0][1], place = lax.optimization_barrier((halves[0][1], place))
        ring_step(halves[0])
        ring_step(halves[1])
    other_sent, own_part = project(place, firsts, seconds, out_weight)
    other_part = swap_pairs(other_sent, "dp", 1)

    if square:
        sent_by = lambda value, flip: lax.ppermute(value, "tp", [(t, t ^ flip) for t in range(n_tp)])
        moved = transposed(moved)
        across = sent_by(moved, subs)
        cot_pieces = [moved, sent_by(moved, 1), across, sent_by(across, 1)]
        table = np.zeros((n_seq, n_tp, n_tp), np.int32)
        for k, s in enumerate(order):
            for r in range(n_seq):
                for t in range(n_tp):
                    table[s, t, t ^ holder(order[k - r])] = r
        sources = jnp.asarray(table)[lax.axis_index("seq"), me_tp]
        halves[0][2], halves[1][1], own_part = lax.optimization_barrier(
            (halves[0][2], halves[1][1], own_part)
        )
        ring_step(halves[0])
        ring_step(halves[1])

        weight_place = jnp.concatenate([sources, me_dp[None].astype(jnp.int32)])

        def weight_all():
            second_sent, second_own = weight_sum(weight_place, cot_pieces, halves[1], rows)
            parts = [(first_own, first_received), (second_own, swap_pairs(second_sent, "dp", 1))]
            return jnp.concatenate(
                [(mine + theirs.astype(f32)) * norm_factor for mine, theirs in parts], axis=1
            )

    else:
        full = lax.all_gather(cot, "tp", axis=1, tiled=True)
        cot_all = lax.all_to_all(full, "seq", 1, 0, tiled=True)
        gated_all = [lax.all_gather(half, "seq", axis=0, tiled=True) for half in gated]

        def part(replica, piece):
            block = lax.dynamic_slice_in_dim(cot_all, replica * rows, rows, axis=1)
            return lax.dot_general(
                block, piece, (((0,), (0,)), ((), ())), preferred_element_type=f32
            )

        def weight_one(piece):
            sent = swap_pairs(part(1 - me_dp, piece).astype(bf16), "dp", 1)
            return (part(me_dp, piece) + sent.astype(f32)) * norm_factor

        def weight_all():
            return jnp.concatenate([weight_one(gated_all[0]), weight_one(gated_all[1])], axis=1)

    grad_query, signal, lags = by_channel(
        lag_kernel,
        tables,
        [own_part, other_part, state, queries, prior, key_rows, value_rows],
        [[rows16], [rows16], [jax.ShapeDtypeStruct((taps, channels), f32)]],
        channels,
        unit * (2 * taps + 4 * length + 3 * taps),
    )
    later = lax.ppermute(signal[:taps], "seq", [(i + 1, i) for i in range(n_seq - 1)])

    share = taps // n_dp
    lag_sum = lax.dynamic_slice_in_dim(lags, me_dp * share, share, axis=0) + swap_pairs(
        lax.dynamic_slice_in_dim(lags, (1 - me_dp) * share, share, axis=0).astype(bf16), "dp", 1
    ).astype(f32)
    if square:
        halves[1][2], lag_sum = lax.optimization_barrier((halves[1][2], lag_sum))
        ring_step(halves[1])
        first_sent, first_own = weight_sum(weight_place, cot_pieces, halves[0], rows)
    distance = 1
    while distance < n_seq:
        rounded = lag_sum.astype(bf16)
        lag_sum = rounded.astype(f32) + swap_pairs(rounded, "seq", distance).astype(f32)
        if square and distance == 1:
            first_sent, lag_sum = lax.optimization_barrier((first_sent, lag_sum))
        distance *= 2
    mine = lag_sum.astype(bf16)
    theirs = swap_pairs(mine, "dp", 1)
    first = me_dp == 0
    lag_sum = jnp.concatenate([jnp.where(first, mine, theirs), jnp.where(first, theirs, mine)], axis=0)
    grad_filter = lag_sum.astype(f32).T * (norm_factor * scale)

    if square:
        first_received = swap_pairs(first_sent, "dp", 1)
        first_received, later = lax.optimization_barrier((first_received, later))
    grad_key, grad_value = by_channel(
        functools.partial(back_kernel, scale),
        tables,
        [signal, later, filter_taps, skip_gain[None], key_rows, value_rows],
        [[rows16], [rows16]],
        channels,
        unit * (4 * taps + 5 * length),
    )
    grad_weight = weight_all()
    return (
        grad_query[None],
        grad_key[None],
        grad_value[None],
        grad_filter,
        grad_filter[:, 0],
        grad_weight,
    )


def solution(mesh):
    tokens = P("dp", "seq", "tp")
    return jax.shard_map(
        per_device,
        mesh=mesh,
        in_specs=(tokens, tokens, tokens, P("tp", None), P("tp"), P("tp", "dp"), tokens),
        out_specs=(tokens, tokens, tokens, P("tp", None), P("tp"), P(("seq", "dp"), "tp")),
        check_vma=False,
    )
```

```python
import functools
import math

import jax
import jax.numpy as jnp
import ml_dtypes
import numpy as np
from jax import lax
from jax.experimental import pallas as pl
from jax.experimental.pallas import tpu as pltpu
from jax.sharding import PartitionSpec as P

f32, bf16 = jnp.float32, jnp.bfloat16
lanes = 512
turn = 256
vmem_bytes = 58 * 1024 * 1024


def analysis_table(size, positions):
    half = size // 2
    omega = 2.0 * np.pi * (np.arange(half) + 0.5) / size
    angle = omega[:, None] * np.asarray(positions)[None, :]
    return np.concatenate([np.cos(angle), -np.sin(angle)], axis=0)


def split_table(table):
    high = table.astype(ml_dtypes.bfloat16)
    low = (table - high.astype(np.float64)).astype(ml_dtypes.bfloat16)
    return np.concatenate([high, low])


def split_rows(rows):
    high = rows.astype(bf16)
    return high, (rows - high.astype(f32)).astype(bf16)


def dot(left, right):
    return jnp.dot(left, right, preferred_element_type=f32)


def dot_nt(left, right):
    return lax.dot_general(left, right, (((1,), (1,)), ((), ())), preferred_element_type=f32)


def add_halves(both):
    half = both.shape[0] // 2
    return both[:half] + both[half:]


def forward_transform(table, rows, start):
    return add_halves(dot(table[:, pl.ds(start, rows.shape[0])], rows))


def inverse_transform(table, spectrum, start, count):
    high, low = split_rows(spectrum)
    upper = table[pl.ds(start, count)]
    lower = table[pl.ds(table.shape[0] // 2 + start, count)]
    return dot(upper, high) + dot(upper, low) + dot(lower, high)


def spectrum_product(left, right, conjugate_right):
    half = left.shape[0] // 2
    left_re, left_im = left[:half], left[half:]
    right_re, right_im = right[:half], right[half:]
    if conjugate_right:
        right_im = -right_im
    return jnp.concatenate(
        [left_re * right_re - left_im * right_im, left_re * right_im + left_im * right_re], axis=0
    )


def mixed_spectrum(table, prior_ref, key_ref, value_ref):
    mixed = (key_ref[...].astype(f32) * value_ref[...].astype(f32)).astype(bf16)
    prior = prior_ref[...]
    return forward_transform(table, prior, 0) + forward_transform(table, mixed, prior.shape[0])


def filter_spectrum(scale, table, taps_ref, skip_ref):
    taps = taps_ref.shape[1]
    filt = add_halves(dot_nt(table[:, :taps], taps_ref[...]))
    half = filt.shape[0] // 2
    return jnp.concatenate([(filt[:half] + skip_ref[...]) * scale, filt[half:] * scale], axis=0)


def state_kernel(
    scale, table, synth, prior_ref, key_ref, value_ref, taps_ref, skip_ref, query_ref, state_ref, gated_ref
):
    spec = mixed_spectrum(table, prior_ref, key_ref, value_ref)
    product = spectrum_product(spec, filter_spectrum(scale, table, taps_ref, skip_ref), False)
    state = inverse_transform(synth, product, prior_ref.shape[0], query_ref.shape[0])
    state_ref[...] = state
    gated_ref[...] = (query_ref[...].astype(f32) * state).astype(bf16)


def project_kernel(
    place_ref, first_mine, second_mine, first_theirs, second_theirs, weight, other, own, pieces, blocks, others, owns, piece_sem, block_sem, out_sem
):
    steps, _, total_width = blocks.shape
    length, width = first_mine.shape

    def piece_copy(n, sub, source):
        rows = pl.ds(n * length, length)
        columns = pl.ds(pl.multiple_of(place_ref[1 + sub] * width, width), width)
        return pltpu.make_async_copy(source, pieces.at[rows, columns], piece_sem.at[n, sub])

    def block_copy(i):
        return pltpu.make_async_copy(weight.at[pl.ds(i * lanes, lanes)], blocks.at[i], block_sem.at[i])

    def out_copies(i):
        columns = pl.ds(pl.multiple_of(i * lanes, lanes), lanes)
        return [
            pltpu.make_async_copy(others.at[i], other.at[:, columns], out_sem.at[0, i]),
            pltpu.make_async_copy(owns.at[i], own.at[:, columns], out_sem.at[1, i]),
        ]

    for i in range(steps):
        block_copy(i).start()

    def fetch(own_first):
        for sub, (first, second) in enumerate([(first_mine, second_mine), (first_theirs, second_theirs)]):
            piece_copy(0, sub, second if own_first else first).start()
            piece_copy(1, sub, first if own_first else second).start()

    pl.when(place_ref[0] != 0)(lambda: fetch(True))
    pl.when(place_ref[0] == 0)(lambda: fetch(False))
    for n in range(2):
        for sub in range(2):
            piece_copy(n, sub, first_mine).wait()

    @pl.loop(0, steps)
    def _(i):
        block_copy(i).wait()
        total = dot_nt(pieces[...], blocks[i])
        others[i] = total[:length].astype(bf16)
        owns[i] = total[length:]
        for copy in out_copies(i):
            copy.start()

    for i in range(steps):
        for copy in out_copies(i):
            copy.wait()


def weight_kernel(count, place_ref, *refs):
    cot_in, gated_in = refs[:count], refs[count : 2 * count]
    other, own, cots, gateds, others, owns, in_sem, out_sem = refs[2 * count :]
    length = gateds.shape[1]
    rows = other.shape[0]
    block = min(rows, lanes)
    copies = [pltpu.make_async_copy(cot_in[n], cots.at[n], in_sem.at[0, n]) for n in range(count)]
    copies += [pltpu.make_async_copy(gated_in[n], gateds.at[n], in_sem.at[1, n]) for n in range(count)]
    for copy in copies:
        copy.start()
    for copy in copies:
        copy.wait()
    outs = [
        pltpu.make_async_copy(others, other, out_sem.at[0]),
        pltpu.make_async_copy(owns, own, out_sem.at[1]),
    ]

    def fill(replica, target):
        @pl.loop(0, rows // block)
        def _(i):
            start = pl.multiple_of(replica * rows + i * block, block)
            total = None
            for n in range(count):
                part = dot(cots[n, pl.ds(start, block), :], gateds[place_ref[n]])
                total = part if total is None else total + part
            target[pl.ds(pl.multiple_of(i * block, block), block), :] = total.astype(target.dtype)

    me = place_ref[count]
    fill(1 - me, others)
    outs[0].start()
    fill(me, owns)
    outs[1].start()
    for copy in outs:
        copy.wait()


def lag_kernel(
    table, synth, own_ref, other_ref, state_ref, query_ref, prior_ref, key_ref, value_ref, grad_ref, signal_ref, lag_ref
):
    length, taps = signal_ref.shape[0], lag_ref.shape[0]
    grad_gated = own_ref[...] + other_ref[...].astype(f32)
    grad_ref[...] = (grad_gated * state_ref[...]).astype(bf16)
    signal = (grad_gated * query_ref[...].astype(f32)).astype(bf16)
    signal_ref[...] = signal
    spec = mixed_spectrum(table, prior_ref, key_ref, value_ref)
    product = spectrum_product(forward_transform(table, signal, 0), spec, True)
    lag_ref[...] = -inverse_transform(synth, product, length, taps)


def back_kernel(
    scale, table, synth, signal_ref, later_ref, taps_ref, skip_ref, key_ref, value_ref, grad_key_ref, grad_value_ref
):
    length = key_ref.shape[0]
    spec = forward_transform(table, signal_ref[...], 0) + forward_transform(table, later_ref[...], length)
    product = spectrum_product(spec, filter_spectrum(scale, table, taps_ref, skip_ref), True)
    back = inverse_transform(synth, product, 0, length)
    grad_key_ref[...] = (back * value_ref[...].astype(f32)).astype(bf16)
    grad_value_ref[...] = (back * key_ref[...].astype(f32)).astype(bf16)


def estimate(flops, arrays):
    moved = sum(a.size * jnp.dtype(a.dtype).itemsize for a in arrays)
    return pl.CostEstimate(flops=flops // 64, bytes_accessed=moved // 64, transcendentals=0)


def by_channel(body, tables, args, outs, channels, flops):
    steps = channels // lanes
    flat_outs = [o for group in outs for o in group]
    n_tables, n_args, n_outs = len(tables), len(args), len(outs)

    def part(ref, i, count):
        start = i * lanes
        if ref.shape[1] == count * lanes:
            return ref.at[:, pl.ds(start, lanes)]
        return ref.at[pl.ds(start, lanes), :]

    def kernel(*refs):
        refs = list(refs)
        take = lambda count: [refs.pop(0) for _ in range(count)]
        table_in, arg_in, outs_to = take(n_tables), take(n_args), take(len(flat_outs))
        table_held, arg_held, out_held = take(n_tables), take(n_args), take(n_outs)
        table_sem, arg_sem, out_sem = refs
        groups = [[outs_to.pop(0) for _ in group] for group in outs]

        def table_copy(k):
            return pltpu.make_async_copy(table_in[k], table_held[k], table_sem.at[k])

        def arg_copy(k):
            return pltpu.make_async_copy(arg_in[k], arg_held[k], arg_sem.at[k])

        def out_copy(k, n, i):
            per = steps // len(groups[k])
            place = part(groups[k][n], i - n * per, per)
            return pltpu.make_async_copy(out_held[k].at[i], place, out_sem.at[k, i])

        for k in range(n_tables):
            table_copy(k).start()
        for k in range(n_args):
            arg_copy(k).start()
        for k in range(n_tables):
            table_copy(k).wait()
        for k in range(n_args):
            arg_copy(k).wait()

        for i in range(steps):
            body(*table_held, *[part(ref, i, steps) for ref in arg_held], *[held.at[i] for held in out_held])
            for k in range(n_outs):
                out_copy(k, i * len(groups[k]) // steps, i).start()

        for i in range(steps):
            for k in range(n_outs):
                out_copy(k, i * len(groups[k]) // steps, i).wait()

    return pl.pallas_call(
        kernel,
        in_specs=[pl.BlockSpec(memory_space=pl.ANY)] * (n_tables + n_args),
        out_specs=[pl.BlockSpec(memory_space=pl.ANY)] * len(flat_outs),
        out_shape=flat_outs,
        scratch_shapes=[
            *[pltpu.VMEM(t.shape, bf16) for t in tables],
            *[pltpu.VMEM(a.shape, a.dtype) for a in args],
            *[pltpu.VMEM((steps, group[0].shape[0], lanes), group[0].dtype) for group in outs],
            pltpu.SemaphoreType.DMA((n_tables,)),
            pltpu.SemaphoreType.DMA((n_args,)),
            pltpu.SemaphoreType.DMA((n_outs, steps)),
        ],
        compiler_params=pltpu.CompilerParams(vmem_limit_bytes=vmem_bytes),
        cost_estimate=estimate(flops, [*args, *flat_outs]),
    )(*[jnp.asarray(t) for t in tables], *args)


def local_call(kernel, places, args, outs, scratch, flops):
    return pl.pallas_call(
        kernel,
        in_specs=[pl.BlockSpec(memory_space=pltpu.SMEM)] + [pl.BlockSpec(memory_space=pl.ANY)] * len(args),
        out_specs=[pl.BlockSpec(memory_space=pl.ANY)] * len(outs),
        out_shape=outs,
        scratch_shapes=scratch,
        compiler_params=pltpu.CompilerParams(vmem_limit_bytes=vmem_bytes),
        cost_estimate=estimate(flops, [*args, *outs]),
    )(places, *args)


def project(places, firsts, seconds, out_weight):
    length, width = firsts[0].shape
    channels, total_width = out_weight.shape
    steps = channels // lanes
    return local_call(
        project_kernel,
        places,
        [firsts[0], seconds[0], firsts[1], seconds[1], out_weight],
        [jax.ShapeDtypeStruct((length, channels), dtype) for dtype in (bf16, f32)],
        [
            pltpu.VMEM((2 * length, total_width), bf16),
            pltpu.VMEM((steps, lanes, total_width), bf16),
            pltpu.VMEM((steps, length, lanes), bf16),
            pltpu.VMEM((steps, length, lanes), f32),
            pltpu.SemaphoreType.DMA((2, 2)),
            pltpu.SemaphoreType.DMA((steps,)),
            pltpu.SemaphoreType.DMA((2, steps)),
        ],
        4 * length * out_weight.size,
    )


def weight_sum(places, cot_pieces, gated_pieces, rows):
    count = len(gated_pieces)
    length, width = gated_pieces[0].shape
    outs = [jax.ShapeDtypeStruct((rows, width), dtype) for dtype in (bf16, f32)]
    return local_call(
        functools.partial(weight_kernel, count),
        places,
        [*cot_pieces, *gated_pieces],
        outs,
        [
            pltpu.VMEM((count, *cot_pieces[0].shape), bf16),
            pltpu.VMEM((count, length, width), bf16),
            *[pltpu.VMEM(o.shape, o.dtype) for o in outs],
            pltpu.SemaphoreType.DMA((2, count)),
            pltpu.SemaphoreType.DMA((2,)),
        ],
        4 * count * length * rows * width,
    )


def transpose_kernel(rows_in, out, rows, turned, sems):
    copy = pltpu.make_async_copy(rows_in, rows, sems.at[0])
    copy.start()
    copy.wait()
    for i in range(rows.shape[1] // turn):
        turned[pl.ds(i * turn, turn), :] = rows[:, pl.ds(i * turn, turn)].T
    copy = pltpu.make_async_copy(turned, out, sems.at[1])
    copy.start()
    copy.wait()


def transposed(rows):
    return pl.pallas_call(
        transpose_kernel,
        in_specs=[pl.BlockSpec(memory_space=pl.ANY)],
        out_specs=pl.BlockSpec(memory_space=pl.ANY),
        out_shape=jax.ShapeDtypeStruct(rows.shape[::-1], rows.dtype),
        scratch_shapes=[
            pltpu.VMEM(rows.shape, rows.dtype),
            pltpu.VMEM(rows.shape[::-1], rows.dtype),
            pltpu.SemaphoreType.DMA((2,)),
        ],
        compiler_params=pltpu.CompilerParams(vmem_limit_bytes=vmem_bytes),
        cost_estimate=estimate(0, [rows, rows]),
    )(rows)


def swap_pairs(value, axis, distance):
    count = lax.axis_size(axis)
    return lax.ppermute(value, axis, [(i, i ^ distance) for i in range(count)])


def after(value, *earlier):
    return lax.optimization_barrier((value, *earlier))[0]


def per_device(query_gate, key_gate, value_input, filter_taps, skip_gain, out_weight, cotangent):
    queries, key_rows, value_rows, cot = (
        query_gate[0],
        key_gate[0],
        value_input[0],
        cotangent[0],
    )
    length, channels = queries.shape
    taps = filter_taps.shape[1]
    n_seq, n_tp, n_dp = lax.axis_size("seq"), lax.axis_size("tp"), lax.axis_size("dp")
    subs = n_tp // n_dp
    me_tp, me_dp = lax.axis_index("tp"), lax.axis_index("dp")
    me_half, me_sub = me_tp // subs, me_tp % subs
    size = length + taps
    norm_factor = 1.0 / math.sqrt(length * n_seq * n_dp)

    whole = analysis_table(size, np.arange(size))
    scale = 2.0 / size
    tables = [split_table(whole), np.ascontiguousarray(split_table(whole.T))]
    rows16 = jax.ShapeDtypeStruct((length, channels), bf16)
    rows32 = jax.ShapeDtypeStruct((length, channels), f32)
    half16 = jax.ShapeDtypeStruct((length, channels // 2), bf16)
    unit = 2 * size * channels

    tail = (
        key_rows[length - taps :].astype(f32) * value_rows[length - taps :].astype(f32)
    ).astype(bf16)
    tail, cot = lax.optimization_barrier((tail, cot))
    prior = lax.ppermute(tail, "seq", [(i, i + 1) for i in range(n_seq - 1)])

    def tp_dp(half, sub, replica):
        return (half * subs + sub) * n_dp + replica

    places = [(h, c, d) for h in range(n_dp) for c in range(subs) for d in range(n_dp)]
    rounds = []
    for turn in range(2):
        route = [(tp_dp(h, c, d), tp_dp(d ^ turn, c, h)) for h, c, d in places]
        rounds.append(lax.ppermute(cot, ("tp", "dp"), route))
    square = n_seq == n_tp == 4 and subs == 2
    if square:

        def holder(s, block):
            return (s + block) % 2 * subs + s // 2

        crossed = {0: (1, 2), 1: (0, 3)}
        route = [
            (s * n_tp + t, s * n_tp + sum(crossed[s % 2]) - t)
            for s in range(n_seq)
            for t in crossed[s % 2]
        ]
        swapped = lax.ppermute(cot, ("seq", "tp"), route)
        moves_now = sum(
            jnp.logical_and(lax.axis_index("seq") % 2 == parity, me_tp == t)
            for parity in crossed
            for t in crossed[parity]
        )
        held = jnp.where(moves_now > 0, swapped, cot)
        route = []
        for s in range(n_seq):
            for t in range(n_tp):
                block = sum(crossed[s % 2]) - t if t in crossed[s % 2] else t
                route.append((s * n_tp + t, block * n_tp + holder(s, block)))
        moved = lax.ppermute(after(held, prior), ("seq", "tp"), route)
    else:
        moved = cot

    state, *gated = by_channel(
        functools.partial(state_kernel, scale),
        tables,
        [prior, key_rows, value_rows, filter_taps, skip_gain[None], queries],
        [[rows32], [half16, half16]],
        channels,
        unit * (4 * taps + 5 * length),
    )
    gated[0], gated[1], moved, *rounds = lax.optimization_barrier((*gated, moved, *rounds))

    route = [(tp_dp(h, c, d), tp_dp(h, (c + 1) % subs, d)) for h, c, d in places]
    theirs = [lax.ppermute(r, ("tp", "dp"), route) for r in rounds]
    firsts, seconds = zip(rounds, theirs)
    same = (me_half == me_dp).astype(jnp.int32)
    subs_of = [me_sub, (me_sub + 1) % subs]
    place = jnp.stack([same, *subs_of]).astype(jnp.int32)
    rows = n_tp * channels // (n_seq * n_dp)
    if square:
        order = [*range(0, n_seq, 2), *reversed(range(1, n_seq, 2))]
        ring = [(order[k], order[(k + 1) % n_seq]) for k in range(n_seq)]
        halves = [[half] for half in gated]

        def ring_step(pieces):
            pieces.append(lax.ppermute(pieces[-1], "seq", ring))

        ring_step(halves[0])
        moved = transposed(moved)
        halves[0][1], moved, place = lax.optimization_barrier((halves[0][1], moved, place))
        ring_step(halves[0])
        ring_step(halves[1])
    other_sent, own_part = project(place, firsts, seconds, out_weight)
    other_part = swap_pairs(other_sent, "dp", 1)

    if square:
        sent_by = lambda value, flip: lax.ppermute(value, "tp", [(t, t ^ flip) for t in range(n_tp)])
        across = sent_by(moved, subs)
        cot_pieces = [moved, sent_by(moved, 1), across, sent_by(across, 1)]
        table = np.zeros((n_seq, n_tp, n_tp), np.int32)
        for k, s in enumerate(order):
            for r in range(n_seq):
                for t in range(n_tp):
                    table[s, t, t ^ holder(order[k - r], s)] = r
        sources = jnp.asarray(table)[lax.axis_index("seq"), me_tp]
        halves[0][2], halves[1][1], own_part = lax.optimization_barrier(
            (halves[0][2], halves[1][1], own_part)
        )
        ring_step(halves[0])
        ring_step(halves[1])

        weight_place = jnp.concatenate([sources, me_dp[None].astype(jnp.int32)])

    else:
        full = lax.all_gather(cot, "tp", axis=1, tiled=True)
        cot_all = lax.all_to_all(full, "seq", 1, 0, tiled=True)
        gated_all = [lax.all_gather(half, "seq", axis=0, tiled=True) for half in gated]

        def part(replica, piece):
            block = lax.dynamic_slice_in_dim(cot_all, replica * rows, rows, axis=1)
            return lax.dot_general(
                block, piece, (((0,), (0,)), ((), ())), preferred_element_type=f32
            )

        def weight_one(piece):
            return part(me_dp, piece), swap_pairs(part(1 - me_dp, piece).astype(bf16), "dp", 1)

    grad_query, signal, lags = by_channel(
        lag_kernel,
        tables,
        [own_part, other_part, state, queries, prior, key_rows, value_rows],
        [[rows16], [rows16], [jax.ShapeDtypeStruct((taps, channels), f32)]],
        channels,
        unit * (2 * taps + 4 * length + 3 * taps),
    )
    later = lax.ppermute(signal[:taps], "seq", [(i + 1, i) for i in range(n_seq - 1)])

    def run_back(later):
        return by_channel(
            functools.partial(back_kernel, scale),
            tables,
            [signal, later, filter_taps, skip_gain[None], key_rows, value_rows],
            [[rows16], [rows16]],
            channels,
            256 * unit * (4 * taps + 5 * length),
        )

    share = taps // n_dp
    received = swap_pairs(
        lax.dynamic_slice_in_dim(lags, (1 - me_dp) * share, share, axis=0).astype(bf16), "dp", 1
    )
    if square:
        halves[1][2], weight_place = lax.optimization_barrier((halves[1][2], weight_place))
        ring_step(halves[1])
        first_sent, first_own = weight_sum(weight_place, cot_pieces, halves[0], rows)
        first_received = swap_pairs(first_sent, "dp", 1)
        received, first_own = lax.optimization_barrier((received, first_own))
    lag_sum = lax.dynamic_slice_in_dim(lags, me_dp * share, share, axis=0) + received.astype(f32)
    distance = 1
    while distance < n_seq:
        rounded = lag_sum.astype(bf16)
        received = swap_pairs(rounded, "seq", distance)
        if square and distance == 1:
            weight_place = after(weight_place, first_own)
            second_sent, second_own = weight_sum(weight_place, cot_pieces, halves[1], rows)
            second_received = swap_pairs(second_sent, "dp", 1)
            received, second_own = lax.optimization_barrier((received, second_own))
        lag_sum = rounded.astype(f32) + received.astype(f32)
        distance *= 2
    if square:
        first_received, lag_sum = lax.optimization_barrier((first_received, lag_sum))
    mine = lag_sum.astype(bf16)
    theirs = swap_pairs(mine, "dp", 1)
    if square:
        later = after(later, second_own)
    grad_key, grad_value = run_back(later)
    first = me_dp == 0
    lag_sum = jnp.concatenate([jnp.where(first, mine, theirs), jnp.where(first, theirs, mine)], axis=0)
    grad_filter = lag_sum.astype(f32).T * (norm_factor * scale)

    if square:
        parts = [(first_own, first_received), (second_own, second_received)]
    else:
        parts = [weight_one(half) for half in gated_all]
    grad_weight = jnp.concatenate(
        [(mine + theirs.astype(f32)) * norm_factor for mine, theirs in parts], axis=1
    )
    return (
        grad_query[None],
        grad_key[None],
        grad_value[None],
        grad_filter,
        grad_filter[:, 0],
        grad_weight,
    )


def solution(mesh):
    tokens = P("dp", "seq", "tp")
    return jax.shard_map(
        per_device,
        mesh=mesh,
        in_specs=(tokens, tokens, tokens, P("tp", None), P("tp"), P("tp", "dp"), tokens),
        out_specs=(tokens, tokens, tokens, P("tp", None), P("tp"), P(("seq", "dp"), "tp")),
        check_vma=False,
    )
```

```python
import functools
import math

import jax
import jax.numpy as jnp
import ml_dtypes
import numpy as np
from jax import lax
from jax.experimental import pallas as pl
from jax.experimental.pallas import tpu as pltpu
from jax.sharding import PartitionSpec as P

f32, bf16 = jnp.float32, jnp.bfloat16
lanes = 512
turn = 256
vmem_bytes = 58 * 1024 * 1024


def analysis_table(size, positions):
    half = size // 2
    omega = 2.0 * np.pi * (np.arange(half) + 0.5) / size
    angle = omega[:, None] * np.asarray(positions)[None, :]
    return np.concatenate([np.cos(angle), -np.sin(angle)], axis=0)


def split_table(table):
    high = table.astype(ml_dtypes.bfloat16)
    low = (table - high.astype(np.float64)).astype(ml_dtypes.bfloat16)
    return np.concatenate([high, low])


def split_rows(rows):
    high = rows.astype(bf16)
    return high, (rows - high.astype(f32)).astype(bf16)


def dot(left, right):
    return jnp.dot(left, right, preferred_element_type=f32)


def dot_nt(left, right):
    return lax.dot_general(left, right, (((1,), (1,)), ((), ())), preferred_element_type=f32)


def add_halves(both):
    half = both.shape[0] // 2
    return both[:half] + both[half:]


def forward_transform(table, rows, start):
    return add_halves(dot(table[:, pl.ds(start, rows.shape[0])], rows))


def inverse_transform(table, spectrum, start, count):
    high, low = split_rows(spectrum)
    upper = table[pl.ds(start, count)]
    lower = table[pl.ds(table.shape[0] // 2 + start, count)]
    return dot(upper, high) + dot(upper, low) + dot(lower, high)


def spectrum_product(left, right, conjugate_right):
    half = left.shape[0] // 2
    left_re, left_im = left[:half], left[half:]
    right_re, right_im = right[:half], right[half:]
    if conjugate_right:
        right_im = -right_im
    return jnp.concatenate(
        [left_re * right_re - left_im * right_im, left_re * right_im + left_im * right_re], axis=0
    )


def mixed_spectrum(table, prior_ref, key_ref, value_ref):
    mixed = (key_ref[...].astype(f32) * value_ref[...].astype(f32)).astype(bf16)
    prior = prior_ref[...]
    return forward_transform(table, prior, 0) + forward_transform(table, mixed, prior.shape[0])


def filter_spectrum(scale, table, taps_ref, skip_ref):
    taps = taps_ref.shape[1]
    filt = add_halves(dot_nt(table[:, :taps], taps_ref[...]))
    half = filt.shape[0] // 2
    return jnp.concatenate([(filt[:half] + skip_ref[...]) * scale, filt[half:] * scale], axis=0)


def state_kernel(
    scale, table, synth, prior_ref, key_ref, value_ref, taps_ref, skip_ref, query_ref, state_ref, gated_ref
):
    spec = mixed_spectrum(table, prior_ref, key_ref, value_ref)
    product = spectrum_product(spec, filter_spectrum(scale, table, taps_ref, skip_ref), False)
    state = inverse_transform(synth, product, prior_ref.shape[0], query_ref.shape[0])
    state_ref[...] = state
    gated_ref[...] = (query_ref[...].astype(f32) * state).astype(bf16)


def project_kernel(
    place_ref, first_mine, second_mine, first_theirs, second_theirs, weight, other, own, pieces, blocks, others, owns, piece_sem, block_sem, out_sem
):
    steps, _, total_width = blocks.shape
    length, width = first_mine.shape

    def piece_copy(n, sub, source):
        rows = pl.ds(n * length, length)
        columns = pl.ds(pl.multiple_of(place_ref[1 + sub] * width, width), width)
        return pltpu.make_async_copy(source, pieces.at[rows, columns], piece_sem.at[n, sub])

    def block_copy(i):
        return pltpu.make_async_copy(weight.at[pl.ds(i * lanes, lanes)], blocks.at[i], block_sem.at[i])

    def out_copies(i):
        columns = pl.ds(pl.multiple_of(i * lanes, lanes), lanes)
        return [
            pltpu.make_async_copy(others.at[i], other.at[:, columns], out_sem.at[0, i]),
            pltpu.make_async_copy(owns.at[i], own.at[:, columns], out_sem.at[1, i]),
        ]

    for i in range(steps):
        block_copy(i).start()

    def fetch(own_first):
        for sub, (first, second) in enumerate([(first_mine, second_mine), (first_theirs, second_theirs)]):
            piece_copy(0, sub, second if own_first else first).start()
            piece_copy(1, sub, first if own_first else second).start()

    pl.when(place_ref[0] != 0)(lambda: fetch(True))
    pl.when(place_ref[0] == 0)(lambda: fetch(False))
    for n in range(2):
        for sub in range(2):
            piece_copy(n, sub, first_mine).wait()

    @pl.loop(0, steps)
    def _(i):
        block_copy(i).wait()
        total = dot_nt(pieces[...], blocks[i])
        others[i] = total[:length].astype(bf16)
        owns[i] = total[length:]
        for copy in out_copies(i):
            copy.start()

    for i in range(steps):
        for copy in out_copies(i):
            copy.wait()


def weight_kernel(count, place_ref, *refs):
    cot_in, gated_in = refs[:count], refs[count : 2 * count]
    other, own, cots, gateds, others, owns, in_sem, out_sem = refs[2 * count :]
    length = gateds.shape[1]
    rows = other.shape[0]
    block = min(rows, lanes)
    copies = [pltpu.make_async_copy(cot_in[n], cots.at[n], in_sem.at[0, n]) for n in range(count)]
    copies += [pltpu.make_async_copy(gated_in[n], gateds.at[n], in_sem.at[1, n]) for n in range(count)]
    for copy in copies:
        copy.start()
    for copy in copies:
        copy.wait()
    outs = [
        pltpu.make_async_copy(others, other, out_sem.at[0]),
        pltpu.make_async_copy(owns, own, out_sem.at[1]),
    ]

    def fill(replica, target):
        @pl.loop(0, rows // block)
        def _(i):
            start = pl.multiple_of(replica * rows + i * block, block)
            total = None
            for n in range(count):
                part = dot(cots[n, pl.ds(start, block), :], gateds[place_ref[n]])
                total = part if total is None else total + part
            target[pl.ds(pl.multiple_of(i * block, block), block), :] = total.astype(target.dtype)

    me = place_ref[count]
    fill(1 - me, others)
    outs[0].start()
    fill(me, owns)
    outs[1].start()
    for copy in outs:
        copy.wait()


def lag_kernel(
    table, synth, own_ref, other_ref, state_ref, query_ref, prior_ref, key_ref, value_ref, grad_ref, signal_ref, lag_ref
):
    length, taps = signal_ref.shape[0], lag_ref.shape[0]
    grad_gated = own_ref[...] + other_ref[...].astype(f32)
    grad_ref[...] = (grad_gated * state_ref[...]).astype(bf16)
    signal = (grad_gated * query_ref[...].astype(f32)).astype(bf16)
    signal_ref[...] = signal
    spec = mixed_spectrum(table, prior_ref, key_ref, value_ref)
    product = spectrum_product(forward_transform(table, signal, 0), spec, True)
    lag_ref[...] = -inverse_transform(synth, product, length, taps)


def back_kernel(
    scale, table, synth, signal_ref, later_ref, taps_ref, skip_ref, key_ref, value_ref, grad_key_ref, grad_value_ref
):
    length = key_ref.shape[0]
    spec = forward_transform(table, signal_ref[...], 0) + forward_transform(table, later_ref[...], length)
    product = spectrum_product(spec, filter_spectrum(scale, table, taps_ref, skip_ref), True)
    back = inverse_transform(synth, product, 0, length)
    grad_key_ref[...] = (back * value_ref[...].astype(f32)).astype(bf16)
    grad_value_ref[...] = (back * key_ref[...].astype(f32)).astype(bf16)


def estimate(flops, arrays):
    moved = sum(a.size * jnp.dtype(a.dtype).itemsize for a in arrays)
    return pl.CostEstimate(flops=flops // 64, bytes_accessed=moved // 64, transcendentals=0)


def by_channel(body, tables, args, outs, channels, flops):
    steps = channels // lanes
    flat_outs = [o for group in outs for o in group]
    n_tables, n_args, n_outs = len(tables), len(args), len(outs)

    def part(ref, i, count):
        start = i * lanes
        if ref.shape[1] == count * lanes:
            return ref.at[:, pl.ds(start, lanes)]
        return ref.at[pl.ds(start, lanes), :]

    def kernel(*refs):
        refs = list(refs)
        take = lambda count: [refs.pop(0) for _ in range(count)]
        table_in, arg_in, outs_to = take(n_tables), take(n_args), take(len(flat_outs))
        table_held, arg_held, out_held = take(n_tables), take(n_args), take(n_outs)
        table_sem, arg_sem, out_sem = refs
        groups = [[outs_to.pop(0) for _ in group] for group in outs]

        def table_copy(k):
            return pltpu.make_async_copy(table_in[k], table_held[k], table_sem.at[k])

        def arg_copy(k):
            return pltpu.make_async_copy(arg_in[k], arg_held[k], arg_sem.at[k])

        def out_copy(k, n, i):
            per = steps // len(groups[k])
            place = part(groups[k][n], i - n * per, per)
            return pltpu.make_async_copy(out_held[k].at[i], place, out_sem.at[k, i])

        for k in range(n_tables):
            table_copy(k).start()
        for k in range(n_args):
            arg_copy(k).start()
        for k in range(n_tables):
            table_copy(k).wait()
        for k in range(n_args):
            arg_copy(k).wait()

        for i in range(steps):
            body(*table_held, *[part(ref, i, steps) for ref in arg_held], *[held.at[i] for held in out_held])
            for k in range(n_outs):
                out_copy(k, i * len(groups[k]) // steps, i).start()

        for i in range(steps):
            for k in range(n_outs):
                out_copy(k, i * len(groups[k]) // steps, i).wait()

    return pl.pallas_call(
        kernel,
        in_specs=[pl.BlockSpec(memory_space=pl.ANY)] * (n_tables + n_args),
        out_specs=[pl.BlockSpec(memory_space=pl.ANY)] * len(flat_outs),
        out_shape=flat_outs,
        scratch_shapes=[
            *[pltpu.VMEM(t.shape, bf16) for t in tables],
            *[pltpu.VMEM(a.shape, a.dtype) for a in args],
            *[pltpu.VMEM((steps, group[0].shape[0], lanes), group[0].dtype) for group in outs],
            pltpu.SemaphoreType.DMA((n_tables,)),
            pltpu.SemaphoreType.DMA((n_args,)),
            pltpu.SemaphoreType.DMA((n_outs, steps)),
        ],
        compiler_params=pltpu.CompilerParams(vmem_limit_bytes=vmem_bytes),
        cost_estimate=estimate(flops, [*args, *flat_outs]),
    )(*[jnp.asarray(t) for t in tables], *args)


def local_call(kernel, places, args, outs, scratch, flops):
    return pl.pallas_call(
        kernel,
        in_specs=[pl.BlockSpec(memory_space=pltpu.SMEM)] + [pl.BlockSpec(memory_space=pl.ANY)] * len(args),
        out_specs=[pl.BlockSpec(memory_space=pl.ANY)] * len(outs),
        out_shape=outs,
        scratch_shapes=scratch,
        compiler_params=pltpu.CompilerParams(vmem_limit_bytes=vmem_bytes),
        cost_estimate=estimate(flops, [*args, *outs]),
    )(places, *args)


def project(places, firsts, seconds, out_weight):
    length, width = firsts[0].shape
    channels, total_width = out_weight.shape
    steps = channels // lanes
    return local_call(
        project_kernel,
        places,
        [firsts[0], seconds[0], firsts[1], seconds[1], out_weight],
        [jax.ShapeDtypeStruct((length, channels), dtype) for dtype in (bf16, f32)],
        [
            pltpu.VMEM((2 * length, total_width), bf16),
            pltpu.VMEM((steps, lanes, total_width), bf16),
            pltpu.VMEM((steps, length, lanes), bf16),
            pltpu.VMEM((steps, length, lanes), f32),
            pltpu.SemaphoreType.DMA((2, 2)),
            pltpu.SemaphoreType.DMA((steps,)),
            pltpu.SemaphoreType.DMA((2, steps)),
        ],
        256 * length * out_weight.size,
    )


def weight_sum(places, cot_pieces, gated_pieces, rows):
    count = len(gated_pieces)
    length, width = gated_pieces[0].shape
    outs = [jax.ShapeDtypeStruct((rows, width), dtype) for dtype in (bf16, f32)]
    return local_call(
        functools.partial(weight_kernel, count),
        places,
        [*cot_pieces, *gated_pieces],
        outs,
        [
            pltpu.VMEM((count, *cot_pieces[0].shape), bf16),
            pltpu.VMEM((count, length, width), bf16),
            *[pltpu.VMEM(o.shape, o.dtype) for o in outs],
            pltpu.SemaphoreType.DMA((2, count)),
            pltpu.SemaphoreType.DMA((2,)),
        ],
        4 * count * length * rows * width,
    )


def transpose_kernel(rows_in, out, rows, turned, sems):
    copy = pltpu.make_async_copy(rows_in, rows, sems.at[0])
    copy.start()
    copy.wait()
    for i in range(rows.shape[1] // turn):
        turned[pl.ds(i * turn, turn), :] = rows[:, pl.ds(i * turn, turn)].T
    copy = pltpu.make_async_copy(turned, out, sems.at[1])
    copy.start()
    copy.wait()


def transposed(rows):
    return pl.pallas_call(
        transpose_kernel,
        in_specs=[pl.BlockSpec(memory_space=pl.ANY)],
        out_specs=pl.BlockSpec(memory_space=pl.ANY),
        out_shape=jax.ShapeDtypeStruct(rows.shape[::-1], rows.dtype),
        scratch_shapes=[
            pltpu.VMEM(rows.shape, rows.dtype),
            pltpu.VMEM(rows.shape[::-1], rows.dtype),
            pltpu.SemaphoreType.DMA((2,)),
        ],
        compiler_params=pltpu.CompilerParams(vmem_limit_bytes=vmem_bytes),
        cost_estimate=estimate(0, [rows, rows]),
    )(rows)


def swap_pairs(value, axis, distance):
    count = lax.axis_size(axis)
    return lax.ppermute(value, axis, [(i, i ^ distance) for i in range(count)])


def after(value, *earlier):
    return lax.optimization_barrier((value, *earlier))[0]


def per_device(query_gate, key_gate, value_input, filter_taps, skip_gain, out_weight, cotangent):
    queries, key_rows, value_rows, cot = (
        query_gate[0],
        key_gate[0],
        value_input[0],
        cotangent[0],
    )
    length, channels = queries.shape
    taps = filter_taps.shape[1]
    n_seq, n_tp, n_dp = lax.axis_size("seq"), lax.axis_size("tp"), lax.axis_size("dp")
    subs = n_tp // n_dp
    me_tp, me_dp = lax.axis_index("tp"), lax.axis_index("dp")
    me_half, me_sub = me_tp // subs, me_tp % subs
    size = length + taps
    norm_factor = 1.0 / math.sqrt(length * n_seq * n_dp)

    whole = analysis_table(size, np.arange(size))
    scale = 2.0 / size
    tables = [split_table(whole), np.ascontiguousarray(split_table(whole.T))]
    rows16 = jax.ShapeDtypeStruct((length, channels), bf16)
    rows32 = jax.ShapeDtypeStruct((length, channels), f32)
    half16 = jax.ShapeDtypeStruct((length, channels // 2), bf16)
    unit = 2 * size * channels

    tail = (
        key_rows[length - taps :].astype(f32) * value_rows[length - taps :].astype(f32)
    ).astype(bf16)
    tail, cot = lax.optimization_barrier((tail, cot))
    prior = lax.ppermute(tail, "seq", [(i, i + 1) for i in range(n_seq - 1)])

    def tp_dp(half, sub, replica):
        return (half * subs + sub) * n_dp + replica

    places = [(h, c, d) for h in range(n_dp) for c in range(subs) for d in range(n_dp)]
    rounds = []
    for turn in range(2):
        route = [(tp_dp(h, c, d), tp_dp(d ^ turn, c, h)) for h, c, d in places]
        rounds.append(lax.ppermute(after(cot, prior) if turn else cot, ("tp", "dp"), route))
    square = n_seq == n_tp == 4 and subs == 2
    if square:

        def holder(s, block):
            return (s + block) % 2 * subs + s // 2

        crossed = {0: (1, 2), 1: (0, 3)}
        route = [
            (s * n_tp + t, s * n_tp + sum(crossed[s % 2]) - t)
            for s in range(n_seq)
            for t in crossed[s % 2]
        ]
        swapped = lax.ppermute(cot, ("seq", "tp"), route)
        moves_now = sum(
            jnp.logical_and(lax.axis_index("seq") % 2 == parity, me_tp == t)
            for parity in crossed
            for t in crossed[parity]
        )
        held = jnp.where(moves_now > 0, swapped, cot)
        route = []
        for s in range(n_seq):
            for t in range(n_tp):
                block = sum(crossed[s % 2]) - t if t in crossed[s % 2] else t
                route.append((s * n_tp + t, block * n_tp + holder(s, block)))
        moved = lax.ppermute(held, ("seq", "tp"), route)
    else:
        moved = cot

    state, *gated = by_channel(
        functools.partial(state_kernel, scale),
        tables,
        [prior, key_rows, value_rows, filter_taps, skip_gain[None], queries],
        [[rows32], [half16, half16]],
        channels,
        unit * (4 * taps + 5 * length),
    )
    gated[0], gated[1], moved, *rounds = lax.optimization_barrier((*gated, moved, *rounds))

    route = [(tp_dp(h, c, d), tp_dp(h, (c + 1) % subs, d)) for h, c, d in places]
    theirs = [lax.ppermute(r, ("tp", "dp"), route) for r in rounds]
    firsts, seconds = zip(rounds, theirs)
    same = (me_half == me_dp).astype(jnp.int32)
    subs_of = [me_sub, (me_sub + 1) % subs]
    place = jnp.stack([same, *subs_of]).astype(jnp.int32)
    rows = n_tp * channels // (n_seq * n_dp)
    if square:
        order = [*range(0, n_seq, 2), *reversed(range(1, n_seq, 2))]
        ring = [(order[k], order[(k + 1) % n_seq]) for k in range(n_seq)]
        halves = [[half] for half in gated]

        def ring_step(pieces):
            pieces.append(lax.ppermute(pieces[-1], "seq", ring))

        ring_step(halves[0])
        table = np.zeros((n_seq, n_tp, n_tp), np.int32)
        for k, s in enumerate(order):
            for r in range(n_seq):
                for t in range(n_tp):
                    table[s, t, t ^ holder(order[k - r], s)] = r
        sources = jnp.asarray(table)[lax.axis_index("seq"), me_tp]
        weight_place = jnp.concatenate([sources, me_dp[None].astype(jnp.int32)])
        moved = transposed(moved)
        halves[0][1], moved, place, weight_place = lax.optimization_barrier(
            (halves[0][1], moved, place, weight_place)
        )
        ring_step(halves[0])
    other_sent, own_part = project(place, firsts, seconds, out_weight)
    if square:
        halves[0][2], halves[1][0], other_sent = lax.optimization_barrier(
            (halves[0][2], halves[1][0], other_sent)
        )
    other_part = swap_pairs(other_sent, "dp", 1)

    if square:
        sent_by = lambda value, flip: lax.ppermute(value, "tp", [(t, t ^ flip) for t in range(n_tp)])
        across = sent_by(moved, subs)
        cot_pieces = [moved, sent_by(moved, 1), across, sent_by(after(across, halves[0][2]), 1)]
        ring_step(halves[0])
        ring_step(halves[1])
        halves[0][3], halves[1][1], own_part = lax.optimization_barrier(
            (halves[0][3], halves[1][1], own_part)
        )
        ring_step(halves[1])
    else:
        full = lax.all_gather(cot, "tp", axis=1, tiled=True)
        cot_all = lax.all_to_all(full, "seq", 1, 0, tiled=True)
        gated_all = [lax.all_gather(half, "seq", axis=0, tiled=True) for half in gated]

        def part(replica, piece):
            block = lax.dynamic_slice_in_dim(cot_all, replica * rows, rows, axis=1)
            return lax.dot_general(
                block, piece, (((0,), (0,)), ((), ())), preferred_element_type=f32
            )

        def weight_one(piece):
            return part(me_dp, piece), swap_pairs(part(1 - me_dp, piece).astype(bf16), "dp", 1)

    grad_query, signal, lags = by_channel(
        lag_kernel,
        tables,
        [own_part, other_part, state, queries, prior, key_rows, value_rows],
        [[rows16], [rows16], [jax.ShapeDtypeStruct((taps, channels), f32)]],
        channels,
        unit * (2 * taps + 4 * length + 3 * taps),
    )
    later = lax.ppermute(signal[:taps], "seq", [(i + 1, i) for i in range(n_seq - 1)])

    def run_back(later):
        return by_channel(
            functools.partial(back_kernel, scale),
            tables,
            [signal, later, filter_taps, skip_gain[None], key_rows, value_rows],
            [[rows16], [rows16]],
            channels,
            256 * unit * (4 * taps + 5 * length),
        )

    share = taps // n_dp
    received = swap_pairs(
        lax.dynamic_slice_in_dim(lags, (1 - me_dp) * share, share, axis=0).astype(bf16), "dp", 1
    )
    if square:
        weight_place, halves[1][2], signal = lax.optimization_barrier((weight_place, halves[1][2], signal))
        ring_step(halves[1])
        first_sent, first_own = weight_sum(weight_place, cot_pieces, halves[0], rows)
        first_received = swap_pairs(first_sent, "dp", 1)
        received, first_own = lax.optimization_barrier((received, first_own))
    lag_sum = lax.dynamic_slice_in_dim(lags, me_dp * share, share, axis=0) + received.astype(f32)
    distance = 1
    while distance < n_seq:
        rounded = lag_sum.astype(bf16)
        received = swap_pairs(rounded, "seq", distance)
        if square and distance == 1:
            second_sent, second_own = weight_sum(weight_place, cot_pieces, halves[1], rows)
            second_received = swap_pairs(second_sent, "dp", 1)
            received, second_own = lax.optimization_barrier((received, second_own))
        lag_sum = rounded.astype(f32) + received.astype(f32)
        distance *= 2
    if square:
        first_received, lag_sum = lax.optimization_barrier((first_received, lag_sum))
    mine = lag_sum.astype(bf16)
    theirs = swap_pairs(mine, "dp", 1)
    grad_key, grad_value = run_back(after(later, second_own) if square else later)
    first = me_dp == 0
    lag_sum = jnp.concatenate([jnp.where(first, mine, theirs), jnp.where(first, theirs, mine)], axis=0)
    grad_filter = lag_sum.astype(f32).T * (norm_factor * scale)

    if square:
        parts = [(first_own, first_received), (second_own, second_received)]
    else:
        parts = [weight_one(half) for half in gated_all]
    grad_weight = jnp.concatenate(
        [(mine + theirs.astype(f32)) * norm_factor for mine, theirs in parts], axis=1
    )
    return (
        grad_query[None],
        grad_key[None],
        grad_value[None],
        grad_filter,
        grad_filter[:, 0],
        grad_weight,
    )


def solution(mesh):
    tokens = P("dp", "seq", "tp")
    return jax.shard_map(
        per_device,
        mesh=mesh,
        in_specs=(tokens, tokens, tokens, P("tp", None), P("tp"), P("tp", "dp"), tokens),
        out_specs=(tokens, tokens, tokens, P("tp", None), P("tp"), P(("seq", "dp"), "tp")),
        check_vma=False,
    )
```

```python
import functools
import math

import jax
import jax.numpy as jnp
import ml_dtypes
import numpy as np
from jax import lax
from jax.experimental import pallas as pl
from jax.experimental.pallas import tpu as pltpu
from jax.sharding import PartitionSpec as P

f32, bf16 = jnp.float32, jnp.bfloat16
lanes = 512
turn = 256
vmem_bytes = 58 * 1024 * 1024


def analysis_table(size, positions):
    half = size // 2
    omega = 2.0 * np.pi * (np.arange(half) + 0.5) / size
    angle = omega[:, None] * np.asarray(positions)[None, :]
    return np.concatenate([np.cos(angle), -np.sin(angle)], axis=0)


def split_table(table):
    high = table.astype(ml_dtypes.bfloat16)
    low = (table - high.astype(np.float64)).astype(ml_dtypes.bfloat16)
    return np.concatenate([high, low])


def split_rows(rows):
    high = rows.astype(bf16)
    return high, (rows - high.astype(f32)).astype(bf16)


def dot(left, right):
    return jnp.dot(left, right, preferred_element_type=f32)


def dot_nt(left, right):
    return lax.dot_general(left, right, (((1,), (1,)), ((), ())), preferred_element_type=f32)


def add_halves(both):
    half = both.shape[0] // 2
    return both[:half] + both[half:]


def forward_transform(table, rows, start):
    return add_halves(dot(table[:, pl.ds(start, rows.shape[0])], rows))


def inverse_transform(table, spectrum, start, count):
    high, low = split_rows(spectrum)
    upper = table[pl.ds(start, count)]
    lower = table[pl.ds(table.shape[0] // 2 + start, count)]
    return dot(upper, high) + dot(upper, low) + dot(lower, high)


def spectrum_product(left, right, conjugate_right):
    half = left.shape[0] // 2
    left_re, left_im = left[:half], left[half:]
    right_re, right_im = right[:half], right[half:]
    if conjugate_right:
        right_im = -right_im
    return jnp.concatenate(
        [left_re * right_re - left_im * right_im, left_re * right_im + left_im * right_re], axis=0
    )


def mixed_spectrum(table, prior_ref, key_ref, value_ref):
    mixed = (key_ref[...].astype(f32) * value_ref[...].astype(f32)).astype(bf16)
    prior = prior_ref[...]
    return forward_transform(table, prior, 0) + forward_transform(table, mixed, prior.shape[0])


def filter_spectrum(scale, table, taps_ref, skip_ref):
    taps = taps_ref.shape[1]
    filt = add_halves(dot_nt(table[:, :taps], taps_ref[...]))
    half = filt.shape[0] // 2
    return jnp.concatenate([(filt[:half] + skip_ref[...]) * scale, filt[half:] * scale], axis=0)


def state_kernel(
    scale, table, synth, prior_ref, key_ref, value_ref, taps_ref, skip_ref, query_ref, state_ref, gated_ref
):
    spec = mixed_spectrum(table, prior_ref, key_ref, value_ref)
    product = spectrum_product(spec, filter_spectrum(scale, table, taps_ref, skip_ref), False)
    state = inverse_transform(synth, product, prior_ref.shape[0], query_ref.shape[0])
    state_ref[...] = state
    gated_ref[...] = (query_ref[...].astype(f32) * state).astype(bf16)


def project_kernel(
    place_ref, first_mine, second_mine, first_theirs, second_theirs, weight, other, own, pieces, blocks, others, owns, piece_sem, block_sem, out_sem
):
    steps, _, total_width = blocks.shape
    length, width = first_mine.shape

    def piece_copy(n, sub, source):
        rows = pl.ds(n * length, length)
        columns = pl.ds(pl.multiple_of(place_ref[1 + sub] * width, width), width)
        return pltpu.make_async_copy(source, pieces.at[rows, columns], piece_sem.at[n, sub])

    def block_copy(i):
        return pltpu.make_async_copy(weight.at[pl.ds(i * lanes, lanes)], blocks.at[i], block_sem.at[i])

    def out_copies(i):
        columns = pl.ds(pl.multiple_of(i * lanes, lanes), lanes)
        return [
            pltpu.make_async_copy(others.at[i], other.at[:, columns], out_sem.at[0, i]),
            pltpu.make_async_copy(owns.at[i], own.at[:, columns], out_sem.at[1, i]),
        ]

    for i in range(steps):
        block_copy(i).start()

    def fetch(own_first):
        for sub, (first, second) in enumerate([(first_mine, second_mine), (first_theirs, second_theirs)]):
            piece_copy(0, sub, second if own_first else first).start()
            piece_copy(1, sub, first if own_first else second).start()

    pl.when(place_ref[0] != 0)(lambda: fetch(True))
    pl.when(place_ref[0] == 0)(lambda: fetch(False))
    for n in range(2):
        for sub in range(2):
            piece_copy(n, sub, first_mine).wait()

    @pl.loop(0, steps)
    def _(i):
        block_copy(i).wait()
        total = dot_nt(pieces[...], blocks[i])
        others[i] = total[:length].astype(bf16)
        owns[i] = total[length:]
        for copy in out_copies(i):
            copy.start()

    for i in range(steps):
        for copy in out_copies(i):
            copy.wait()


def weight_kernel(count, place_ref, *refs):
    cot_in, gated_in = refs[:count], refs[count : 2 * count]
    other, own, cots, gateds, others, owns, in_sem, out_sem = refs[2 * count :]
    length = gateds.shape[1]
    rows = other.shape[0]
    block = min(rows, lanes)
    copies = [pltpu.make_async_copy(cot_in[n], cots.at[n], in_sem.at[0, n]) for n in range(count)]
    copies += [pltpu.make_async_copy(gated_in[n], gateds.at[n], in_sem.at[1, n]) for n in range(count)]
    for copy in copies:
        copy.start()
    for copy in copies:
        copy.wait()
    outs = [
        pltpu.make_async_copy(others, other, out_sem.at[0]),
        pltpu.make_async_copy(owns, own, out_sem.at[1]),
    ]

    def fill(replica, target):
        @pl.loop(0, rows // block)
        def _(i):
            start = pl.multiple_of(replica * rows + i * block, block)
            total = None
            for n in range(count):
                part = dot(cots[n, pl.ds(start, block), :], gateds[place_ref[n]])
                total = part if total is None else total + part
            target[pl.ds(pl.multiple_of(i * block, block), block), :] = total.astype(target.dtype)

    me = place_ref[count]
    fill(1 - me, others)
    outs[0].start()
    fill(me, owns)
    outs[1].start()
    for copy in outs:
        copy.wait()


def lag_kernel(
    table,
    synth,
    own_ref,
    other_ref,
    state_ref,
    query_ref,
    prior_ref,
    key_ref,
    value_ref,
    place_ref,
    grad_ref,
    signal_ref,
    head_ref,
    sent_lag_ref,
    own_lag_ref,
):
    length, taps, share = signal_ref.shape[0], prior_ref.shape[0], own_lag_ref.shape[0]
    grad_gated = own_ref[...] + other_ref[...].astype(f32)
    grad_ref[...] = (grad_gated * state_ref[...]).astype(bf16)
    signal = (grad_gated * query_ref[...].astype(f32)).astype(bf16)
    signal_ref[...] = signal
    head_ref[...] = signal[:taps]
    spec = mixed_spectrum(table, prior_ref, key_ref, value_ref)
    product = spectrum_product(forward_transform(table, signal, 0), spec, True)
    lags = -inverse_transform(synth, product, length, taps)
    first = place_ref[...] == 0.0
    own_lag_ref[...] = jnp.where(first, lags[:share], lags[share:])
    sent_lag_ref[...] = jnp.where(first, lags[share:], lags[:share]).astype(bf16)


def back_kernel(
    scale, table, synth, signal_ref, later_ref, taps_ref, skip_ref, key_ref, value_ref, grad_key_ref, grad_value_ref
):
    length = key_ref.shape[0]
    spec = forward_transform(table, signal_ref[...], 0) + forward_transform(table, later_ref[...], length)
    product = spectrum_product(spec, filter_spectrum(scale, table, taps_ref, skip_ref), True)
    back = inverse_transform(synth, product, 0, length)
    grad_key_ref[...] = (back * value_ref[...].astype(f32)).astype(bf16)
    grad_value_ref[...] = (back * key_ref[...].astype(f32)).astype(bf16)


def estimate(flops, arrays):
    moved = sum(a.size * jnp.dtype(a.dtype).itemsize for a in arrays)
    return pl.CostEstimate(flops=flops // 64, bytes_accessed=moved // 64, transcendentals=0)


def by_channel(body, tables, args, outs, channels, flops):
    steps = channels // lanes
    flat_outs = [o for group in outs for o in group]
    n_tables, n_args, n_outs = len(tables), len(args), len(outs)

    def part(ref, i, count):
        start = i * lanes
        if ref.shape[1] == count * lanes:
            return ref.at[:, pl.ds(start, lanes)]
        return ref.at[pl.ds(start, lanes), :]

    def kernel(*refs):
        refs = list(refs)
        take = lambda count: [refs.pop(0) for _ in range(count)]
        table_in, arg_in, outs_to = take(n_tables), take(n_args), take(len(flat_outs))
        table_held, arg_held, out_held = take(n_tables), take(n_args), take(n_outs)
        table_sem, arg_sem, out_sem = refs
        groups = [[outs_to.pop(0) for _ in group] for group in outs]

        def table_copy(k):
            return pltpu.make_async_copy(table_in[k], table_held[k], table_sem.at[k])

        def arg_copy(k):
            return pltpu.make_async_copy(arg_in[k], arg_held[k], arg_sem.at[k])

        def out_copy(k, n, i):
            per = steps // len(groups[k])
            place = part(groups[k][n], i - n * per, per)
            return pltpu.make_async_copy(out_held[k].at[i], place, out_sem.at[k, i])

        for k in range(n_tables):
            table_copy(k).start()
        for k in range(n_args):
            arg_copy(k).start()
        for k in range(n_tables):
            table_copy(k).wait()
        for k in range(n_args):
            arg_copy(k).wait()

        for i in range(steps):
            body(*table_held, *[part(ref, i, steps) for ref in arg_held], *[held.at[i] for held in out_held])
            for k in range(n_outs):
                out_copy(k, i * len(groups[k]) // steps, i).start()

        for i in range(steps):
            for k in range(n_outs):
                out_copy(k, i * len(groups[k]) // steps, i).wait()

    return pl.pallas_call(
        kernel,
        in_specs=[pl.BlockSpec(memory_space=pl.ANY)] * (n_tables + n_args),
        out_specs=[pl.BlockSpec(memory_space=pl.ANY)] * len(flat_outs),
        out_shape=flat_outs,
        scratch_shapes=[
            *[pltpu.VMEM(t.shape, bf16) for t in tables],
            *[pltpu.VMEM(a.shape, a.dtype) for a in args],
            *[pltpu.VMEM((steps, group[0].shape[0], lanes), group[0].dtype) for group in outs],
            pltpu.SemaphoreType.DMA((n_tables,)),
            pltpu.SemaphoreType.DMA((n_args,)),
            pltpu.SemaphoreType.DMA((n_outs, steps)),
        ],
        compiler_params=pltpu.CompilerParams(vmem_limit_bytes=vmem_bytes),
        cost_estimate=estimate(flops, [*args, *flat_outs]),
    )(*[jnp.asarray(t) for t in tables], *args)


def local_call(kernel, places, args, outs, scratch, flops):
    return pl.pallas_call(
        kernel,
        in_specs=[pl.BlockSpec(memory_space=pltpu.SMEM)] + [pl.BlockSpec(memory_space=pl.ANY)] * len(args),
        out_specs=[pl.BlockSpec(memory_space=pl.ANY)] * len(outs),
        out_shape=outs,
        scratch_shapes=scratch,
        compiler_params=pltpu.CompilerParams(vmem_limit_bytes=vmem_bytes),
        cost_estimate=estimate(flops, [*args, *outs]),
    )(places, *args)


def project(places, firsts, seconds, out_weight):
    length, width = firsts[0].shape
    channels, total_width = out_weight.shape
    steps = channels // lanes
    return local_call(
        project_kernel,
        places,
        [firsts[0], seconds[0], firsts[1], seconds[1], out_weight],
        [jax.ShapeDtypeStruct((length, channels), dtype) for dtype in (bf16, f32)],
        [
            pltpu.VMEM((2 * length, total_width), bf16),
            pltpu.VMEM((steps, lanes, total_width), bf16),
            pltpu.VMEM((steps, length, lanes), bf16),
            pltpu.VMEM((steps, length, lanes), f32),
            pltpu.SemaphoreType.DMA((2, 2)),
            pltpu.SemaphoreType.DMA((steps,)),
            pltpu.SemaphoreType.DMA((2, steps)),
        ],
        256 * length * out_weight.size,
    )


def weight_sum(places, cot_pieces, gated_pieces, rows):
    count = len(gated_pieces)
    length, width = gated_pieces[0].shape
    outs = [jax.ShapeDtypeStruct((rows, width), dtype) for dtype in (bf16, f32)]
    return local_call(
        functools.partial(weight_kernel, count),
        places,
        [*cot_pieces, *gated_pieces],
        outs,
        [
            pltpu.VMEM((count, *cot_pieces[0].shape), bf16),
            pltpu.VMEM((count, length, width), bf16),
            *[pltpu.VMEM(o.shape, o.dtype) for o in outs],
            pltpu.SemaphoreType.DMA((2, count)),
            pltpu.SemaphoreType.DMA((2,)),
        ],
        4 * count * length * rows * width,
    )


def transpose_kernel(rows_in, out, rows, turned, sems):
    copy = pltpu.make_async_copy(rows_in, rows, sems.at[0])
    copy.start()
    copy.wait()
    for i in range(rows.shape[1] // turn):
        turned[pl.ds(i * turn, turn), :] = rows[:, pl.ds(i * turn, turn)].T
    copy = pltpu.make_async_copy(turned, out, sems.at[1])
    copy.start()
    copy.wait()


def transposed(rows):
    return pl.pallas_call(
        transpose_kernel,
        in_specs=[pl.BlockSpec(memory_space=pl.ANY)],
        out_specs=pl.BlockSpec(memory_space=pl.ANY),
        out_shape=jax.ShapeDtypeStruct(rows.shape[::-1], rows.dtype),
        scratch_shapes=[
            pltpu.VMEM(rows.shape, rows.dtype),
            pltpu.VMEM(rows.shape[::-1], rows.dtype),
            pltpu.SemaphoreType.DMA((2,)),
        ],
        compiler_params=pltpu.CompilerParams(vmem_limit_bytes=vmem_bytes),
        cost_estimate=estimate(0, [rows, rows]),
    )(rows)


def swap_pairs(value, axis, distance):
    count = lax.axis_size(axis)
    return lax.ppermute(value, axis, [(i, i ^ distance) for i in range(count)])


def after(value, *earlier):
    return lax.optimization_barrier((value, *earlier))[0]


def per_device(query_gate, key_gate, value_input, filter_taps, skip_gain, out_weight, cotangent):
    queries, key_rows, value_rows, cot = (
        query_gate[0],
        key_gate[0],
        value_input[0],
        cotangent[0],
    )
    length, channels = queries.shape
    taps = filter_taps.shape[1]
    n_seq, n_tp, n_dp = lax.axis_size("seq"), lax.axis_size("tp"), lax.axis_size("dp")
    subs = n_tp // n_dp
    me_tp, me_dp = lax.axis_index("tp"), lax.axis_index("dp")
    me_half, me_sub = me_tp // subs, me_tp % subs
    size = length + taps
    norm_factor = 1.0 / math.sqrt(length * n_seq * n_dp)

    whole = analysis_table(size, np.arange(size))
    scale = 2.0 / size
    tables = [split_table(whole), np.ascontiguousarray(split_table(whole.T))]
    rows16 = jax.ShapeDtypeStruct((length, channels), bf16)
    rows32 = jax.ShapeDtypeStruct((length, channels), f32)
    half16 = jax.ShapeDtypeStruct((length, channels // 2), bf16)
    unit = 2 * size * channels

    tail = (
        key_rows[length - taps :].astype(f32) * value_rows[length - taps :].astype(f32)
    ).astype(bf16)
    tail, cot = lax.optimization_barrier((tail, cot))
    prior = lax.ppermute(tail, "seq", [(i, i + 1) for i in range(n_seq - 1)])

    def tp_dp(half, sub, replica):
        return (half * subs + sub) * n_dp + replica

    places = [(h, c, d) for h in range(n_dp) for c in range(subs) for d in range(n_dp)]
    rounds = []
    for turn in range(2):
        route = [(tp_dp(h, c, d), tp_dp(d ^ turn, c, h)) for h, c, d in places]
        rounds.append(lax.ppermute(after(cot, prior) if turn else cot, ("tp", "dp"), route))
    square = n_seq == n_tp == 4 and subs == 2
    if square:

        def holder(s, block):
            return (s + block) % 2 * subs + s // 2

        crossed = {0: (1, 2), 1: (0, 3)}
        route = [
            (s * n_tp + t, s * n_tp + sum(crossed[s % 2]) - t)
            for s in range(n_seq)
            for t in crossed[s % 2]
        ]
        swapped = lax.ppermute(cot, ("seq", "tp"), route)
        moves_now = sum(
            jnp.logical_and(lax.axis_index("seq") % 2 == parity, me_tp == t)
            for parity in crossed
            for t in crossed[parity]
        )
        held = jnp.where(moves_now > 0, swapped, cot)
        route = []
        for s in range(n_seq):
            for t in range(n_tp):
                block = sum(crossed[s % 2]) - t if t in crossed[s % 2] else t
                route.append((s * n_tp + t, block * n_tp + holder(s, block)))
        moved = lax.ppermute(held, ("seq", "tp"), route)
    else:
        moved = cot

    state, *gated = by_channel(
        functools.partial(state_kernel, scale),
        tables,
        [prior, key_rows, value_rows, filter_taps, skip_gain[None], queries],
        [[rows32], [half16, half16]],
        channels,
        unit * (4 * taps + 5 * length),
    )
    dp_row = jnp.broadcast_to(me_dp.astype(f32), (1, channels))
    if square:
        order = [*range(0, n_seq, 2), *reversed(range(1, n_seq, 2))]
        ring = [(order[k], order[(k + 1) % n_seq]) for k in range(n_seq)]
        halves = [[half] for half in gated]

        def ring_step(pieces):
            pieces.append(lax.ppermute(pieces[-1], "seq", ring))

        ring_step(halves[0])
        table = np.zeros((n_seq, n_tp, n_tp), np.int32)
        for k, s in enumerate(order):
            for r in range(n_seq):
                for t in range(n_tp):
                    table[s, t, t ^ holder(order[k - r], s)] = r
        sources = jnp.asarray(table)[lax.axis_index("seq"), me_tp]
        weight_place = jnp.concatenate([sources, me_dp[None].astype(jnp.int32)])
        halves[0][1], halves[1][0], weight_place, dp_row, moved, *rounds = lax.optimization_barrier(
            (halves[0][1], halves[1][0], weight_place, dp_row, moved, *rounds)
        )
        ring_step(halves[0])
        ring_step(halves[1])
        moved = transposed(moved)
    else:
        gated[0], *rounds = lax.optimization_barrier((gated[0], *rounds))

    route = [(tp_dp(h, c, d), tp_dp(h, (c + 1) % subs, d)) for h, c, d in places]
    theirs = [lax.ppermute(r, ("tp", "dp"), route) for r in rounds]
    firsts, seconds = zip(rounds, theirs)
    same = (me_half == me_dp).astype(jnp.int32)
    subs_of = [me_sub, (me_sub + 1) % subs]
    place = jnp.stack([same, *subs_of]).astype(jnp.int32)
    rows = n_tp * channels // (n_seq * n_dp)
    if square:
        moved, place = lax.optimization_barrier((moved, place))
    other_sent, own_part = project(place, firsts, seconds, out_weight)
    other_part = swap_pairs(other_sent, "dp", 1)

    if square:
        sent_by = lambda value, flip: lax.ppermute(value, "tp", [(t, t ^ flip) for t in range(n_tp)])
        across = sent_by(moved, subs)
        cot_pieces = [moved, sent_by(moved, 1), across, sent_by(after(across, halves[0][2]), 1)]
        ring_step(halves[0])
        ring_step(halves[1])
        halves[0][3], halves[1][2], own_part = lax.optimization_barrier(
            (halves[0][3], halves[1][2], own_part)
        )
    else:
        full = lax.all_gather(cot, "tp", axis=1, tiled=True)
        cot_all = lax.all_to_all(full, "seq", 1, 0, tiled=True)
        gated_all = [lax.all_gather(half, "seq", axis=0, tiled=True) for half in gated]

        def part(replica, piece):
            block = lax.dynamic_slice_in_dim(cot_all, replica * rows, rows, axis=1)
            return lax.dot_general(
                block, piece, (((0,), (0,)), ((), ())), preferred_element_type=f32
            )

        def weight_one(piece):
            return part(me_dp, piece), swap_pairs(part(1 - me_dp, piece).astype(bf16), "dp", 1)

    share = taps // n_dp
    grad_query, signal, head, sent_lag, own_lag = by_channel(
        lag_kernel,
        tables,
        [own_part, other_part, state, queries, prior, key_rows, value_rows, dp_row],
        [
            [rows16],
            [rows16],
            [jax.ShapeDtypeStruct((taps, channels), bf16)],
            [jax.ShapeDtypeStruct((share, channels), bf16)],
            [jax.ShapeDtypeStruct((share, channels), f32)],
        ],
        channels,
        unit * (2 * taps + 4 * length + 3 * taps),
    )
    later = lax.ppermute(head, "seq", [(i + 1, i) for i in range(n_seq - 1)])

    def run_back(later):
        return by_channel(
            functools.partial(back_kernel, scale),
            tables,
            [signal, later, filter_taps, skip_gain[None], key_rows, value_rows],
            [[rows16], [rows16]],
            channels,
            256 * unit * (4 * taps + 5 * length),
        )

    received = swap_pairs(sent_lag, "dp", 1)
    if square:
        ring_step(halves[1])
        weight_place, signal = lax.optimization_barrier((weight_place, signal))
        first_sent, first_own = weight_sum(weight_place, cot_pieces, halves[0], rows)
        first_received = swap_pairs(first_sent, "dp", 1)
        received, first_own = lax.optimization_barrier((received, first_own))
    lag_sum = own_lag + received.astype(f32)
    distance = 1
    while distance < n_seq:
        rounded = lag_sum.astype(bf16)
        received = swap_pairs(rounded, "seq", distance)
        if square and distance == 1:
            second_sent, second_own = weight_sum(weight_place, cot_pieces, halves[1], rows)
            second_received = swap_pairs(second_sent, "dp", 1)
            received, second_own = lax.optimization_barrier((received, second_own))
        lag_sum = rounded.astype(f32) + received.astype(f32)
        distance *= 2
    if square:
        first_received, lag_sum = lax.optimization_barrier((first_received, lag_sum))
    mine = lag_sum.astype(bf16)
    theirs = swap_pairs(mine, "dp", 1)
    grad_key, grad_value = run_back(after(later, second_own) if square else later)
    first = me_dp == 0
    lag_sum = jnp.concatenate([jnp.where(first, mine, theirs), jnp.where(first, theirs, mine)], axis=0)
    grad_filter = lag_sum.astype(f32).T * (norm_factor * scale)

    if square:
        parts = [(first_own, first_received), (second_own, second_received)]
    else:
        parts = [weight_one(half) for half in gated_all]
    grad_weight = jnp.concatenate(
        [(mine + theirs.astype(f32)) * norm_factor for mine, theirs in parts], axis=1
    )
    return (
        grad_query[None],
        grad_key[None],
        grad_value[None],
        grad_filter,
        grad_filter[:, 0],
        grad_weight,
    )


def solution(mesh):
    tokens = P("dp", "seq", "tp")
    return jax.shard_map(
        per_device,
        mesh=mesh,
        in_specs=(tokens, tokens, tokens, P("tp", None), P("tp"), P("tp", "dp"), tokens),
        out_specs=(tokens, tokens, tokens, P("tp", None), P("tp"), P(("seq", "dp"), "tp")),
        check_vma=False,
    )
```

```python
import functools
import math

import jax
import jax.numpy as jnp
import ml_dtypes
import numpy as np
from jax import lax
from jax.experimental import pallas as pl
from jax.experimental.pallas import tpu as pltpu
from jax.sharding import PartitionSpec as P

f32, bf16 = jnp.float32, jnp.bfloat16
lanes = 512
turn = 256
vmem_bytes = 58 * 1024 * 1024


def analysis_table(size, positions):
    half = size // 2
    omega = 2.0 * np.pi * (np.arange(half) + 0.5) / size
    angle = omega[:, None] * np.asarray(positions)[None, :]
    return np.concatenate([np.cos(angle), -np.sin(angle)], axis=0)


def split_table(table):
    high = table.astype(ml_dtypes.bfloat16)
    low = (table - high.astype(np.float64)).astype(ml_dtypes.bfloat16)
    return np.concatenate([high, low])


def split_rows(rows):
    high = rows.astype(bf16)
    return high, (rows - high.astype(f32)).astype(bf16)


def dot(left, right):
    return jnp.dot(left, right, preferred_element_type=f32)


def dot_nt(left, right):
    return lax.dot_general(left, right, (((1,), (1,)), ((), ())), preferred_element_type=f32)


def add_halves(both):
    half = both.shape[0] // 2
    return both[:half] + both[half:]


def forward_transform(table, rows, start):
    return add_halves(dot(table[:, pl.ds(start, rows.shape[0])], rows))


def inverse_transform(table, spectrum, start, count):
    high, low = split_rows(spectrum)
    upper = table[pl.ds(start, count)]
    lower = table[pl.ds(table.shape[0] // 2 + start, count)]
    return dot(upper, high) + dot(upper, low) + dot(lower, high)


def spectrum_product(left, right, conjugate_right):
    half = left.shape[0] // 2
    left_re, left_im = left[:half], left[half:]
    right_re, right_im = right[:half], right[half:]
    if conjugate_right:
        right_im = -right_im
    return jnp.concatenate(
        [left_re * right_re - left_im * right_im, left_re * right_im + left_im * right_re], axis=0
    )


def mixed_spectrum(table, prior_ref, key_ref, value_ref):
    mixed = (key_ref[...].astype(f32) * value_ref[...].astype(f32)).astype(bf16)
    prior = prior_ref[...]
    return forward_transform(table, prior, 0) + forward_transform(table, mixed, prior.shape[0])


def filter_spectrum(scale, table, taps_ref, skip_ref):
    taps = taps_ref.shape[1]
    filt = add_halves(dot_nt(table[:, :taps], taps_ref[...]))
    half = filt.shape[0] // 2
    return jnp.concatenate([(filt[:half] + skip_ref[...]) * scale, filt[half:] * scale], axis=0)


def state_kernel(
    scale, table, synth, prior_ref, key_ref, value_ref, taps_ref, skip_ref, query_ref, state_ref, gated_ref
):
    spec = mixed_spectrum(table, prior_ref, key_ref, value_ref)
    product = spectrum_product(spec, filter_spectrum(scale, table, taps_ref, skip_ref), False)
    state = inverse_transform(synth, product, prior_ref.shape[0], query_ref.shape[0])
    state_ref[...] = state
    gated_ref[...] = (query_ref[...].astype(f32) * state).astype(bf16)


def project_kernel(
    place_ref, first_mine, second_mine, first_theirs, second_theirs, weight, other, own, pieces, blocks, others, owns, piece_sem, block_sem, out_sem
):
    steps, _, total_width = blocks.shape
    length, width = first_mine.shape

    def piece_copy(n, sub, source):
        rows = pl.ds(n * length, length)
        columns = pl.ds(pl.multiple_of(place_ref[1 + sub] * width, width), width)
        return pltpu.make_async_copy(source, pieces.at[rows, columns], piece_sem.at[n, sub])

    def block_copy(i):
        return pltpu.make_async_copy(weight.at[pl.ds(i * lanes, lanes)], blocks.at[i], block_sem.at[i])

    def out_copies(i):
        columns = pl.ds(pl.multiple_of(i * lanes, lanes), lanes)
        return [
            pltpu.make_async_copy(others.at[i], other.at[:, columns], out_sem.at[0, i]),
            pltpu.make_async_copy(owns.at[i], own.at[:, columns], out_sem.at[1, i]),
        ]

    for i in range(steps):
        block_copy(i).start()

    def fetch(own_first):
        for sub, (first, second) in enumerate([(first_mine, second_mine), (first_theirs, second_theirs)]):
            piece_copy(0, sub, second if own_first else first).start()
            piece_copy(1, sub, first if own_first else second).start()

    pl.when(place_ref[0] != 0)(lambda: fetch(True))
    pl.when(place_ref[0] == 0)(lambda: fetch(False))
    for n in range(2):
        for sub in range(2):
            piece_copy(n, sub, first_mine).wait()

    @pl.loop(0, steps)
    def _(i):
        block_copy(i).wait()
        total = dot_nt(pieces[...], blocks[i])
        others[i] = total[:length].astype(bf16)
        owns[i] = total[length:]
        for copy in out_copies(i):
            copy.start()

    for i in range(steps):
        for copy in out_copies(i):
            copy.wait()


def weight_kernel(count, place_ref, *refs):
    cot_in, gated_in = refs[:count], refs[count : 2 * count]
    other, own, cots, gateds, others, owns, in_sem, out_sem = refs[2 * count :]
    length = gateds.shape[1]
    rows = other.shape[0]
    block = min(rows, lanes)
    copies = [pltpu.make_async_copy(cot_in[n], cots.at[n], in_sem.at[0, n]) for n in range(count)]
    copies += [pltpu.make_async_copy(gated_in[n], gateds.at[n], in_sem.at[1, n]) for n in range(count)]
    for copy in copies:
        copy.start()
    for copy in copies:
        copy.wait()
    outs = [
        pltpu.make_async_copy(others, other, out_sem.at[0]),
        pltpu.make_async_copy(owns, own, out_sem.at[1]),
    ]

    def fill(replica, target):
        @pl.loop(0, rows // block)
        def _(i):
            start = pl.multiple_of(replica * rows + i * block, block)
            total = None
            for n in range(count):
                part = dot(cots[n, pl.ds(start, block), :], gateds[place_ref[n]])
                total = part if total is None else total + part
            target[pl.ds(pl.multiple_of(i * block, block), block), :] = total.astype(target.dtype)

    me = place_ref[count]
    fill(1 - me, others)
    outs[0].start()
    fill(me, owns)
    outs[1].start()
    for copy in outs:
        copy.wait()


def lag_kernel(
    table,
    synth,
    own_ref,
    other_ref,
    state_ref,
    query_ref,
    prior_ref,
    key_ref,
    value_ref,
    place_ref,
    grad_ref,
    signal_ref,
    head_ref,
    sent_lag_ref,
    own_lag_ref,
):
    length, taps, share = signal_ref.shape[0], prior_ref.shape[0], own_lag_ref.shape[0]
    grad_gated = own_ref[...] + other_ref[...].astype(f32)
    grad_ref[...] = (grad_gated * state_ref[...]).astype(bf16)
    signal = (grad_gated * query_ref[...].astype(f32)).astype(bf16)
    signal_ref[...] = signal
    head_ref[...] = signal[:taps]
    spec = mixed_spectrum(table, prior_ref, key_ref, value_ref)
    product = spectrum_product(forward_transform(table, signal, 0), spec, True)
    lags = -inverse_transform(synth, product, length, taps)
    first = place_ref[...] == 0.0
    own_lag_ref[...] = jnp.where(first, lags[:share], lags[share:])
    sent_lag_ref[...] = jnp.where(first, lags[share:], lags[:share]).astype(bf16)


def back_kernel(
    scale, table, synth, signal_ref, later_ref, taps_ref, skip_ref, key_ref, value_ref, grad_key_ref, grad_value_ref
):
    length = key_ref.shape[0]
    spec = forward_transform(table, signal_ref[...], 0) + forward_transform(table, later_ref[...], length)
    product = spectrum_product(spec, filter_spectrum(scale, table, taps_ref, skip_ref), True)
    back = inverse_transform(synth, product, 0, length)
    grad_key_ref[...] = (back * value_ref[...].astype(f32)).astype(bf16)
    grad_value_ref[...] = (back * key_ref[...].astype(f32)).astype(bf16)


def estimate(flops, arrays):
    moved = sum(a.size * jnp.dtype(a.dtype).itemsize for a in arrays)
    return pl.CostEstimate(flops=flops // 64, bytes_accessed=moved // 64, transcendentals=0)


def by_channel(body, tables, args, outs, channels, flops):
    steps = channels // lanes
    flat_outs = [o for group in outs for o in group]
    n_tables, n_args, n_outs = len(tables), len(args), len(outs)

    def part(ref, i, count):
        start = i * lanes
        if ref.shape[1] == count * lanes:
            return ref.at[:, pl.ds(start, lanes)]
        return ref.at[pl.ds(start, lanes), :]

    def kernel(*refs):
        refs = list(refs)
        take = lambda count: [refs.pop(0) for _ in range(count)]
        table_in, arg_in, outs_to = take(n_tables), take(n_args), take(len(flat_outs))
        table_held, arg_held, out_held = take(n_tables), take(n_args), take(n_outs)
        table_sem, arg_sem, out_sem = refs
        groups = [[outs_to.pop(0) for _ in group] for group in outs]

        def table_copy(k):
            return pltpu.make_async_copy(table_in[k], table_held[k], table_sem.at[k])

        def arg_copy(k):
            return pltpu.make_async_copy(arg_in[k], arg_held[k], arg_sem.at[k])

        def out_copy(k, n, i):
            per = steps // len(groups[k])
            place = part(groups[k][n], i - n * per, per)
            return pltpu.make_async_copy(out_held[k].at[i], place, out_sem.at[k, i])

        for k in range(n_tables):
            table_copy(k).start()
        for k in range(n_args):
            arg_copy(k).start()
        for k in range(n_tables):
            table_copy(k).wait()
        for k in range(n_args):
            arg_copy(k).wait()

        for i in range(steps):
            body(*table_held, *[part(ref, i, steps) for ref in arg_held], *[held.at[i] for held in out_held])
            for k in range(n_outs):
                out_copy(k, i * len(groups[k]) // steps, i).start()

        for i in range(steps):
            for k in range(n_outs):
                out_copy(k, i * len(groups[k]) // steps, i).wait()

    return pl.pallas_call(
        kernel,
        in_specs=[pl.BlockSpec(memory_space=pl.ANY)] * (n_tables + n_args),
        out_specs=[pl.BlockSpec(memory_space=pl.ANY)] * len(flat_outs),
        out_shape=flat_outs,
        scratch_shapes=[
            *[pltpu.VMEM(t.shape, bf16) for t in tables],
            *[pltpu.VMEM(a.shape, a.dtype) for a in args],
            *[pltpu.VMEM((steps, group[0].shape[0], lanes), group[0].dtype) for group in outs],
            pltpu.SemaphoreType.DMA((n_tables,)),
            pltpu.SemaphoreType.DMA((n_args,)),
            pltpu.SemaphoreType.DMA((n_outs, steps)),
        ],
        compiler_params=pltpu.CompilerParams(vmem_limit_bytes=vmem_bytes),
        cost_estimate=estimate(flops, [*args, *flat_outs]),
    )(*[jnp.asarray(t) for t in tables], *args)


def local_call(kernel, places, args, outs, scratch, flops):
    return pl.pallas_call(
        kernel,
        in_specs=[pl.BlockSpec(memory_space=pltpu.SMEM)] + [pl.BlockSpec(memory_space=pl.ANY)] * len(args),
        out_specs=[pl.BlockSpec(memory_space=pl.ANY)] * len(outs),
        out_shape=outs,
        scratch_shapes=scratch,
        compiler_params=pltpu.CompilerParams(vmem_limit_bytes=vmem_bytes),
        cost_estimate=estimate(flops, [*args, *outs]),
    )(places, *args)


def project(places, firsts, seconds, out_weight):
    length, width = firsts[0].shape
    channels, total_width = out_weight.shape
    steps = channels // lanes
    return local_call(
        project_kernel,
        places,
        [firsts[0], seconds[0], firsts[1], seconds[1], out_weight],
        [jax.ShapeDtypeStruct((length, channels), dtype) for dtype in (bf16, f32)],
        [
            pltpu.VMEM((2 * length, total_width), bf16),
            pltpu.VMEM((steps, lanes, total_width), bf16),
            pltpu.VMEM((steps, length, lanes), bf16),
            pltpu.VMEM((steps, length, lanes), f32),
            pltpu.SemaphoreType.DMA((2, 2)),
            pltpu.SemaphoreType.DMA((steps,)),
            pltpu.SemaphoreType.DMA((2, steps)),
        ],
        4 * length * out_weight.size,
    )


def weight_sum(places, cot_pieces, gated_pieces, rows):
    count = len(gated_pieces)
    length, width = gated_pieces[0].shape
    outs = [jax.ShapeDtypeStruct((rows, width), dtype) for dtype in (bf16, f32)]
    return local_call(
        functools.partial(weight_kernel, count),
        places,
        [*cot_pieces, *gated_pieces],
        outs,
        [
            pltpu.VMEM((count, *cot_pieces[0].shape), bf16),
            pltpu.VMEM((count, length, width), bf16),
            *[pltpu.VMEM(o.shape, o.dtype) for o in outs],
            pltpu.SemaphoreType.DMA((2, count)),
            pltpu.SemaphoreType.DMA((2,)),
        ],
        4 * count * length * rows * width,
    )


def transpose_kernel(rows_in, out, rows, turned, sems):
    copy = pltpu.make_async_copy(rows_in, rows, sems.at[0])
    copy.start()
    copy.wait()
    for i in range(rows.shape[1] // turn):
        turned[pl.ds(i * turn, turn), :] = rows[:, pl.ds(i * turn, turn)].T
    copy = pltpu.make_async_copy(turned, out, sems.at[1])
    copy.start()
    copy.wait()


def transposed(rows):
    return pl.pallas_call(
        transpose_kernel,
        in_specs=[pl.BlockSpec(memory_space=pl.ANY)],
        out_specs=pl.BlockSpec(memory_space=pl.ANY),
        out_shape=jax.ShapeDtypeStruct(rows.shape[::-1], rows.dtype),
        scratch_shapes=[
            pltpu.VMEM(rows.shape, rows.dtype),
            pltpu.VMEM(rows.shape[::-1], rows.dtype),
            pltpu.SemaphoreType.DMA((2,)),
        ],
        compiler_params=pltpu.CompilerParams(vmem_limit_bytes=vmem_bytes),
        cost_estimate=estimate(0, [rows, rows]),
    )(rows)


def swap_pairs(value, axis, distance):
    count = lax.axis_size(axis)
    return lax.ppermute(value, axis, [(i, i ^ distance) for i in range(count)])


def after(value, *earlier):
    return lax.optimization_barrier((value, *earlier))[0]


def per_device(query_gate, key_gate, value_input, filter_taps, skip_gain, out_weight, cotangent):
    queries, key_rows, value_rows, cot = (
        query_gate[0],
        key_gate[0],
        value_input[0],
        cotangent[0],
    )
    length, channels = queries.shape
    taps = filter_taps.shape[1]
    n_seq, n_tp, n_dp = lax.axis_size("seq"), lax.axis_size("tp"), lax.axis_size("dp")
    subs = n_tp // n_dp
    me_tp, me_dp = lax.axis_index("tp"), lax.axis_index("dp")
    me_half, me_sub = me_tp // subs, me_tp % subs
    size = length + taps
    norm_factor = 1.0 / math.sqrt(length * n_seq * n_dp)

    whole = analysis_table(size, np.arange(size))
    scale = 2.0 / size
    tables = [split_table(whole), np.ascontiguousarray(split_table(whole.T))]
    rows16 = jax.ShapeDtypeStruct((length, channels), bf16)
    rows32 = jax.ShapeDtypeStruct((length, channels), f32)
    half16 = jax.ShapeDtypeStruct((length, channels // 2), bf16)
    unit = 2 * size * channels

    tail = (
        key_rows[length - taps :].astype(f32) * value_rows[length - taps :].astype(f32)
    ).astype(bf16)
    tail, cot = lax.optimization_barrier((tail, cot))
    prior = lax.ppermute(tail, "seq", [(i, i + 1) for i in range(n_seq - 1)])

    def tp_dp(half, sub, replica):
        return (half * subs + sub) * n_dp + replica

    places = [(h, c, d) for h in range(n_dp) for c in range(subs) for d in range(n_dp)]
    rounds = []
    for turn in range(2):
        route = [(tp_dp(h, c, d), tp_dp(d ^ turn, c, h)) for h, c, d in places]
        rounds.append(lax.ppermute(after(cot, prior) if turn else cot, ("tp", "dp"), route))
    square = n_seq == n_tp == 4 and subs == 2
    if square:

        def holder(s, block):
            return (s + block) % 2 * subs + s // 2

        crossed = {0: (1, 2), 1: (0, 3)}
        route = [
            (s * n_tp + t, s * n_tp + sum(crossed[s % 2]) - t)
            for s in range(n_seq)
            for t in crossed[s % 2]
        ]
        swapped = lax.ppermute(cot, ("seq", "tp"), route)
        moves_now = sum(
            jnp.logical_and(lax.axis_index("seq") % 2 == parity, me_tp == t)
            for parity in crossed
            for t in crossed[parity]
        )
        held = jnp.where(moves_now > 0, swapped, cot)
        route = []
        for s in range(n_seq):
            for t in range(n_tp):
                block = sum(crossed[s % 2]) - t if t in crossed[s % 2] else t
                route.append((s * n_tp + t, block * n_tp + holder(s, block)))
        moved = lax.ppermute(held, ("seq", "tp"), route)
    else:
        moved = cot

    same = (me_half == me_dp).astype(jnp.int32)
    subs_of = [me_sub, (me_sub + 1) % subs]
    place = jnp.stack([same, *subs_of]).astype(jnp.int32)
    dp_row = jnp.broadcast_to(me_dp.astype(f32), (1, channels))
    if square:
        order = [*range(0, n_seq, 2), *reversed(range(1, n_seq, 2))]
        ring = [(order[k], order[(k + 1) % n_seq]) for k in range(n_seq)]
        table = np.zeros((n_seq, n_tp, n_tp), np.int32)
        for k, s in enumerate(order):
            for r in range(n_seq):
                for t in range(n_tp):
                    table[s, t, t ^ holder(order[k - r], s)] = r
        sources = jnp.asarray(table)[lax.axis_index("seq"), me_tp]
        weight_place = jnp.concatenate([sources, me_dp[None].astype(jnp.int32)])
        prior, place, weight_place, dp_row = lax.optimization_barrier(
            (prior, place, weight_place, dp_row)
        )
    state, *gated = by_channel(
        functools.partial(state_kernel, scale),
        tables,
        [prior, key_rows, value_rows, filter_taps, skip_gain[None], queries],
        [[rows32], [half16, half16]],
        channels,
        unit * (4 * taps + 5 * length),
    )
    if square:
        halves = [[half] for half in gated]

        def ring_step(pieces):
            pieces.append(lax.ppermute(pieces[-1], "seq", ring))

        halves[0][0], moved = lax.optimization_barrier((halves[0][0], moved))
        ring_step(halves[0])
        halves[1][0], *rounds = lax.optimization_barrier((halves[1][0], *rounds))
    else:
        gated[0], *rounds = lax.optimization_barrier((gated[0], *rounds))

    route = [(tp_dp(h, c, d), tp_dp(h, (c + 1) % subs, d)) for h, c, d in places]
    theirs = [lax.ppermute(r, ("tp", "dp"), route) for r in rounds]
    firsts, seconds = zip(rounds, theirs)
    rows = n_tp * channels // (n_seq * n_dp)
    if square:
        moved = transposed(after(moved, *rounds))
        moved, place = lax.optimization_barrier((moved, place))
    other_sent, own_part = project(place, firsts, seconds, out_weight)
    other_part = swap_pairs(other_sent, "dp", 1)
    if square:
        halves[0][1], halves[1][0], _ = lax.optimization_barrier(
            (halves[0][1], halves[1][0], other_sent)
        )
        ring_step(halves[0])
        ring_step(halves[1])

    if square:
        sent_by = lambda value, flip: lax.ppermute(value, "tp", [(t, t ^ flip) for t in range(n_tp)])
        across = sent_by(moved, subs)
        cot_pieces = [moved, sent_by(moved, 1), across, sent_by(after(across, halves[0][2]), 1)]
        halves[0][2], halves[1][1], own_part = lax.optimization_barrier(
            (halves[0][2], halves[1][1], own_part)
        )
        ring_step(halves[0])
        ring_step(halves[1])
    else:
        full = lax.all_gather(cot, "tp", axis=1, tiled=True)
        cot_all = lax.all_to_all(full, "seq", 1, 0, tiled=True)
        gated_all = [lax.all_gather(half, "seq", axis=0, tiled=True) for half in gated]

        def part(replica, piece):
            block = lax.dynamic_slice_in_dim(cot_all, replica * rows, rows, axis=1)
            return lax.dot_general(
                block, piece, (((0,), (0,)), ((), ())), preferred_element_type=f32
            )

        def weight_one(piece):
            return part(me_dp, piece), swap_pairs(part(1 - me_dp, piece).astype(bf16), "dp", 1)

    share = taps // n_dp
    grad_query, signal, head, sent_lag, own_lag = by_channel(
        lag_kernel,
        tables,
        [own_part, other_part, state, queries, prior, key_rows, value_rows, dp_row],
        [
            [rows16],
            [rows16],
            [jax.ShapeDtypeStruct((taps, channels), bf16)],
            [jax.ShapeDtypeStruct((share, channels), bf16)],
            [jax.ShapeDtypeStruct((share, channels), f32)],
        ],
        channels,
        unit * (2 * taps + 4 * length + 3 * taps),
    )
    later = lax.ppermute(head, "seq", [(i + 1, i) for i in range(n_seq - 1)])

    def run_back(later):
        return by_channel(
            functools.partial(back_kernel, scale),
            tables,
            [signal, later, filter_taps, skip_gain[None], key_rows, value_rows],
            [[rows16], [rows16]],
            channels,
            256 * unit * (4 * taps + 5 * length),
        )

    received = swap_pairs(sent_lag, "dp", 1)
    if square:
        weight_place, halves[1][2], signal = lax.optimization_barrier((weight_place, halves[1][2], signal))
        ring_step(halves[1])
        first_sent, first_own = weight_sum(weight_place, cot_pieces, halves[0], rows)
        first_received = swap_pairs(first_sent, "dp", 1)
        received, first_own = lax.optimization_barrier((received, first_own))
    lag_sum = own_lag + received.astype(f32)
    distance = 1
    while distance < n_seq:
        rounded = lag_sum.astype(bf16)
        received = swap_pairs(rounded, "seq", distance)
        if square and distance == 1:
            second_sent, second_own = weight_sum(weight_place, cot_pieces, halves[1], rows)
            second_received = swap_pairs(second_sent, "dp", 1)
            received, second_own = lax.optimization_barrier((received, second_own))
        lag_sum = rounded.astype(f32) + received.astype(f32)
        distance *= 2
    if square:
        first_received, lag_sum = lax.optimization_barrier((first_received, lag_sum))
    mine = lag_sum.astype(bf16)
    theirs = swap_pairs(mine, "dp", 1)
    grad_key, grad_value = run_back(after(later, second_own) if square else later)
    first = me_dp == 0
    lag_sum = jnp.concatenate([jnp.where(first, mine, theirs), jnp.where(first, theirs, mine)], axis=0)
    grad_filter = lag_sum.astype(f32).T * (norm_factor * scale)

    if square:
        parts = [(first_own, first_received), (second_own, second_received)]
    else:
        parts = [weight_one(half) for half in gated_all]
    grad_weight = jnp.concatenate(
        [(mine + theirs.astype(f32)) * norm_factor for mine, theirs in parts], axis=1
    )
    return (
        grad_query[None],
        grad_key[None],
        grad_value[None],
        grad_filter,
        grad_filter[:, 0],
        grad_weight,
    )


def solution(mesh):
    tokens = P("dp", "seq", "tp")
    return jax.shard_map(
        per_device,
        mesh=mesh,
        in_specs=(tokens, tokens, tokens, P("tp", None), P("tp"), P("tp", "dp"), tokens),
        out_specs=(tokens, tokens, tokens, P("tp", None), P("tp"), P(("seq", "dp"), "tp")),
        check_vma=False,
    )
```

```python
import functools
import math

import jax
import jax.numpy as jnp
import ml_dtypes
import numpy as np
from jax import lax
from jax.experimental import pallas as pl
from jax.experimental.pallas import tpu as pltpu
from jax.sharding import PartitionSpec as P

f32, bf16 = jnp.float32, jnp.bfloat16
lanes = 512
turn = 256
vmem_bytes = 58 * 1024 * 1024


def analysis_table(size, positions):
    half = size // 2
    omega = 2.0 * np.pi * (np.arange(half) + 0.5) / size
    angle = omega[:, None] * np.asarray(positions)[None, :]
    return np.concatenate([np.cos(angle), -np.sin(angle)], axis=0)


def split_table(table):
    high = table.astype(ml_dtypes.bfloat16)
    low = (table - high.astype(np.float64)).astype(ml_dtypes.bfloat16)
    return np.concatenate([high, low])


def split_rows(rows):
    high = rows.astype(bf16)
    return high, (rows - high.astype(f32)).astype(bf16)


def dot(left, right):
    return jnp.dot(left, right, preferred_element_type=f32)


def dot_nt(left, right):
    return lax.dot_general(left, right, (((1,), (1,)), ((), ())), preferred_element_type=f32)


def add_halves(both):
    half = both.shape[0] // 2
    return both[:half] + both[half:]


def forward_transform(table, rows, start):
    return add_halves(dot(table[:, pl.ds(start, rows.shape[0])], rows))


def inverse_transform(table, spectrum, start, count):
    high, low = split_rows(spectrum)
    upper = table[pl.ds(start, count)]
    lower = table[pl.ds(table.shape[0] // 2 + start, count)]
    return dot(upper, high) + dot(upper, low) + dot(lower, high)


def spectrum_product(left, right, conjugate_right):
    half = left.shape[0] // 2
    left_re, left_im = left[:half], left[half:]
    right_re, right_im = right[:half], right[half:]
    if conjugate_right:
        right_im = -right_im
    return jnp.concatenate(
        [left_re * right_re - left_im * right_im, left_re * right_im + left_im * right_re], axis=0
    )


def mixed_spectrum(table, prior_ref, key_ref, value_ref):
    mixed = (key_ref[...].astype(f32) * value_ref[...].astype(f32)).astype(bf16)
    prior = prior_ref[...]
    return forward_transform(table, prior, 0) + forward_transform(table, mixed, prior.shape[0])


def filter_spectrum(scale, table, taps_ref, skip_ref):
    taps = taps_ref.shape[1]
    filt = add_halves(dot_nt(table[:, :taps], taps_ref[...]))
    half = filt.shape[0] // 2
    return jnp.concatenate([(filt[:half] + skip_ref[...]) * scale, filt[half:] * scale], axis=0)


def state_kernel(
    scale, table, synth, prior_ref, key_ref, value_ref, taps_ref, skip_ref, query_ref, state_ref, gated_ref
):
    spec = mixed_spectrum(table, prior_ref, key_ref, value_ref)
    product = spectrum_product(spec, filter_spectrum(scale, table, taps_ref, skip_ref), False)
    state = inverse_transform(synth, product, prior_ref.shape[0], query_ref.shape[0])
    state_ref[...] = state
    gated_ref[...] = (query_ref[...].astype(f32) * state).astype(bf16)


def project_kernel(
    place_ref, first_mine, second_mine, first_theirs, second_theirs, weight, other, own, pieces, blocks, others, owns, piece_sem, block_sem, out_sem
):
    steps, _, total_width = blocks.shape
    length, width = first_mine.shape

    def piece_copy(n, sub, source):
        rows = pl.ds(n * length, length)
        columns = pl.ds(pl.multiple_of(place_ref[1 + sub] * width, width), width)
        return pltpu.make_async_copy(source, pieces.at[rows, columns], piece_sem.at[n, sub])

    def block_copy(i):
        return pltpu.make_async_copy(weight.at[pl.ds(i * lanes, lanes)], blocks.at[i], block_sem.at[i])

    def out_copies(i):
        columns = pl.ds(pl.multiple_of(i * lanes, lanes), lanes)
        return [
            pltpu.make_async_copy(others.at[i], other.at[:, columns], out_sem.at[0, i]),
            pltpu.make_async_copy(owns.at[i], own.at[:, columns], out_sem.at[1, i]),
        ]

    for i in range(steps):
        block_copy(i).start()

    def fetch(own_first):
        for sub, (first, second) in enumerate([(first_mine, second_mine), (first_theirs, second_theirs)]):
            piece_copy(0, sub, second if own_first else first).start()
            piece_copy(1, sub, first if own_first else second).start()

    pl.when(place_ref[0] != 0)(lambda: fetch(True))
    pl.when(place_ref[0] == 0)(lambda: fetch(False))
    for n in range(2):
        for sub in range(2):
            piece_copy(n, sub, first_mine).wait()

    @pl.loop(0, steps)
    def _(i):
        block_copy(i).wait()
        total = dot_nt(pieces[...], blocks[i])
        others[i] = total[:length].astype(bf16)
        owns[i] = total[length:]
        for copy in out_copies(i):
            copy.start()

    for i in range(steps):
        for copy in out_copies(i):
            copy.wait()


def weight_kernel(count, place_ref, *refs):
    cot_in, gated_in = refs[:count], refs[count : 2 * count]
    other, own, cots, gateds, others, owns, in_sem, out_sem = refs[2 * count :]
    length = gateds.shape[1]
    rows = other.shape[0]
    block = min(rows, lanes)
    copies = [pltpu.make_async_copy(cot_in[n], cots.at[n], in_sem.at[0, n]) for n in range(count)]
    copies += [pltpu.make_async_copy(gated_in[n], gateds.at[n], in_sem.at[1, n]) for n in range(count)]
    for copy in copies:
        copy.start()
    for copy in copies:
        copy.wait()
    outs = [
        pltpu.make_async_copy(others, other, out_sem.at[0]),
        pltpu.make_async_copy(owns, own, out_sem.at[1]),
    ]

    def fill(replica, target):
        @pl.loop(0, rows // block)
        def _(i):
            start = pl.multiple_of(replica * rows + i * block, block)
            total = None
            for n in range(count):
                part = dot(cots[n, pl.ds(start, block), :], gateds[place_ref[n]])
                total = part if total is None else total + part
            target[pl.ds(pl.multiple_of(i * block, block), block), :] = total.astype(target.dtype)

    me = place_ref[count]
    fill(1 - me, others)
    outs[0].start()
    fill(me, owns)
    outs[1].start()
    for copy in outs:
        copy.wait()


def lag_kernel(
    table,
    synth,
    own_ref,
    other_ref,
    state_ref,
    query_ref,
    prior_ref,
    key_ref,
    value_ref,
    place_ref,
    grad_ref,
    signal_ref,
    head_ref,
    sent_lag_ref,
    own_lag_ref,
):
    length, taps, share = signal_ref.shape[0], prior_ref.shape[0], own_lag_ref.shape[0]
    grad_gated = own_ref[...] + other_ref[...].astype(f32)
    grad_ref[...] = (grad_gated * state_ref[...]).astype(bf16)
    signal = (grad_gated * query_ref[...].astype(f32)).astype(bf16)
    signal_ref[...] = signal
    head_ref[...] = signal[:taps]
    spec = mixed_spectrum(table, prior_ref, key_ref, value_ref)
    product = spectrum_product(forward_transform(table, signal, 0), spec, True)
    lags = -inverse_transform(synth, product, length, taps)
    first = place_ref[...] == 0.0
    own_lag_ref[...] = jnp.where(first, lags[:share], lags[share:])
    sent_lag_ref[...] = jnp.where(first, lags[share:], lags[:share]).astype(bf16)


def back_kernel(
    scale, table, synth, signal_ref, later_ref, taps_ref, skip_ref, key_ref, value_ref, grad_key_ref, grad_value_ref
):
    length = key_ref.shape[0]
    spec = forward_transform(table, signal_ref[...], 0) + forward_transform(table, later_ref[...], length)
    product = spectrum_product(spec, filter_spectrum(scale, table, taps_ref, skip_ref), True)
    back = inverse_transform(synth, product, 0, length)
    grad_key_ref[...] = (back * value_ref[...].astype(f32)).astype(bf16)
    grad_value_ref[...] = (back * key_ref[...].astype(f32)).astype(bf16)


def estimate(flops, arrays):
    moved = sum(a.size * jnp.dtype(a.dtype).itemsize for a in arrays)
    return pl.CostEstimate(flops=flops // 64, bytes_accessed=moved // 64, transcendentals=0)


def by_channel(body, tables, args, outs, channels, flops):
    steps = channels // lanes
    flat_outs = [o for group in outs for o in group]
    n_tables, n_args, n_outs = len(tables), len(args), len(outs)

    def part(ref, i, count):
        start = i * lanes
        if ref.shape[1] == count * lanes:
            return ref.at[:, pl.ds(start, lanes)]
        return ref.at[pl.ds(start, lanes), :]

    def kernel(*refs):
        refs = list(refs)
        take = lambda count: [refs.pop(0) for _ in range(count)]
        table_in, arg_in, outs_to = take(n_tables), take(n_args), take(len(flat_outs))
        table_held, arg_held, out_held = take(n_tables), take(n_args), take(n_outs)
        table_sem, arg_sem, out_sem = refs
        groups = [[outs_to.pop(0) for _ in group] for group in outs]

        def table_copy(k):
            return pltpu.make_async_copy(table_in[k], table_held[k], table_sem.at[k])

        def arg_copy(k):
            return pltpu.make_async_copy(arg_in[k], arg_held[k], arg_sem.at[k])

        def out_copy(k, n, i):
            per = steps // len(groups[k])
            place = part(groups[k][n], i - n * per, per)
            return pltpu.make_async_copy(out_held[k].at[i], place, out_sem.at[k, i])

        for k in range(n_tables):
            table_copy(k).start()
        for k in range(n_args):
            arg_copy(k).start()
        for k in range(n_tables):
            table_copy(k).wait()
        for k in range(n_args):
            arg_copy(k).wait()

        for i in range(steps):
            body(*table_held, *[part(ref, i, steps) for ref in arg_held], *[held.at[i] for held in out_held])
            for k in range(n_outs):
                out_copy(k, i * len(groups[k]) // steps, i).start()

        for i in range(steps):
            for k in range(n_outs):
                out_copy(k, i * len(groups[k]) // steps, i).wait()

    return pl.pallas_call(
        kernel,
        in_specs=[pl.BlockSpec(memory_space=pl.ANY)] * (n_tables + n_args),
        out_specs=[pl.BlockSpec(memory_space=pl.ANY)] * len(flat_outs),
        out_shape=flat_outs,
        scratch_shapes=[
            *[pltpu.VMEM(t.shape, bf16) for t in tables],
            *[pltpu.VMEM(a.shape, a.dtype) for a in args],
            *[pltpu.VMEM((steps, group[0].shape[0], lanes), group[0].dtype) for group in outs],
            pltpu.SemaphoreType.DMA((n_tables,)),
            pltpu.SemaphoreType.DMA((n_args,)),
            pltpu.SemaphoreType.DMA((n_outs, steps)),
        ],
        compiler_params=pltpu.CompilerParams(vmem_limit_bytes=vmem_bytes),
        cost_estimate=estimate(flops, [*args, *flat_outs]),
    )(*[jnp.asarray(t) for t in tables], *args)


def local_call(kernel, places, args, outs, scratch, flops):
    return pl.pallas_call(
        kernel,
        in_specs=[pl.BlockSpec(memory_space=pltpu.SMEM)] + [pl.BlockSpec(memory_space=pl.ANY)] * len(args),
        out_specs=[pl.BlockSpec(memory_space=pl.ANY)] * len(outs),
        out_shape=outs,
        scratch_shapes=scratch,
        compiler_params=pltpu.CompilerParams(vmem_limit_bytes=vmem_bytes),
        cost_estimate=estimate(flops, [*args, *outs]),
    )(places, *args)


def project(places, firsts, seconds, out_weight):
    length, width = firsts[0].shape
    channels, total_width = out_weight.shape
    steps = channels // lanes
    return local_call(
        project_kernel,
        places,
        [firsts[0], seconds[0], firsts[1], seconds[1], out_weight],
        [jax.ShapeDtypeStruct((length, channels), dtype) for dtype in (bf16, f32)],
        [
            pltpu.VMEM((2 * length, total_width), bf16),
            pltpu.VMEM((steps, lanes, total_width), bf16),
            pltpu.VMEM((steps, length, lanes), bf16),
            pltpu.VMEM((steps, length, lanes), f32),
            pltpu.SemaphoreType.DMA((2, 2)),
            pltpu.SemaphoreType.DMA((steps,)),
            pltpu.SemaphoreType.DMA((2, steps)),
        ],
        4 * length * out_weight.size,
    )


def weight_sum(places, cot_pieces, gated_pieces, rows):
    count = len(gated_pieces)
    length, width = gated_pieces[0].shape
    outs = [jax.ShapeDtypeStruct((rows, width), dtype) for dtype in (bf16, f32)]
    return local_call(
        functools.partial(weight_kernel, count),
        places,
        [*cot_pieces, *gated_pieces],
        outs,
        [
            pltpu.VMEM((count, *cot_pieces[0].shape), bf16),
            pltpu.VMEM((count, length, width), bf16),
            *[pltpu.VMEM(o.shape, o.dtype) for o in outs],
            pltpu.SemaphoreType.DMA((2, count)),
            pltpu.SemaphoreType.DMA((2,)),
        ],
        4 * count * length * rows * width,
    )


def transpose_kernel(rows_in, out, rows, turned, sems):
    copy = pltpu.make_async_copy(rows_in, rows, sems.at[0])
    copy.start()
    copy.wait()
    for i in range(rows.shape[1] // turn):
        turned[pl.ds(i * turn, turn), :] = rows[:, pl.ds(i * turn, turn)].T
    copy = pltpu.make_async_copy(turned, out, sems.at[1])
    copy.start()
    copy.wait()


def transposed(rows):
    return pl.pallas_call(
        transpose_kernel,
        in_specs=[pl.BlockSpec(memory_space=pl.ANY)],
        out_specs=pl.BlockSpec(memory_space=pl.ANY),
        out_shape=jax.ShapeDtypeStruct(rows.shape[::-1], rows.dtype),
        scratch_shapes=[
            pltpu.VMEM(rows.shape, rows.dtype),
            pltpu.VMEM(rows.shape[::-1], rows.dtype),
            pltpu.SemaphoreType.DMA((2,)),
        ],
        compiler_params=pltpu.CompilerParams(vmem_limit_bytes=vmem_bytes),
        cost_estimate=estimate(0, [rows, rows]),
    )(rows)


def swap_pairs(value, axis, distance):
    count = lax.axis_size(axis)
    return lax.ppermute(value, axis, [(i, i ^ distance) for i in range(count)])


def after(value, *earlier):
    return lax.optimization_barrier((value, *earlier))[0]


def per_device(query_gate, key_gate, value_input, filter_taps, skip_gain, out_weight, cotangent):
    queries, key_rows, value_rows, cot = (
        query_gate[0],
        key_gate[0],
        value_input[0],
        cotangent[0],
    )
    length, channels = queries.shape
    taps = filter_taps.shape[1]
    n_seq, n_tp, n_dp = lax.axis_size("seq"), lax.axis_size("tp"), lax.axis_size("dp")
    subs = n_tp // n_dp
    me_tp, me_dp = lax.axis_index("tp"), lax.axis_index("dp")
    me_half, me_sub = me_tp // subs, me_tp % subs
    size = length + taps
    norm_factor = 1.0 / math.sqrt(length * n_seq * n_dp)

    whole = analysis_table(size, np.arange(size))
    scale = 2.0 / size
    tables = [split_table(whole), np.ascontiguousarray(split_table(whole.T))]
    rows16 = jax.ShapeDtypeStruct((length, channels), bf16)
    rows32 = jax.ShapeDtypeStruct((length, channels), f32)
    half16 = jax.ShapeDtypeStruct((length, channels // 2), bf16)
    unit = 2 * size * channels

    tail = (
        key_rows[length - taps :].astype(f32) * value_rows[length - taps :].astype(f32)
    ).astype(bf16)
    tail, cot = lax.optimization_barrier((tail, cot))
    prior = lax.ppermute(tail, "seq", [(i, i + 1) for i in range(n_seq - 1)])

    def tp_dp(half, sub, replica):
        return (half * subs + sub) * n_dp + replica

    places = [(h, c, d) for h in range(n_dp) for c in range(subs) for d in range(n_dp)]
    rounds = []
    for turn in range(2):
        route = [(tp_dp(h, c, d), tp_dp(d ^ turn, c, h)) for h, c, d in places]
        rounds.append(lax.ppermute(after(cot, prior) if turn else cot, ("tp", "dp"), route))
    square = n_seq == n_tp == 4 and subs == 2
    if square:

        def holder(s, block):
            return (s + block) % 2 * subs + s // 2

        crossed = {0: (1, 2), 1: (0, 3)}
        route = [
            (s * n_tp + t, s * n_tp + sum(crossed[s % 2]) - t)
            for s in range(n_seq)
            for t in crossed[s % 2]
        ]
        swapped = lax.ppermute(cot, ("seq", "tp"), route)
        moves_now = sum(
            jnp.logical_and(lax.axis_index("seq") % 2 == parity, me_tp == t)
            for parity in crossed
            for t in crossed[parity]
        )
        held = jnp.where(moves_now > 0, swapped, cot)
        route = []
        for s in range(n_seq):
            for t in range(n_tp):
                block = sum(crossed[s % 2]) - t if t in crossed[s % 2] else t
                route.append((s * n_tp + t, block * n_tp + holder(s, block)))
        moved = lax.ppermute(held, ("seq", "tp"), route)
    else:
        moved = cot

    same = (me_half == me_dp).astype(jnp.int32)
    subs_of = [me_sub, (me_sub + 1) % subs]
    place = jnp.stack([same, *subs_of]).astype(jnp.int32)
    dp_row = jnp.broadcast_to(me_dp.astype(f32), (1, channels))
    if square:
        order = [*range(0, n_seq, 2), *reversed(range(1, n_seq, 2))]
        ring = [(order[k], order[(k + 1) % n_seq]) for k in range(n_seq)]
        table = np.zeros((n_seq, n_tp, n_tp), np.int32)
        for k, s in enumerate(order):
            for r in range(n_seq):
                for t in range(n_tp):
                    table[s, t, t ^ holder(order[k - r], s)] = r
        sources = jnp.asarray(table)[lax.axis_index("seq"), me_tp]
        weight_place = jnp.concatenate([sources, me_dp[None].astype(jnp.int32)])
        prior, place, weight_place, dp_row = lax.optimization_barrier(
            (prior, place, weight_place, dp_row)
        )
    state, *gated = by_channel(
        functools.partial(state_kernel, scale),
        tables,
        [prior, key_rows, value_rows, filter_taps, skip_gain[None], queries],
        [[rows32], [half16, half16]],
        channels,
        unit * (4 * taps + 5 * length),
    )
    if square:
        halves = [[half] for half in gated]

        def ring_step(pieces):
            pieces.append(lax.ppermute(pieces[-1], "seq", ring))

        ring_step(halves[0])
        halves[1][0], *rounds = lax.optimization_barrier((halves[1][0], *rounds))
    else:
        gated[0], *rounds = lax.optimization_barrier((gated[0], *rounds))

    route = [(tp_dp(h, c, d), tp_dp(h, (c + 1) % subs, d)) for h, c, d in places]
    theirs = [lax.ppermute(r, ("tp", "dp"), route) for r in rounds]
    firsts, seconds = zip(rounds, theirs)
    rows = n_tp * channels // (n_seq * n_dp)
    if square:
        moved = transposed(after(moved, *rounds))
        moved, place = lax.optimization_barrier((moved, place))
    other_sent, own_part = project(place, firsts, seconds, out_weight)
    other_part = swap_pairs(other_sent, "dp", 1)
    if square:
        halves[0][1] = after(halves[0][1], other_sent)
        ring_step(halves[0])

    if square:
        sent_by = lambda value, flip: lax.ppermute(value, "tp", [(t, t ^ flip) for t in range(n_tp)])
        across = sent_by(moved, subs)
        cot_pieces = [moved, sent_by(moved, 1), across, sent_by(after(across, halves[0][2]), 1)]
        halves[0][2], halves[1][0], own_part = lax.optimization_barrier(
            (halves[0][2], halves[1][0], own_part)
        )
        ring_step(halves[0])
        ring_step(halves[1])
    else:
        full = lax.all_gather(cot, "tp", axis=1, tiled=True)
        cot_all = lax.all_to_all(full, "seq", 1, 0, tiled=True)
        gated_all = [lax.all_gather(half, "seq", axis=0, tiled=True) for half in gated]

        def part(replica, piece):
            block = lax.dynamic_slice_in_dim(cot_all, replica * rows, rows, axis=1)
            return lax.dot_general(
                block, piece, (((0,), (0,)), ((), ())), preferred_element_type=f32
            )

        def weight_one(piece):
            return part(me_dp, piece), swap_pairs(part(1 - me_dp, piece).astype(bf16), "dp", 1)

    share = taps // n_dp
    grad_query, signal, head, sent_lag, own_lag = by_channel(
        lag_kernel,
        tables,
        [own_part, other_part, state, queries, prior, key_rows, value_rows, dp_row],
        [
            [rows16],
            [rows16],
            [jax.ShapeDtypeStruct((taps, channels), bf16)],
            [jax.ShapeDtypeStruct((share, channels), bf16)],
            [jax.ShapeDtypeStruct((share, channels), f32)],
        ],
        channels,
        unit * (2 * taps + 4 * length + 3 * taps),
    )
    later = lax.ppermute(head, "seq", [(i + 1, i) for i in range(n_seq - 1)])

    def run_back(later):
        return by_channel(
            functools.partial(back_kernel, scale),
            tables,
            [signal, later, filter_taps, skip_gain[None], key_rows, value_rows],
            [[rows16], [rows16]],
            channels,
            256 * unit * (4 * taps + 5 * length),
        )

    received = swap_pairs(sent_lag, "dp", 1)
    if square:
        weight_place, halves[1][1], signal = lax.optimization_barrier((weight_place, halves[1][1], signal))
        ring_step(halves[1])
        first_sent, first_own = weight_sum(weight_place, cot_pieces, halves[0], rows)
        first_received = swap_pairs(first_sent, "dp", 1)
        received, first_own, halves[1][2] = lax.optimization_barrier((received, first_own, halves[1][2]))
        ring_step(halves[1])
    lag_sum = own_lag + received.astype(f32)
    distance = 1
    while distance < n_seq:
        rounded = lag_sum.astype(bf16)
        received = swap_pairs(rounded, "seq", distance)
        if square and distance == 1:
            second_sent, second_own = weight_sum(weight_place, cot_pieces, halves[1], rows)
            second_received = swap_pairs(second_sent, "dp", 1)
            received, second_own = lax.optimization_barrier((received, second_own))
        lag_sum = rounded.astype(f32) + received.astype(f32)
        distance *= 2
    if square:
        first_received, lag_sum = lax.optimization_barrier((first_received, lag_sum))
    mine = lag_sum.astype(bf16)
    theirs = swap_pairs(mine, "dp", 1)
    grad_key, grad_value = run_back(after(later, second_own) if square else later)
    first = me_dp == 0
    lag_sum = jnp.concatenate([jnp.where(first, mine, theirs), jnp.where(first, theirs, mine)], axis=0)
    grad_filter = lag_sum.astype(f32).T * (norm_factor * scale)

    if square:
        parts = [(first_own, first_received), (second_own, second_received)]
    else:
        parts = [weight_one(half) for half in gated_all]
    grad_weight = jnp.concatenate(
        [(mine + theirs.astype(f32)) * norm_factor for mine, theirs in parts], axis=1
    )
    return (
        grad_query[None],
        grad_key[None],
        grad_value[None],
        grad_filter,
        grad_filter[:, 0],
        grad_weight,
    )


def solution(mesh):
    tokens = P("dp", "seq", "tp")
    return jax.shard_map(
        per_device,
        mesh=mesh,
        in_specs=(tokens, tokens, tokens, P("tp", None), P("tp"), P("tp", "dp"), tokens),
        out_specs=(tokens, tokens, tokens, P("tp", None), P("tp"), P(("seq", "dp"), "tp")),
        check_vma=False,
    )
```

```python
import functools
import math

import jax
import jax.numpy as jnp
import ml_dtypes
import numpy as np
from jax import lax
from jax.experimental import pallas as pl
from jax.experimental.pallas import tpu as pltpu
from jax.sharding import PartitionSpec as P

f32, bf16 = jnp.float32, jnp.bfloat16
lanes = 512
turn = 256
vmem_bytes = 58 * 1024 * 1024


def analysis_table(size, positions):
    half = size // 2
    omega = 2.0 * np.pi * (np.arange(half) + 0.5) / size
    angle = omega[:, None] * np.asarray(positions)[None, :]
    return np.concatenate([np.cos(angle), -np.sin(angle)], axis=0)


def split_table(table):
    high = table.astype(ml_dtypes.bfloat16)
    low = (table - high.astype(np.float64)).astype(ml_dtypes.bfloat16)
    return np.concatenate([high, low])


def split_rows(rows):
    high = rows.astype(bf16)
    return high, (rows - high.astype(f32)).astype(bf16)


def dot(left, right):
    return jnp.dot(left, right, preferred_element_type=f32)


def dot_nt(left, right):
    return lax.dot_general(left, right, (((1,), (1,)), ((), ())), preferred_element_type=f32)


def add_halves(both):
    half = both.shape[0] // 2
    return both[:half] + both[half:]


def forward_transform(table, rows, start):
    return add_halves(dot(table[:, pl.ds(start, rows.shape[0])], rows))


def inverse_transform(table, spectrum, start, count):
    high, low = split_rows(spectrum)
    upper = table[pl.ds(start, count)]
    lower = table[pl.ds(table.shape[0] // 2 + start, count)]
    return dot(upper, high) + dot(upper, low) + dot(lower, high)


def spectrum_product(left, right, conjugate_right):
    half = left.shape[0] // 2
    left_re, left_im = left[:half], left[half:]
    right_re, right_im = right[:half], right[half:]
    if conjugate_right:
        right_im = -right_im
    return jnp.concatenate(
        [left_re * right_re - left_im * right_im, left_re * right_im + left_im * right_re], axis=0
    )


def mixed_spectrum(table, prior_ref, key_ref, value_ref):
    mixed = (key_ref[...].astype(f32) * value_ref[...].astype(f32)).astype(bf16)
    prior = prior_ref[...]
    return forward_transform(table, prior, 0) + forward_transform(table, mixed, prior.shape[0])


def filter_spectrum(scale, table, taps_ref, skip_ref):
    taps = taps_ref.shape[1]
    filt = add_halves(dot_nt(table[:, :taps], taps_ref[...]))
    half = filt.shape[0] // 2
    return jnp.concatenate([(filt[:half] + skip_ref[...]) * scale, filt[half:] * scale], axis=0)


def state_kernel(
    scale, table, synth, prior_ref, key_ref, value_ref, taps_ref, skip_ref, query_ref, state_ref, gated_ref
):
    spec = mixed_spectrum(table, prior_ref, key_ref, value_ref)
    product = spectrum_product(spec, filter_spectrum(scale, table, taps_ref, skip_ref), False)
    state = inverse_transform(synth, product, prior_ref.shape[0], query_ref.shape[0])
    state_ref[...] = state
    gated_ref[...] = (query_ref[...].astype(f32) * state).astype(bf16)


def project_kernel(
    place_ref, first_mine, second_mine, first_theirs, second_theirs, weight, other, own, pieces, blocks, others, owns, piece_sem, block_sem, out_sem
):
    steps, _, total_width = blocks.shape
    length, width = first_mine.shape

    def piece_copy(n, sub, source):
        rows = pl.ds(n * length, length)
        columns = pl.ds(pl.multiple_of(place_ref[1 + sub] * width, width), width)
        return pltpu.make_async_copy(source, pieces.at[rows, columns], piece_sem.at[n, sub])

    def block_copy(i):
        return pltpu.make_async_copy(weight.at[pl.ds(i * lanes, lanes)], blocks.at[i], block_sem.at[i])

    def out_copies(i):
        columns = pl.ds(pl.multiple_of(i * lanes, lanes), lanes)
        return [
            pltpu.make_async_copy(others.at[i], other.at[:, columns], out_sem.at[0, i]),
            pltpu.make_async_copy(owns.at[i], own.at[:, columns], out_sem.at[1, i]),
        ]

    for i in range(steps):
        block_copy(i).start()

    def fetch(own_first):
        for sub, (first, second) in enumerate([(first_mine, second_mine), (first_theirs, second_theirs)]):
            piece_copy(0, sub, second if own_first else first).start()
            piece_copy(1, sub, first if own_first else second).start()

    pl.when(place_ref[0] != 0)(lambda: fetch(True))
    pl.when(place_ref[0] == 0)(lambda: fetch(False))
    for n in range(2):
        for sub in range(2):
            piece_copy(n, sub, first_mine).wait()

    @pl.loop(0, steps)
    def _(i):
        block_copy(i).wait()
        total = dot_nt(pieces[...], blocks[i])
        others[i] = total[:length].astype(bf16)
        owns[i] = total[length:]
        for copy in out_copies(i):
            copy.start()

    for i in range(steps):
        for copy in out_copies(i):
            copy.wait()


def weight_kernel(count, place_ref, *refs):
    cot_in, gated_in = refs[: 2 * count], refs[2 * count : 3 * count]
    other, own, cots, gateds, others, owns, cot_sem, gated_sem, out_sem = refs[3 * count :]
    rows = other.shape[0]
    block = min(rows, turn)
    copies = [pltpu.make_async_copy(gated_in[n], gateds.at[n], gated_sem.at[n]) for n in range(count)]
    copies += [pltpu.make_async_copy(cot_in[n], cots.at[n], cot_sem.at[n]) for n in range(2 * count)]
    for copy in copies:
        copy.start()
    for copy in copies:
        copy.wait()
    outs = [
        pltpu.make_async_copy(others, other, out_sem.at[0]),
        pltpu.make_async_copy(owns, own, out_sem.at[1]),
    ]

    def fill(replica, target):
        @pl.loop(0, rows // block)
        def _(i):
            start = pl.multiple_of(replica * rows + i * block, block)
            total = None
            for n in range(2 * count):
                gated = gateds[place_ref[n % count], n // count]
                part = dot(cots[n, pl.ds(start, block), :], gated)
                total = part if total is None else total + part
            target[pl.ds(pl.multiple_of(i * block, block), block), :] = total.astype(target.dtype)

    me = place_ref[count]
    fill(1 - me, others)
    outs[0].start()
    fill(me, owns)
    outs[1].start()
    for copy in outs:
        copy.wait()


def lag_kernel(
    table,
    synth,
    own_ref,
    other_ref,
    state_ref,
    query_ref,
    prior_ref,
    key_ref,
    value_ref,
    place_ref,
    grad_ref,
    signal_ref,
    head_ref,
    sent_lag_ref,
    own_lag_ref,
):
    length, taps, share = signal_ref.shape[0], prior_ref.shape[0], own_lag_ref.shape[0]
    grad_gated = own_ref[...] + other_ref[...].astype(f32)
    grad_ref[...] = (grad_gated * state_ref[...]).astype(bf16)
    signal = (grad_gated * query_ref[...].astype(f32)).astype(bf16)
    signal_ref[...] = signal
    head_ref[...] = signal[:taps]
    spec = mixed_spectrum(table, prior_ref, key_ref, value_ref)
    product = spectrum_product(forward_transform(table, signal, 0), spec, True)
    lags = -inverse_transform(synth, product, length, taps)
    first = place_ref[...] == 0.0
    own_lag_ref[...] = jnp.where(first, lags[:share], lags[share:])
    sent_lag_ref[...] = jnp.where(first, lags[share:], lags[:share]).astype(bf16)


def back_kernel(
    scale, table, synth, signal_ref, later_ref, taps_ref, skip_ref, key_ref, value_ref, grad_key_ref, grad_value_ref
):
    length = key_ref.shape[0]
    spec = forward_transform(table, signal_ref[...], 0) + forward_transform(table, later_ref[...], length)
    product = spectrum_product(spec, filter_spectrum(scale, table, taps_ref, skip_ref), True)
    back = inverse_transform(synth, product, 0, length)
    grad_key_ref[...] = (back * value_ref[...].astype(f32)).astype(bf16)
    grad_value_ref[...] = (back * key_ref[...].astype(f32)).astype(bf16)


def estimate(flops, arrays):
    moved = sum(a.size * jnp.dtype(a.dtype).itemsize for a in arrays)
    return pl.CostEstimate(flops=flops // 64, bytes_accessed=moved // 64, transcendentals=0)


def by_channel(body, tables, args, outs, channels, flops, swap=None):
    steps = channels // lanes
    flat_outs = [o for group in outs for o in group]
    n_tables, n_args, n_outs = len(tables), len(args), len(outs)

    def part(ref, i, count):
        start = i * lanes
        if ref.shape[1] == count * lanes:
            return ref.at[:, pl.ds(start, lanes)]
        return ref.at[pl.ds(start, lanes), :]

    def kernel(*refs):
        refs = list(refs)
        take = lambda count: [refs.pop(0) for _ in range(count)]
        swap_ref = None if swap is None else refs.pop(0)
        table_in, arg_in, outs_to = take(n_tables), take(n_args), take(len(flat_outs))
        table_held, arg_held, out_held = take(n_tables), take(n_args), take(n_outs)
        table_sem, arg_sem, out_sem = refs
        groups = [[outs_to.pop(0) for _ in group] for group in outs]

        def table_copy(k):
            return pltpu.make_async_copy(table_in[k], table_held[k], table_sem.at[k])

        def arg_copy(k):
            return pltpu.make_async_copy(arg_in[k], arg_held[k], arg_sem.at[k])

        def out_copy(k, n, i):
            place = groups[k][n] if len(groups[k]) > 1 else part(groups[k][n], i, steps)
            return pltpu.make_async_copy(out_held[k].at[i], place, out_sem.at[k, i])

        for k in range(n_tables):
            table_copy(k).start()
        for k in range(n_args):
            arg_copy(k).start()
        for k in range(n_tables):
            table_copy(k).wait()
        for k in range(n_args):
            arg_copy(k).wait()

        for i in range(steps):
            body(*table_held, *[part(ref, i, steps) for ref in arg_held], *[held.at[i] for held in out_held])
            for k in range(n_outs):
                count = len(groups[k])
                if count == 1:
                    out_copy(k, 0, i).start()
                else:
                    pl.when(swap_ref[0] == 0)(out_copy(k, i, i).start)
                    pl.when(swap_ref[0] != 0)(out_copy(k, count - 1 - i, i).start)

        for i in range(steps):
            for k in range(n_outs):
                out_copy(k, 0 if len(groups[k]) == 1 else i, i).wait()

    return pl.pallas_call(
        kernel,
        in_specs=[pl.BlockSpec(memory_space=pltpu.SMEM)] * (swap is not None)
        + [pl.BlockSpec(memory_space=pl.ANY)] * (n_tables + n_args),
        out_specs=[pl.BlockSpec(memory_space=pl.ANY)] * len(flat_outs),
        out_shape=flat_outs,
        scratch_shapes=[
            *[pltpu.VMEM(t.shape, bf16) for t in tables],
            *[pltpu.VMEM(a.shape, a.dtype) for a in args],
            *[pltpu.VMEM((steps, group[0].shape[0], lanes), group[0].dtype) for group in outs],
            pltpu.SemaphoreType.DMA((n_tables,)),
            pltpu.SemaphoreType.DMA((n_args,)),
            pltpu.SemaphoreType.DMA((n_outs, steps)),
        ],
        compiler_params=pltpu.CompilerParams(vmem_limit_bytes=vmem_bytes),
        cost_estimate=estimate(flops, [*args, *flat_outs]),
    )(*([] if swap is None else [swap]), *[jnp.asarray(t) for t in tables], *args)


def local_call(kernel, places, args, outs, scratch, flops):
    return pl.pallas_call(
        kernel,
        in_specs=[pl.BlockSpec(memory_space=pltpu.SMEM)] + [pl.BlockSpec(memory_space=pl.ANY)] * len(args),
        out_specs=[pl.BlockSpec(memory_space=pl.ANY)] * len(outs),
        out_shape=outs,
        scratch_shapes=scratch,
        compiler_params=pltpu.CompilerParams(vmem_limit_bytes=vmem_bytes),
        cost_estimate=estimate(flops, [*args, *outs]),
    )(places, *args)


def project(places, firsts, seconds, out_weight):
    length, width = firsts[0].shape
    channels, total_width = out_weight.shape
    steps = channels // lanes
    return local_call(
        project_kernel,
        places,
        [firsts[0], seconds[0], firsts[1], seconds[1], out_weight],
        [jax.ShapeDtypeStruct((length, channels), dtype) for dtype in (bf16, f32)],
        [
            pltpu.VMEM((2 * length, total_width), bf16),
            pltpu.VMEM((steps, lanes, total_width), bf16),
            pltpu.VMEM((steps, length, lanes), bf16),
            pltpu.VMEM((steps, length, lanes), f32),
            pltpu.SemaphoreType.DMA((2, 2)),
            pltpu.SemaphoreType.DMA((steps,)),
            pltpu.SemaphoreType.DMA((2, steps)),
        ],
        4 * length * out_weight.size,
    )


def weight_sum(places, cot_pieces, gated_pieces, rows):
    count = len(gated_pieces)
    _, length, width = gated_pieces[0].shape
    outs = [jax.ShapeDtypeStruct((rows, width), dtype) for dtype in (bf16, f32)]
    return local_call(
        functools.partial(weight_kernel, count),
        places,
        [*cot_pieces, *gated_pieces],
        outs,
        [
            pltpu.VMEM((2 * count, *cot_pieces[0].shape), bf16),
            pltpu.VMEM((count, *gated_pieces[0].shape), bf16),
            *[pltpu.VMEM(o.shape, o.dtype) for o in outs],
            pltpu.SemaphoreType.DMA((2 * count,)),
            pltpu.SemaphoreType.DMA((count,)),
            pltpu.SemaphoreType.DMA((2,)),
        ],
        8 * count * length * rows * width,
    )


def transpose_kernel(rows_in, out, rows, turned, sems):
    copy = pltpu.make_async_copy(rows_in, rows, sems.at[0])
    copy.start()
    copy.wait()
    for i in range(rows.shape[1] // turn):
        turned[pl.ds(i * turn, turn), :] = rows[:, pl.ds(i * turn, turn)].T
    copy = pltpu.make_async_copy(turned, out, sems.at[1])
    copy.start()
    copy.wait()


def transposed(rows):
    return pl.pallas_call(
        transpose_kernel,
        in_specs=[pl.BlockSpec(memory_space=pl.ANY)],
        out_specs=pl.BlockSpec(memory_space=pl.ANY),
        out_shape=jax.ShapeDtypeStruct(rows.shape[::-1], rows.dtype),
        scratch_shapes=[
            pltpu.VMEM(rows.shape, rows.dtype),
            pltpu.VMEM(rows.shape[::-1], rows.dtype),
            pltpu.SemaphoreType.DMA((2,)),
        ],
        compiler_params=pltpu.CompilerParams(vmem_limit_bytes=vmem_bytes),
        cost_estimate=estimate(0, [rows, rows]),
    )(rows)


def swap_pairs(value, axis, distance):
    count = lax.axis_size(axis)
    return lax.ppermute(value, axis, [(i, i ^ distance) for i in range(count)])


def after(value, *earlier):
    return lax.optimization_barrier((value, *earlier))[0]


def per_device(query_gate, key_gate, value_input, filter_taps, skip_gain, out_weight, cotangent):
    queries, key_rows, value_rows, cot = (
        query_gate[0],
        key_gate[0],
        value_input[0],
        cotangent[0],
    )
    length, channels = queries.shape
    taps = filter_taps.shape[1]
    n_seq, n_tp, n_dp = lax.axis_size("seq"), lax.axis_size("tp"), lax.axis_size("dp")
    subs = n_tp // n_dp
    me_tp, me_dp = lax.axis_index("tp"), lax.axis_index("dp")
    me_half, me_sub = me_tp // subs, me_tp % subs
    size = length + taps
    norm_factor = 1.0 / math.sqrt(length * n_seq * n_dp)

    whole = analysis_table(size, np.arange(size))
    scale = 2.0 / size
    tables = [split_table(whole), np.ascontiguousarray(split_table(whole.T))]
    rows16 = jax.ShapeDtypeStruct((length, channels), bf16)
    rows32 = jax.ShapeDtypeStruct((length, channels), f32)
    half16 = jax.ShapeDtypeStruct((length, channels // 2), bf16)
    unit = 2 * size * channels

    tail = (
        key_rows[length - taps :].astype(f32) * value_rows[length - taps :].astype(f32)
    ).astype(bf16)
    tail, cot = lax.optimization_barrier((tail, cot))
    prior = lax.ppermute(tail, "seq", [(i, i + 1) for i in range(n_seq - 1)])

    def tp_dp(half, sub, replica):
        return (half * subs + sub) * n_dp + replica

    places = [(h, c, d) for h in range(n_dp) for c in range(subs) for d in range(n_dp)]
    rounds = []
    for turn in range(2):
        route = [(tp_dp(h, c, d), tp_dp(d ^ turn, c, h)) for h, c, d in places]
        rounds.append(lax.ppermute(after(cot, prior) if turn else cot, ("tp", "dp"), route))
    square = n_seq == n_tp == 4 and subs == 2
    if square:

        def holder(s, block):
            return (s + block) % 2 * subs + s // 2

        crossed = {0: (1, 2), 1: (0, 3)}
        route = [
            (s * n_tp + t, s * n_tp + sum(crossed[s % 2]) - t)
            for s in range(n_seq)
            for t in crossed[s % 2]
        ]
        swapped = lax.ppermute(cot, ("seq", "tp"), route)
        moves_now = sum(
            jnp.logical_and(lax.axis_index("seq") % 2 == parity, me_tp == t)
            for parity in crossed
            for t in crossed[parity]
        )
        held = jnp.where(moves_now > 0, swapped, cot)
        route = []
        for s in range(n_seq):
            for t in range(n_tp):
                block = sum(crossed[s % 2]) - t if t in crossed[s % 2] else t
                route.append((s * n_tp + t, block * n_tp + holder(s, block)))
        moved = lax.ppermute(held, ("seq", "tp"), route)
    else:
        moved = cot

    same = (me_half == me_dp).astype(jnp.int32)
    subs_of = [me_sub, (me_sub + 1) % subs]
    place = jnp.stack([same, *subs_of]).astype(jnp.int32)
    dp_row = jnp.broadcast_to(me_dp.astype(f32), (1, channels))
    if square:
        order = [*range(0, n_seq, 2), *reversed(range(1, n_seq, 2))]
        ring = [(order[k], order[(k + 1) % n_seq]) for k in range(n_seq)]
        table = np.zeros((n_seq, n_tp, n_tp), np.int32)
        for k, s in enumerate(order):
            for r in range(n_seq):
                for t in range(n_tp):
                    table[s, t, t ^ holder(order[k - r], s)] = r
        sources = jnp.asarray(table)[lax.axis_index("seq"), me_tp]
        weight_place = jnp.concatenate([sources, me_dp[None].astype(jnp.int32)])
        prior, place, weight_place, dp_row = lax.optimization_barrier(
            (prior, place, weight_place, dp_row)
        )
    state, *gated = by_channel(
        functools.partial(state_kernel, scale),
        tables,
        [prior, key_rows, value_rows, filter_taps, skip_gain[None], queries],
        [[rows32], [half16, half16]],
        channels,
        unit * (4 * taps + 5 * length),
        jnp.reshape(me_dp if square else 0 * me_dp, (1,)).astype(jnp.int32),
    )
    if square:
        ring_pieces = [jnp.stack([gated[0], swap_pairs(gated[1], "dp", 1)])]

        def ring_step():
            ring_pieces.append(lax.ppermute(ring_pieces[-1], "seq", ring))

        ring_step()
    gated[0], *rounds = lax.optimization_barrier((gated[0], *rounds))

    route = [(tp_dp(h, c, d), tp_dp(h, (c + 1) % subs, d)) for h, c, d in places]
    theirs = [lax.ppermute(r, ("tp", "dp"), route) for r in rounds]
    firsts, seconds = zip(rounds, theirs)
    rows = n_tp * channels // (n_seq * n_dp)
    if square:
        moved = after(moved, *rounds)
        moved_other = swap_pairs(moved, "dp", 1)
        moved = transposed(moved)
        moved, place = lax.optimization_barrier((moved, place))
    other_sent, own_part = project(place, firsts, seconds, out_weight)
    other_part = swap_pairs(other_sent, "dp", 1)
    if square:

        def spread(piece, gate):
            across = lax.ppermute(piece, "tp", [(t, t ^ subs) for t in range(n_tp)])
            near = [(t, t ^ 1) for t in range(n_tp)]
            return [
                piece,
                lax.ppermute(piece, "tp", near),
                across,
                lax.ppermute(after(across, gate), "tp", near),
            ]

        moved_other = transposed(after(moved_other, other_sent))
        ring_pieces[1] = after(ring_pieces[1], other_sent)
        ring_step()
        ring_pieces[2], own_part = lax.optimization_barrier((ring_pieces[2], own_part))
        ring_step()
        cot_pieces = spread(moved, ring_pieces[2]) + spread(moved_other, own_part)
    else:
        full = lax.all_gather(cot, "tp", axis=1, tiled=True)
        cot_all = lax.all_to_all(full, "seq", 1, 0, tiled=True)
        gated_all = [lax.all_gather(half, "seq", axis=0, tiled=True) for half in gated]

        def part(replica, piece):
            block = lax.dynamic_slice_in_dim(cot_all, replica * rows, rows, axis=1)
            return lax.dot_general(
                block, piece, (((0,), (0,)), ((), ())), preferred_element_type=f32
            )

        def weight_one(piece):
            return part(me_dp, piece), swap_pairs(part(1 - me_dp, piece).astype(bf16), "dp", 1)

    share = taps // n_dp
    grad_query, signal, head, sent_lag, own_lag = by_channel(
        lag_kernel,
        tables,
        [own_part, other_part, state, queries, prior, key_rows, value_rows, dp_row],
        [
            [rows16],
            [rows16],
            [jax.ShapeDtypeStruct((taps, channels), bf16)],
            [jax.ShapeDtypeStruct((share, channels), bf16)],
            [jax.ShapeDtypeStruct((share, channels), f32)],
        ],
        channels,
        unit * (2 * taps + 4 * length + 3 * taps),
    )
    later = lax.ppermute(head, "seq", [(i + 1, i) for i in range(n_seq - 1)])

    def run_back(later):
        return by_channel(
            functools.partial(back_kernel, scale),
            tables,
            [signal, later, filter_taps, skip_gain[None], key_rows, value_rows],
            [[rows16], [rows16]],
            channels,
            256 * unit * (4 * taps + 5 * length),
        )

    received = swap_pairs(sent_lag, "dp", 1)
    if square:
        ring_pieces[3], received = lax.optimization_barrier((ring_pieces[3], received))
    lag_sum = own_lag + received.astype(f32)
    distance = 1
    while distance < n_seq:
        rounded = lag_sum.astype(bf16)
        received = swap_pairs(rounded, "seq", distance)
        if square and distance == 1:
            weight_place, rounded = lax.optimization_barrier((weight_place, rounded))
            weight_sent, weight_own = weight_sum(weight_place, cot_pieces, ring_pieces, rows)
            weight_received = swap_pairs(weight_sent, "dp", 1)
            received, weight_own = lax.optimization_barrier((received, weight_own))
        lag_sum = rounded.astype(f32) + received.astype(f32)
        distance *= 2
    mine = lag_sum.astype(bf16)
    theirs = swap_pairs(mine, "dp", 1)
    grad_key, grad_value = run_back(after(later, weight_own) if square else later)
    first = me_dp == 0
    lag_sum = jnp.concatenate([jnp.where(first, mine, theirs), jnp.where(first, theirs, mine)], axis=0)
    grad_filter = lag_sum.astype(f32).T * (norm_factor * scale)

    if square:
        weight_own, weight_received = weight_own * norm_factor, weight_received.astype(f32) * norm_factor
        grad_weight = jnp.concatenate(
            [
                jnp.where(first, weight_own, weight_received),
                jnp.where(first, weight_received, weight_own),
            ],
            axis=1,
        )
    else:
        parts = [weight_one(half) for half in gated_all]
        grad_weight = jnp.concatenate(
            [(mine + theirs.astype(f32)) * norm_factor for mine, theirs in parts], axis=1
        )
    return (
        grad_query[None],
        grad_key[None],
        grad_value[None],
        grad_filter,
        grad_filter[:, 0],
        grad_weight,
    )


def solution(mesh):
    tokens = P("dp", "seq", "tp")
    return jax.shard_map(
        per_device,
        mesh=mesh,
        in_specs=(tokens, tokens, tokens, P("tp", None), P("tp"), P("tp", "dp"), tokens),
        out_specs=(tokens, tokens, tokens, P("tp", None), P("tp"), P(("seq", "dp"), "tp")),
        check_vma=False,
    )
```

```python
import functools
import math

import jax
import jax.numpy as jnp
import ml_dtypes
import numpy as np
from jax import lax
from jax.experimental import pallas as pl
from jax.experimental.pallas import tpu as pltpu
from jax.sharding import PartitionSpec as P

f32, bf16 = jnp.float32, jnp.bfloat16
lanes = 512
turn = 256
vmem_bytes = 58 * 1024 * 1024


def analysis_table(size, positions):
    half = size // 2
    omega = 2.0 * np.pi * (np.arange(half) + 0.5) / size
    angle = omega[:, None] * np.asarray(positions)[None, :]
    return np.concatenate([np.cos(angle), -np.sin(angle)], axis=0)


def split_table(table):
    high = table.astype(ml_dtypes.bfloat16)
    low = (table - high.astype(np.float64)).astype(ml_dtypes.bfloat16)
    return np.concatenate([high, low])


def split_rows(rows):
    high = rows.astype(bf16)
    return high, (rows - high.astype(f32)).astype(bf16)


def dot(left, right):
    return jnp.dot(left, right, preferred_element_type=f32)


def dot_nt(left, right):
    return lax.dot_general(left, right, (((1,), (1,)), ((), ())), preferred_element_type=f32)


def add_halves(both):
    half = both.shape[0] // 2
    return both[:half] + both[half:]


def forward_transform(table, rows, start):
    return add_halves(dot(table[:, pl.ds(start, rows.shape[0])], rows))


def inverse_transform(table, spectrum, start, count):
    high, low = split_rows(spectrum)
    upper = table[pl.ds(start, count)]
    lower = table[pl.ds(table.shape[0] // 2 + start, count)]
    return dot(upper, high) + dot(upper, low) + dot(lower, high)


def spectrum_product(left, right, conjugate_right):
    half = left.shape[0] // 2
    left_re, left_im = left[:half], left[half:]
    right_re, right_im = right[:half], right[half:]
    if conjugate_right:
        right_im = -right_im
    return jnp.concatenate(
        [left_re * right_re - left_im * right_im, left_re * right_im + left_im * right_re], axis=0
    )


def mixed_spectrum(table, prior_ref, key_ref, value_ref):
    mixed = (key_ref[...].astype(f32) * value_ref[...].astype(f32)).astype(bf16)
    prior = prior_ref[...]
    return forward_transform(table, prior, 0) + forward_transform(table, mixed, prior.shape[0])


def filter_spectrum(scale, table, taps_ref, skip_ref):
    taps = taps_ref.shape[1]
    filt = add_halves(dot_nt(table[:, :taps], taps_ref[...]))
    half = filt.shape[0] // 2
    return jnp.concatenate([(filt[:half] + skip_ref[...]) * scale, filt[half:] * scale], axis=0)


def state_kernel(
    scale, table, synth, prior_ref, key_ref, value_ref, taps_ref, skip_ref, query_ref, state_ref, gated_ref
):
    spec = mixed_spectrum(table, prior_ref, key_ref, value_ref)
    product = spectrum_product(spec, filter_spectrum(scale, table, taps_ref, skip_ref), False)
    state = inverse_transform(synth, product, prior_ref.shape[0], query_ref.shape[0])
    state_ref[...] = state
    gated_ref[...] = (query_ref[...].astype(f32) * state).astype(bf16)


def project_kernel(
    place_ref, first_mine, second_mine, first_theirs, second_theirs, weight, other, own, pieces, blocks, others, owns, piece_sem, block_sem, out_sem
):
    steps, _, total_width = blocks.shape
    length, width = first_mine.shape

    def piece_copy(n, sub, source):
        rows = pl.ds(n * length, length)
        columns = pl.ds(pl.multiple_of(place_ref[1 + sub] * width, width), width)
        return pltpu.make_async_copy(source, pieces.at[rows, columns], piece_sem.at[n, sub])

    def block_copy(i):
        return pltpu.make_async_copy(weight.at[pl.ds(i * lanes, lanes)], blocks.at[i], block_sem.at[i])

    def out_copies(i):
        columns = pl.ds(pl.multiple_of(i * lanes, lanes), lanes)
        return [
            pltpu.make_async_copy(others.at[i], other.at[:, columns], out_sem.at[0, i]),
            pltpu.make_async_copy(owns.at[i], own.at[:, columns], out_sem.at[1, i]),
        ]

    for i in range(steps):
        block_copy(i).start()

    def fetch(own_first):
        for sub, (first, second) in enumerate([(first_mine, second_mine), (first_theirs, second_theirs)]):
            piece_copy(0, sub, second if own_first else first).start()
            piece_copy(1, sub, first if own_first else second).start()

    pl.when(place_ref[0] != 0)(lambda: fetch(True))
    pl.when(place_ref[0] == 0)(lambda: fetch(False))
    for n in range(2):
        for sub in range(2):
            piece_copy(n, sub, first_mine).wait()

    @pl.loop(0, steps)
    def _(i):
        block_copy(i).wait()
        total = dot_nt(pieces[...], blocks[i])
        others[i] = total[:length].astype(bf16)
        owns[i] = total[length:]
        for copy in out_copies(i):
            copy.start()

    for i in range(steps):
        for copy in out_copies(i):
            copy.wait()


def weight_kernel(count, place_ref, *refs):
    cot_in, gated_in = refs[: 2 * count], list(refs[2 * count : 4 * count - 1])
    other, own, cots, gateds, others, owns, cot_sem, gated_sem, out_sem = refs[4 * count - 1 :]
    gated_in[-1:] = [gated_in[-1].at[0], gated_in[-1].at[1]]
    rows = other.shape[0]
    block = min(rows, turn)
    copies = [pltpu.make_async_copy(gated_in[n], gateds.at[n], gated_sem.at[n]) for n in range(2 * count)]
    copies += [pltpu.make_async_copy(cot_in[n], cots.at[n], cot_sem.at[n]) for n in range(2 * count)]
    for copy in copies:
        copy.start()
    for copy in copies:
        copy.wait()
    outs = [
        pltpu.make_async_copy(others, other, out_sem.at[0]),
        pltpu.make_async_copy(owns, own, out_sem.at[1]),
    ]

    def fill(replica, target):
        @pl.loop(0, rows // block)
        def _(i):
            start = pl.multiple_of(replica * rows + i * block, block)
            total = None
            for n in range(2 * count):
                gated = gateds[2 * place_ref[n % count] + n // count]
                part = dot(cots[n, pl.ds(start, block), :], gated)
                total = part if total is None else total + part
            target[pl.ds(pl.multiple_of(i * block, block), block), :] = total.astype(target.dtype)

    me = place_ref[count]
    fill(1 - me, others)
    outs[0].start()
    fill(me, owns)
    outs[1].start()
    for copy in outs:
        copy.wait()


def lag_kernel(
    table,
    synth,
    own_ref,
    other_ref,
    state_ref,
    query_ref,
    prior_ref,
    key_ref,
    value_ref,
    place_ref,
    grad_ref,
    signal_ref,
    head_ref,
    sent_lag_ref,
    own_lag_ref,
):
    length, taps, share = signal_ref.shape[0], prior_ref.shape[0], own_lag_ref.shape[0]
    grad_gated = own_ref[...] + other_ref[...].astype(f32)
    grad_ref[...] = (grad_gated * state_ref[...]).astype(bf16)
    signal = (grad_gated * query_ref[...].astype(f32)).astype(bf16)
    signal_ref[...] = signal
    head_ref[...] = signal[:taps]
    spec = mixed_spectrum(table, prior_ref, key_ref, value_ref)
    product = spectrum_product(forward_transform(table, signal, 0), spec, True)
    lags = -inverse_transform(synth, product, length, taps)
    first = place_ref[...] == 0.0
    own_lag_ref[...] = jnp.where(first, lags[:share], lags[share:])
    sent_lag_ref[...] = jnp.where(first, lags[share:], lags[:share]).astype(bf16)


def back_kernel(
    scale, table, synth, signal_ref, later_ref, taps_ref, skip_ref, key_ref, value_ref, grad_key_ref, grad_value_ref
):
    length = key_ref.shape[0]
    spec = forward_transform(table, signal_ref[...], 0) + forward_transform(table, later_ref[...], length)
    product = spectrum_product(spec, filter_spectrum(scale, table, taps_ref, skip_ref), True)
    back = inverse_transform(synth, product, 0, length)
    grad_key_ref[...] = (back * value_ref[...].astype(f32)).astype(bf16)
    grad_value_ref[...] = (back * key_ref[...].astype(f32)).astype(bf16)


def estimate(flops, arrays):
    moved = sum(a.size * jnp.dtype(a.dtype).itemsize for a in arrays)
    return pl.CostEstimate(flops=flops // 64, bytes_accessed=moved // 64, transcendentals=0)


def by_channel(body, tables, args, outs, channels, flops, swap=None):
    steps = channels // lanes
    flat_outs = [o for group in outs for o in group]
    n_tables, n_args, n_outs = len(tables), len(args), len(outs)

    def part(ref, i, count):
        start = i * lanes
        if ref.shape[1] == count * lanes:
            return ref.at[:, pl.ds(start, lanes)]
        return ref.at[pl.ds(start, lanes), :]

    def kernel(*refs):
        refs = list(refs)
        take = lambda count: [refs.pop(0) for _ in range(count)]
        swap_ref = None if swap is None else refs.pop(0)
        table_in, arg_in, outs_to = take(n_tables), take(n_args), take(len(flat_outs))
        table_held, arg_held, out_held = take(n_tables), take(n_args), take(n_outs)
        table_sem, arg_sem, out_sem = refs
        groups = [[outs_to.pop(0) for _ in group] for group in outs]

        def table_copy(k):
            return pltpu.make_async_copy(table_in[k], table_held[k], table_sem.at[k])

        def arg_copy(k):
            return pltpu.make_async_copy(arg_in[k], arg_held[k], arg_sem.at[k])

        def out_copy(k, n, i):
            place = groups[k][n] if len(groups[k]) > 1 else part(groups[k][n], i, steps)
            return pltpu.make_async_copy(out_held[k].at[i], place, out_sem.at[k, i])

        for k in range(n_tables):
            table_copy(k).start()
        for k in range(n_args):
            arg_copy(k).start()
        for k in range(n_tables):
            table_copy(k).wait()
        for k in range(n_args):
            arg_copy(k).wait()

        for i in range(steps):
            body(*table_held, *[part(ref, i, steps) for ref in arg_held], *[held.at[i] for held in out_held])
            for k in range(n_outs):
                count = len(groups[k])
                if count == 1:
                    out_copy(k, 0, i).start()
                else:
                    pl.when(swap_ref[0] == 0)(out_copy(k, i, i).start)
                    pl.when(swap_ref[0] != 0)(out_copy(k, count - 1 - i, i).start)

        for i in range(steps):
            for k in range(n_outs):
                out_copy(k, 0 if len(groups[k]) == 1 else i, i).wait()

    return pl.pallas_call(
        kernel,
        in_specs=[pl.BlockSpec(memory_space=pltpu.SMEM)] * (swap is not None)
        + [pl.BlockSpec(memory_space=pl.ANY)] * (n_tables + n_args),
        out_specs=[pl.BlockSpec(memory_space=pl.ANY)] * len(flat_outs),
        out_shape=flat_outs,
        scratch_shapes=[
            *[pltpu.VMEM(t.shape, bf16) for t in tables],
            *[pltpu.VMEM(a.shape, a.dtype) for a in args],
            *[pltpu.VMEM((steps, group[0].shape[0], lanes), group[0].dtype) for group in outs],
            pltpu.SemaphoreType.DMA((n_tables,)),
            pltpu.SemaphoreType.DMA((n_args,)),
            pltpu.SemaphoreType.DMA((n_outs, steps)),
        ],
        compiler_params=pltpu.CompilerParams(vmem_limit_bytes=vmem_bytes),
        cost_estimate=estimate(flops, [*args, *flat_outs]),
    )(*([] if swap is None else [swap]), *[jnp.asarray(t) for t in tables], *args)


def local_call(kernel, places, args, outs, scratch, flops):
    return pl.pallas_call(
        kernel,
        in_specs=[pl.BlockSpec(memory_space=pltpu.SMEM)] + [pl.BlockSpec(memory_space=pl.ANY)] * len(args),
        out_specs=[pl.BlockSpec(memory_space=pl.ANY)] * len(outs),
        out_shape=outs,
        scratch_shapes=scratch,
        compiler_params=pltpu.CompilerParams(vmem_limit_bytes=vmem_bytes),
        cost_estimate=estimate(flops, [*args, *outs]),
    )(places, *args)


def project(places, firsts, seconds, out_weight):
    length, width = firsts[0].shape
    channels, total_width = out_weight.shape
    steps = channels // lanes
    return local_call(
        project_kernel,
        places,
        [firsts[0], seconds[0], firsts[1], seconds[1], out_weight],
        [jax.ShapeDtypeStruct((length, channels), dtype) for dtype in (bf16, f32)],
        [
            pltpu.VMEM((2 * length, total_width), bf16),
            pltpu.VMEM((steps, lanes, total_width), bf16),
            pltpu.VMEM((steps, length, lanes), bf16),
            pltpu.VMEM((steps, length, lanes), f32),
            pltpu.SemaphoreType.DMA((2, 2)),
            pltpu.SemaphoreType.DMA((steps,)),
            pltpu.SemaphoreType.DMA((2, steps)),
        ],
        4 * length * out_weight.size,
    )


def weight_sum(places, cot_pieces, gated_pieces, rows):
    count = (len(gated_pieces) + 1) // 2
    length, width = gated_pieces[0].shape
    outs = [jax.ShapeDtypeStruct((rows, width), dtype) for dtype in (bf16, f32)]
    return local_call(
        functools.partial(weight_kernel, count),
        places,
        [*cot_pieces, *gated_pieces],
        outs,
        [
            pltpu.VMEM((2 * count, *cot_pieces[0].shape), bf16),
            pltpu.VMEM((2 * count, *gated_pieces[0].shape), bf16),
            *[pltpu.VMEM(o.shape, o.dtype) for o in outs],
            pltpu.SemaphoreType.DMA((2 * count,)),
            pltpu.SemaphoreType.DMA((2 * count,)),
            pltpu.SemaphoreType.DMA((2,)),
        ],
        8 * count * length * rows * width,
    )


def transpose_kernel(rows_in, out, rows, turned, sems):
    copy = pltpu.make_async_copy(rows_in, rows, sems.at[0])
    copy.start()
    copy.wait()
    for i in range(rows.shape[1] // turn):
        turned[pl.ds(i * turn, turn), :] = rows[:, pl.ds(i * turn, turn)].T
    copy = pltpu.make_async_copy(turned, out, sems.at[1])
    copy.start()
    copy.wait()


def transposed(rows):
    return pl.pallas_call(
        transpose_kernel,
        in_specs=[pl.BlockSpec(memory_space=pl.ANY)],
        out_specs=pl.BlockSpec(memory_space=pl.ANY),
        out_shape=jax.ShapeDtypeStruct(rows.shape[::-1], rows.dtype),
        scratch_shapes=[
            pltpu.VMEM(rows.shape, rows.dtype),
            pltpu.VMEM(rows.shape[::-1], rows.dtype),
            pltpu.SemaphoreType.DMA((2,)),
        ],
        compiler_params=pltpu.CompilerParams(vmem_limit_bytes=vmem_bytes),
        cost_estimate=estimate(0, [rows, rows]),
    )(rows)


def swap_pairs(value, axis, distance):
    count = lax.axis_size(axis)
    return lax.ppermute(value, axis, [(i, i ^ distance) for i in range(count)])


def after(value, *earlier):
    return lax.optimization_barrier((value, *earlier))[0]


def per_device(query_gate, key_gate, value_input, filter_taps, skip_gain, out_weight, cotangent):
    queries, key_rows, value_rows, cot = (
        query_gate[0],
        key_gate[0],
        value_input[0],
        cotangent[0],
    )
    length, channels = queries.shape
    taps = filter_taps.shape[1]
    n_seq, n_tp, n_dp = lax.axis_size("seq"), lax.axis_size("tp"), lax.axis_size("dp")
    subs = n_tp // n_dp
    me_tp, me_dp = lax.axis_index("tp"), lax.axis_index("dp")
    me_half, me_sub = me_tp // subs, me_tp % subs
    size = length + taps
    norm_factor = 1.0 / math.sqrt(length * n_seq * n_dp)

    whole = analysis_table(size, np.arange(size))
    scale = 2.0 / size
    tables = [split_table(whole), np.ascontiguousarray(split_table(whole.T))]
    rows16 = jax.ShapeDtypeStruct((length, channels), bf16)
    rows32 = jax.ShapeDtypeStruct((length, channels), f32)
    half16 = jax.ShapeDtypeStruct((length, channels // 2), bf16)
    unit = 2 * size * channels

    tail = (
        key_rows[length - taps :].astype(f32) * value_rows[length - taps :].astype(f32)
    ).astype(bf16)
    tail, cot = lax.optimization_barrier((tail, cot))
    prior = lax.ppermute(tail, "seq", [(i, i + 1) for i in range(n_seq - 1)])

    def tp_dp(half, sub, replica):
        return (half * subs + sub) * n_dp + replica

    places = [(h, c, d) for h in range(n_dp) for c in range(subs) for d in range(n_dp)]
    rounds = []
    for turn in range(2):
        route = [(tp_dp(h, c, d), tp_dp(d ^ turn, c, h)) for h, c, d in places]
        rounds.append(lax.ppermute(after(cot, prior) if turn else cot, ("tp", "dp"), route))
    square = n_seq == n_tp == 4 and subs == 2
    if square:

        def holder(s, block):
            return (s + block) % 2 * subs + s // 2

        crossed = {0: (1, 2), 1: (0, 3)}
        route = [
            (s * n_tp + t, s * n_tp + sum(crossed[s % 2]) - t)
            for s in range(n_seq)
            for t in crossed[s % 2]
        ]
        swapped = lax.ppermute(cot, ("seq", "tp"), route)
        moves_now = sum(
            jnp.logical_and(lax.axis_index("seq") % 2 == parity, me_tp == t)
            for parity in crossed
            for t in crossed[parity]
        )
        held = jnp.where(moves_now > 0, swapped, cot)
        route = []
        for s in range(n_seq):
            for t in range(n_tp):
                block = sum(crossed[s % 2]) - t if t in crossed[s % 2] else t
                route.append((s * n_tp + t, block * n_tp + holder(s, block)))
        moved = lax.ppermute(held, ("seq", "tp"), route)
    else:
        moved = cot

    same = (me_half == me_dp).astype(jnp.int32)
    subs_of = [me_sub, (me_sub + 1) % subs]
    place = jnp.stack([same, *subs_of]).astype(jnp.int32)
    dp_row = jnp.broadcast_to(me_dp.astype(f32), (1, channels))
    if square:
        order = [*range(0, n_seq, 2), *reversed(range(1, n_seq, 2))]
        ring = [(order[k], order[(k + 1) % n_seq]) for k in range(n_seq)]
        table = np.zeros((n_seq, n_tp, n_tp), np.int32)
        for k, s in enumerate(order):
            for r in range(n_seq):
                for t in range(n_tp):
                    table[s, t, t ^ holder(order[k - r], s)] = r
        sources = jnp.asarray(table)[lax.axis_index("seq"), me_tp]
        weight_place = jnp.concatenate([sources, me_dp[None].astype(jnp.int32)])
        prior, place, weight_place, dp_row = lax.optimization_barrier(
            (prior, place, weight_place, dp_row)
        )
    state, *gated = by_channel(
        functools.partial(state_kernel, scale),
        tables,
        [prior, key_rows, value_rows, filter_taps, skip_gain[None], queries],
        [[rows32], [half16, half16]],
        channels,
        unit * (4 * taps + 5 * length),
        jnp.reshape(me_dp if square else 0 * me_dp, (1,)).astype(jnp.int32),
    )
    if square:
        ring_pieces = [gated[0], swap_pairs(gated[1], "dp", 1)]
        ring_pieces[0], ring_pieces[1], moved = lax.optimization_barrier((*ring_pieces, moved))

        def ring_step():
            for _ in range(2):
                ring_pieces.append(lax.ppermute(ring_pieces[-2], "seq", ring))

        ring_step()
    gated[0], *rounds = lax.optimization_barrier((gated[0], *rounds))

    route = [(tp_dp(h, c, d), tp_dp(h, (c + 1) % subs, d)) for h, c, d in places]
    theirs = [lax.ppermute(r, ("tp", "dp"), route) for r in rounds]
    firsts, seconds = zip(rounds, theirs)
    rows = n_tp * channels // (n_seq * n_dp)
    if square:
        moved = after(moved, *rounds)
        moved_other = swap_pairs(moved, "dp", 1)
        moved = transposed(moved)
        moved, place = lax.optimization_barrier((moved, place))
    other_sent, own_part = project(place, firsts, seconds, out_weight)
    if square:
        other_sent, moved_other = lax.optimization_barrier((other_sent, moved_other))
    other_part = swap_pairs(other_sent, "dp", 1)
    if square:

        def spread(piece, gate):
            across = lax.ppermute(piece, "tp", [(t, t ^ subs) for t in range(n_tp)])
            near = [(t, t ^ 1) for t in range(n_tp)]
            return [
                piece,
                lax.ppermute(piece, "tp", near),
                across,
                lax.ppermute(after(across, gate), "tp", near),
            ]

        ring_pieces[2], ring_pieces[3], _ = lax.optimization_barrier((*ring_pieces[2:4], other_sent))
        ring_step()
        *last, own_part, other_part = lax.optimization_barrier((*ring_pieces[4:6], own_part, other_part))
        last = lax.ppermute(jnp.stack(last), "seq", ring)
        moved_other = transposed(after(moved_other, ring_pieces[2]))
        cot_pieces = spread(moved, ring_pieces[4]) + spread(moved_other, own_part)
    else:
        full = lax.all_gather(cot, "tp", axis=1, tiled=True)
        cot_all = lax.all_to_all(full, "seq", 1, 0, tiled=True)
        gated_all = [lax.all_gather(half, "seq", axis=0, tiled=True) for half in gated]

        def part(replica, piece):
            block = lax.dynamic_slice_in_dim(cot_all, replica * rows, rows, axis=1)
            return lax.dot_general(
                block, piece, (((0,), (0,)), ((), ())), preferred_element_type=f32
            )

        def weight_one(piece):
            return part(me_dp, piece), swap_pairs(part(1 - me_dp, piece).astype(bf16), "dp", 1)

    share = taps // n_dp
    grad_query, signal, head, sent_lag, own_lag = by_channel(
        lag_kernel,
        tables,
        [own_part, other_part, state, queries, prior, key_rows, value_rows, dp_row],
        [
            [rows16],
            [rows16],
            [jax.ShapeDtypeStruct((taps, channels), bf16)],
            [jax.ShapeDtypeStruct((share, channels), bf16)],
            [jax.ShapeDtypeStruct((share, channels), f32)],
        ],
        channels,
        unit * (2 * taps + 4 * length + 3 * taps),
    )
    later = lax.ppermute(head, "seq", [(i + 1, i) for i in range(n_seq - 1)])

    def run_back(later):
        return by_channel(
            functools.partial(back_kernel, scale),
            tables,
            [signal, later, filter_taps, skip_gain[None], key_rows, value_rows],
            [[rows16], [rows16]],
            channels,
            256 * unit * (4 * taps + 5 * length),
        )

    received = swap_pairs(sent_lag, "dp", 1)
    if square:
        last, received = lax.optimization_barrier((last, received))
        ring_pieces.append(last)
    lag_sum = own_lag + received.astype(f32)
    distance = 1
    while distance < n_seq:
        rounded = lag_sum.astype(bf16)
        received = swap_pairs(rounded, "seq", distance)
        if square and distance == 1:
            weight_place, rounded = lax.optimization_barrier((weight_place, rounded))
            weight_sent, weight_own = weight_sum(weight_place, cot_pieces, ring_pieces, rows)
            weight_received = swap_pairs(weight_sent, "dp", 1)
            received, weight_own = lax.optimization_barrier((received, weight_own))
        lag_sum = rounded.astype(f32) + received.astype(f32)
        distance *= 2
    mine = lag_sum.astype(bf16)
    theirs = swap_pairs(mine, "dp", 1)
    grad_key, grad_value = run_back(after(later, weight_own) if square else later)
    first = me_dp == 0
    lag_sum = jnp.concatenate([jnp.where(first, mine, theirs), jnp.where(first, theirs, mine)], axis=0)
    grad_filter = lag_sum.astype(f32).T * (norm_factor * scale)

    if square:
        weight_own, weight_received = weight_own * norm_factor, weight_received.astype(f32) * norm_factor
        grad_weight = jnp.concatenate(
            [
                jnp.where(first, weight_own, weight_received),
                jnp.where(first, weight_received, weight_own),
            ],
            axis=1,
        )
    else:
        parts = [weight_one(half) for half in gated_all]
        grad_weight = jnp.concatenate(
            [(mine + theirs.astype(f32)) * norm_factor for mine, theirs in parts], axis=1
        )
    return (
        grad_query[None],
        grad_key[None],
        grad_value[None],
        grad_filter,
        grad_filter[:, 0],
        grad_weight,
    )


def solution(mesh):
    tokens = P("dp", "seq", "tp")
    return jax.shard_map(
        per_device,
        mesh=mesh,
        in_specs=(tokens, tokens, tokens, P("tp", None), P("tp"), P("tp", "dp"), tokens),
        out_specs=(tokens, tokens, tokens, P("tp", None), P("tp"), P(("seq", "dp"), "tp")),
        check_vma=False,
    )
```

```python
import functools
import math

import jax
import jax.numpy as jnp
import ml_dtypes
import numpy as np
from jax import lax
from jax.experimental import pallas as pl
from jax.experimental.pallas import tpu as pltpu
from jax.sharding import PartitionSpec as P

f32, bf16 = jnp.float32, jnp.bfloat16
lanes = 512
turn = 256
vmem_bytes = 58 * 1024 * 1024


def analysis_table(size, positions):
    half = size // 2
    omega = 2.0 * np.pi * (np.arange(half) + 0.5) / size
    angle = omega[:, None] * np.asarray(positions)[None, :]
    return np.concatenate([np.cos(angle), -np.sin(angle)], axis=0)


def split_table(table):
    high = table.astype(ml_dtypes.bfloat16)
    low = (table - high.astype(np.float64)).astype(ml_dtypes.bfloat16)
    return np.concatenate([high, low])


def split_rows(rows):
    high = rows.astype(bf16)
    return high, (rows - high.astype(f32)).astype(bf16)


def dot(left, right):
    return jnp.dot(left, right, preferred_element_type=f32)


def dot_nt(left, right):
    return lax.dot_general(left, right, (((1,), (1,)), ((), ())), preferred_element_type=f32)


def add_halves(both):
    half = both.shape[0] // 2
    return both[:half] + both[half:]


def forward_transform(table, rows, start):
    return add_halves(dot(table[:, pl.ds(start, rows.shape[0])], rows))


def inverse_transform(table, spectrum, start, count):
    high, low = split_rows(spectrum)
    upper = table[pl.ds(start, count)]
    lower = table[pl.ds(table.shape[0] // 2 + start, count)]
    return dot(upper, high) + dot(upper, low) + dot(lower, high)


def spectrum_product(left, right, conjugate_right):
    half = left.shape[0] // 2
    left_re, left_im = left[:half], left[half:]
    right_re, right_im = right[:half], right[half:]
    if conjugate_right:
        right_im = -right_im
    return jnp.concatenate(
        [left_re * right_re - left_im * right_im, left_re * right_im + left_im * right_re], axis=0
    )


def mixed_spectrum(table, prior_ref, key_ref, value_ref):
    mixed = (key_ref[...].astype(f32) * value_ref[...].astype(f32)).astype(bf16)
    prior = prior_ref[...]
    return forward_transform(table, prior, 0) + forward_transform(table, mixed, prior.shape[0])


def filter_spectrum(scale, table, taps_ref, skip_ref):
    taps = taps_ref.shape[1]
    filt = add_halves(dot_nt(table[:, :taps], taps_ref[...]))
    half = filt.shape[0] // 2
    return jnp.concatenate([(filt[:half] + skip_ref[...]) * scale, filt[half:] * scale], axis=0)


def state_kernel(
    scale, table, synth, prior_ref, key_ref, value_ref, taps_ref, skip_ref, query_ref, state_ref, gated_ref
):
    spec = mixed_spectrum(table, prior_ref, key_ref, value_ref)
    product = spectrum_product(spec, filter_spectrum(scale, table, taps_ref, skip_ref), False)
    state = inverse_transform(synth, product, prior_ref.shape[0], query_ref.shape[0])
    state_ref[...] = state
    gated_ref[...] = (query_ref[...].astype(f32) * state).astype(bf16)


def project_kernel(
    place_ref, first_mine, second_mine, first_theirs, second_theirs, weight, other, own, pieces, blocks, others, owns, piece_sem, block_sem, out_sem
):
    steps, _, total_width = blocks.shape
    length, width = first_mine.shape

    def piece_copy(n, sub, source):
        rows = pl.ds(n * length, length)
        columns = pl.ds(pl.multiple_of(place_ref[1 + sub] * width, width), width)
        return pltpu.make_async_copy(source, pieces.at[rows, columns], piece_sem.at[n, sub])

    def block_copy(i):
        return pltpu.make_async_copy(weight.at[pl.ds(i * lanes, lanes)], blocks.at[i], block_sem.at[i])

    def out_copies(i):
        columns = pl.ds(pl.multiple_of(i * lanes, lanes), lanes)
        return [
            pltpu.make_async_copy(others.at[i], other.at[:, columns], out_sem.at[0, i]),
            pltpu.make_async_copy(owns.at[i], own.at[:, columns], out_sem.at[1, i]),
        ]

    for i in range(steps):
        block_copy(i).start()

    def fetch(own_first):
        for sub, (first, second) in enumerate([(first_mine, second_mine), (first_theirs, second_theirs)]):
            piece_copy(0, sub, second if own_first else first).start()
            piece_copy(1, sub, first if own_first else second).start()

    pl.when(place_ref[0] != 0)(lambda: fetch(True))
    pl.when(place_ref[0] == 0)(lambda: fetch(False))
    for n in range(2):
        for sub in range(2):
            piece_copy(n, sub, first_mine).wait()

    @pl.loop(0, steps)
    def _(i):
        block_copy(i).wait()
        total = dot_nt(pieces[...], blocks[i])
        others[i] = total[:length].astype(bf16)
        owns[i] = total[length:]
        for copy in out_copies(i):
            copy.start()

    for i in range(steps):
        for copy in out_copies(i):
            copy.wait()


def weight_kernel(count, place_ref, *refs):
    cot_in, gated_in = refs[: 2 * count], list(refs[2 * count : 4 * count - 1])
    other, own, cots, gateds, others, owns, cot_sem, gated_sem, out_sem = refs[4 * count - 1 :]
    gated_in[-1:] = [gated_in[-1].at[0], gated_in[-1].at[1]]
    rows = other.shape[0]
    block = min(rows, turn)
    copies = [pltpu.make_async_copy(gated_in[n], gateds.at[n], gated_sem.at[n]) for n in range(2 * count)]
    copies += [pltpu.make_async_copy(cot_in[n], cots.at[n], cot_sem.at[n]) for n in range(2 * count)]
    for copy in copies:
        copy.start()
    for copy in copies:
        copy.wait()
    outs = [
        pltpu.make_async_copy(others, other, out_sem.at[0]),
        pltpu.make_async_copy(owns, own, out_sem.at[1]),
    ]

    def fill(replica, target):
        @pl.loop(0, rows // block)
        def _(i):
            start = pl.multiple_of(replica * rows + i * block, block)
            total = None
            for n in range(2 * count):
                gated = gateds[2 * place_ref[n % count] + n // count]
                part = dot(cots[n, pl.ds(start, block), :], gated)
                total = part if total is None else total + part
            target[pl.ds(pl.multiple_of(i * block, block), block), :] = total.astype(target.dtype)

    me = place_ref[count]
    fill(1 - me, others)
    outs[0].start()
    fill(me, owns)
    outs[1].start()
    for copy in outs:
        copy.wait()


def lag_kernel(
    table,
    synth,
    own_ref,
    other_ref,
    state_ref,
    query_ref,
    prior_ref,
    key_ref,
    value_ref,
    place_ref,
    grad_ref,
    signal_ref,
    head_ref,
    sent_lag_ref,
    own_lag_ref,
):
    length, taps, share = signal_ref.shape[0], prior_ref.shape[0], own_lag_ref.shape[0]
    grad_gated = own_ref[...] + other_ref[...].astype(f32)
    grad_ref[...] = (grad_gated * state_ref[...]).astype(bf16)
    signal = (grad_gated * query_ref[...].astype(f32)).astype(bf16)
    signal_ref[...] = signal
    head_ref[...] = signal[:taps]
    spec = mixed_spectrum(table, prior_ref, key_ref, value_ref)
    product = spectrum_product(forward_transform(table, signal, 0), spec, True)
    lags = -inverse_transform(synth, product, length, taps)
    first = place_ref[...] == 0.0
    own_lag_ref[...] = jnp.where(first, lags[:share], lags[share:])
    sent_lag_ref[...] = jnp.where(first, lags[share:], lags[:share]).astype(bf16)


def back_kernel(
    scale, table, synth, signal_ref, later_ref, taps_ref, skip_ref, key_ref, value_ref, grad_key_ref, grad_value_ref
):
    length = key_ref.shape[0]
    spec = forward_transform(table, signal_ref[...], 0) + forward_transform(table, later_ref[...], length)
    product = spectrum_product(spec, filter_spectrum(scale, table, taps_ref, skip_ref), True)
    back = inverse_transform(synth, product, 0, length)
    grad_key_ref[...] = (back * value_ref[...].astype(f32)).astype(bf16)
    grad_value_ref[...] = (back * key_ref[...].astype(f32)).astype(bf16)


def estimate(flops, arrays):
    moved = sum(a.size * jnp.dtype(a.dtype).itemsize for a in arrays)
    return pl.CostEstimate(flops=flops // 64, bytes_accessed=moved // 64, transcendentals=0)


def by_channel(body, tables, args, outs, channels, flops, swap=None):
    steps = channels // lanes
    flat_outs = [o for group in outs for o in group]
    n_tables, n_args, n_outs = len(tables), len(args), len(outs)

    def part(ref, i, count):
        start = i * lanes
        if ref.shape[1] == count * lanes:
            return ref.at[:, pl.ds(start, lanes)]
        return ref.at[pl.ds(start, lanes), :]

    def kernel(*refs):
        refs = list(refs)
        take = lambda count: [refs.pop(0) for _ in range(count)]
        swap_ref = None if swap is None else refs.pop(0)
        table_in, arg_in, outs_to = take(n_tables), take(n_args), take(len(flat_outs))
        table_held, arg_held, out_held = take(n_tables), take(n_args), take(n_outs)
        table_sem, arg_sem, out_sem = refs
        groups = [[outs_to.pop(0) for _ in group] for group in outs]

        def table_copy(k):
            return pltpu.make_async_copy(table_in[k], table_held[k], table_sem.at[k])

        def arg_copy(k):
            return pltpu.make_async_copy(arg_in[k], arg_held[k], arg_sem.at[k])

        def out_copy(k, n, i):
            place = groups[k][n] if len(groups[k]) > 1 else part(groups[k][n], i, steps)
            return pltpu.make_async_copy(out_held[k].at[i], place, out_sem.at[k, i])

        for k in range(n_tables):
            table_copy(k).start()
        for k in range(n_args):
            arg_copy(k).start()
        for k in range(n_tables):
            table_copy(k).wait()
        for k in range(n_args):
            arg_copy(k).wait()

        for i in range(steps):
            body(*table_held, *[part(ref, i, steps) for ref in arg_held], *[held.at[i] for held in out_held])
            for k in range(n_outs):
                count = len(groups[k])
                if count == 1:
                    out_copy(k, 0, i).start()
                else:
                    pl.when(swap_ref[0] == 0)(out_copy(k, i, i).start)
                    pl.when(swap_ref[0] != 0)(out_copy(k, count - 1 - i, i).start)

        for i in range(steps):
            for k in range(n_outs):
                out_copy(k, 0 if len(groups[k]) == 1 else i, i).wait()

    return pl.pallas_call(
        kernel,
        in_specs=[pl.BlockSpec(memory_space=pltpu.SMEM)] * (swap is not None)
        + [pl.BlockSpec(memory_space=pl.ANY)] * (n_tables + n_args),
        out_specs=[pl.BlockSpec(memory_space=pl.ANY)] * len(flat_outs),
        out_shape=flat_outs,
        scratch_shapes=[
            *[pltpu.VMEM(t.shape, bf16) for t in tables],
            *[pltpu.VMEM(a.shape, a.dtype) for a in args],
            *[pltpu.VMEM((steps, group[0].shape[0], lanes), group[0].dtype) for group in outs],
            pltpu.SemaphoreType.DMA((n_tables,)),
            pltpu.SemaphoreType.DMA((n_args,)),
            pltpu.SemaphoreType.DMA((n_outs, steps)),
        ],
        compiler_params=pltpu.CompilerParams(vmem_limit_bytes=vmem_bytes),
        cost_estimate=estimate(flops, [*args, *flat_outs]),
    )(*([] if swap is None else [swap]), *[jnp.asarray(t) for t in tables], *args)


def local_call(kernel, places, args, outs, scratch, flops):
    return pl.pallas_call(
        kernel,
        in_specs=[pl.BlockSpec(memory_space=pltpu.SMEM)] + [pl.BlockSpec(memory_space=pl.ANY)] * len(args),
        out_specs=[pl.BlockSpec(memory_space=pl.ANY)] * len(outs),
        out_shape=outs,
        scratch_shapes=scratch,
        compiler_params=pltpu.CompilerParams(vmem_limit_bytes=vmem_bytes),
        cost_estimate=estimate(flops, [*args, *outs]),
    )(places, *args)


def project(places, firsts, seconds, out_weight):
    length, width = firsts[0].shape
    channels, total_width = out_weight.shape
    steps = channels // lanes
    return local_call(
        project_kernel,
        places,
        [firsts[0], seconds[0], firsts[1], seconds[1], out_weight],
        [jax.ShapeDtypeStruct((length, channels), dtype) for dtype in (bf16, f32)],
        [
            pltpu.VMEM((2 * length, total_width), bf16),
            pltpu.VMEM((steps, lanes, total_width), bf16),
            pltpu.VMEM((steps, length, lanes), bf16),
            pltpu.VMEM((steps, length, lanes), f32),
            pltpu.SemaphoreType.DMA((2, 2)),
            pltpu.SemaphoreType.DMA((steps,)),
            pltpu.SemaphoreType.DMA((2, steps)),
        ],
        4 * length * out_weight.size,
    )


def weight_sum(places, cot_pieces, gated_pieces, rows):
    count = (len(gated_pieces) + 1) // 2
    length, width = gated_pieces[0].shape
    outs = [jax.ShapeDtypeStruct((rows, width), dtype) for dtype in (bf16, f32)]
    return local_call(
        functools.partial(weight_kernel, count),
        places,
        [*cot_pieces, *gated_pieces],
        outs,
        [
            pltpu.VMEM((2 * count, *cot_pieces[0].shape), bf16),
            pltpu.VMEM((2 * count, *gated_pieces[0].shape), bf16),
            *[pltpu.VMEM(o.shape, o.dtype) for o in outs],
            pltpu.SemaphoreType.DMA((2 * count,)),
            pltpu.SemaphoreType.DMA((2 * count,)),
            pltpu.SemaphoreType.DMA((2,)),
        ],
        8 * count * length * rows * width,
    )


def transpose_kernel(rows_in, out, rows, turned, sems):
    copy = pltpu.make_async_copy(rows_in, rows, sems.at[0])
    copy.start()
    copy.wait()
    for i in range(rows.shape[1] // turn):
        turned[pl.ds(i * turn, turn), :] = rows[:, pl.ds(i * turn, turn)].T
    copy = pltpu.make_async_copy(turned, out, sems.at[1])
    copy.start()
    copy.wait()


def transposed(rows):
    return pl.pallas_call(
        transpose_kernel,
        in_specs=[pl.BlockSpec(memory_space=pl.ANY)],
        out_specs=pl.BlockSpec(memory_space=pl.ANY),
        out_shape=jax.ShapeDtypeStruct(rows.shape[::-1], rows.dtype),
        scratch_shapes=[
            pltpu.VMEM(rows.shape, rows.dtype),
            pltpu.VMEM(rows.shape[::-1], rows.dtype),
            pltpu.SemaphoreType.DMA((2,)),
        ],
        compiler_params=pltpu.CompilerParams(vmem_limit_bytes=vmem_bytes),
        cost_estimate=estimate(0, [rows, rows]),
    )(rows)


def swap_pairs(value, axis, distance):
    count = lax.axis_size(axis)
    return lax.ppermute(value, axis, [(i, i ^ distance) for i in range(count)])


def after(value, *earlier):
    return lax.optimization_barrier((value, *earlier))[0]


def per_device(query_gate, key_gate, value_input, filter_taps, skip_gain, out_weight, cotangent):
    queries, key_rows, value_rows, cot = (
        query_gate[0],
        key_gate[0],
        value_input[0],
        cotangent[0],
    )
    length, channels = queries.shape
    taps = filter_taps.shape[1]
    n_seq, n_tp, n_dp = lax.axis_size("seq"), lax.axis_size("tp"), lax.axis_size("dp")
    subs = n_tp // n_dp
    me_tp, me_dp = lax.axis_index("tp"), lax.axis_index("dp")
    me_half, me_sub = me_tp // subs, me_tp % subs
    size = length + taps
    norm_factor = 1.0 / math.sqrt(length * n_seq * n_dp)

    whole = analysis_table(size, np.arange(size))
    scale = 2.0 / size
    tables = [split_table(whole), np.ascontiguousarray(split_table(whole.T))]
    rows16 = jax.ShapeDtypeStruct((length, channels), bf16)
    rows32 = jax.ShapeDtypeStruct((length, channels), f32)
    half16 = jax.ShapeDtypeStruct((length, channels // 2), bf16)
    unit = 2 * size * channels

    tail = (
        key_rows[length - taps :].astype(f32) * value_rows[length - taps :].astype(f32)
    ).astype(bf16)
    tail, cot = lax.optimization_barrier((tail, cot))
    prior = lax.ppermute(tail, "seq", [(i, i + 1) for i in range(n_seq - 1)])

    def tp_dp(half, sub, replica):
        return (half * subs + sub) * n_dp + replica

    places = [(h, c, d) for h in range(n_dp) for c in range(subs) for d in range(n_dp)]
    rounds = []
    for turn in range(2):
        route = [(tp_dp(h, c, d), tp_dp(d ^ turn, c, h)) for h, c, d in places]
        rounds.append(lax.ppermute(after(cot, prior) if turn else cot, ("tp", "dp"), route))
    square = n_seq == n_tp == 4 and subs == 2
    if square:

        def holder(s, block):
            return (s + block) % 2 * subs + s // 2

        crossed = {0: (1, 2), 1: (0, 3)}
        route = [
            (s * n_tp + t, s * n_tp + sum(crossed[s % 2]) - t)
            for s in range(n_seq)
            for t in crossed[s % 2]
        ]
        swapped = lax.ppermute(cot, ("seq", "tp"), route)
        moves_now = sum(
            jnp.logical_and(lax.axis_index("seq") % 2 == parity, me_tp == t)
            for parity in crossed
            for t in crossed[parity]
        )
        held = jnp.where(moves_now > 0, swapped, cot)
        route = []
        for s in range(n_seq):
            for t in range(n_tp):
                block = sum(crossed[s % 2]) - t if t in crossed[s % 2] else t
                route.append((s * n_tp + t, block * n_tp + holder(s, block)))
        moved = lax.ppermute(held, ("seq", "tp"), route)
    else:
        moved = cot

    same = (me_half == me_dp).astype(jnp.int32)
    subs_of = [me_sub, (me_sub + 1) % subs]
    place = jnp.stack([same, *subs_of]).astype(jnp.int32)
    dp_row = jnp.broadcast_to(me_dp.astype(f32), (1, channels))
    if square:
        order = [*range(0, n_seq, 2), *reversed(range(1, n_seq, 2))]
        ring = [(order[k], order[(k + 1) % n_seq]) for k in range(n_seq)]
        table = np.zeros((n_seq, n_tp, n_tp), np.int32)
        for k, s in enumerate(order):
            for r in range(n_seq):
                for t in range(n_tp):
                    table[s, t, t ^ holder(order[k - r], s)] = r
        sources = jnp.asarray(table)[lax.axis_index("seq"), me_tp]
        weight_place = jnp.concatenate([sources, me_dp[None].astype(jnp.int32)])
        prior, place, weight_place, dp_row = lax.optimization_barrier(
            (prior, place, weight_place, dp_row)
        )
    state, *gated = by_channel(
        functools.partial(state_kernel, scale),
        tables,
        [prior, key_rows, value_rows, filter_taps, skip_gain[None], queries],
        [[rows32], [half16, half16]],
        channels,
        unit * (4 * taps + 5 * length),
        jnp.reshape(me_dp if square else 0 * me_dp, (1,)).astype(jnp.int32),
    )
    if square:
        ring_pieces = [gated[0], swap_pairs(gated[1], "dp", 1)]
        ring_pieces[0], ring_pieces[1], moved = lax.optimization_barrier((*ring_pieces, moved))

        def ring_step():
            for _ in range(2):
                ring_pieces.append(lax.ppermute(ring_pieces[-2], "seq", ring))

        ring_step()
    gated[0], *rounds = lax.optimization_barrier((gated[0], *rounds))

    route = [(tp_dp(h, c, d), tp_dp(h, (c + 1) % subs, d)) for h, c, d in places]
    theirs = [lax.ppermute(r, ("tp", "dp"), route) for r in rounds]
    firsts, seconds = zip(rounds, theirs)
    rows = n_tp * channels // (n_seq * n_dp)
    if square:
        moved = after(moved, *rounds)
        moved_other = swap_pairs(moved, "dp", 1)
        moved = transposed(moved)
        moved, place = lax.optimization_barrier((moved, place))
    other_sent, own_part = project(place, firsts, seconds, out_weight)
    if square:
        other_sent, moved_other = lax.optimization_barrier((other_sent, moved_other))
    other_part = swap_pairs(other_sent, "dp", 1)
    if square:

        def spread(piece, across, gate):
            near = [(t, t ^ 1) for t in range(n_tp)]
            return [
                piece,
                lax.ppermute(piece, "tp", near),
                across,
                lax.ppermute(after(across, gate), "tp", near),
            ]

        opposite = [(t, t ^ subs) for t in range(n_tp)]
        across = lax.ppermute(moved, "tp", opposite)
        ring_pieces[2], ring_pieces[3], _ = lax.optimization_barrier((*ring_pieces[2:4], other_sent))
        ring_step()
        *last, own_part, other_part = lax.optimization_barrier((*ring_pieces[4:6], own_part, other_part))
        last = lax.ppermute(jnp.stack(last), "seq", ring)
        moved_other = transposed(after(moved_other, across))
        across_other = lax.ppermute(moved_other, "tp", opposite)
        cot_pieces = spread(moved, across, other_part) + spread(moved_other, across_other, own_part)
    else:
        full = lax.all_gather(cot, "tp", axis=1, tiled=True)
        cot_all = lax.all_to_all(full, "seq", 1, 0, tiled=True)
        gated_all = [lax.all_gather(half, "seq", axis=0, tiled=True) for half in gated]

        def part(replica, piece):
            block = lax.dynamic_slice_in_dim(cot_all, replica * rows, rows, axis=1)
            return lax.dot_general(
                block, piece, (((0,), (0,)), ((), ())), preferred_element_type=f32
            )

        def weight_one(piece):
            return part(me_dp, piece), swap_pairs(part(1 - me_dp, piece).astype(bf16), "dp", 1)

    share = taps // n_dp
    grad_query, signal, head, sent_lag, own_lag = by_channel(
        lag_kernel,
        tables,
        [own_part, other_part, state, queries, prior, key_rows, value_rows, dp_row],
        [
            [rows16],
            [rows16],
            [jax.ShapeDtypeStruct((taps, channels), bf16)],
            [jax.ShapeDtypeStruct((share, channels), bf16)],
            [jax.ShapeDtypeStruct((share, channels), f32)],
        ],
        channels,
        unit * (2 * taps + 4 * length + 3 * taps),
    )
    later = lax.ppermute(head, "seq", [(i + 1, i) for i in range(n_seq - 1)])

    def run_back(later):
        return by_channel(
            functools.partial(back_kernel, scale),
            tables,
            [signal, later, filter_taps, skip_gain[None], key_rows, value_rows],
            [[rows16], [rows16]],
            channels,
            256 * unit * (4 * taps + 5 * length),
        )

    received = swap_pairs(sent_lag, "dp", 1)
    if square:
        last, received = lax.optimization_barrier((last, received))
        ring_pieces.append(last)
    lag_sum = own_lag + received.astype(f32)
    distance = 1
    while distance < n_seq:
        rounded = lag_sum.astype(bf16)
        received = swap_pairs(rounded, "seq", distance)
        if square and distance == 2:
            weight_place, rounded = lax.optimization_barrier((weight_place, rounded))
            weight_sent, weight_own = weight_sum(weight_place, cot_pieces, ring_pieces, rows)
            weight_received = swap_pairs(weight_sent, "dp", 1)
            received, weight_own = lax.optimization_barrier((received, weight_own))
        lag_sum = rounded.astype(f32) + received.astype(f32)
        distance *= 2
    mine = lag_sum.astype(bf16)
    grad_key, grad_value = run_back(after(later, weight_own) if square else later)
    if square:
        mine, grad_key = lax.optimization_barrier((mine, grad_key))
    theirs = swap_pairs(mine, "dp", 1)
    first = me_dp == 0
    lag_sum = jnp.concatenate([jnp.where(first, mine, theirs), jnp.where(first, theirs, mine)], axis=0)
    grad_filter = lag_sum.astype(f32).T * (norm_factor * scale)

    if square:
        weight_own, weight_received = weight_own * norm_factor, weight_received.astype(f32) * norm_factor
        grad_weight = jnp.concatenate(
            [
                jnp.where(first, weight_own, weight_received),
                jnp.where(first, weight_received, weight_own),
            ],
            axis=1,
        )
    else:
        parts = [weight_one(half) for half in gated_all]
        grad_weight = jnp.concatenate(
            [(mine + theirs.astype(f32)) * norm_factor for mine, theirs in parts], axis=1
        )
    return (
        grad_query[None],
        grad_key[None],
        grad_value[None],
        grad_filter,
        grad_filter[:, 0],
        grad_weight,
    )


def solution(mesh):
    tokens = P("dp", "seq", "tp")
    return jax.shard_map(
        per_device,
        mesh=mesh,
        in_specs=(tokens, tokens, tokens, P("tp", None), P("tp"), P("tp", "dp"), tokens),
        out_specs=(tokens, tokens, tokens, P("tp", None), P("tp"), P(("seq", "dp"), "tp")),
        check_vma=False,
    )
```

```python
import functools
import math

import jax
import jax.numpy as jnp
import ml_dtypes
import numpy as np
from jax import lax
from jax.experimental import pallas as pl
from jax.experimental.pallas import tpu as pltpu
from jax.sharding import PartitionSpec as P

f32, bf16 = jnp.float32, jnp.bfloat16
lanes = 512
turn = 256
vmem_bytes = 58 * 1024 * 1024


def analysis_table(size, positions):
    half = size // 2
    omega = 2.0 * np.pi * (np.arange(half) + 0.5) / size
    angle = omega[:, None] * np.asarray(positions)[None, :]
    return np.concatenate([np.cos(angle), -np.sin(angle)], axis=0)


def split_table(table):
    high = table.astype(ml_dtypes.bfloat16)
    low = (table - high.astype(np.float64)).astype(ml_dtypes.bfloat16)
    return np.concatenate([high, low])


def split_rows(rows):
    high = rows.astype(bf16)
    return high, (rows - high.astype(f32)).astype(bf16)


def dot(left, right):
    return jnp.dot(left, right, preferred_element_type=f32)


def dot_nt(left, right):
    return lax.dot_general(left, right, (((1,), (1,)), ((), ())), preferred_element_type=f32)


def add_halves(both):
    half = both.shape[0] // 2
    return both[:half] + both[half:]


def forward_transform(table, rows, start):
    return add_halves(dot(table[:, pl.ds(start, rows.shape[0])], rows))


def inverse_transform(table, spectrum, start, count):
    high, low = split_rows(spectrum)
    upper = table[pl.ds(start, count)]
    lower = table[pl.ds(table.shape[0] // 2 + start, count)]
    return dot(upper, high) + dot(upper, low) + dot(lower, high)


def spectrum_product(left, right, conjugate_right):
    half = left.shape[0] // 2
    left_re, left_im = left[:half], left[half:]
    right_re, right_im = right[:half], right[half:]
    if conjugate_right:
        right_im = -right_im
    return jnp.concatenate(
        [left_re * right_re - left_im * right_im, left_re * right_im + left_im * right_re], axis=0
    )


def mixed_spectrum(table, prior_ref, key_ref, value_ref):
    mixed = (key_ref[...].astype(f32) * value_ref[...].astype(f32)).astype(bf16)
    prior = prior_ref[...]
    return forward_transform(table, prior, 0) + forward_transform(table, mixed, prior.shape[0])


def filter_spectrum(scale, table, taps_ref, skip_ref):
    taps = taps_ref.shape[1]
    filt = add_halves(dot_nt(table[:, :taps], taps_ref[...]))
    half = filt.shape[0] // 2
    return jnp.concatenate([(filt[:half] + skip_ref[...]) * scale, filt[half:] * scale], axis=0)


def state_kernel(
    scale, table, synth, prior_ref, key_ref, value_ref, taps_ref, skip_ref, query_ref, state_ref, gated_ref
):
    spec = mixed_spectrum(table, prior_ref, key_ref, value_ref)
    product = spectrum_product(spec, filter_spectrum(scale, table, taps_ref, skip_ref), False)
    state = inverse_transform(synth, product, prior_ref.shape[0], query_ref.shape[0])
    state_ref[...] = state
    gated_ref[...] = (query_ref[...].astype(f32) * state).astype(bf16)


def project_kernel(
    place_ref, first_mine, second_mine, first_theirs, second_theirs, weight, other, own, pieces, blocks, others, owns, piece_sem, block_sem, out_sem
):
    steps, _, total_width = blocks.shape
    length, width = first_mine.shape

    def piece_copy(n, sub, source):
        rows = pl.ds(n * length, length)
        columns = pl.ds(pl.multiple_of(place_ref[1 + sub] * width, width), width)
        return pltpu.make_async_copy(source, pieces.at[rows, columns], piece_sem.at[n, sub])

    def block_copy(i):
        return pltpu.make_async_copy(weight.at[pl.ds(i * lanes, lanes)], blocks.at[i], block_sem.at[i])

    def out_copies(i):
        columns = pl.ds(pl.multiple_of(i * lanes, lanes), lanes)
        return [
            pltpu.make_async_copy(others.at[i], other.at[:, columns], out_sem.at[0, i]),
            pltpu.make_async_copy(owns.at[i], own.at[:, columns], out_sem.at[1, i]),
        ]

    for i in range(steps):
        block_copy(i).start()

    def fetch(own_first):
        for sub, (first, second) in enumerate([(first_mine, second_mine), (first_theirs, second_theirs)]):
            piece_copy(0, sub, second if own_first else first).start()
            piece_copy(1, sub, first if own_first else second).start()

    pl.when(place_ref[0] != 0)(lambda: fetch(True))
    pl.when(place_ref[0] == 0)(lambda: fetch(False))
    for n in range(2):
        for sub in range(2):
            piece_copy(n, sub, first_mine).wait()

    @pl.loop(0, steps)
    def _(i):
        block_copy(i).wait()
        total = dot_nt(pieces[...], blocks[i])
        others[i] = total[:length].astype(bf16)
        owns[i] = total[length:]
        for copy in out_copies(i):
            copy.start()

    for i in range(steps):
        for copy in out_copies(i):
            copy.wait()


def weight_kernel(count, place_ref, *refs):
    cot_in, gated_in = refs[: 2 * count], list(refs[2 * count : 4 * count - 1])
    other, own, cots, gateds, others, owns, cot_sem, gated_sem, out_sem = refs[4 * count - 1 :]
    gated_in[-1:] = [gated_in[-1].at[0], gated_in[-1].at[1]]
    rows = other.shape[0]
    block = min(rows, turn)
    copies = [pltpu.make_async_copy(gated_in[n], gateds.at[n], gated_sem.at[n]) for n in range(2 * count)]
    copies += [pltpu.make_async_copy(cot_in[n], cots.at[n], cot_sem.at[n]) for n in range(2 * count)]
    for copy in copies:
        copy.start()
    for copy in copies:
        copy.wait()
    outs = [
        pltpu.make_async_copy(others, other, out_sem.at[0]),
        pltpu.make_async_copy(owns, own, out_sem.at[1]),
    ]

    def fill(replica, target):
        @pl.loop(0, rows // block)
        def _(i):
            start = pl.multiple_of(replica * rows + i * block, block)
            total = None
            for n in range(2 * count):
                gated = gateds[2 * place_ref[n % count] + n // count]
                part = dot(cots[n, pl.ds(start, block), :], gated)
                total = part if total is None else total + part
            target[pl.ds(pl.multiple_of(i * block, block), block), :] = total.astype(target.dtype)

    me = place_ref[count]
    fill(1 - me, others)
    outs[0].start()
    fill(me, owns)
    outs[1].start()
    for copy in outs:
        copy.wait()


def lag_kernel(
    table,
    synth,
    own_ref,
    other_ref,
    state_ref,
    query_ref,
    prior_ref,
    key_ref,
    value_ref,
    place_ref,
    grad_ref,
    signal_ref,
    head_ref,
    sent_lag_ref,
    own_lag_ref,
):
    length, taps, share = signal_ref.shape[0], prior_ref.shape[0], own_lag_ref.shape[0]
    grad_gated = own_ref[...] + other_ref[...].astype(f32)
    grad_ref[...] = (grad_gated * state_ref[...]).astype(bf16)
    signal = (grad_gated * query_ref[...].astype(f32)).astype(bf16)
    signal_ref[...] = signal
    head_ref[...] = signal[:taps]
    spec = mixed_spectrum(table, prior_ref, key_ref, value_ref)
    product = spectrum_product(forward_transform(table, signal, 0), spec, True)
    lags = -inverse_transform(synth, product, length, taps)
    first = place_ref[...] == 0.0
    own_lag_ref[...] = jnp.where(first, lags[:share], lags[share:])
    sent_lag_ref[...] = jnp.where(first, lags[share:], lags[:share]).astype(bf16)


def back_kernel(
    scale, table, synth, signal_ref, later_ref, taps_ref, skip_ref, key_ref, value_ref, grad_key_ref, grad_value_ref
):
    length = key_ref.shape[0]
    spec = forward_transform(table, signal_ref[...], 0) + forward_transform(table, later_ref[...], length)
    product = spectrum_product(spec, filter_spectrum(scale, table, taps_ref, skip_ref), True)
    back = inverse_transform(synth, product, 0, length)
    grad_key_ref[...] = (back * value_ref[...].astype(f32)).astype(bf16)
    grad_value_ref[...] = (back * key_ref[...].astype(f32)).astype(bf16)


def estimate(flops, arrays):
    moved = sum(a.size * jnp.dtype(a.dtype).itemsize for a in arrays)
    return pl.CostEstimate(flops=flops // 64, bytes_accessed=moved // 64, transcendentals=0)


def by_channel(body, tables, args, outs, channels, flops, swap=None):
    steps = channels // lanes
    flat_outs = [o for group in outs for o in group]
    n_tables, n_args, n_outs = len(tables), len(args), len(outs)

    def part(ref, i, count):
        start = i * lanes
        if ref.shape[1] == count * lanes:
            return ref.at[:, pl.ds(start, lanes)]
        return ref.at[pl.ds(start, lanes), :]

    def kernel(*refs):
        refs = list(refs)
        take = lambda count: [refs.pop(0) for _ in range(count)]
        swap_ref = None if swap is None else refs.pop(0)
        table_in, arg_in, outs_to = take(n_tables), take(n_args), take(len(flat_outs))
        table_held, arg_held, out_held = take(n_tables), take(n_args), take(n_outs)
        table_sem, arg_sem, out_sem = refs
        groups = [[outs_to.pop(0) for _ in group] for group in outs]

        def table_copy(k):
            return pltpu.make_async_copy(table_in[k], table_held[k], table_sem.at[k])

        def arg_copy(k):
            return pltpu.make_async_copy(arg_in[k], arg_held[k], arg_sem.at[k])

        def out_copy(k, n, i):
            place = groups[k][n] if len(groups[k]) > 1 else part(groups[k][n], i, steps)
            return pltpu.make_async_copy(out_held[k].at[i], place, out_sem.at[k, i])

        for k in range(n_tables):
            table_copy(k).start()
        for k in range(n_args):
            arg_copy(k).start()
        for k in range(n_tables):
            table_copy(k).wait()
        for k in range(n_args):
            arg_copy(k).wait()

        for i in range(steps):
            body(*table_held, *[part(ref, i, steps) for ref in arg_held], *[held.at[i] for held in out_held])
            for k in range(n_outs):
                count = len(groups[k])
                if count == 1:
                    out_copy(k, 0, i).start()
                else:
                    pl.when(swap_ref[0] == 0)(out_copy(k, i, i).start)
                    pl.when(swap_ref[0] != 0)(out_copy(k, count - 1 - i, i).start)

        for i in range(steps):
            for k in range(n_outs):
                out_copy(k, 0 if len(groups[k]) == 1 else i, i).wait()

    return pl.pallas_call(
        kernel,
        in_specs=[pl.BlockSpec(memory_space=pltpu.SMEM)] * (swap is not None)
        + [pl.BlockSpec(memory_space=pl.ANY)] * (n_tables + n_args),
        out_specs=[pl.BlockSpec(memory_space=pl.ANY)] * len(flat_outs),
        out_shape=flat_outs,
        scratch_shapes=[
            *[pltpu.VMEM(t.shape, bf16) for t in tables],
            *[pltpu.VMEM(a.shape, a.dtype) for a in args],
            *[pltpu.VMEM((steps, group[0].shape[0], lanes), group[0].dtype) for group in outs],
            pltpu.SemaphoreType.DMA((n_tables,)),
            pltpu.SemaphoreType.DMA((n_args,)),
            pltpu.SemaphoreType.DMA((n_outs, steps)),
        ],
        compiler_params=pltpu.CompilerParams(vmem_limit_bytes=vmem_bytes),
        cost_estimate=estimate(flops, [*args, *flat_outs]),
    )(*([] if swap is None else [swap]), *[jnp.asarray(t) for t in tables], *args)


def local_call(kernel, places, args, outs, scratch, flops):
    return pl.pallas_call(
        kernel,
        in_specs=[pl.BlockSpec(memory_space=pltpu.SMEM)] + [pl.BlockSpec(memory_space=pl.ANY)] * len(args),
        out_specs=[pl.BlockSpec(memory_space=pl.ANY)] * len(outs),
        out_shape=outs,
        scratch_shapes=scratch,
        compiler_params=pltpu.CompilerParams(vmem_limit_bytes=vmem_bytes),
        cost_estimate=estimate(flops, [*args, *outs]),
    )(places, *args)


def project(places, firsts, seconds, out_weight):
    length, width = firsts[0].shape
    channels, total_width = out_weight.shape
    steps = channels // lanes
    return local_call(
        project_kernel,
        places,
        [firsts[0], seconds[0], firsts[1], seconds[1], out_weight],
        [jax.ShapeDtypeStruct((length, channels), dtype) for dtype in (bf16, f32)],
        [
            pltpu.VMEM((2 * length, total_width), bf16),
            pltpu.VMEM((steps, lanes, total_width), bf16),
            pltpu.VMEM((steps, length, lanes), bf16),
            pltpu.VMEM((steps, length, lanes), f32),
            pltpu.SemaphoreType.DMA((2, 2)),
            pltpu.SemaphoreType.DMA((steps,)),
            pltpu.SemaphoreType.DMA((2, steps)),
        ],
        4 * length * out_weight.size,
    )


def weight_sum(places, cot_pieces, gated_pieces, rows):
    count = (len(gated_pieces) + 1) // 2
    length, width = gated_pieces[0].shape
    outs = [jax.ShapeDtypeStruct((rows, width), dtype) for dtype in (bf16, f32)]
    return local_call(
        functools.partial(weight_kernel, count),
        places,
        [*cot_pieces, *gated_pieces],
        outs,
        [
            pltpu.VMEM((2 * count, *cot_pieces[0].shape), bf16),
            pltpu.VMEM((2 * count, *gated_pieces[0].shape), bf16),
            *[pltpu.VMEM(o.shape, o.dtype) for o in outs],
            pltpu.SemaphoreType.DMA((2 * count,)),
            pltpu.SemaphoreType.DMA((2 * count,)),
            pltpu.SemaphoreType.DMA((2,)),
        ],
        8 * count * length * rows * width,
    )


def transpose_kernel(rows_in, out, rows, turned, sems):
    copy = pltpu.make_async_copy(rows_in, rows, sems.at[0])
    copy.start()
    copy.wait()
    for i in range(rows.shape[1] // turn):
        turned[pl.ds(i * turn, turn), :] = rows[:, pl.ds(i * turn, turn)].T
    copy = pltpu.make_async_copy(turned, out, sems.at[1])
    copy.start()
    copy.wait()


def transposed(rows):
    return pl.pallas_call(
        transpose_kernel,
        in_specs=[pl.BlockSpec(memory_space=pl.ANY)],
        out_specs=pl.BlockSpec(memory_space=pl.ANY),
        out_shape=jax.ShapeDtypeStruct(rows.shape[::-1], rows.dtype),
        scratch_shapes=[
            pltpu.VMEM(rows.shape, rows.dtype),
            pltpu.VMEM(rows.shape[::-1], rows.dtype),
            pltpu.SemaphoreType.DMA((2,)),
        ],
        compiler_params=pltpu.CompilerParams(vmem_limit_bytes=vmem_bytes),
        cost_estimate=estimate(0, [rows, rows]),
    )(rows)


def swap_pairs(value, axis, distance):
    count = lax.axis_size(axis)
    return lax.ppermute(value, axis, [(i, i ^ distance) for i in range(count)])


def after(value, *earlier):
    return lax.optimization_barrier((value, *earlier))[0]


def per_device(query_gate, key_gate, value_input, filter_taps, skip_gain, out_weight, cotangent):
    queries, key_rows, value_rows, cot = (
        query_gate[0],
        key_gate[0],
        value_input[0],
        cotangent[0],
    )
    length, channels = queries.shape
    taps = filter_taps.shape[1]
    n_seq, n_tp, n_dp = lax.axis_size("seq"), lax.axis_size("tp"), lax.axis_size("dp")
    subs = n_tp // n_dp
    me_tp, me_dp = lax.axis_index("tp"), lax.axis_index("dp")
    me_half, me_sub = me_tp // subs, me_tp % subs
    size = length + taps
    norm_factor = 1.0 / math.sqrt(length * n_seq * n_dp)

    whole = analysis_table(size, np.arange(size))
    scale = 2.0 / size
    tables = [split_table(whole), np.ascontiguousarray(split_table(whole.T))]
    rows16 = jax.ShapeDtypeStruct((length, channels), bf16)
    rows32 = jax.ShapeDtypeStruct((length, channels), f32)
    half16 = jax.ShapeDtypeStruct((length, channels // 2), bf16)
    unit = 2 * size * channels

    tail = (
        key_rows[length - taps :].astype(f32) * value_rows[length - taps :].astype(f32)
    ).astype(bf16)
    tail, cot = lax.optimization_barrier((tail, cot))
    prior = lax.ppermute(tail, "seq", [(i, i + 1) for i in range(n_seq - 1)])

    def tp_dp(half, sub, replica):
        return (half * subs + sub) * n_dp + replica

    places = [(h, c, d) for h in range(n_dp) for c in range(subs) for d in range(n_dp)]
    rounds = []
    for turn in range(2):
        route = [(tp_dp(h, c, d), tp_dp(d ^ turn, c, h)) for h, c, d in places]
        rounds.append(lax.ppermute(after(cot, prior) if turn else cot, ("tp", "dp"), route))
    square = n_seq == n_tp == 4 and subs == 2
    if square:

        def holder(s, block):
            return (s + block) % 2 * subs + s // 2

        crossed = {0: (1, 2), 1: (0, 3)}
        route = [
            (s * n_tp + t, s * n_tp + sum(crossed[s % 2]) - t)
            for s in range(n_seq)
            for t in crossed[s % 2]
        ]
        swapped = lax.ppermute(cot, ("seq", "tp"), route)
        moves_now = sum(
            jnp.logical_and(lax.axis_index("seq") % 2 == parity, me_tp == t)
            for parity in crossed
            for t in crossed[parity]
        )
        held = jnp.where(moves_now > 0, swapped, cot)
        route = []
        for s in range(n_seq):
            for t in range(n_tp):
                block = sum(crossed[s % 2]) - t if t in crossed[s % 2] else t
                route.append((s * n_tp + t, block * n_tp + holder(s, block)))
        moved = lax.ppermute(held, ("seq", "tp"), route)
    else:
        moved = cot

    same = (me_half == me_dp).astype(jnp.int32)
    subs_of = [me_sub, (me_sub + 1) % subs]
    place = jnp.stack([same, *subs_of]).astype(jnp.int32)
    dp_row = jnp.broadcast_to(me_dp.astype(f32), (1, channels))
    if square:
        order = [*range(0, n_seq, 2), *reversed(range(1, n_seq, 2))]
        ring = [(order[k], order[(k + 1) % n_seq]) for k in range(n_seq)]
        table = np.zeros((n_seq, n_tp, n_tp), np.int32)
        for k, s in enumerate(order):
            for r in range(n_seq):
                for t in range(n_tp):
                    table[s, t, t ^ holder(order[k - r], s)] = r
        sources = jnp.asarray(table)[lax.axis_index("seq"), me_tp]
        weight_place = jnp.concatenate([sources, me_dp[None].astype(jnp.int32)])
        prior, place, weight_place, dp_row = lax.optimization_barrier(
            (prior, place, weight_place, dp_row)
        )
    state, *gated = by_channel(
        functools.partial(state_kernel, scale),
        tables,
        [prior, key_rows, value_rows, filter_taps, skip_gain[None], queries],
        [[rows32], [half16, half16]],
        channels,
        unit * (4 * taps + 5 * length),
        jnp.reshape(me_dp if square else 0 * me_dp, (1,)).astype(jnp.int32),
    )
    if square:
        ring_pieces = [gated[0], swap_pairs(gated[1], "dp", 1)]
        ring_pieces[0], ring_pieces[1], moved = lax.optimization_barrier((*ring_pieces, moved))

        def ring_step():
            for _ in range(2):
                ring_pieces.append(lax.ppermute(ring_pieces[-2], "seq", ring))

        ring_step()
    gated[0], *rounds = lax.optimization_barrier((gated[0], *rounds))

    route = [(tp_dp(h, c, d), tp_dp(h, (c + 1) % subs, d)) for h, c, d in places]
    theirs = [lax.ppermute(r, ("tp", "dp"), route) for r in rounds]
    firsts, seconds = zip(rounds, theirs)
    rows = n_tp * channels // (n_seq * n_dp)
    if square:
        moved = after(moved, *rounds)
        moved_other = swap_pairs(moved, "dp", 1)
        moved = transposed(moved)
        moved, place = lax.optimization_barrier((moved, place))
    other_sent, own_part = project(place, firsts, seconds, out_weight)
    if square:
        other_sent, moved_other = lax.optimization_barrier((other_sent, moved_other))
    other_part = swap_pairs(other_sent, "dp", 1)
    if square:

        def spread(piece, across, gate):
            near = [(t, t ^ 1) for t in range(n_tp)]
            return [
                piece,
                lax.ppermute(piece, "tp", near),
                across,
                lax.ppermute(after(across, gate), "tp", near),
            ]

        opposite = [(t, t ^ subs) for t in range(n_tp)]
        across = lax.ppermute(moved, "tp", opposite)
        ring_pieces[2], ring_pieces[3], _ = lax.optimization_barrier((*ring_pieces[2:4], other_sent))
        ring_step()
        *last, own_part, other_part = lax.optimization_barrier((*ring_pieces[4:6], own_part, other_part))
        last = lax.ppermute(jnp.stack(last), "seq", ring)
        moved_other = transposed(after(moved_other, across))
        across_other = lax.ppermute(moved_other, "tp", opposite)
        cot_pieces = spread(moved, across, other_part) + spread(moved_other, across_other, own_part)
    else:
        full = lax.all_gather(cot, "tp", axis=1, tiled=True)
        cot_all = lax.all_to_all(full, "seq", 1, 0, tiled=True)
        gated_all = [lax.all_gather(half, "seq", axis=0, tiled=True) for half in gated]

        def part(replica, piece):
            block = lax.dynamic_slice_in_dim(cot_all, replica * rows, rows, axis=1)
            return lax.dot_general(
                block, piece, (((0,), (0,)), ((), ())), preferred_element_type=f32
            )

        def weight_one(piece):
            return part(me_dp, piece), swap_pairs(part(1 - me_dp, piece).astype(bf16), "dp", 1)

    share = taps // n_dp
    grad_query, signal, head, sent_lag, own_lag = by_channel(
        lag_kernel,
        tables,
        [own_part, other_part, state, queries, prior, key_rows, value_rows, dp_row],
        [
            [rows16],
            [rows16],
            [jax.ShapeDtypeStruct((taps, channels), bf16)],
            [jax.ShapeDtypeStruct((share, channels), bf16)],
            [jax.ShapeDtypeStruct((share, channels), f32)],
        ],
        channels,
        unit * (2 * taps + 4 * length + 3 * taps),
    )
    later = lax.ppermute(head, "seq", [(i + 1, i) for i in range(n_seq - 1)])

    def run_back(later):
        return by_channel(
            functools.partial(back_kernel, scale),
            tables,
            [signal, later, filter_taps, skip_gain[None], key_rows, value_rows],
            [[rows16], [rows16]],
            channels,
            256 * unit * (4 * taps + 5 * length),
        )

    received = swap_pairs(sent_lag, "dp", 1)
    if square:
        last, received = lax.optimization_barrier((last, received))
        ring_pieces.append(last)
    lag_sum = own_lag + received.astype(f32)
    distance = 1
    while distance < n_seq:
        rounded = lag_sum.astype(bf16)
        received = swap_pairs(rounded, "seq", distance)
        if square and distance == 1:
            weight_place, rounded = lax.optimization_barrier((weight_place, rounded))
            weight_sent, weight_own = weight_sum(weight_place, cot_pieces, ring_pieces, rows)
            weight_received = swap_pairs(weight_sent, "dp", 1)
            received, weight_own = lax.optimization_barrier((received, weight_own))
        if square and distance == 2:
            grad_key, grad_value = run_back(after(later, weight_own))
            received, grad_key = lax.optimization_barrier((received, grad_key))
        lag_sum = rounded.astype(f32) + received.astype(f32)
        distance *= 2
    mine = lag_sum.astype(bf16)
    if not square:
        grad_key, grad_value = run_back(later)
    theirs = swap_pairs(mine, "dp", 1)
    first = me_dp == 0
    lag_sum = jnp.concatenate([jnp.where(first, mine, theirs), jnp.where(first, theirs, mine)], axis=0)
    grad_filter = lag_sum.astype(f32).T * (norm_factor * scale)

    if square:
        weight_own, weight_received = weight_own * norm_factor, weight_received.astype(f32) * norm_factor
        grad_weight = jnp.concatenate(
            [
                jnp.where(first, weight_own, weight_received),
                jnp.where(first, weight_received, weight_own),
            ],
            axis=1,
        )
    else:
        parts = [weight_one(half) for half in gated_all]
        grad_weight = jnp.concatenate(
            [(mine + theirs.astype(f32)) * norm_factor for mine, theirs in parts], axis=1
        )
    return (
        grad_query[None],
        grad_key[None],
        grad_value[None],
        grad_filter,
        grad_filter[:, 0],
        grad_weight,
    )


def solution(mesh):
    tokens = P("dp", "seq", "tp")
    return jax.shard_map(
        per_device,
        mesh=mesh,
        in_specs=(tokens, tokens, tokens, P("tp", None), P("tp"), P("tp", "dp"), tokens),
        out_specs=(tokens, tokens, tokens, P("tp", None), P("tp"), P(("seq", "dp"), "tp")),
        check_vma=False,
    )
```

```python
import functools
import math

import jax
import jax.numpy as jnp
import ml_dtypes
import numpy as np
from jax import lax
from jax.experimental import pallas as pl
from jax.experimental.pallas import tpu as pltpu
from jax.sharding import PartitionSpec as P

f32, bf16 = jnp.float32, jnp.bfloat16
lanes = 512
turn = 256
vmem_bytes = 58 * 1024 * 1024


def analysis_table(size, positions):
    half = size // 2
    omega = 2.0 * np.pi * (np.arange(half) + 0.5) / size
    angle = omega[:, None] * np.asarray(positions)[None, :]
    return np.concatenate([np.cos(angle), -np.sin(angle)], axis=0)


def split_table(table):
    high = table.astype(ml_dtypes.bfloat16)
    low = (table - high.astype(np.float64)).astype(ml_dtypes.bfloat16)
    return np.concatenate([high, low])


def split_rows(rows):
    high = rows.astype(bf16)
    return high, (rows - high.astype(f32)).astype(bf16)


def dot(left, right):
    return jnp.dot(left, right, preferred_element_type=f32)


def dot_nt(left, right):
    return lax.dot_general(left, right, (((1,), (1,)), ((), ())), preferred_element_type=f32)


def add_halves(both):
    half = both.shape[0] // 2
    return both[:half] + both[half:]


def forward_transform(table, rows, start):
    return add_halves(dot(table[:, pl.ds(start, rows.shape[0])], rows))


def inverse_transform(table, spectrum, start, count):
    high, low = split_rows(spectrum)
    upper = table[pl.ds(start, count)]
    lower = table[pl.ds(table.shape[0] // 2 + start, count)]
    return dot(upper, high) + dot(upper, low) + dot(lower, high)


def spectrum_product(left, right, conjugate_right):
    half = left.shape[0] // 2
    left_re, left_im = left[:half], left[half:]
    right_re, right_im = right[:half], right[half:]
    if conjugate_right:
        right_im = -right_im
    return jnp.concatenate(
        [left_re * right_re - left_im * right_im, left_re * right_im + left_im * right_re], axis=0
    )


def mixed_spectrum(table, prior_ref, key_ref, value_ref):
    mixed = (key_ref[...].astype(f32) * value_ref[...].astype(f32)).astype(bf16)
    prior = prior_ref[...]
    return forward_transform(table, prior, 0) + forward_transform(table, mixed, prior.shape[0])


def filter_spectrum(scale, table, taps_ref, skip_ref):
    taps = taps_ref.shape[1]
    filt = add_halves(dot_nt(table[:, :taps], taps_ref[...]))
    half = filt.shape[0] // 2
    return jnp.concatenate([(filt[:half] + skip_ref[...]) * scale, filt[half:] * scale], axis=0)


def state_kernel(
    scale, table, synth, prior_ref, key_ref, value_ref, taps_ref, skip_ref, query_ref, state_ref, gated_ref
):
    spec = mixed_spectrum(table, prior_ref, key_ref, value_ref)
    product = spectrum_product(spec, filter_spectrum(scale, table, taps_ref, skip_ref), False)
    state = inverse_transform(synth, product, prior_ref.shape[0], query_ref.shape[0])
    state_ref[...] = state
    gated_ref[...] = (query_ref[...].astype(f32) * state).astype(bf16)


def project_kernel(
    place_ref, first_mine, second_mine, first_theirs, second_theirs, weight, other, own, pieces, blocks, others, owns, piece_sem, block_sem, out_sem
):
    steps, _, total_width = blocks.shape
    length, width = first_mine.shape

    def piece_copy(n, sub, source):
        rows = pl.ds(n * length, length)
        columns = pl.ds(pl.multiple_of(place_ref[1 + sub] * width, width), width)
        return pltpu.make_async_copy(source, pieces.at[rows, columns], piece_sem.at[n, sub])

    def block_copy(i):
        return pltpu.make_async_copy(weight.at[pl.ds(i * lanes, lanes)], blocks.at[i], block_sem.at[i])

    def out_copies(i):
        columns = pl.ds(pl.multiple_of(i * lanes, lanes), lanes)
        return [
            pltpu.make_async_copy(others.at[i], other.at[:, columns], out_sem.at[0, i]),
            pltpu.make_async_copy(owns.at[i], own.at[:, columns], out_sem.at[1, i]),
        ]

    for i in range(steps):
        block_copy(i).start()

    def fetch(own_first):
        for sub, (first, second) in enumerate([(first_mine, second_mine), (first_theirs, second_theirs)]):
            piece_copy(0, sub, second if own_first else first).start()
            piece_copy(1, sub, first if own_first else second).start()

    pl.when(place_ref[0] != 0)(lambda: fetch(True))
    pl.when(place_ref[0] == 0)(lambda: fetch(False))
    for n in range(2):
        for sub in range(2):
            piece_copy(n, sub, first_mine).wait()

    @pl.loop(0, steps)
    def _(i):
        block_copy(i).wait()
        total = dot_nt(pieces[...], blocks[i])
        others[i] = total[:length].astype(bf16)
        owns[i] = total[length:]
        for copy in out_copies(i):
            copy.start()

    for i in range(steps):
        for copy in out_copies(i):
            copy.wait()


def weight_kernel(count, place_ref, *refs):
    cot_in, gated_in = refs[: 2 * count], list(refs[2 * count : 4 * count - 1])
    other, own, cots, gateds, others, owns, cot_sem, gated_sem, out_sem = refs[4 * count - 1 :]
    gated_in[-1:] = [gated_in[-1].at[0], gated_in[-1].at[1]]
    rows = other.shape[0]
    block = min(rows, turn)
    copies = [pltpu.make_async_copy(gated_in[n], gateds.at[n], gated_sem.at[n]) for n in range(2 * count)]
    copies += [pltpu.make_async_copy(cot_in[n], cots.at[n], cot_sem.at[n]) for n in range(2 * count)]
    for copy in copies:
        copy.start()
    for copy in copies:
        copy.wait()
    outs = [
        pltpu.make_async_copy(others, other, out_sem.at[0]),
        pltpu.make_async_copy(owns, own, out_sem.at[1]),
    ]

    def fill(replica, target):
        @pl.loop(0, rows // block)
        def _(i):
            start = pl.multiple_of(replica * rows + i * block, block)
            total = None
            for n in range(2 * count):
                gated = gateds[2 * place_ref[n % count] + n // count]
                part = dot(cots[n, pl.ds(start, block), :], gated)
                total = part if total is None else total + part
            target[pl.ds(pl.multiple_of(i * block, block), block), :] = total.astype(target.dtype)

    me = place_ref[count]
    fill(1 - me, others)
    outs[0].start()
    fill(me, owns)
    outs[1].start()
    for copy in outs:
        copy.wait()


def lag_kernel(
    table,
    synth,
    own_ref,
    other_ref,
    state_ref,
    query_ref,
    prior_ref,
    key_ref,
    value_ref,
    place_ref,
    grad_ref,
    signal_ref,
    head_ref,
    sent_lag_ref,
    own_lag_ref,
):
    length, taps, share = signal_ref.shape[0], prior_ref.shape[0], own_lag_ref.shape[0]
    grad_gated = own_ref[...] + other_ref[...].astype(f32)
    grad_ref[...] = (grad_gated * state_ref[...]).astype(bf16)
    signal = (grad_gated * query_ref[...].astype(f32)).astype(bf16)
    signal_ref[...] = signal
    head_ref[...] = signal[:taps]
    spec = mixed_spectrum(table, prior_ref, key_ref, value_ref)
    product = spectrum_product(forward_transform(table, signal, 0), spec, True)
    lags = -inverse_transform(synth, product, length, taps)
    first = place_ref[...] == 0.0
    own_lag_ref[...] = jnp.where(first, lags[:share], lags[share:])
    sent_lag_ref[...] = jnp.where(first, lags[share:], lags[:share]).astype(bf16)


def back_kernel(
    scale, table, synth, signal_ref, later_ref, taps_ref, skip_ref, key_ref, value_ref, grad_key_ref, grad_value_ref
):
    length = key_ref.shape[0]
    spec = forward_transform(table, signal_ref[...], 0) + forward_transform(table, later_ref[...], length)
    product = spectrum_product(spec, filter_spectrum(scale, table, taps_ref, skip_ref), True)
    back = inverse_transform(synth, product, 0, length)
    grad_key_ref[...] = (back * value_ref[...].astype(f32)).astype(bf16)
    grad_value_ref[...] = (back * key_ref[...].astype(f32)).astype(bf16)


def estimate(flops, arrays):
    moved = sum(a.size * jnp.dtype(a.dtype).itemsize for a in arrays)
    return pl.CostEstimate(flops=flops // 64, bytes_accessed=moved // 64, transcendentals=0)


def by_channel(body, tables, args, outs, channels, flops, swap=None):
    steps = channels // lanes
    flat_outs = [o for group in outs for o in group]
    n_tables, n_args, n_outs = len(tables), len(args), len(outs)

    def part(ref, i, count):
        start = i * lanes
        if ref.shape[1] == count * lanes:
            return ref.at[:, pl.ds(start, lanes)]
        return ref.at[pl.ds(start, lanes), :]

    def kernel(*refs):
        refs = list(refs)
        take = lambda count: [refs.pop(0) for _ in range(count)]
        swap_ref = None if swap is None else refs.pop(0)
        table_in, arg_in, outs_to = take(n_tables), take(n_args), take(len(flat_outs))
        table_held, arg_held, out_held = take(n_tables), take(n_args), take(n_outs)
        table_sem, arg_sem, out_sem = refs
        groups = [[outs_to.pop(0) for _ in group] for group in outs]

        def table_copy(k):
            return pltpu.make_async_copy(table_in[k], table_held[k], table_sem.at[k])

        def arg_copy(k):
            return pltpu.make_async_copy(arg_in[k], arg_held[k], arg_sem.at[k])

        def out_copy(k, n, i):
            place = groups[k][n] if len(groups[k]) > 1 else part(groups[k][n], i, steps)
            return pltpu.make_async_copy(out_held[k].at[i], place, out_sem.at[k, i])

        for k in range(n_tables):
            table_copy(k).start()
        for k in range(n_args):
            arg_copy(k).start()
        for k in range(n_tables):
            table_copy(k).wait()
        for k in range(n_args):
            arg_copy(k).wait()

        for i in range(steps):
            body(*table_held, *[part(ref, i, steps) for ref in arg_held], *[held.at[i] for held in out_held])
            for k in range(n_outs):
                count = len(groups[k])
                if count == 1:
                    out_copy(k, 0, i).start()
                else:
                    pl.when(swap_ref[0] == 0)(out_copy(k, i, i).start)
                    pl.when(swap_ref[0] != 0)(out_copy(k, count - 1 - i, i).start)

        for i in range(steps):
            for k in range(n_outs):
                out_copy(k, 0 if len(groups[k]) == 1 else i, i).wait()

    return pl.pallas_call(
        kernel,
        in_specs=[pl.BlockSpec(memory_space=pltpu.SMEM)] * (swap is not None)
        + [pl.BlockSpec(memory_space=pl.ANY)] * (n_tables + n_args),
        out_specs=[pl.BlockSpec(memory_space=pl.ANY)] * len(flat_outs),
        out_shape=flat_outs,
        scratch_shapes=[
            *[pltpu.VMEM(t.shape, bf16) for t in tables],
            *[pltpu.VMEM(a.shape, a.dtype) for a in args],
            *[pltpu.VMEM((steps, group[0].shape[0], lanes), group[0].dtype) for group in outs],
            pltpu.SemaphoreType.DMA((n_tables,)),
            pltpu.SemaphoreType.DMA((n_args,)),
            pltpu.SemaphoreType.DMA((n_outs, steps)),
        ],
        compiler_params=pltpu.CompilerParams(vmem_limit_bytes=vmem_bytes),
        cost_estimate=estimate(flops, [*args, *flat_outs]),
    )(*([] if swap is None else [swap]), *[jnp.asarray(t) for t in tables], *args)


def local_call(kernel, places, args, outs, scratch, flops):
    return pl.pallas_call(
        kernel,
        in_specs=[pl.BlockSpec(memory_space=pltpu.SMEM)] + [pl.BlockSpec(memory_space=pl.ANY)] * len(args),
        out_specs=[pl.BlockSpec(memory_space=pl.ANY)] * len(outs),
        out_shape=outs,
        scratch_shapes=scratch,
        compiler_params=pltpu.CompilerParams(vmem_limit_bytes=vmem_bytes),
        cost_estimate=estimate(flops, [*args, *outs]),
    )(places, *args)


def project(places, firsts, seconds, out_weight):
    length, width = firsts[0].shape
    channels, total_width = out_weight.shape
    steps = channels // lanes
    return local_call(
        project_kernel,
        places,
        [firsts[0], seconds[0], firsts[1], seconds[1], out_weight],
        [jax.ShapeDtypeStruct((length, channels), dtype) for dtype in (bf16, f32)],
        [
            pltpu.VMEM((2 * length, total_width), bf16),
            pltpu.VMEM((steps, lanes, total_width), bf16),
            pltpu.VMEM((steps, length, lanes), bf16),
            pltpu.VMEM((steps, length, lanes), f32),
            pltpu.SemaphoreType.DMA((2, 2)),
            pltpu.SemaphoreType.DMA((steps,)),
            pltpu.SemaphoreType.DMA((2, steps)),
        ],
        4 * length * out_weight.size,
    )


def weight_sum(places, cot_pieces, gated_pieces, rows):
    count = (len(gated_pieces) + 1) // 2
    length, width = gated_pieces[0].shape
    outs = [jax.ShapeDtypeStruct((rows, width), dtype) for dtype in (bf16, f32)]
    return local_call(
        functools.partial(weight_kernel, count),
        places,
        [*cot_pieces, *gated_pieces],
        outs,
        [
            pltpu.VMEM((2 * count, *cot_pieces[0].shape), bf16),
            pltpu.VMEM((2 * count, *gated_pieces[0].shape), bf16),
            *[pltpu.VMEM(o.shape, o.dtype) for o in outs],
            pltpu.SemaphoreType.DMA((2 * count,)),
            pltpu.SemaphoreType.DMA((2 * count,)),
            pltpu.SemaphoreType.DMA((2,)),
        ],
        8 * count * length * rows * width,
    )


def transpose_kernel(rows_in, out, rows, turned, sems):
    copy = pltpu.make_async_copy(rows_in, rows, sems.at[0])
    copy.start()
    copy.wait()
    for i in range(rows.shape[1] // turn):
        turned[pl.ds(i * turn, turn), :] = rows[:, pl.ds(i * turn, turn)].T
    copy = pltpu.make_async_copy(turned, out, sems.at[1])
    copy.start()
    copy.wait()


def transposed(rows):
    return pl.pallas_call(
        transpose_kernel,
        in_specs=[pl.BlockSpec(memory_space=pl.ANY)],
        out_specs=pl.BlockSpec(memory_space=pl.ANY),
        out_shape=jax.ShapeDtypeStruct(rows.shape[::-1], rows.dtype),
        scratch_shapes=[
            pltpu.VMEM(rows.shape, rows.dtype),
            pltpu.VMEM(rows.shape[::-1], rows.dtype),
            pltpu.SemaphoreType.DMA((2,)),
        ],
        compiler_params=pltpu.CompilerParams(vmem_limit_bytes=vmem_bytes),
        cost_estimate=estimate(0, [rows, rows]),
    )(rows)


def swap_pairs(value, axis, distance):
    count = lax.axis_size(axis)
    return lax.ppermute(value, axis, [(i, i ^ distance) for i in range(count)])


def after(value, *earlier):
    return lax.optimization_barrier((value, *earlier))[0]


def per_device(query_gate, key_gate, value_input, filter_taps, skip_gain, out_weight, cotangent):
    queries, key_rows, value_rows, cot = (
        query_gate[0],
        key_gate[0],
        value_input[0],
        cotangent[0],
    )
    length, channels = queries.shape
    taps = filter_taps.shape[1]
    n_seq, n_tp, n_dp = lax.axis_size("seq"), lax.axis_size("tp"), lax.axis_size("dp")
    subs = n_tp // n_dp
    me_tp, me_dp = lax.axis_index("tp"), lax.axis_index("dp")
    me_half, me_sub = me_tp // subs, me_tp % subs
    size = length + taps
    norm_factor = 1.0 / math.sqrt(length * n_seq * n_dp)

    whole = analysis_table(size, np.arange(size))
    scale = 2.0 / size
    tables = [split_table(whole), np.ascontiguousarray(split_table(whole.T))]
    rows16 = jax.ShapeDtypeStruct((length, channels), bf16)
    rows32 = jax.ShapeDtypeStruct((length, channels), f32)
    half16 = jax.ShapeDtypeStruct((length, channels // 2), bf16)
    unit = 2 * size * channels

    tail = (
        key_rows[length - taps :].astype(f32) * value_rows[length - taps :].astype(f32)
    ).astype(bf16)
    tail, cot = lax.optimization_barrier((tail, cot))
    prior = lax.ppermute(tail, "seq", [(i, i + 1) for i in range(n_seq - 1)])

    def tp_dp(half, sub, replica):
        return (half * subs + sub) * n_dp + replica

    places = [(h, c, d) for h in range(n_dp) for c in range(subs) for d in range(n_dp)]
    rounds = []
    for turn in range(2):
        route = [(tp_dp(h, c, d), tp_dp(d ^ turn, c, h)) for h, c, d in places]
        rounds.append(lax.ppermute(after(cot, prior) if turn else cot, ("tp", "dp"), route))
    square = n_seq == n_tp == 4 and subs == 2
    if square:

        def holder(s, block):
            return (s + block) % 2 * subs + s // 2

        crossed = {0: (1, 2), 1: (0, 3)}
        route = [
            (s * n_tp + t, s * n_tp + sum(crossed[s % 2]) - t)
            for s in range(n_seq)
            for t in crossed[s % 2]
        ]
        swapped = lax.ppermute(cot, ("seq", "tp"), route)
        moves_now = sum(
            jnp.logical_and(lax.axis_index("seq") % 2 == parity, me_tp == t)
            for parity in crossed
            for t in crossed[parity]
        )
        held = jnp.where(moves_now > 0, swapped, cot)
        route = []
        for s in range(n_seq):
            for t in range(n_tp):
                block = sum(crossed[s % 2]) - t if t in crossed[s % 2] else t
                route.append((s * n_tp + t, block * n_tp + holder(s, block)))
        moved = lax.ppermute(held, ("seq", "tp"), route)
    else:
        moved = cot

    same = (me_half == me_dp).astype(jnp.int32)
    subs_of = [me_sub, (me_sub + 1) % subs]
    place = jnp.stack([same, *subs_of]).astype(jnp.int32)
    dp_row = jnp.broadcast_to(me_dp.astype(f32), (1, channels))
    if square:
        order = [*range(0, n_seq, 2), *reversed(range(1, n_seq, 2))]
        ring = [(order[k], order[(k + 1) % n_seq]) for k in range(n_seq)]
        table = np.zeros((n_seq, n_tp, n_tp), np.int32)
        for k, s in enumerate(order):
            for r in range(n_seq):
                for t in range(n_tp):
                    table[s, t, t ^ holder(order[k - r], s)] = r
        sources = jnp.asarray(table)[lax.axis_index("seq"), me_tp]
        weight_place = jnp.concatenate([sources, me_dp[None].astype(jnp.int32)])
        prior, place, weight_place, dp_row = lax.optimization_barrier(
            (prior, place, weight_place, dp_row)
        )
    state, *gated = by_channel(
        functools.partial(state_kernel, scale),
        tables,
        [prior, key_rows, value_rows, filter_taps, skip_gain[None], queries],
        [[rows32], [half16, half16]],
        channels,
        unit * (4 * taps + 5 * length),
        jnp.reshape(me_dp if square else 0 * me_dp, (1,)).astype(jnp.int32),
    )
    if square:
        ring_pieces = [gated[0], swap_pairs(gated[1], "dp", 1)]

        def ring_step():
            for _ in range(2):
                ring_pieces.append(lax.ppermute(ring_pieces[-2], "seq", ring))

        ring_step()
    gated[0], *rounds = lax.optimization_barrier((gated[0], *rounds))

    route = [(tp_dp(h, c, d), tp_dp(h, (c + 1) % subs, d)) for h, c, d in places]
    if square:
        rounds[1], moved, _ = lax.optimization_barrier((rounds[1], moved, ring_pieces[1]))
    theirs = [lax.ppermute(r, ("tp", "dp"), route) for r in rounds]
    firsts, seconds = zip(rounds, theirs)
    rows = n_tp * channels // (n_seq * n_dp)
    if square:
        moved = after(moved, *rounds)
        moved_other = swap_pairs(moved, "dp", 1)
    other_sent, own_part = project(place, firsts, seconds, out_weight)
    if square:
        other_sent, moved_other = lax.optimization_barrier((other_sent, moved_other))
    other_part = swap_pairs(other_sent, "dp", 1)
    if square:

        def spread(piece, across, gate):
            near = [(t, t ^ 1) for t in range(n_tp)]
            return [
                piece,
                lax.ppermute(piece, "tp", near),
                across,
                lax.ppermute(after(across, gate), "tp", near),
            ]

        opposite = [(t, t ^ subs) for t in range(n_tp)]
        ring_pieces[2], ring_pieces[3], _ = lax.optimization_barrier((*ring_pieces[2:4], other_sent))
        moved = transposed(after(moved, ring_pieces[2]))
        across = lax.ppermute(moved, "tp", opposite)
        ring_step()
        last = jnp.stack([after(piece, other_part) for piece in ring_pieces[4:6]])
        last = lax.ppermute(last, "seq", ring)
        moved_other = transposed(after(moved_other, across))
        across_other = lax.ppermute(moved_other, "tp", opposite)
        cot_pieces = spread(moved, across, other_part) + spread(moved_other, across_other, own_part)
    else:
        full = lax.all_gather(cot, "tp", axis=1, tiled=True)
        cot_all = lax.all_to_all(full, "seq", 1, 0, tiled=True)
        gated_all = [lax.all_gather(half, "seq", axis=0, tiled=True) for half in gated]

        def part(replica, piece):
            block = lax.dynamic_slice_in_dim(cot_all, replica * rows, rows, axis=1)
            return lax.dot_general(
                block, piece, (((0,), (0,)), ((), ())), preferred_element_type=f32
            )

        def weight_one(piece):
            return part(me_dp, piece), swap_pairs(part(1 - me_dp, piece).astype(bf16), "dp", 1)

    share = taps // n_dp
    grad_query, signal, head, sent_lag, own_lag = by_channel(
        lag_kernel,
        tables,
        [own_part, other_part, state, queries, prior, key_rows, value_rows, dp_row],
        [
            [rows16],
            [rows16],
            [jax.ShapeDtypeStruct((taps, channels), bf16)],
            [jax.ShapeDtypeStruct((share, channels), bf16)],
            [jax.ShapeDtypeStruct((share, channels), f32)],
        ],
        channels,
        unit * (2 * taps + 4 * length + 3 * taps),
    )
    later = lax.ppermute(head, "seq", [(i + 1, i) for i in range(n_seq - 1)])

    def run_back(later):
        return by_channel(
            functools.partial(back_kernel, scale),
            tables,
            [signal, later, filter_taps, skip_gain[None], key_rows, value_rows],
            [[rows16], [rows16]],
            channels,
            256 * unit * (4 * taps + 5 * length),
        )

    received = swap_pairs(sent_lag, "dp", 1)
    if square:
        last, received = lax.optimization_barrier((last, received))
        ring_pieces.append(last)
    lag_sum = own_lag + received.astype(f32)
    distance = 1
    while distance < n_seq:
        rounded = lag_sum.astype(bf16)
        received = swap_pairs(rounded, "seq", distance)
        if square and distance == 1:
            weight_place, rounded = lax.optimization_barrier((weight_place, rounded))
            weight_sent, weight_own = weight_sum(weight_place, cot_pieces, ring_pieces, rows)
            weight_received = swap_pairs(weight_sent, "dp", 1)
            received, weight_own = lax.optimization_barrier((received, weight_own))
        if square and distance == 2:
            grad_key, grad_value = run_back(after(later, weight_own))
            received, grad_key = lax.optimization_barrier((received, grad_key))
        lag_sum = rounded.astype(f32) + received.astype(f32)
        distance *= 2
    mine = lag_sum.astype(bf16)
    if not square:
        grad_key, grad_value = run_back(later)
    theirs = swap_pairs(mine, "dp", 1)
    first = me_dp == 0
    lag_sum = jnp.concatenate([jnp.where(first, mine, theirs), jnp.where(first, theirs, mine)], axis=0)
    grad_filter = lag_sum.astype(f32).T * (norm_factor * scale)

    if square:
        weight_own, weight_received = weight_own * norm_factor, weight_received.astype(f32) * norm_factor
        grad_weight = jnp.concatenate(
            [
                jnp.where(first, weight_own, weight_received),
                jnp.where(first, weight_received, weight_own),
            ],
            axis=1,
        )
    else:
        parts = [weight_one(half) for half in gated_all]
        grad_weight = jnp.concatenate(
            [(mine + theirs.astype(f32)) * norm_factor for mine, theirs in parts], axis=1
        )
    return (
        grad_query[None],
        grad_key[None],
        grad_value[None],
        grad_filter,
        grad_filter[:, 0],
        grad_weight,
    )


def solution(mesh):
    tokens = P("dp", "seq", "tp")
    return jax.shard_map(
        per_device,
        mesh=mesh,
        in_specs=(tokens, tokens, tokens, P("tp", None), P("tp"), P("tp", "dp"), tokens),
        out_specs=(tokens, tokens, tokens, P("tp", None), P("tp"), P(("seq", "dp"), "tp")),
        check_vma=False,
    )
```

```python
import functools
import math

import jax
import jax.numpy as jnp
import ml_dtypes
import numpy as np
from jax import lax
from jax.experimental import pallas as pl
from jax.experimental.pallas import tpu as pltpu
from jax.sharding import PartitionSpec as P

f32, bf16 = jnp.float32, jnp.bfloat16
lanes = 512
turn = 256
vmem_bytes = 58 * 1024 * 1024


def analysis_table(size, positions):
    half = size // 2
    omega = 2.0 * np.pi * (np.arange(half) + 0.5) / size
    angle = omega[:, None] * np.asarray(positions)[None, :]
    return np.concatenate([np.cos(angle), -np.sin(angle)], axis=0)


def split_table(table):
    high = table.astype(ml_dtypes.bfloat16)
    low = (table - high.astype(np.float64)).astype(ml_dtypes.bfloat16)
    return np.concatenate([high, low])


def split_rows(rows):
    high = rows.astype(bf16)
    return high, (rows - high.astype(f32)).astype(bf16)


def dot(left, right):
    return jnp.dot(left, right, preferred_element_type=f32)


def dot_nt(left, right):
    return lax.dot_general(left, right, (((1,), (1,)), ((), ())), preferred_element_type=f32)


def add_halves(both):
    half = both.shape[0] // 2
    return both[:half] + both[half:]


def forward_transform(table, rows, start):
    return add_halves(dot(table[:, pl.ds(start, rows.shape[0])], rows))


def inverse_transform(table, spectrum, start, count):
    high, low = split_rows(spectrum)
    upper = table[pl.ds(start, count)]
    lower = table[pl.ds(table.shape[0] // 2 + start, count)]
    return dot(upper, high) + dot(upper, low) + dot(lower, high)


def spectrum_product(left, right, conjugate_right):
    half = left.shape[0] // 2
    left_re, left_im = left[:half], left[half:]
    right_re, right_im = right[:half], right[half:]
    if conjugate_right:
        right_im = -right_im
    return jnp.concatenate(
        [left_re * right_re - left_im * right_im, left_re * right_im + left_im * right_re], axis=0
    )


def mixed_spectrum(table, prior_ref, key_ref, value_ref):
    mixed = (key_ref[...].astype(f32) * value_ref[...].astype(f32)).astype(bf16)
    prior = prior_ref[...]
    return forward_transform(table, prior, 0) + forward_transform(table, mixed, prior.shape[0])


def filter_spectrum(scale, table, taps_ref, skip_ref):
    taps = taps_ref.shape[1]
    filt = add_halves(dot_nt(table[:, :taps], taps_ref[...]))
    half = filt.shape[0] // 2
    return jnp.concatenate([(filt[:half] + skip_ref[...]) * scale, filt[half:] * scale], axis=0)


def state_kernel(
    scale, table, synth, prior_ref, key_ref, value_ref, taps_ref, skip_ref, query_ref, state_ref, gated_ref
):
    spec = mixed_spectrum(table, prior_ref, key_ref, value_ref)
    product = spectrum_product(spec, filter_spectrum(scale, table, taps_ref, skip_ref), False)
    state = inverse_transform(synth, product, prior_ref.shape[0], query_ref.shape[0])
    state_ref[...] = state
    gated_ref[...] = (query_ref[...].astype(f32) * state).astype(bf16)


def project_kernel(
    place_ref, first_mine, second_mine, first_theirs, second_theirs, weight, other, own, pieces, blocks, others, owns, piece_sem, block_sem, out_sem
):
    steps, _, total_width = blocks.shape
    length, width = first_mine.shape

    def piece_copy(n, sub, source):
        rows = pl.ds(n * length, length)
        columns = pl.ds(pl.multiple_of(place_ref[1 + sub] * width, width), width)
        return pltpu.make_async_copy(source, pieces.at[rows, columns], piece_sem.at[n, sub])

    def block_copy(i):
        return pltpu.make_async_copy(weight.at[pl.ds(i * lanes, lanes)], blocks.at[i], block_sem.at[i])

    def out_copies(i):
        columns = pl.ds(pl.multiple_of(i * lanes, lanes), lanes)
        return [
            pltpu.make_async_copy(others.at[i], other.at[:, columns], out_sem.at[0, i]),
            pltpu.make_async_copy(owns.at[i], own.at[:, columns], out_sem.at[1, i]),
        ]

    for i in range(steps):
        block_copy(i).start()

    def fetch(own_first):
        for sub, (first, second) in enumerate([(first_mine, second_mine), (first_theirs, second_theirs)]):
            piece_copy(0, sub, second if own_first else first).start()
            piece_copy(1, sub, first if own_first else second).start()

    pl.when(place_ref[0] != 0)(lambda: fetch(True))
    pl.when(place_ref[0] == 0)(lambda: fetch(False))
    for n in range(2):
        for sub in range(2):
            piece_copy(n, sub, first_mine).wait()

    @pl.loop(0, steps)
    def _(i):
        block_copy(i).wait()
        total = dot_nt(pieces[...], blocks[i])
        others[i] = total[:length].astype(bf16)
        owns[i] = total[length:]
        for copy in out_copies(i):
            copy.start()

    for i in range(steps):
        for copy in out_copies(i):
            copy.wait()


def weight_kernel(count, place_ref, *refs):
    cot_in, gated_in = refs[:count], refs[count : 2 * count]
    other, own, cots, gateds, others, owns, in_sem, out_sem = refs[2 * count :]
    length = gateds.shape[1]
    rows = other.shape[0]
    block = min(rows, lanes)
    copies = [pltpu.make_async_copy(cot_in[n], cots.at[n], in_sem.at[0, n]) for n in range(count)]
    copies += [pltpu.make_async_copy(gated_in[n], gateds.at[n], in_sem.at[1, n]) for n in range(count)]
    for copy in copies:
        copy.start()
    for copy in copies:
        copy.wait()
    outs = [
        pltpu.make_async_copy(others, other, out_sem.at[0]),
        pltpu.make_async_copy(owns, own, out_sem.at[1]),
    ]

    def fill(replica, target):
        @pl.loop(0, rows // block)
        def _(i):
            start = pl.multiple_of(replica * rows + i * block, block)
            total = None
            for n in range(count):
                part = dot(cots[n, pl.ds(start, block), :], gateds[place_ref[n]])
                total = part if total is None else total + part
            target[pl.ds(pl.multiple_of(i * block, block), block), :] = total.astype(target.dtype)

    me = place_ref[count]
    fill(1 - me, others)
    outs[0].start()
    fill(me, owns)
    outs[1].start()
    for copy in outs:
        copy.wait()


def lag_kernel(
    table,
    synth,
    own_ref,
    other_ref,
    state_ref,
    query_ref,
    prior_ref,
    key_ref,
    value_ref,
    place_ref,
    grad_ref,
    signal_ref,
    head_ref,
    sent_lag_ref,
    own_lag_ref,
):
    length, taps, share = signal_ref.shape[0], prior_ref.shape[0], own_lag_ref.shape[0]
    grad_gated = own_ref[...] + other_ref[...].astype(f32)
    grad_ref[...] = (grad_gated * state_ref[...]).astype(bf16)
    signal = (grad_gated * query_ref[...].astype(f32)).astype(bf16)
    signal_ref[...] = signal
    head_ref[...] = signal[:taps]
    spec = mixed_spectrum(table, prior_ref, key_ref, value_ref)
    product = spectrum_product(forward_transform(table, signal, 0), spec, True)
    lags = -inverse_transform(synth, product, length, taps)
    first = place_ref[...] == 0.0
    own_lag_ref[...] = jnp.where(first, lags[:share], lags[share:])
    sent_lag_ref[...] = jnp.where(first, lags[share:], lags[:share]).astype(bf16)


def back_kernel(
    scale, table, synth, signal_ref, later_ref, taps_ref, skip_ref, key_ref, value_ref, grad_key_ref, grad_value_ref
):
    length = key_ref.shape[0]
    spec = forward_transform(table, signal_ref[...], 0) + forward_transform(table, later_ref[...], length)
    product = spectrum_product(spec, filter_spectrum(scale, table, taps_ref, skip_ref), True)
    back = inverse_transform(synth, product, 0, length)
    grad_key_ref[...] = (back * value_ref[...].astype(f32)).astype(bf16)
    grad_value_ref[...] = (back * key_ref[...].astype(f32)).astype(bf16)


def estimate(flops, arrays):
    moved = sum(a.size * jnp.dtype(a.dtype).itemsize for a in arrays)
    return pl.CostEstimate(flops=flops // 64, bytes_accessed=moved // 64, transcendentals=0)


def by_channel(body, tables, args, outs, channels, flops):
    steps = channels // lanes
    flat_outs = [o for group in outs for o in group]
    n_tables, n_args, n_outs = len(tables), len(args), len(outs)

    def part(ref, i, count):
        start = i * lanes
        if ref.shape[1] == count * lanes:
            return ref.at[:, pl.ds(start, lanes)]
        return ref.at[pl.ds(start, lanes), :]

    def kernel(*refs):
        refs = list(refs)
        take = lambda count: [refs.pop(0) for _ in range(count)]
        table_in, arg_in, outs_to = take(n_tables), take(n_args), take(len(flat_outs))
        table_held, arg_held, out_held = take(n_tables), take(n_args), take(n_outs)
        table_sem, arg_sem, out_sem = refs
        groups = [[outs_to.pop(0) for _ in group] for group in outs]

        def table_copy(k):
            return pltpu.make_async_copy(table_in[k], table_held[k], table_sem.at[k])

        def arg_copy(k):
            return pltpu.make_async_copy(arg_in[k], arg_held[k], arg_sem.at[k])

        def out_copy(k, n, i):
            per = steps // len(groups[k])
            place = part(groups[k][n], i - n * per, per)
            return pltpu.make_async_copy(out_held[k].at[i], place, out_sem.at[k, i])

        for k in range(n_tables):
            table_copy(k).start()
        for k in range(n_args):
            arg_copy(k).start()
        for k in range(n_tables):
            table_copy(k).wait()
        for k in range(n_args):
            arg_copy(k).wait()

        for i in range(steps):
            body(*table_held, *[part(ref, i, steps) for ref in arg_held], *[held.at[i] for held in out_held])
            for k in range(n_outs):
                out_copy(k, i * len(groups[k]) // steps, i).start()

        for i in range(steps):
            for k in range(n_outs):
                out_copy(k, i * len(groups[k]) // steps, i).wait()

    return pl.pallas_call(
        kernel,
        in_specs=[pl.BlockSpec(memory_space=pl.ANY)] * (n_tables + n_args),
        out_specs=[pl.BlockSpec(memory_space=pl.ANY)] * len(flat_outs),
        out_shape=flat_outs,
        scratch_shapes=[
            *[pltpu.VMEM(t.shape, bf16) for t in tables],
            *[pltpu.VMEM(a.shape, a.dtype) for a in args],
            *[pltpu.VMEM((steps, group[0].shape[0], lanes), group[0].dtype) for group in outs],
            pltpu.SemaphoreType.DMA((n_tables,)),
            pltpu.SemaphoreType.DMA((n_args,)),
            pltpu.SemaphoreType.DMA((n_outs, steps)),
        ],
        compiler_params=pltpu.CompilerParams(vmem_limit_bytes=vmem_bytes),
        cost_estimate=estimate(flops, [*args, *flat_outs]),
    )(*[jnp.asarray(t) for t in tables], *args)


def local_call(kernel, places, args, outs, scratch, flops):
    return pl.pallas_call(
        kernel,
        in_specs=[pl.BlockSpec(memory_space=pltpu.SMEM)] + [pl.BlockSpec(memory_space=pl.ANY)] * len(args),
        out_specs=[pl.BlockSpec(memory_space=pl.ANY)] * len(outs),
        out_shape=outs,
        scratch_shapes=scratch,
        compiler_params=pltpu.CompilerParams(vmem_limit_bytes=vmem_bytes),
        cost_estimate=estimate(flops, [*args, *outs]),
    )(places, *args)


def project(places, firsts, seconds, out_weight):
    length, width = firsts[0].shape
    channels, total_width = out_weight.shape
    steps = channels // lanes
    return local_call(
        project_kernel,
        places,
        [firsts[0], seconds[0], firsts[1], seconds[1], out_weight],
        [jax.ShapeDtypeStruct((length, channels), dtype) for dtype in (bf16, f32)],
        [
            pltpu.VMEM((2 * length, total_width), bf16),
            pltpu.VMEM((steps, lanes, total_width), bf16),
            pltpu.VMEM((steps, length, lanes), bf16),
            pltpu.VMEM((steps, length, lanes), f32),
            pltpu.SemaphoreType.DMA((2, 2)),
            pltpu.SemaphoreType.DMA((steps,)),
            pltpu.SemaphoreType.DMA((2, steps)),
        ],
        4 * length * out_weight.size,
    )


def weight_sum(places, cot_pieces, gated_pieces, rows):
    count = len(gated_pieces)
    length, width = gated_pieces[0].shape
    outs = [jax.ShapeDtypeStruct((rows, width), dtype) for dtype in (bf16, f32)]
    return local_call(
        functools.partial(weight_kernel, count),
        places,
        [*cot_pieces, *gated_pieces],
        outs,
        [
            pltpu.VMEM((count, *cot_pieces[0].shape), bf16),
            pltpu.VMEM((count, length, width), bf16),
            *[pltpu.VMEM(o.shape, o.dtype) for o in outs],
            pltpu.SemaphoreType.DMA((2, count)),
            pltpu.SemaphoreType.DMA((2,)),
        ],
        4 * count * length * rows * width,
    )


def transpose_kernel(rows_in, out, rows, turned, sems):
    copy = pltpu.make_async_copy(rows_in, rows, sems.at[0])
    copy.start()
    copy.wait()
    for i in range(rows.shape[1] // turn):
        turned[pl.ds(i * turn, turn), :] = rows[:, pl.ds(i * turn, turn)].T
    copy = pltpu.make_async_copy(turned, out, sems.at[1])
    copy.start()
    copy.wait()


def transposed(rows):
    return pl.pallas_call(
        transpose_kernel,
        in_specs=[pl.BlockSpec(memory_space=pl.ANY)],
        out_specs=pl.BlockSpec(memory_space=pl.ANY),
        out_shape=jax.ShapeDtypeStruct(rows.shape[::-1], rows.dtype),
        scratch_shapes=[
            pltpu.VMEM(rows.shape, rows.dtype),
            pltpu.VMEM(rows.shape[::-1], rows.dtype),
            pltpu.SemaphoreType.DMA((2,)),
        ],
        compiler_params=pltpu.CompilerParams(vmem_limit_bytes=vmem_bytes),
        cost_estimate=estimate(0, [rows, rows]),
    )(rows)


def swap_pairs(value, axis, distance):
    count = lax.axis_size(axis)
    return lax.ppermute(value, axis, [(i, i ^ distance) for i in range(count)])


def after(value, *earlier):
    return lax.optimization_barrier((value, *earlier))[0]


def per_device(query_gate, key_gate, value_input, filter_taps, skip_gain, out_weight, cotangent):
    queries, key_rows, value_rows, cot = (
        query_gate[0],
        key_gate[0],
        value_input[0],
        cotangent[0],
    )
    length, channels = queries.shape
    taps = filter_taps.shape[1]
    n_seq, n_tp, n_dp = lax.axis_size("seq"), lax.axis_size("tp"), lax.axis_size("dp")
    subs = n_tp // n_dp
    me_tp, me_dp = lax.axis_index("tp"), lax.axis_index("dp")
    me_half, me_sub = me_tp // subs, me_tp % subs
    size = length + taps
    norm_factor = 1.0 / math.sqrt(length * n_seq * n_dp)

    whole = analysis_table(size, np.arange(size))
    scale = 2.0 / size
    tables = [split_table(whole), np.ascontiguousarray(split_table(whole.T))]
    rows16 = jax.ShapeDtypeStruct((length, channels), bf16)
    rows32 = jax.ShapeDtypeStruct((length, channels), f32)
    half16 = jax.ShapeDtypeStruct((length, channels // 2), bf16)
    unit = 2 * size * channels

    tail = (
        key_rows[length - taps :].astype(f32) * value_rows[length - taps :].astype(f32)
    ).astype(bf16)
    tail, cot = lax.optimization_barrier((tail, cot))
    prior = lax.ppermute(tail, "seq", [(i, i + 1) for i in range(n_seq - 1)])

    def tp_dp(half, sub, replica):
        return (half * subs + sub) * n_dp + replica

    places = [(h, c, d) for h in range(n_dp) for c in range(subs) for d in range(n_dp)]
    rounds = []
    for turn in range(2):
        route = [(tp_dp(h, c, d), tp_dp(d ^ turn, c, h)) for h, c, d in places]
        rounds.append(lax.ppermute(after(cot, prior) if turn else cot, ("tp", "dp"), route))
    square = n_seq == n_tp == 4 and subs == 2
    if square:

        def holder(s, block):
            return (s + block) % 2 * subs + s // 2

        crossed = {0: (1, 2), 1: (0, 3)}
        route = [
            (s * n_tp + t, s * n_tp + sum(crossed[s % 2]) - t)
            for s in range(n_seq)
            for t in crossed[s % 2]
        ]
        swapped = lax.ppermute(cot, ("seq", "tp"), route)
        moves_now = sum(
            jnp.logical_and(lax.axis_index("seq") % 2 == parity, me_tp == t)
            for parity in crossed
            for t in crossed[parity]
        )
        held = jnp.where(moves_now > 0, swapped, cot)
        route = []
        for s in range(n_seq):
            for t in range(n_tp):
                block = sum(crossed[s % 2]) - t if t in crossed[s % 2] else t
                route.append((s * n_tp + t, block * n_tp + holder(s, block)))
        moved = lax.ppermute(held, ("seq", "tp"), route)
    else:
        moved = cot

    same = (me_half == me_dp).astype(jnp.int32)
    subs_of = [me_sub, (me_sub + 1) % subs]
    place = jnp.stack([same, *subs_of]).astype(jnp.int32)
    dp_row = jnp.broadcast_to(me_dp.astype(f32), (1, channels))
    if square:
        order = [*range(0, n_seq, 2), *reversed(range(1, n_seq, 2))]
        ring = [(order[k], order[(k + 1) % n_seq]) for k in range(n_seq)]
        table = np.zeros((n_seq, n_tp, n_tp), np.int32)
        for k, s in enumerate(order):
            for r in range(n_seq):
                for t in range(n_tp):
                    table[s, t, t ^ holder(order[k - r], s)] = r
        sources = jnp.asarray(table)[lax.axis_index("seq"), me_tp]
        weight_place = jnp.concatenate([sources, me_dp[None].astype(jnp.int32)])
        prior, place, weight_place, dp_row = lax.optimization_barrier(
            (prior, place, weight_place, dp_row)
        )
    state, *gated = by_channel(
        functools.partial(state_kernel, scale),
        tables,
        [prior, key_rows, value_rows, filter_taps, skip_gain[None], queries],
        [[rows32], [half16, half16]],
        channels,
        unit * (4 * taps + 5 * length),
    )
    if square:
        halves = [[half] for half in gated]

        def ring_step(pieces):
            pieces.append(lax.ppermute(pieces[-1], "seq", ring))

        ring_step(halves[0])
        halves[1][0], *rounds = lax.optimization_barrier((halves[1][0], *rounds))
    else:
        gated[0], *rounds = lax.optimization_barrier((gated[0], *rounds))

    route = [(tp_dp(h, c, d), tp_dp(h, (c + 1) % subs, d)) for h, c, d in places]
    theirs = [lax.ppermute(r, ("tp", "dp"), route) for r in rounds]
    firsts, seconds = zip(rounds, theirs)
    rows = n_tp * channels // (n_seq * n_dp)
    if square:
        moved = transposed(after(moved, *rounds))
        moved, place = lax.optimization_barrier((moved, place))
    other_sent, own_part = project(place, firsts, seconds, out_weight)
    other_part = swap_pairs(other_sent, "dp", 1)
    if square:
        halves[0][1], halves[1][0], _ = lax.optimization_barrier(
            (halves[0][1], halves[1][0], other_sent)
        )
        ring_step(halves[0])
        ring_step(halves[1])

    if square:
        sent_by = lambda value, flip: lax.ppermute(value, "tp", [(t, t ^ flip) for t in range(n_tp)])
        across = sent_by(moved, subs)
        cot_pieces = [moved, sent_by(moved, 1), across, sent_by(after(across, halves[0][2]), 1)]
        halves[0][2], own_part = lax.optimization_barrier((halves[0][2], own_part))
        ring_step(halves[0])
    else:
        full = lax.all_gather(cot, "tp", axis=1, tiled=True)
        cot_all = lax.all_to_all(full, "seq", 1, 0, tiled=True)
        gated_all = [lax.all_gather(half, "seq", axis=0, tiled=True) for half in gated]

        def part(replica, piece):
            block = lax.dynamic_slice_in_dim(cot_all, replica * rows, rows, axis=1)
            return lax.dot_general(
                block, piece, (((0,), (0,)), ((), ())), preferred_element_type=f32
            )

        def weight_one(piece):
            return part(me_dp, piece), swap_pairs(part(1 - me_dp, piece).astype(bf16), "dp", 1)

    share = taps // n_dp
    grad_query, signal, head, sent_lag, own_lag = by_channel(
        lag_kernel,
        tables,
        [own_part, other_part, state, queries, prior, key_rows, value_rows, dp_row],
        [
            [rows16],
            [rows16],
            [jax.ShapeDtypeStruct((taps, channels), bf16)],
            [jax.ShapeDtypeStruct((share, channels), bf16)],
            [jax.ShapeDtypeStruct((share, channels), f32)],
        ],
        channels,
        unit * (2 * taps + 4 * length + 3 * taps),
    )
    def run_back(later):
        return by_channel(
            functools.partial(back_kernel, scale),
            tables,
            [signal, later, filter_taps, skip_gain[None], key_rows, value_rows],
            [[rows16], [rows16]],
            channels,
            256 * unit * (4 * taps + 5 * length),
        )

    received = swap_pairs(sent_lag, "dp", 1)
    back_route = [(i + 1, i) for i in range(n_seq - 1)]
    if square:
        weight_place, halves[1][1], signal = lax.optimization_barrier((weight_place, halves[1][1], signal))
        ring_step(halves[1])
        first_sent, first_own = weight_sum(weight_place, cot_pieces, halves[0], rows)
        first_received = swap_pairs(first_sent, "dp", 1)
        received, first_own, halves[1][2], head = lax.optimization_barrier(
            (received, first_own, halves[1][2], head)
        )
        ring_step(halves[1])
    later = lax.ppermute(head, "seq", back_route)
    lag_sum = own_lag + received.astype(f32)
    distance = 1
    while distance < n_seq:
        rounded = lag_sum.astype(bf16)
        received = swap_pairs(rounded, "seq", distance)
        if square and distance == 1:
            weight_place, first_received = lax.optimization_barrier((weight_place, first_received))
            second_sent, second_own = weight_sum(weight_place, cot_pieces, halves[1], rows)
            second_received = swap_pairs(second_sent, "dp", 1)
        if square and distance == 2:
            received, second_own = lax.optimization_barrier((received, second_own))
        lag_sum = rounded.astype(f32) + received.astype(f32)
        distance *= 2
    mine = lag_sum.astype(bf16)
    theirs = swap_pairs(mine, "dp", 1)
    grad_key, grad_value = run_back(after(later, second_own) if square else later)
    first = me_dp == 0
    lag_sum = jnp.concatenate([jnp.where(first, mine, theirs), jnp.where(first, theirs, mine)], axis=0)
    grad_filter = lag_sum.astype(f32).T * (norm_factor * scale)

    if square:
        parts = [(first_own, first_received), (second_own, second_received)]
    else:
        parts = [weight_one(half) for half in gated_all]
    grad_weight = jnp.concatenate(
        [(mine + theirs.astype(f32)) * norm_factor for mine, theirs in parts], axis=1
    )
    return (
        grad_query[None],
        grad_key[None],
        grad_value[None],
        grad_filter,
        grad_filter[:, 0],
        grad_weight,
    )


def solution(mesh):
    tokens = P("dp", "seq", "tp")
    return jax.shard_map(
        per_device,
        mesh=mesh,
        in_specs=(tokens, tokens, tokens, P("tp", None), P("tp"), P("tp", "dp"), tokens),
        out_specs=(tokens, tokens, tokens, P("tp", None), P("tp"), P(("seq", "dp"), "tp")),
        check_vma=False,
    )
```

```python
import functools
import math

import jax
import jax.numpy as jnp
import ml_dtypes
import numpy as np
from jax import lax
from jax.experimental import pallas as pl
from jax.experimental.pallas import tpu as pltpu
from jax.sharding import PartitionSpec as P

f32, bf16 = jnp.float32, jnp.bfloat16
lanes = 512
turn = 256
vmem_bytes = 58 * 1024 * 1024


def analysis_table(size, positions):
    half = size // 2
    omega = 2.0 * np.pi * (np.arange(half) + 0.5) / size
    angle = omega[:, None] * np.asarray(positions)[None, :]
    return np.concatenate([np.cos(angle), -np.sin(angle)], axis=0)


def split_table(table):
    high = table.astype(ml_dtypes.bfloat16)
    low = (table - high.astype(np.float64)).astype(ml_dtypes.bfloat16)
    return np.concatenate([high, low])


def split_rows(rows):
    high = rows.astype(bf16)
    return high, (rows - high.astype(f32)).astype(bf16)


def dot(left, right):
    return jnp.dot(left, right, preferred_element_type=f32)


def dot_nt(left, right):
    return lax.dot_general(left, right, (((1,), (1,)), ((), ())), preferred_element_type=f32)


def add_halves(both):
    half = both.shape[0] // 2
    return both[:half] + both[half:]


def forward_transform(table, rows, start):
    return add_halves(dot(table[:, pl.ds(start, rows.shape[0])], rows))


def inverse_transform(table, spectrum, start, count):
    high, low = split_rows(spectrum)
    upper = table[pl.ds(start, count)]
    lower = table[pl.ds(table.shape[0] // 2 + start, count)]
    return dot(upper, high) + dot(upper, low) + dot(lower, high)


def spectrum_product(left, right, conjugate_right):
    half = left.shape[0] // 2
    left_re, left_im = left[:half], left[half:]
    right_re, right_im = right[:half], right[half:]
    if conjugate_right:
        right_im = -right_im
    return jnp.concatenate(
        [left_re * right_re - left_im * right_im, left_re * right_im + left_im * right_re], axis=0
    )


def mixed_spectrum(table, prior_ref, key_ref, value_ref):
    mixed = (key_ref[...].astype(f32) * value_ref[...].astype(f32)).astype(bf16)
    prior = prior_ref[...]
    return forward_transform(table, prior, 0) + forward_transform(table, mixed, prior.shape[0])


def filter_spectrum(scale, table, taps_ref, skip_ref):
    taps = taps_ref.shape[1]
    filt = add_halves(dot_nt(table[:, :taps], taps_ref[...]))
    half = filt.shape[0] // 2
    return jnp.concatenate([(filt[:half] + skip_ref[...]) * scale, filt[half:] * scale], axis=0)


def state_kernel(
    scale, table, synth, prior_ref, key_ref, value_ref, taps_ref, skip_ref, query_ref, state_ref, gated_ref
):
    spec = mixed_spectrum(table, prior_ref, key_ref, value_ref)
    product = spectrum_product(spec, filter_spectrum(scale, table, taps_ref, skip_ref), False)
    state = inverse_transform(synth, product, prior_ref.shape[0], query_ref.shape[0])
    state_ref[...] = state
    gated_ref[...] = (query_ref[...].astype(f32) * state).astype(bf16)


def project_kernel(
    place_ref, first_mine, second_mine, first_theirs, second_theirs, weight, other, own, pieces, blocks, others, owns, piece_sem, block_sem, out_sem
):
    steps, _, total_width = blocks.shape
    length, width = first_mine.shape

    def piece_copy(n, sub, source):
        rows = pl.ds(n * length, length)
        columns = pl.ds(pl.multiple_of(place_ref[1 + sub] * width, width), width)
        return pltpu.make_async_copy(source, pieces.at[rows, columns], piece_sem.at[n, sub])

    def block_copy(i):
        return pltpu.make_async_copy(weight.at[pl.ds(i * lanes, lanes)], blocks.at[i], block_sem.at[i])

    def out_copies(i):
        columns = pl.ds(pl.multiple_of(i * lanes, lanes), lanes)
        return [
            pltpu.make_async_copy(others.at[i], other.at[:, columns], out_sem.at[0, i]),
            pltpu.make_async_copy(owns.at[i], own.at[:, columns], out_sem.at[1, i]),
        ]

    for i in range(steps):
        block_copy(i).start()

    def fetch(own_first):
        for sub, (first, second) in enumerate([(first_mine, second_mine), (first_theirs, second_theirs)]):
            piece_copy(0, sub, second if own_first else first).start()
            piece_copy(1, sub, first if own_first else second).start()

    pl.when(place_ref[0] != 0)(lambda: fetch(True))
    pl.when(place_ref[0] == 0)(lambda: fetch(False))
    for n in range(2):
        for sub in range(2):
            piece_copy(n, sub, first_mine).wait()

    @pl.loop(0, steps)
    def _(i):
        block_copy(i).wait()
        total = dot_nt(pieces[...], blocks[i])
        others[i] = total[:length].astype(bf16)
        owns[i] = total[length:]
        for copy in out_copies(i):
            copy.start()

    for i in range(steps):
        for copy in out_copies(i):
            copy.wait()


def weight_kernel(count, place_ref, *refs):
    cot_in, gated_in = refs[:count], refs[count : 2 * count]
    other, own, cots, gateds, others, owns, in_sem, out_sem = refs[2 * count :]
    length = gateds.shape[1]
    rows = other.shape[0]
    block = min(rows, lanes)
    copies = [pltpu.make_async_copy(cot_in[n], cots.at[n], in_sem.at[0, n]) for n in range(count)]
    copies += [pltpu.make_async_copy(gated_in[n], gateds.at[n], in_sem.at[1, n]) for n in range(count)]
    for copy in copies:
        copy.start()
    for copy in copies:
        copy.wait()
    outs = [
        pltpu.make_async_copy(others, other, out_sem.at[0]),
        pltpu.make_async_copy(owns, own, out_sem.at[1]),
    ]

    def fill(replica, target):
        @pl.loop(0, rows // block)
        def _(i):
            start = pl.multiple_of(replica * rows + i * block, block)
            total = None
            for n in range(count):
                part = dot(cots[n, pl.ds(start, block), :], gateds[place_ref[n]])
                total = part if total is None else total + part
            target[pl.ds(pl.multiple_of(i * block, block), block), :] = total.astype(target.dtype)

    me = place_ref[count]
    fill(1 - me, others)
    outs[0].start()
    fill(me, owns)
    outs[1].start()
    for copy in outs:
        copy.wait()


def lag_kernel(
    table,
    synth,
    own_ref,
    other_ref,
    state_ref,
    query_ref,
    prior_ref,
    key_ref,
    value_ref,
    place_ref,
    grad_ref,
    signal_ref,
    head_ref,
    sent_lag_ref,
    own_lag_ref,
):
    length, taps, share = signal_ref.shape[0], prior_ref.shape[0], own_lag_ref.shape[0]
    grad_gated = own_ref[...] + other_ref[...].astype(f32)
    grad_ref[...] = (grad_gated * state_ref[...]).astype(bf16)
    signal = (grad_gated * query_ref[...].astype(f32)).astype(bf16)
    signal_ref[...] = signal
    head_ref[...] = signal[:taps]
    spec = mixed_spectrum(table, prior_ref, key_ref, value_ref)
    product = spectrum_product(forward_transform(table, signal, 0), spec, True)
    lags = -inverse_transform(synth, product, length, taps)
    first = place_ref[...] == 0.0
    own_lag_ref[...] = jnp.where(first, lags[:share], lags[share:])
    sent_lag_ref[...] = jnp.where(first, lags[share:], lags[:share]).astype(bf16)


def back_kernel(
    scale, table, synth, signal_ref, later_ref, taps_ref, skip_ref, key_ref, value_ref, grad_key_ref, grad_value_ref
):
    length = key_ref.shape[0]
    spec = forward_transform(table, signal_ref[...], 0) + forward_transform(table, later_ref[...], length)
    product = spectrum_product(spec, filter_spectrum(scale, table, taps_ref, skip_ref), True)
    back = inverse_transform(synth, product, 0, length)
    grad_key_ref[...] = (back * value_ref[...].astype(f32)).astype(bf16)
    grad_value_ref[...] = (back * key_ref[...].astype(f32)).astype(bf16)


def estimate(flops, arrays):
    moved = sum(a.size * jnp.dtype(a.dtype).itemsize for a in arrays)
    return pl.CostEstimate(flops=flops // 64, bytes_accessed=moved // 64, transcendentals=0)


def by_channel(body, tables, args, outs, channels, flops):
    steps = channels // lanes
    flat_outs = [o for group in outs for o in group]
    n_tables, n_args, n_outs = len(tables), len(args), len(outs)

    def part(ref, i, count):
        start = i * lanes
        if ref.shape[1] == count * lanes:
            return ref.at[:, pl.ds(start, lanes)]
        return ref.at[pl.ds(start, lanes), :]

    def kernel(*refs):
        refs = list(refs)
        take = lambda count: [refs.pop(0) for _ in range(count)]
        table_in, arg_in, outs_to = take(n_tables), take(n_args), take(len(flat_outs))
        table_held, arg_held, out_held = take(n_tables), take(n_args), take(n_outs)
        table_sem, arg_sem, out_sem = refs
        groups = [[outs_to.pop(0) for _ in group] for group in outs]

        def table_copy(k):
            return pltpu.make_async_copy(table_in[k], table_held[k], table_sem.at[k])

        def arg_copy(k):
            return pltpu.make_async_copy(arg_in[k], arg_held[k], arg_sem.at[k])

        def out_copy(k, n, i):
            per = steps // len(groups[k])
            place = part(groups[k][n], i - n * per, per)
            return pltpu.make_async_copy(out_held[k].at[i], place, out_sem.at[k, i])

        for k in range(n_tables):
            table_copy(k).start()
        for k in range(n_args):
            arg_copy(k).start()
        for k in range(n_tables):
            table_copy(k).wait()
        for k in range(n_args):
            arg_copy(k).wait()

        for i in range(steps):
            body(*table_held, *[part(ref, i, steps) for ref in arg_held], *[held.at[i] for held in out_held])
            for k in range(n_outs):
                out_copy(k, i * len(groups[k]) // steps, i).start()

        for i in range(steps):
            for k in range(n_outs):
                out_copy(k, i * len(groups[k]) // steps, i).wait()

    return pl.pallas_call(
        kernel,
        in_specs=[pl.BlockSpec(memory_space=pl.ANY)] * (n_tables + n_args),
        out_specs=[pl.BlockSpec(memory_space=pl.ANY)] * len(flat_outs),
        out_shape=flat_outs,
        scratch_shapes=[
            *[pltpu.VMEM(t.shape, bf16) for t in tables],
            *[pltpu.VMEM(a.shape, a.dtype) for a in args],
            *[pltpu.VMEM((steps, group[0].shape[0], lanes), group[0].dtype) for group in outs],
            pltpu.SemaphoreType.DMA((n_tables,)),
            pltpu.SemaphoreType.DMA((n_args,)),
            pltpu.SemaphoreType.DMA((n_outs, steps)),
        ],
        compiler_params=pltpu.CompilerParams(vmem_limit_bytes=vmem_bytes),
        cost_estimate=estimate(flops, [*args, *flat_outs]),
    )(*[jnp.asarray(t) for t in tables], *args)


def local_call(kernel, places, args, outs, scratch, flops):
    return pl.pallas_call(
        kernel,
        in_specs=[pl.BlockSpec(memory_space=pltpu.SMEM)] + [pl.BlockSpec(memory_space=pl.ANY)] * len(args),
        out_specs=[pl.BlockSpec(memory_space=pl.ANY)] * len(outs),
        out_shape=outs,
        scratch_shapes=scratch,
        compiler_params=pltpu.CompilerParams(vmem_limit_bytes=vmem_bytes),
        cost_estimate=estimate(flops, [*args, *outs]),
    )(places, *args)


def project(places, firsts, seconds, out_weight):
    length, width = firsts[0].shape
    channels, total_width = out_weight.shape
    steps = channels // lanes
    return local_call(
        project_kernel,
        places,
        [firsts[0], seconds[0], firsts[1], seconds[1], out_weight],
        [jax.ShapeDtypeStruct((length, channels), dtype) for dtype in (bf16, f32)],
        [
            pltpu.VMEM((2 * length, total_width), bf16),
            pltpu.VMEM((steps, lanes, total_width), bf16),
            pltpu.VMEM((steps, length, lanes), bf16),
            pltpu.VMEM((steps, length, lanes), f32),
            pltpu.SemaphoreType.DMA((2, 2)),
            pltpu.SemaphoreType.DMA((steps,)),
            pltpu.SemaphoreType.DMA((2, steps)),
        ],
        4 * length * out_weight.size,
    )


def weight_sum(places, cot_pieces, gated_pieces, rows):
    count = len(gated_pieces)
    length, width = gated_pieces[0].shape
    outs = [jax.ShapeDtypeStruct((rows, width), dtype) for dtype in (bf16, f32)]
    return local_call(
        functools.partial(weight_kernel, count),
        places,
        [*cot_pieces, *gated_pieces],
        outs,
        [
            pltpu.VMEM((count, *cot_pieces[0].shape), bf16),
            pltpu.VMEM((count, length, width), bf16),
            *[pltpu.VMEM(o.shape, o.dtype) for o in outs],
            pltpu.SemaphoreType.DMA((2, count)),
            pltpu.SemaphoreType.DMA((2,)),
        ],
        4 * count * length * rows * width,
    )


def transpose_kernel(rows_in, out, rows, turned, sems):
    copy = pltpu.make_async_copy(rows_in, rows, sems.at[0])
    copy.start()
    copy.wait()
    for i in range(rows.shape[1] // turn):
        turned[pl.ds(i * turn, turn), :] = rows[:, pl.ds(i * turn, turn)].T
    copy = pltpu.make_async_copy(turned, out, sems.at[1])
    copy.start()
    copy.wait()


def transposed(rows):
    return pl.pallas_call(
        transpose_kernel,
        in_specs=[pl.BlockSpec(memory_space=pl.ANY)],
        out_specs=pl.BlockSpec(memory_space=pl.ANY),
        out_shape=jax.ShapeDtypeStruct(rows.shape[::-1], rows.dtype),
        scratch_shapes=[
            pltpu.VMEM(rows.shape, rows.dtype),
            pltpu.VMEM(rows.shape[::-1], rows.dtype),
            pltpu.SemaphoreType.DMA((2,)),
        ],
        compiler_params=pltpu.CompilerParams(vmem_limit_bytes=vmem_bytes),
        cost_estimate=estimate(0, [rows, rows]),
    )(rows)


def swap_pairs(value, axis, distance):
    count = lax.axis_size(axis)
    return lax.ppermute(value, axis, [(i, i ^ distance) for i in range(count)])


def after(value, *earlier):
    return lax.optimization_barrier((value, *earlier))[0]


def per_device(query_gate, key_gate, value_input, filter_taps, skip_gain, out_weight, cotangent):
    queries, key_rows, value_rows, cot = (
        query_gate[0],
        key_gate[0],
        value_input[0],
        cotangent[0],
    )
    length, channels = queries.shape
    taps = filter_taps.shape[1]
    n_seq, n_tp, n_dp = lax.axis_size("seq"), lax.axis_size("tp"), lax.axis_size("dp")
    subs = n_tp // n_dp
    me_tp, me_dp = lax.axis_index("tp"), lax.axis_index("dp")
    me_half, me_sub = me_tp // subs, me_tp % subs
    size = length + taps
    norm_factor = 1.0 / math.sqrt(length * n_seq * n_dp)

    whole = analysis_table(size, np.arange(size))
    scale = 2.0 / size
    tables = [split_table(whole), np.ascontiguousarray(split_table(whole.T))]
    rows16 = jax.ShapeDtypeStruct((length, channels), bf16)
    rows32 = jax.ShapeDtypeStruct((length, channels), f32)
    half16 = jax.ShapeDtypeStruct((length, channels // 2), bf16)
    unit = 2 * size * channels

    tail = (
        key_rows[length - taps :].astype(f32) * value_rows[length - taps :].astype(f32)
    ).astype(bf16)
    tail, cot = lax.optimization_barrier((tail, cot))
    prior = lax.ppermute(tail, "seq", [(i, i + 1) for i in range(n_seq - 1)])

    def tp_dp(half, sub, replica):
        return (half * subs + sub) * n_dp + replica

    places = [(h, c, d) for h in range(n_dp) for c in range(subs) for d in range(n_dp)]
    rounds = []
    for turn in range(2):
        route = [(tp_dp(h, c, d), tp_dp(d ^ turn, c, h)) for h, c, d in places]
        rounds.append(lax.ppermute(after(cot, prior) if turn else cot, ("tp", "dp"), route))
    square = n_seq == n_tp == 4 and subs == 2
    if square:

        def holder(s, block):
            return (s + block) % 2 * subs + s // 2

        crossed = {0: (1, 2), 1: (0, 3)}
        route = [
            (s * n_tp + t, s * n_tp + sum(crossed[s % 2]) - t)
            for s in range(n_seq)
            for t in crossed[s % 2]
        ]
        swapped = lax.ppermute(cot, ("seq", "tp"), route)
        moves_now = sum(
            jnp.logical_and(lax.axis_index("seq") % 2 == parity, me_tp == t)
            for parity in crossed
            for t in crossed[parity]
        )
        held = jnp.where(moves_now > 0, swapped, cot)
        route = []
        for s in range(n_seq):
            for t in range(n_tp):
                block = sum(crossed[s % 2]) - t if t in crossed[s % 2] else t
                route.append((s * n_tp + t, block * n_tp + holder(s, block)))
        moved = lax.ppermute(held, ("seq", "tp"), route)
    else:
        moved = cot

    same = (me_half == me_dp).astype(jnp.int32)
    subs_of = [me_sub, (me_sub + 1) % subs]
    place = jnp.stack([same, *subs_of]).astype(jnp.int32)
    dp_row = jnp.broadcast_to(me_dp.astype(f32), (1, channels))
    if square:
        order = [*range(0, n_seq, 2), *reversed(range(1, n_seq, 2))]
        ring = [(order[k], order[(k + 1) % n_seq]) for k in range(n_seq)]
        table = np.zeros((n_seq, n_tp, n_tp), np.int32)
        for k, s in enumerate(order):
            for r in range(n_seq):
                for t in range(n_tp):
                    table[s, t, t ^ holder(order[k - r], s)] = r
        sources = jnp.asarray(table)[lax.axis_index("seq"), me_tp]
        weight_place = jnp.concatenate([sources, me_dp[None].astype(jnp.int32)])
        prior, place, weight_place, dp_row = lax.optimization_barrier(
            (prior, place, weight_place, dp_row)
        )
    state, *gated = by_channel(
        functools.partial(state_kernel, scale),
        tables,
        [prior, key_rows, value_rows, filter_taps, skip_gain[None], queries],
        [[rows32], [half16, half16]],
        channels,
        unit * (4 * taps + 5 * length),
    )
    if square:
        halves = [[half] for half in gated]

        def ring_step(pieces):
            pieces.append(lax.ppermute(pieces[-1], "seq", ring))

        halves[0][0], moved = lax.optimization_barrier((halves[0][0], moved))
        ring_step(halves[0])
        halves[1][0], *rounds = lax.optimization_barrier((halves[1][0], *rounds))
    else:
        gated[0], *rounds = lax.optimization_barrier((gated[0], *rounds))

    route = [(tp_dp(h, c, d), tp_dp(h, (c + 1) % subs, d)) for h, c, d in places]
    theirs = [lax.ppermute(r, ("tp", "dp"), route) for r in rounds]
    firsts, seconds = zip(rounds, theirs)
    rows = n_tp * channels // (n_seq * n_dp)
    if square:
        moved = transposed(after(moved, *rounds))
        moved, place = lax.optimization_barrier((moved, place))
    other_sent, own_part = project(place, firsts, seconds, out_weight)
    other_part = swap_pairs(other_sent, "dp", 1)
    if square:
        halves[0][1], halves[1][0], _ = lax.optimization_barrier(
            (halves[0][1], halves[1][0], other_sent)
        )
        ring_step(halves[0])
        ring_step(halves[1])

    if square:
        sent_by = lambda value, flip: lax.ppermute(value, "tp", [(t, t ^ flip) for t in range(n_tp)])
        across = sent_by(moved, subs)
        cot_pieces = [moved, sent_by(moved, 1), across, sent_by(after(across, halves[0][2]), 1)]
        ring_step(halves[0])
        halves[1][1], own_part = lax.optimization_barrier((halves[1][1], own_part))
        ring_step(halves[1])
        halves[0][3], own_part = lax.optimization_barrier((halves[0][3], own_part))
    else:
        full = lax.all_gather(cot, "tp", axis=1, tiled=True)
        cot_all = lax.all_to_all(full, "seq", 1, 0, tiled=True)
        gated_all = [lax.all_gather(half, "seq", axis=0, tiled=True) for half in gated]

        def part(replica, piece):
            block = lax.dynamic_slice_in_dim(cot_all, replica * rows, rows, axis=1)
            return lax.dot_general(
                block, piece, (((0,), (0,)), ((), ())), preferred_element_type=f32
            )

        def weight_one(piece):
            return part(me_dp, piece), swap_pairs(part(1 - me_dp, piece).astype(bf16), "dp", 1)

    share = taps // n_dp
    grad_query, signal, head, sent_lag, own_lag = by_channel(
        lag_kernel,
        tables,
        [own_part, other_part, state, queries, prior, key_rows, value_rows, dp_row],
        [
            [rows16],
            [rows16],
            [jax.ShapeDtypeStruct((taps, channels), bf16)],
            [jax.ShapeDtypeStruct((share, channels), bf16)],
            [jax.ShapeDtypeStruct((share, channels), f32)],
        ],
        channels,
        unit * (2 * taps + 4 * length + 3 * taps),
    )
    later = lax.ppermute(head, "seq", [(i + 1, i) for i in range(n_seq - 1)])

    def run_back(later):
        return by_channel(
            functools.partial(back_kernel, scale),
            tables,
            [signal, later, filter_taps, skip_gain[None], key_rows, value_rows],
            [[rows16], [rows16]],
            channels,
            256 * unit * (4 * taps + 5 * length),
        )

    received = swap_pairs(sent_lag, "dp", 1)
    if square:
        weight_place, halves[1][2], signal = lax.optimization_barrier((weight_place, halves[1][2], signal))
        ring_step(halves[1])
        first_sent, first_own = weight_sum(weight_place, cot_pieces, halves[0], rows)
        first_received = swap_pairs(first_sent, "dp", 1)
        received, first_own = lax.optimization_barrier((received, first_own))
    lag_sum = own_lag + received.astype(f32)
    distance = 1
    while distance < n_seq:
        rounded = lag_sum.astype(bf16)
        received = swap_pairs(rounded, "seq", distance)
        if square and distance == 1:
            second_sent, second_own = weight_sum(weight_place, cot_pieces, halves[1], rows)
            second_received = swap_pairs(second_sent, "dp", 1)
            received, second_own = lax.optimization_barrier((received, second_own))
        lag_sum = rounded.astype(f32) + received.astype(f32)
        distance *= 2
    if square:
        first_received, lag_sum = lax.optimization_barrier((first_received, lag_sum))
    mine = lag_sum.astype(bf16)
    theirs = swap_pairs(mine, "dp", 1)
    grad_key, grad_value = run_back(after(later, second_own) if square else later)
    first = me_dp == 0
    lag_sum = jnp.concatenate([jnp.where(first, mine, theirs), jnp.where(first, theirs, mine)], axis=0)
    grad_filter = lag_sum.astype(f32).T * (norm_factor * scale)

    if square:
        parts = [(first_own, first_received), (second_own, second_received)]
    else:
        parts = [weight_one(half) for half in gated_all]
    grad_weight = jnp.concatenate(
        [(mine + theirs.astype(f32)) * norm_factor for mine, theirs in parts], axis=1
    )
    return (
        grad_query[None],
        grad_key[None],
        grad_value[None],
        grad_filter,
        grad_filter[:, 0],
        grad_weight,
    )


def solution(mesh):
    tokens = P("dp", "seq", "tp")
    return jax.shard_map(
        per_device,
        mesh=mesh,
        in_specs=(tokens, tokens, tokens, P("tp", None), P("tp"), P("tp", "dp"), tokens),
        out_specs=(tokens, tokens, tokens, P("tp", None), P("tp"), P(("seq", "dp"), "tp")),
        check_vma=False,
    )
```

```python
import functools
import math

import jax
import jax.numpy as jnp
import ml_dtypes
import numpy as np
from jax import lax
from jax.experimental import pallas as pl
from jax.experimental.pallas import tpu as pltpu
from jax.sharding import PartitionSpec as P

f32, bf16 = jnp.float32, jnp.bfloat16
lanes = 512
turn = 256
vmem_bytes = 46 * 1024 * 1024


def analysis_table(size, positions):
    half = size // 2
    omega = 2.0 * np.pi * (np.arange(half) + 0.5) / size
    angle = omega[:, None] * np.asarray(positions)[None, :]
    return np.concatenate([np.cos(angle), -np.sin(angle)], axis=0)


def split_table(table):
    high = table.astype(ml_dtypes.bfloat16)
    low = (table - high.astype(np.float64)).astype(ml_dtypes.bfloat16)
    return np.concatenate([high, low])


def split_rows(rows):
    high = rows.astype(bf16)
    return high, (rows - high.astype(f32)).astype(bf16)


def dot(left, right):
    return jnp.dot(left, right, preferred_element_type=f32)


def dot_nt(left, right):
    return lax.dot_general(left, right, (((1,), (1,)), ((), ())), preferred_element_type=f32)


def add_halves(both):
    half = both.shape[0] // 2
    return both[:half] + both[half:]


def forward_transform(table, rows, start):
    return add_halves(dot(table[:, pl.ds(start, rows.shape[0])], rows))


def inverse_transform(table, spectrum, start, count):
    high, low = split_rows(spectrum)
    upper = table[pl.ds(start, count)]
    lower = table[pl.ds(table.shape[0] // 2 + start, count)]
    return dot(upper, high) + dot(upper, low) + dot(lower, high)


def spectrum_product(left, right, conjugate_right):
    half = left.shape[0] // 2
    left_re, left_im = left[:half], left[half:]
    right_re, right_im = right[:half], right[half:]
    if conjugate_right:
        right_im = -right_im
    return jnp.concatenate(
        [left_re * right_re - left_im * right_im, left_re * right_im + left_im * right_re], axis=0
    )


def mixed_spectrum(table, prior_ref, key_ref, value_ref):
    mixed = (key_ref[...].astype(f32) * value_ref[...].astype(f32)).astype(bf16)
    prior = prior_ref[...]
    return forward_transform(table, prior, 0) + forward_transform(table, mixed, prior.shape[0])


def filter_spectrum(scale, table, taps_ref, skip_ref):
    taps = taps_ref.shape[1]
    filt = add_halves(dot_nt(table[:, :taps], taps_ref[...]))
    half = filt.shape[0] // 2
    return jnp.concatenate([(filt[:half] + skip_ref[...]) * scale, filt[half:] * scale], axis=0)


def state_kernel(
    scale, table, synth, prior_ref, key_ref, value_ref, taps_ref, skip_ref, query_ref, state_ref, gated_ref
):
    spec = mixed_spectrum(table, prior_ref, key_ref, value_ref)
    product = spectrum_product(spec, filter_spectrum(scale, table, taps_ref, skip_ref), False)
    state = inverse_transform(synth, product, prior_ref.shape[0], query_ref.shape[0])
    state_ref[...] = state
    gated_ref[...] = (query_ref[...].astype(f32) * state).astype(bf16)


def project_kernel(
    place_ref, first_mine, second_mine, first_theirs, second_theirs, weight, other, own, pieces, blocks, others, owns, piece_sem, block_sem, out_sem
):
    steps, _, total_width = blocks.shape
    length, width = first_mine.shape

    def piece_copy(n, sub, source):
        rows = pl.ds(n * length, length)
        columns = pl.ds(pl.multiple_of(place_ref[1 + sub] * width, width), width)
        return pltpu.make_async_copy(source, pieces.at[rows, columns], piece_sem.at[n, sub])

    def block_copy(i):
        return pltpu.make_async_copy(weight.at[pl.ds(i * lanes, lanes)], blocks.at[i], block_sem.at[i])

    def out_copies(i):
        columns = pl.ds(pl.multiple_of(i * lanes, lanes), lanes)
        return [
            pltpu.make_async_copy(others.at[i], other.at[:, columns], out_sem.at[0, i]),
            pltpu.make_async_copy(owns.at[i], own.at[:, columns], out_sem.at[1, i]),
        ]

    for i in range(steps):
        block_copy(i).start()

    def fetch(own_first):
        for sub, (first, second) in enumerate([(first_mine, second_mine), (first_theirs, second_theirs)]):
            piece_copy(0, sub, second if own_first else first).start()
            piece_copy(1, sub, first if own_first else second).start()

    pl.when(place_ref[0] != 0)(lambda: fetch(True))
    pl.when(place_ref[0] == 0)(lambda: fetch(False))
    for n in range(2):
        for sub in range(2):
            piece_copy(n, sub, first_mine).wait()

    @pl.loop(0, steps)
    def _(i):
        block_copy(i).wait()
        total = dot_nt(pieces[...], blocks[i])
        others[i] = total[:length].astype(bf16)
        owns[i] = total[length:]
        for copy in out_copies(i):
            copy.start()

    for i in range(steps):
        for copy in out_copies(i):
            copy.wait()


def weight_kernel(count, place_ref, *refs):
    cot_in, gated_in = refs[:count], refs[count : 2 * count]
    other, own, cots, gateds, others, owns, in_sem, out_sem = refs[2 * count :]
    length = gateds.shape[1]
    rows = other.shape[0]
    block = min(rows, lanes)
    copies = [pltpu.make_async_copy(cot_in[n], cots.at[n], in_sem.at[0, n]) for n in range(count)]
    copies += [pltpu.make_async_copy(gated_in[n], gateds.at[n], in_sem.at[1, n]) for n in range(count)]
    for copy in copies:
        copy.start()
    for copy in copies:
        copy.wait()
    outs = [
        pltpu.make_async_copy(others, other, out_sem.at[0]),
        pltpu.make_async_copy(owns, own, out_sem.at[1]),
    ]

    def fill(replica, target):
        @pl.loop(0, rows // block)
        def _(i):
            start = pl.multiple_of(replica * rows + i * block, block)
            total = None
            for n in range(count):
                part = dot(cots[n, pl.ds(start, block), :], gateds[place_ref[n]])
                total = part if total is None else total + part
            target[pl.ds(pl.multiple_of(i * block, block), block), :] = total.astype(target.dtype)

    me = place_ref[count]
    fill(1 - me, others)
    outs[0].start()
    fill(me, owns)
    outs[1].start()
    for copy in outs:
        copy.wait()


def lag_kernel(
    table,
    synth,
    own_ref,
    other_ref,
    state_ref,
    query_ref,
    prior_ref,
    key_ref,
    value_ref,
    place_ref,
    grad_ref,
    signal_ref,
    head_ref,
    sent_lag_ref,
    own_lag_ref,
):
    length, taps, share = signal_ref.shape[0], prior_ref.shape[0], own_lag_ref.shape[0]
    grad_gated = own_ref[...] + other_ref[...].astype(f32)
    grad_ref[...] = (grad_gated * state_ref[...]).astype(bf16)
    signal = (grad_gated * query_ref[...].astype(f32)).astype(bf16)
    signal_ref[...] = signal
    head_ref[...] = signal[:taps]
    spec = mixed_spectrum(table, prior_ref, key_ref, value_ref)
    product = spectrum_product(forward_transform(table, signal, 0), spec, True)
    lags = -inverse_transform(synth, product, length, taps)
    first = place_ref[...] == 0.0
    own_lag_ref[...] = jnp.where(first, lags[:share], lags[share:])
    sent_lag_ref[...] = jnp.where(first, lags[share:], lags[:share]).astype(bf16)


def back_kernel(
    scale, table, synth, signal_ref, later_ref, taps_ref, skip_ref, key_ref, value_ref, grad_key_ref, grad_value_ref
):
    length = key_ref.shape[0]
    spec = forward_transform(table, signal_ref[...], 0) + forward_transform(table, later_ref[...], length)
    product = spectrum_product(spec, filter_spectrum(scale, table, taps_ref, skip_ref), True)
    back = inverse_transform(synth, product, 0, length)
    grad_key_ref[...] = (back * value_ref[...].astype(f32)).astype(bf16)
    grad_value_ref[...] = (back * key_ref[...].astype(f32)).astype(bf16)


def estimate(flops, arrays):
    moved = sum(a.size * jnp.dtype(a.dtype).itemsize for a in arrays)
    return pl.CostEstimate(flops=flops // 64, bytes_accessed=moved // 64, transcendentals=0)


def by_channel(body, tables, args, outs, channels, flops):
    steps = channels // lanes
    flat_outs = [o for group in outs for o in group]
    n_tables, n_args, n_outs = len(tables), len(args), len(outs)

    def part(ref, i, count):
        start = i * lanes
        if ref.shape[1] == count * lanes:
            return ref.at[:, pl.ds(start, lanes)]
        return ref.at[pl.ds(start, lanes), :]

    def kernel(*refs):
        refs = list(refs)
        take = lambda count: [refs.pop(0) for _ in range(count)]
        table_in, arg_in, outs_to = take(n_tables), take(n_args), take(len(flat_outs))
        table_held, arg_held, out_held = take(n_tables), take(n_args), take(n_outs)
        table_sem, arg_sem, out_sem = refs
        groups = [[outs_to.pop(0) for _ in group] for group in outs]

        def table_copy(k):
            return pltpu.make_async_copy(table_in[k], table_held[k], table_sem.at[k])

        def arg_copy(k):
            return pltpu.make_async_copy(arg_in[k], arg_held[k], arg_sem.at[k])

        def out_copy(k, n, i):
            per = steps // len(groups[k])
            place = part(groups[k][n], i - n * per, per)
            return pltpu.make_async_copy(out_held[k].at[i], place, out_sem.at[k, i])

        for k in range(n_tables):
            table_copy(k).start()
        for k in range(n_args):
            arg_copy(k).start()
        for k in range(n_tables):
            table_copy(k).wait()
        for k in range(n_args):
            arg_copy(k).wait()

        for i in range(steps):
            body(*table_held, *[part(ref, i, steps) for ref in arg_held], *[held.at[i] for held in out_held])
            for k in range(n_outs):
                out_copy(k, i * len(groups[k]) // steps, i).start()

        for i in range(steps):
            for k in range(n_outs):
                out_copy(k, i * len(groups[k]) // steps, i).wait()

    return pl.pallas_call(
        kernel,
        in_specs=[pl.BlockSpec(memory_space=pl.ANY)] * (n_tables + n_args),
        out_specs=[pl.BlockSpec(memory_space=pl.ANY)] * len(flat_outs),
        out_shape=flat_outs,
        scratch_shapes=[
            *[pltpu.VMEM(t.shape, bf16) for t in tables],
            *[pltpu.VMEM(a.shape, a.dtype) for a in args],
            *[pltpu.VMEM((steps, group[0].shape[0], lanes), group[0].dtype) for group in outs],
            pltpu.SemaphoreType.DMA((n_tables,)),
            pltpu.SemaphoreType.DMA((n_args,)),
            pltpu.SemaphoreType.DMA((n_outs, steps)),
        ],
        compiler_params=pltpu.CompilerParams(vmem_limit_bytes=vmem_bytes),
        cost_estimate=estimate(flops, [*args, *flat_outs]),
    )(*[jnp.asarray(t) for t in tables], *args)


def local_call(kernel, places, args, outs, scratch, flops):
    return pl.pallas_call(
        kernel,
        in_specs=[pl.BlockSpec(memory_space=pltpu.SMEM)] + [pl.BlockSpec(memory_space=pl.ANY)] * len(args),
        out_specs=[pl.BlockSpec(memory_space=pl.ANY)] * len(outs),
        out_shape=outs,
        scratch_shapes=scratch,
        compiler_params=pltpu.CompilerParams(vmem_limit_bytes=vmem_bytes),
        cost_estimate=estimate(flops, [*args, *outs]),
    )(places, *args)


def project(places, firsts, seconds, out_weight):
    length, width = firsts[0].shape
    channels, total_width = out_weight.shape
    steps = channels // lanes
    return local_call(
        project_kernel,
        places,
        [firsts[0], seconds[0], firsts[1], seconds[1], out_weight],
        [jax.ShapeDtypeStruct((length, channels), dtype) for dtype in (bf16, f32)],
        [
            pltpu.VMEM((2 * length, total_width), bf16),
            pltpu.VMEM((steps, lanes, total_width), bf16),
            pltpu.VMEM((steps, length, lanes), bf16),
            pltpu.VMEM((steps, length, lanes), f32),
            pltpu.SemaphoreType.DMA((2, 2)),
            pltpu.SemaphoreType.DMA((steps,)),
            pltpu.SemaphoreType.DMA((2, steps)),
        ],
        4 * length * out_weight.size,
    )


def weight_sum(places, cot_pieces, gated_pieces, rows):
    count = len(gated_pieces)
    length, width = gated_pieces[0].shape
    outs = [jax.ShapeDtypeStruct((rows, width), dtype) for dtype in (bf16, f32)]
    return local_call(
        functools.partial(weight_kernel, count),
        places,
        [*cot_pieces, *gated_pieces],
        outs,
        [
            pltpu.VMEM((count, *cot_pieces[0].shape), bf16),
            pltpu.VMEM((count, length, width), bf16),
            *[pltpu.VMEM(o.shape, o.dtype) for o in outs],
            pltpu.SemaphoreType.DMA((2, count)),
            pltpu.SemaphoreType.DMA((2,)),
        ],
        4 * count * length * rows * width,
    )


def transpose_kernel(rows_in, out, rows, turned, sems):
    copy = pltpu.make_async_copy(rows_in, rows, sems.at[0])
    copy.start()
    copy.wait()
    for i in range(rows.shape[1] // turn):
        turned[pl.ds(i * turn, turn), :] = rows[:, pl.ds(i * turn, turn)].T
    copy = pltpu.make_async_copy(turned, out, sems.at[1])
    copy.start()
    copy.wait()


def transposed(rows):
    return pl.pallas_call(
        transpose_kernel,
        in_specs=[pl.BlockSpec(memory_space=pl.ANY)],
        out_specs=pl.BlockSpec(memory_space=pl.ANY),
        out_shape=jax.ShapeDtypeStruct(rows.shape[::-1], rows.dtype),
        scratch_shapes=[
            pltpu.VMEM(rows.shape, rows.dtype),
            pltpu.VMEM(rows.shape[::-1], rows.dtype),
            pltpu.SemaphoreType.DMA((2,)),
        ],
        compiler_params=pltpu.CompilerParams(vmem_limit_bytes=vmem_bytes),
        cost_estimate=estimate(0, [rows, rows]),
    )(rows)


def swap_pairs(value, axis, distance):
    count = lax.axis_size(axis)
    return lax.ppermute(value, axis, [(i, i ^ distance) for i in range(count)])


def after(value, *earlier):
    return lax.optimization_barrier((value, *earlier))[0]


def per_device(query_gate, key_gate, value_input, filter_taps, skip_gain, out_weight, cotangent):
    queries, key_rows, value_rows, cot = (
        query_gate[0],
        key_gate[0],
        value_input[0],
        cotangent[0],
    )
    length, channels = queries.shape
    taps = filter_taps.shape[1]
    n_seq, n_tp, n_dp = lax.axis_size("seq"), lax.axis_size("tp"), lax.axis_size("dp")
    subs = n_tp // n_dp
    me_tp, me_dp = lax.axis_index("tp"), lax.axis_index("dp")
    me_half, me_sub = me_tp // subs, me_tp % subs
    size = length + taps
    norm_factor = 1.0 / math.sqrt(length * n_seq * n_dp)

    whole = analysis_table(size, np.arange(size))
    scale = 2.0 / size
    tables = [split_table(whole), np.ascontiguousarray(split_table(whole.T))]
    rows16 = jax.ShapeDtypeStruct((length, channels), bf16)
    rows32 = jax.ShapeDtypeStruct((length, channels), f32)
    half16 = jax.ShapeDtypeStruct((length, channels // 2), bf16)
    unit = 2 * size * channels

    tail = (
        key_rows[length - taps :].astype(f32) * value_rows[length - taps :].astype(f32)
    ).astype(bf16)
    tail, cot = lax.optimization_barrier((tail, cot))
    prior = lax.ppermute(tail, "seq", [(i, i + 1) for i in range(n_seq - 1)])

    def tp_dp(half, sub, replica):
        return (half * subs + sub) * n_dp + replica

    places = [(h, c, d) for h in range(n_dp) for c in range(subs) for d in range(n_dp)]
    rounds = []
    for turn in range(2):
        route = [(tp_dp(h, c, d), tp_dp(d ^ turn, c, h)) for h, c, d in places]
        rounds.append(lax.ppermute(after(cot, prior) if turn else cot, ("tp", "dp"), route))
    square = n_seq == n_tp == 4 and subs == 2
    if square:

        def holder(s, block):
            return (s + block) % 2 * subs + s // 2

        crossed = {0: (1, 2), 1: (0, 3)}
        route = [
            (s * n_tp + t, s * n_tp + sum(crossed[s % 2]) - t)
            for s in range(n_seq)
            for t in crossed[s % 2]
        ]
        swapped = lax.ppermute(cot, ("seq", "tp"), route)
        moves_now = sum(
            jnp.logical_and(lax.axis_index("seq") % 2 == parity, me_tp == t)
            for parity in crossed
            for t in crossed[parity]
        )
        held = jnp.where(moves_now > 0, swapped, cot)
        route = []
        for s in range(n_seq):
            for t in range(n_tp):
                block = sum(crossed[s % 2]) - t if t in crossed[s % 2] else t
                route.append((s * n_tp + t, block * n_tp + holder(s, block)))
        moved = lax.ppermute(held, ("seq", "tp"), route)
    else:
        moved = cot

    same = (me_half == me_dp).astype(jnp.int32)
    subs_of = [me_sub, (me_sub + 1) % subs]
    place = jnp.stack([same, *subs_of]).astype(jnp.int32)
    dp_row = jnp.broadcast_to(me_dp.astype(f32), (1, channels))
    if square:
        order = [*range(0, n_seq, 2), *reversed(range(1, n_seq, 2))]
        ring = [(order[k], order[(k + 1) % n_seq]) for k in range(n_seq)]
        table = np.zeros((n_seq, n_tp, n_tp), np.int32)
        for k, s in enumerate(order):
            for r in range(n_seq):
                for t in range(n_tp):
                    table[s, t, t ^ holder(order[k - r], s)] = r
        sources = jnp.asarray(table)[lax.axis_index("seq"), me_tp]
        weight_place = jnp.concatenate([sources, me_dp[None].astype(jnp.int32)])
        prior, place, weight_place, dp_row = lax.optimization_barrier(
            (prior, place, weight_place, dp_row)
        )
    state, *gated = by_channel(
        functools.partial(state_kernel, scale),
        tables,
        [prior, key_rows, value_rows, filter_taps, skip_gain[None], queries],
        [[rows32], [half16, half16]],
        channels,
        unit * (4 * taps + 5 * length),
    )
    if square:
        halves = [[half] for half in gated]

        def ring_step(pieces):
            pieces.append(lax.ppermute(pieces[-1], "seq", ring))

        halves[0][0], moved = lax.optimization_barrier((halves[0][0], moved))
        ring_step(halves[0])
        halves[1][0], *rounds = lax.optimization_barrier((halves[1][0], *rounds))
    else:
        gated[0], *rounds = lax.optimization_barrier((gated[0], *rounds))

    route = [(tp_dp(h, c, d), tp_dp(h, (c + 1) % subs, d)) for h, c, d in places]
    theirs = [lax.ppermute(r, ("tp", "dp"), route) for r in rounds]
    firsts, seconds = zip(rounds, theirs)
    rows = n_tp * channels // (n_seq * n_dp)
    if square:
        moved = transposed(after(moved, *rounds))
        moved, place = lax.optimization_barrier((moved, place))
    other_sent, own_part = project(place, firsts, seconds, out_weight)
    other_part = swap_pairs(other_sent, "dp", 1)
    if square:
        halves[0][1], halves[1][0], _ = lax.optimization_barrier(
            (halves[0][1], halves[1][0], other_sent)
        )
        ring_step(halves[0])
        ring_step(halves[1])

    if square:
        sent_by = lambda value, flip: lax.ppermute(value, "tp", [(t, t ^ flip) for t in range(n_tp)])
        across = sent_by(moved, subs)
        cot_pieces = [moved, sent_by(moved, 1), across, sent_by(after(across, halves[0][2]), 1)]
        halves[0][2], halves[1][1], own_part = lax.optimization_barrier(
            (halves[0][2], halves[1][1], own_part)
        )
        ring_step(halves[0])
        ring_step(halves[1])
    else:
        full = lax.all_gather(cot, "tp", axis=1, tiled=True)
        cot_all = lax.all_to_all(full, "seq", 1, 0, tiled=True)
        gated_all = [lax.all_gather(half, "seq", axis=0, tiled=True) for half in gated]

        def part(replica, piece):
            block = lax.dynamic_slice_in_dim(cot_all, replica * rows, rows, axis=1)
            return lax.dot_general(
                block, piece, (((0,), (0,)), ((), ())), preferred_element_type=f32
            )

        def weight_one(piece):
            return part(me_dp, piece), swap_pairs(part(1 - me_dp, piece).astype(bf16), "dp", 1)

    share = taps // n_dp
    grad_query, signal, head, sent_lag, own_lag = by_channel(
        lag_kernel,
        tables,
        [own_part, other_part, state, queries, prior, key_rows, value_rows, dp_row],
        [
            [rows16],
            [rows16],
            [jax.ShapeDtypeStruct((taps, channels), bf16)],
            [jax.ShapeDtypeStruct((share, channels), bf16)],
            [jax.ShapeDtypeStruct((share, channels), f32)],
        ],
        channels,
        unit * (2 * taps + 4 * length + 3 * taps),
    )
    later = lax.ppermute(head, "seq", [(i + 1, i) for i in range(n_seq - 1)])

    def run_back(later):
        return by_channel(
            functools.partial(back_kernel, scale),
            tables,
            [signal, later, filter_taps, skip_gain[None], key_rows, value_rows],
            [[rows16], [rows16]],
            channels,
            256 * unit * (4 * taps + 5 * length),
        )

    received = swap_pairs(sent_lag, "dp", 1)
    if square:
        weight_place, halves[1][2], signal = lax.optimization_barrier((weight_place, halves[1][2], signal))
        ring_step(halves[1])
        first_sent, first_own = weight_sum(weight_place, cot_pieces, halves[0], rows)
        first_received = swap_pairs(first_sent, "dp", 1)
        received, first_own = lax.optimization_barrier((received, first_own))
    lag_sum = own_lag + received.astype(f32)
    distance = 1
    while distance < n_seq:
        rounded = lag_sum.astype(bf16)
        received = swap_pairs(rounded, "seq", distance)
        if square and distance == 1:
            second_sent, second_own = weight_sum(weight_place, cot_pieces, halves[1], rows)
            second_received = swap_pairs(second_sent, "dp", 1)
            received, second_own = lax.optimization_barrier((received, second_own))
        lag_sum = rounded.astype(f32) + received.astype(f32)
        distance *= 2
    if square:
        first_received, lag_sum = lax.optimization_barrier((first_received, lag_sum))
    mine = lag_sum.astype(bf16)
    theirs = swap_pairs(mine, "dp", 1)
    grad_key, grad_value = run_back(after(later, second_own) if square else later)
    first = me_dp == 0
    lag_sum = jnp.concatenate([jnp.where(first, mine, theirs), jnp.where(first, theirs, mine)], axis=0)
    grad_filter = lag_sum.astype(f32).T * (norm_factor * scale)

    if square:
        parts = [(first_own, first_received), (second_own, second_received)]
    else:
        parts = [weight_one(half) for half in gated_all]
    grad_weight = jnp.concatenate(
        [(mine + theirs.astype(f32)) * norm_factor for mine, theirs in parts], axis=1
    )
    return (
        grad_query[None],
        grad_key[None],
        grad_value[None],
        grad_filter,
        grad_filter[:, 0],
        grad_weight,
    )


def solution(mesh):
    tokens = P("dp", "seq", "tp")
    return jax.shard_map(
        per_device,
        mesh=mesh,
        in_specs=(tokens, tokens, tokens, P("tp", None), P("tp"), P("tp", "dp"), tokens),
        out_specs=(tokens, tokens, tokens, P("tp", None), P("tp"), P(("seq", "dp"), "tp")),
        check_vma=False,
    )
```

```python
import functools
import math

import jax
import jax.numpy as jnp
import ml_dtypes
import numpy as np
from jax import lax
from jax.experimental import pallas as pl
from jax.experimental.pallas import tpu as pltpu
from jax.sharding import PartitionSpec as P

f32, bf16 = jnp.float32, jnp.bfloat16
lanes = 512
turn = 256
vmem_bytes = 20 * 1024 * 1024


def analysis_table(size, positions):
    half = size // 2
    omega = 2.0 * np.pi * (np.arange(half) + 0.5) / size
    angle = omega[:, None] * np.asarray(positions)[None, :]
    return np.concatenate([np.cos(angle), -np.sin(angle)], axis=0)


def split_table(table):
    high = table.astype(ml_dtypes.bfloat16)
    low = (table - high.astype(np.float64)).astype(ml_dtypes.bfloat16)
    return np.concatenate([high, low])


def split_rows(rows):
    high = rows.astype(bf16)
    return high, (rows - high.astype(f32)).astype(bf16)


def dot(left, right):
    return jnp.dot(left, right, preferred_element_type=f32)


def dot_nt(left, right):
    return lax.dot_general(left, right, (((1,), (1,)), ((), ())), preferred_element_type=f32)


def add_halves(both):
    half = both.shape[0] // 2
    return both[:half] + both[half:]


def forward_transform(table, rows, start):
    return add_halves(dot(table[:, pl.ds(start, rows.shape[0])], rows))


def inverse_transform(table, spectrum, start, count):
    high, low = split_rows(spectrum)
    upper = table[pl.ds(start, count)]
    lower = table[pl.ds(table.shape[0] // 2 + start, count)]
    return dot(upper, high) + dot(upper, low) + dot(lower, high)


def spectrum_product(left, right, conjugate_right):
    half = left.shape[0] // 2
    left_re, left_im = left[:half], left[half:]
    right_re, right_im = right[:half], right[half:]
    if conjugate_right:
        right_im = -right_im
    return jnp.concatenate(
        [left_re * right_re - left_im * right_im, left_re * right_im + left_im * right_re], axis=0
    )


def mixed_spectrum(table, prior_ref, key_ref, value_ref):
    mixed = (key_ref[...].astype(f32) * value_ref[...].astype(f32)).astype(bf16)
    prior = prior_ref[...]
    return forward_transform(table, prior, 0) + forward_transform(table, mixed, prior.shape[0])


def filter_spectrum(scale, table, taps_ref, skip_ref):
    taps = taps_ref.shape[1]
    filt = add_halves(dot_nt(table[:, :taps], taps_ref[...]))
    half = filt.shape[0] // 2
    return jnp.concatenate([(filt[:half] + skip_ref[...]) * scale, filt[half:] * scale], axis=0)


def state_kernel(
    scale, table, synth, prior_ref, key_ref, value_ref, taps_ref, skip_ref, query_ref, state_ref, gated_ref
):
    spec = mixed_spectrum(table, prior_ref, key_ref, value_ref)
    product = spectrum_product(spec, filter_spectrum(scale, table, taps_ref, skip_ref), False)
    state = inverse_transform(synth, product, prior_ref.shape[0], query_ref.shape[0])
    state_ref[...] = state
    gated_ref[...] = (query_ref[...].astype(f32) * state).astype(bf16)


def project_kernel(
    place_ref, first_mine, second_mine, first_theirs, second_theirs, weight, other, own, pieces, blocks, others, owns, piece_sem, block_sem, out_sem
):
    steps, _, total_width = blocks.shape
    length, width = first_mine.shape

    def piece_copy(n, sub, source):
        rows = pl.ds(n * length, length)
        columns = pl.ds(pl.multiple_of(place_ref[1 + sub] * width, width), width)
        return pltpu.make_async_copy(source, pieces.at[rows, columns], piece_sem.at[n, sub])

    def block_copy(i):
        return pltpu.make_async_copy(weight.at[pl.ds(i * lanes, lanes)], blocks.at[i], block_sem.at[i])

    def out_copies(i):
        columns = pl.ds(pl.multiple_of(i * lanes, lanes), lanes)
        return [
            pltpu.make_async_copy(others.at[i], other.at[:, columns], out_sem.at[0, i]),
            pltpu.make_async_copy(owns.at[i], own.at[:, columns], out_sem.at[1, i]),
        ]

    for i in range(steps):
        block_copy(i).start()

    def fetch(own_first):
        for sub, (first, second) in enumerate([(first_mine, second_mine), (first_theirs, second_theirs)]):
            piece_copy(0, sub, second if own_first else first).start()
            piece_copy(1, sub, first if own_first else second).start()

    pl.when(place_ref[0] != 0)(lambda: fetch(True))
    pl.when(place_ref[0] == 0)(lambda: fetch(False))
    for n in range(2):
        for sub in range(2):
            piece_copy(n, sub, first_mine).wait()

    @pl.loop(0, steps)
    def _(i):
        block_copy(i).wait()
        total = dot_nt(pieces[...], blocks[i])
        others[i] = total[:length].astype(bf16)
        owns[i] = total[length:]
        for copy in out_copies(i):
            copy.start()

    for i in range(steps):
        for copy in out_copies(i):
            copy.wait()


def weight_kernel(count, place_ref, *refs):
    cot_in, gated_in = refs[:count], refs[count : 2 * count]
    other, own, cots, gateds, others, owns, in_sem, out_sem = refs[2 * count :]
    length = gateds.shape[1]
    rows = other.shape[0]
    block = min(rows, lanes)
    copies = [pltpu.make_async_copy(cot_in[n], cots.at[n], in_sem.at[0, n]) for n in range(count)]
    copies += [pltpu.make_async_copy(gated_in[n], gateds.at[n], in_sem.at[1, n]) for n in range(count)]
    for copy in copies:
        copy.start()
    for copy in copies:
        copy.wait()
    outs = [
        pltpu.make_async_copy(others, other, out_sem.at[0]),
        pltpu.make_async_copy(owns, own, out_sem.at[1]),
    ]

    def fill(replica, target):
        @pl.loop(0, rows // block)
        def _(i):
            start = pl.multiple_of(replica * rows + i * block, block)
            total = None
            for n in range(count):
                part = dot(cots[n, pl.ds(start, block), :], gateds[place_ref[n]])
                total = part if total is None else total + part
            target[pl.ds(pl.multiple_of(i * block, block), block), :] = total.astype(target.dtype)

    me = place_ref[count]
    fill(1 - me, others)
    outs[0].start()
    fill(me, owns)
    outs[1].start()
    for copy in outs:
        copy.wait()


def lag_kernel(
    table,
    synth,
    own_ref,
    other_ref,
    state_ref,
    query_ref,
    prior_ref,
    key_ref,
    value_ref,
    place_ref,
    grad_ref,
    signal_ref,
    head_ref,
    sent_lag_ref,
    own_lag_ref,
):
    length, taps, share = signal_ref.shape[0], prior_ref.shape[0], own_lag_ref.shape[0]
    grad_gated = own_ref[...] + other_ref[...].astype(f32)
    grad_ref[...] = (grad_gated * state_ref[...]).astype(bf16)
    signal = (grad_gated * query_ref[...].astype(f32)).astype(bf16)
    signal_ref[...] = signal
    head_ref[...] = signal[:taps]
    spec = mixed_spectrum(table, prior_ref, key_ref, value_ref)
    product = spectrum_product(forward_transform(table, signal, 0), spec, True)
    lags = -inverse_transform(synth, product, length, taps)
    first = place_ref[...] == 0.0
    own_lag_ref[...] = jnp.where(first, lags[:share], lags[share:])
    sent_lag_ref[...] = jnp.where(first, lags[share:], lags[:share]).astype(bf16)


def back_kernel(
    scale, table, synth, signal_ref, later_ref, taps_ref, skip_ref, key_ref, value_ref, grad_key_ref, grad_value_ref
):
    length = key_ref.shape[0]
    spec = forward_transform(table, signal_ref[...], 0) + forward_transform(table, later_ref[...], length)
    product = spectrum_product(spec, filter_spectrum(scale, table, taps_ref, skip_ref), True)
    back = inverse_transform(synth, product, 0, length)
    grad_key_ref[...] = (back * value_ref[...].astype(f32)).astype(bf16)
    grad_value_ref[...] = (back * key_ref[...].astype(f32)).astype(bf16)


def estimate(flops, arrays):
    moved = sum(a.size * jnp.dtype(a.dtype).itemsize for a in arrays)
    return pl.CostEstimate(flops=flops // 64, bytes_accessed=moved // 64, transcendentals=0)


def by_channel(body, tables, args, outs, channels, flops):
    steps = channels // lanes
    flat_outs = [o for group in outs for o in group]
    n_tables, n_args, n_outs = len(tables), len(args), len(outs)

    def part(ref, i, count):
        start = i * lanes
        if ref.shape[1] == count * lanes:
            return ref.at[:, pl.ds(start, lanes)]
        return ref.at[pl.ds(start, lanes), :]

    def kernel(*refs):
        refs = list(refs)
        take = lambda count: [refs.pop(0) for _ in range(count)]
        table_in, arg_in, outs_to = take(n_tables), take(n_args), take(len(flat_outs))
        table_held, arg_held, out_held = take(n_tables), take(n_args), take(n_outs)
        table_sem, arg_sem, out_sem = refs
        groups = [[outs_to.pop(0) for _ in group] for group in outs]

        def table_copy(k):
            return pltpu.make_async_copy(table_in[k], table_held[k], table_sem.at[k])

        def arg_copy(k):
            return pltpu.make_async_copy(arg_in[k], arg_held[k], arg_sem.at[k])

        def out_copy(k, n, i):
            per = steps // len(groups[k])
            place = part(groups[k][n], i - n * per, per)
            return pltpu.make_async_copy(out_held[k].at[i], place, out_sem.at[k, i])

        for k in range(n_tables):
            table_copy(k).start()
        for k in range(n_args):
            arg_copy(k).start()
        for k in range(n_tables):
            table_copy(k).wait()
        for k in range(n_args):
            arg_copy(k).wait()

        for i in range(steps):
            body(*table_held, *[part(ref, i, steps) for ref in arg_held], *[held.at[i] for held in out_held])
            for k in range(n_outs):
                out_copy(k, i * len(groups[k]) // steps, i).start()

        for i in range(steps):
            for k in range(n_outs):
                out_copy(k, i * len(groups[k]) // steps, i).wait()

    return pl.pallas_call(
        kernel,
        in_specs=[pl.BlockSpec(memory_space=pl.ANY)] * (n_tables + n_args),
        out_specs=[pl.BlockSpec(memory_space=pl.ANY)] * len(flat_outs),
        out_shape=flat_outs,
        scratch_shapes=[
            *[pltpu.VMEM(t.shape, bf16) for t in tables],
            *[pltpu.VMEM(a.shape, a.dtype) for a in args],
            *[pltpu.VMEM((steps, group[0].shape[0], lanes), group[0].dtype) for group in outs],
            pltpu.SemaphoreType.DMA((n_tables,)),
            pltpu.SemaphoreType.DMA((n_args,)),
            pltpu.SemaphoreType.DMA((n_outs, steps)),
        ],
        compiler_params=pltpu.CompilerParams(vmem_limit_bytes=vmem_bytes),
        cost_estimate=estimate(flops, [*args, *flat_outs]),
    )(*[jnp.asarray(t) for t in tables], *args)


def local_call(kernel, places, args, outs, scratch, flops):
    return pl.pallas_call(
        kernel,
        in_specs=[pl.BlockSpec(memory_space=pltpu.SMEM)] + [pl.BlockSpec(memory_space=pl.ANY)] * len(args),
        out_specs=[pl.BlockSpec(memory_space=pl.ANY)] * len(outs),
        out_shape=outs,
        scratch_shapes=scratch,
        compiler_params=pltpu.CompilerParams(vmem_limit_bytes=vmem_bytes),
        cost_estimate=estimate(flops, [*args, *outs]),
    )(places, *args)


def project(places, firsts, seconds, out_weight):
    length, width = firsts[0].shape
    channels, total_width = out_weight.shape
    steps = channels // lanes
    return local_call(
        project_kernel,
        places,
        [firsts[0], seconds[0], firsts[1], seconds[1], out_weight],
        [jax.ShapeDtypeStruct((length, channels), dtype) for dtype in (bf16, f32)],
        [
            pltpu.VMEM((2 * length, total_width), bf16),
            pltpu.VMEM((steps, lanes, total_width), bf16),
            pltpu.VMEM((steps, length, lanes), bf16),
            pltpu.VMEM((steps, length, lanes), f32),
            pltpu.SemaphoreType.DMA((2, 2)),
            pltpu.SemaphoreType.DMA((steps,)),
            pltpu.SemaphoreType.DMA((2, steps)),
        ],
        4 * length * out_weight.size,
    )


def weight_sum(places, cot_pieces, gated_pieces, rows):
    count = len(gated_pieces)
    length, width = gated_pieces[0].shape
    outs = [jax.ShapeDtypeStruct((rows, width), dtype) for dtype in (bf16, f32)]
    return local_call(
        functools.partial(weight_kernel, count),
        places,
        [*cot_pieces, *gated_pieces],
        outs,
        [
            pltpu.VMEM((count, *cot_pieces[0].shape), bf16),
            pltpu.VMEM((count, length, width), bf16),
            *[pltpu.VMEM(o.shape, o.dtype) for o in outs],
            pltpu.SemaphoreType.DMA((2, count)),
            pltpu.SemaphoreType.DMA((2,)),
        ],
        4 * count * length * rows * width,
    )


def transpose_kernel(rows_in, out, rows, turned, sems):
    copy = pltpu.make_async_copy(rows_in, rows, sems.at[0])
    copy.start()
    copy.wait()
    for i in range(rows.shape[1] // turn):
        turned[pl.ds(i * turn, turn), :] = rows[:, pl.ds(i * turn, turn)].T
    copy = pltpu.make_async_copy(turned, out, sems.at[1])
    copy.start()
    copy.wait()


def transposed(rows):
    return pl.pallas_call(
        transpose_kernel,
        in_specs=[pl.BlockSpec(memory_space=pl.ANY)],
        out_specs=pl.BlockSpec(memory_space=pl.ANY),
        out_shape=jax.ShapeDtypeStruct(rows.shape[::-1], rows.dtype),
        scratch_shapes=[
            pltpu.VMEM(rows.shape, rows.dtype),
            pltpu.VMEM(rows.shape[::-1], rows.dtype),
            pltpu.SemaphoreType.DMA((2,)),
        ],
        compiler_params=pltpu.CompilerParams(vmem_limit_bytes=vmem_bytes),
        cost_estimate=estimate(0, [rows, rows]),
    )(rows)


def swap_pairs(value, axis, distance):
    count = lax.axis_size(axis)
    return lax.ppermute(value, axis, [(i, i ^ distance) for i in range(count)])


def after(value, *earlier):
    return lax.optimization_barrier((value, *earlier))[0]


def per_device(query_gate, key_gate, value_input, filter_taps, skip_gain, out_weight, cotangent):
    queries, key_rows, value_rows, cot = (
        query_gate[0],
        key_gate[0],
        value_input[0],
        cotangent[0],
    )
    length, channels = queries.shape
    taps = filter_taps.shape[1]
    n_seq, n_tp, n_dp = lax.axis_size("seq"), lax.axis_size("tp"), lax.axis_size("dp")
    subs = n_tp // n_dp
    me_tp, me_dp = lax.axis_index("tp"), lax.axis_index("dp")
    me_half, me_sub = me_tp // subs, me_tp % subs
    size = length + taps
    norm_factor = 1.0 / math.sqrt(length * n_seq * n_dp)

    whole = analysis_table(size, np.arange(size))
    scale = 2.0 / size
    tables = [split_table(whole), np.ascontiguousarray(split_table(whole.T))]
    rows16 = jax.ShapeDtypeStruct((length, channels), bf16)
    rows32 = jax.ShapeDtypeStruct((length, channels), f32)
    half16 = jax.ShapeDtypeStruct((length, channels // 2), bf16)
    unit = 2 * size * channels

    tail = (
        key_rows[length - taps :].astype(f32) * value_rows[length - taps :].astype(f32)
    ).astype(bf16)
    tail, cot = lax.optimization_barrier((tail, cot))
    prior = lax.ppermute(tail, "seq", [(i, i + 1) for i in range(n_seq - 1)])

    def tp_dp(half, sub, replica):
        return (half * subs + sub) * n_dp + replica

    places = [(h, c, d) for h in range(n_dp) for c in range(subs) for d in range(n_dp)]
    rounds = []
    for turn in range(2):
        route = [(tp_dp(h, c, d), tp_dp(d ^ turn, c, h)) for h, c, d in places]
        rounds.append(lax.ppermute(after(cot, prior) if turn else cot, ("tp", "dp"), route))
    square = n_seq == n_tp == 4 and subs == 2
    if square:

        def holder(s, block):
            return (s + block) % 2 * subs + s // 2

        crossed = {0: (1, 2), 1: (0, 3)}
        route = [
            (s * n_tp + t, s * n_tp + sum(crossed[s % 2]) - t)
            for s in range(n_seq)
            for t in crossed[s % 2]
        ]
        swapped = lax.ppermute(cot, ("seq", "tp"), route)
        moves_now = sum(
            jnp.logical_and(lax.axis_index("seq") % 2 == parity, me_tp == t)
            for parity in crossed
            for t in crossed[parity]
        )
        held = jnp.where(moves_now > 0, swapped, cot)
        route = []
        for s in range(n_seq):
            for t in range(n_tp):
                block = sum(crossed[s % 2]) - t if t in crossed[s % 2] else t
                route.append((s * n_tp + t, block * n_tp + holder(s, block)))
        moved = lax.ppermute(held, ("seq", "tp"), route)
    else:
        moved = cot

    same = (me_half == me_dp).astype(jnp.int32)
    subs_of = [me_sub, (me_sub + 1) % subs]
    place = jnp.stack([same, *subs_of]).astype(jnp.int32)
    dp_row = jnp.broadcast_to(me_dp.astype(f32), (1, channels))
    if square:
        order = [*range(0, n_seq, 2), *reversed(range(1, n_seq, 2))]
        ring = [(order[k], order[(k + 1) % n_seq]) for k in range(n_seq)]
        table = np.zeros((n_seq, n_tp, n_tp), np.int32)
        for k, s in enumerate(order):
            for r in range(n_seq):
                for t in range(n_tp):
                    table[s, t, t ^ holder(order[k - r], s)] = r
        sources = jnp.asarray(table)[lax.axis_index("seq"), me_tp]
        weight_place = jnp.concatenate([sources, me_dp[None].astype(jnp.int32)])
        prior, place, weight_place, dp_row = lax.optimization_barrier(
            (prior, place, weight_place, dp_row)
        )
    state, *gated = by_channel(
        functools.partial(state_kernel, scale),
        tables,
        [prior, key_rows, value_rows, filter_taps, skip_gain[None], queries],
        [[rows32], [half16, half16]],
        channels,
        unit * (4 * taps + 5 * length),
    )
    if square:
        halves = [[half] for half in gated]

        def ring_step(pieces):
            pieces.append(lax.ppermute(pieces[-1], "seq", ring))

        halves[0][0], moved = lax.optimization_barrier((halves[0][0], moved))
        ring_step(halves[0])
        halves[1][0], *rounds = lax.optimization_barrier((halves[1][0], *rounds))
    else:
        gated[0], *rounds = lax.optimization_barrier((gated[0], *rounds))

    route = [(tp_dp(h, c, d), tp_dp(h, (c + 1) % subs, d)) for h, c, d in places]
    theirs = [lax.ppermute(r, ("tp", "dp"), route) for r in rounds]
    firsts, seconds = zip(rounds, theirs)
    rows = n_tp * channels // (n_seq * n_dp)
    if square:
        moved = transposed(after(moved, *rounds))
        moved, place = lax.optimization_barrier((moved, place))
    other_sent, own_part = project(place, firsts, seconds, out_weight)
    other_part = swap_pairs(other_sent, "dp", 1)
    if square:
        halves[0][1], halves[1][0], _ = lax.optimization_barrier(
            (halves[0][1], halves[1][0], other_sent)
        )
        ring_step(halves[0])
        ring_step(halves[1])

    if square:
        sent_by = lambda value, flip: lax.ppermute(value, "tp", [(t, t ^ flip) for t in range(n_tp)])
        across = sent_by(moved, subs)
        cot_pieces = [moved, sent_by(moved, 1), across, sent_by(after(across, halves[0][2]), 1)]
        halves[0][2], halves[1][1], own_part = lax.optimization_barrier(
            (halves[0][2], halves[1][1], own_part)
        )
        ring_step(halves[0])
        ring_step(halves[1])
    else:
        full = lax.all_gather(cot, "tp", axis=1, tiled=True)
        cot_all = lax.all_to_all(full, "seq", 1, 0, tiled=True)
        gated_all = [lax.all_gather(half, "seq", axis=0, tiled=True) for half in gated]

        def part(replica, piece):
            block = lax.dynamic_slice_in_dim(cot_all, replica * rows, rows, axis=1)
            return lax.dot_general(
                block, piece, (((0,), (0,)), ((), ())), preferred_element_type=f32
            )

        def weight_one(piece):
            return part(me_dp, piece), swap_pairs(part(1 - me_dp, piece).astype(bf16), "dp", 1)

    share = taps // n_dp
    grad_query, signal, head, sent_lag, own_lag = by_channel(
        lag_kernel,
        tables,
        [own_part, other_part, state, queries, prior, key_rows, value_rows, dp_row],
        [
            [rows16],
            [rows16],
            [jax.ShapeDtypeStruct((taps, channels), bf16)],
            [jax.ShapeDtypeStruct((share, channels), bf16)],
            [jax.ShapeDtypeStruct((share, channels), f32)],
        ],
        channels,
        unit * (2 * taps + 4 * length + 3 * taps),
    )
    later = lax.ppermute(head, "seq", [(i + 1, i) for i in range(n_seq - 1)])

    def run_back(later):
        return by_channel(
            functools.partial(back_kernel, scale),
            tables,
            [signal, later, filter_taps, skip_gain[None], key_rows, value_rows],
            [[rows16], [rows16]],
            channels,
            256 * unit * (4 * taps + 5 * length),
        )

    received = swap_pairs(sent_lag, "dp", 1)
    if square:
        weight_place, halves[1][2], signal = lax.optimization_barrier((weight_place, halves[1][2], signal))
        ring_step(halves[1])
        first_sent, first_own = weight_sum(weight_place, cot_pieces, halves[0], rows)
        first_received = swap_pairs(first_sent, "dp", 1)
        received, first_own = lax.optimization_barrier((received, first_own))
    lag_sum = own_lag + received.astype(f32)
    distance = 1
    while distance < n_seq:
        rounded = lag_sum.astype(bf16)
        received = swap_pairs(rounded, "seq", distance)
        if square and distance == 1:
            second_sent, second_own = weight_sum(weight_place, cot_pieces, halves[1], rows)
            second_received = swap_pairs(second_sent, "dp", 1)
            received, second_own = lax.optimization_barrier((received, second_own))
        lag_sum = rounded.astype(f32) + received.astype(f32)
        distance *= 2
    if square:
        first_received, lag_sum = lax.optimization_barrier((first_received, lag_sum))
    mine = lag_sum.astype(bf16)
    theirs = swap_pairs(mine, "dp", 1)
    grad_key, grad_value = run_back(after(later, second_own) if square else later)
    first = me_dp == 0
    lag_sum = jnp.concatenate([jnp.where(first, mine, theirs), jnp.where(first, theirs, mine)], axis=0)
    grad_filter = lag_sum.astype(f32).T * (norm_factor * scale)

    if square:
        parts = [(first_own, first_received), (second_own, second_received)]
    else:
        parts = [weight_one(half) for half in gated_all]
    grad_weight = jnp.concatenate(
        [(mine + theirs.astype(f32)) * norm_factor for mine, theirs in parts], axis=1
    )
    return (
        grad_query[None],
        grad_key[None],
        grad_value[None],
        grad_filter,
        grad_filter[:, 0],
        grad_weight,
    )


def solution(mesh):
    tokens = P("dp", "seq", "tp")
    return jax.shard_map(
        per_device,
        mesh=mesh,
        in_specs=(tokens, tokens, tokens, P("tp", None), P("tp"), P("tp", "dp"), tokens),
        out_specs=(tokens, tokens, tokens, P("tp", None), P("tp"), P(("seq", "dp"), "tp")),
        check_vma=False,
    )
```

```python
import functools
import math

import jax
import jax.numpy as jnp
import ml_dtypes
import numpy as np
from jax import lax
from jax.experimental import pallas as pl
from jax.experimental.pallas import tpu as pltpu
from jax.sharding import PartitionSpec as P

f32, bf16 = jnp.float32, jnp.bfloat16
lanes = 512
turn = 256
vmem_bytes = 46 * 1024 * 1024


def analysis_table(size, positions):
    half = size // 2
    omega = 2.0 * np.pi * (np.arange(half) + 0.5) / size
    angle = omega[:, None] * np.asarray(positions)[None, :]
    return np.concatenate([np.cos(angle), -np.sin(angle)], axis=0)


def split_table(table):
    high = table.astype(ml_dtypes.bfloat16)
    low = (table - high.astype(np.float64)).astype(ml_dtypes.bfloat16)
    return np.concatenate([high, low])


def split_rows(rows):
    high = rows.astype(bf16)
    return high, (rows - high.astype(f32)).astype(bf16)


def dot(left, right):
    return jnp.dot(left, right, preferred_element_type=f32)


def dot_nt(left, right):
    return lax.dot_general(left, right, (((1,), (1,)), ((), ())), preferred_element_type=f32)


def add_halves(both):
    half = both.shape[0] // 2
    return both[:half] + both[half:]


def forward_transform(table, rows, start):
    return add_halves(dot(table[:, pl.ds(start, rows.shape[0])], rows))


def inverse_transform(table, spectrum, start, count):
    high, low = split_rows(spectrum)
    upper = table[pl.ds(start, count)]
    lower = table[pl.ds(table.shape[0] // 2 + start, count)]
    return dot(upper, high) + dot(upper, low) + dot(lower, high)


def spectrum_product(left, right, conjugate_right):
    half = left.shape[0] // 2
    left_re, left_im = left[:half], left[half:]
    right_re, right_im = right[:half], right[half:]
    if conjugate_right:
        right_im = -right_im
    return jnp.concatenate(
        [left_re * right_re - left_im * right_im, left_re * right_im + left_im * right_re], axis=0
    )


def mixed_spectrum(table, prior_ref, key_ref, value_ref):
    mixed = (key_ref[...].astype(f32) * value_ref[...].astype(f32)).astype(bf16)
    prior = prior_ref[...]
    return forward_transform(table, prior, 0) + forward_transform(table, mixed, prior.shape[0])


def filter_spectrum(scale, table, taps_ref, skip_ref):
    taps = taps_ref.shape[1]
    filt = add_halves(dot_nt(table[:, :taps], taps_ref[...]))
    half = filt.shape[0] // 2
    return jnp.concatenate([(filt[:half] + skip_ref[...]) * scale, filt[half:] * scale], axis=0)


def state_kernel(
    scale, table, synth, prior_ref, key_ref, value_ref, taps_ref, skip_ref, query_ref, state_ref, gated_ref
):
    spec = mixed_spectrum(table, prior_ref, key_ref, value_ref)
    product = spectrum_product(spec, filter_spectrum(scale, table, taps_ref, skip_ref), False)
    state = inverse_transform(synth, product, prior_ref.shape[0], query_ref.shape[0])
    state_ref[...] = state
    gated_ref[...] = (query_ref[...].astype(f32) * state).astype(bf16)


def project_kernel(
    place_ref, first_mine, second_mine, first_theirs, second_theirs, weight, other, own, pieces, blocks, others, owns, piece_sem, block_sem, out_sem
):
    steps, _, total_width = blocks.shape
    length, width = first_mine.shape

    def piece_copy(n, sub, source):
        rows = pl.ds(n * length, length)
        columns = pl.ds(pl.multiple_of(place_ref[1 + sub] * width, width), width)
        return pltpu.make_async_copy(source, pieces.at[rows, columns], piece_sem.at[n, sub])

    def block_copy(i):
        return pltpu.make_async_copy(weight.at[pl.ds(i * lanes, lanes)], blocks.at[i], block_sem.at[i])

    def out_copies(i):
        columns = pl.ds(pl.multiple_of(i * lanes, lanes), lanes)
        return [
            pltpu.make_async_copy(others.at[i], other.at[:, columns], out_sem.at[0, i]),
            pltpu.make_async_copy(owns.at[i], own.at[:, columns], out_sem.at[1, i]),
        ]

    for i in range(steps):
        block_copy(i).start()

    def fetch(own_first):
        for sub, (first, second) in enumerate([(first_mine, second_mine), (first_theirs, second_theirs)]):
            piece_copy(0, sub, second if own_first else first).start()
            piece_copy(1, sub, first if own_first else second).start()

    pl.when(place_ref[0] != 0)(lambda: fetch(True))
    pl.when(place_ref[0] == 0)(lambda: fetch(False))
    for n in range(2):
        for sub in range(2):
            piece_copy(n, sub, first_mine).wait()

    @pl.loop(0, steps)
    def _(i):
        block_copy(i).wait()
        total = dot_nt(pieces[...], blocks[i])
        others[i] = total[:length].astype(bf16)
        owns[i] = total[length:]
        for copy in out_copies(i):
            copy.start()

    for i in range(steps):
        for copy in out_copies(i):
            copy.wait()


def weight_kernel(count, place_ref, *refs):
    cot_in, gated_in = refs[:count], refs[count : 2 * count]
    other, own, cots, gateds, others, owns, in_sem, out_sem = refs[2 * count :]
    length = gateds.shape[1]
    rows = other.shape[0]
    block = min(rows, lanes)
    copies = [pltpu.make_async_copy(cot_in[n], cots.at[n], in_sem.at[0, n]) for n in range(count)]
    copies += [pltpu.make_async_copy(gated_in[n], gateds.at[n], in_sem.at[1, n]) for n in range(count)]
    for copy in copies:
        copy.start()
    for copy in copies:
        copy.wait()
    outs = [
        pltpu.make_async_copy(others, other, out_sem.at[0]),
        pltpu.make_async_copy(owns, own, out_sem.at[1]),
    ]

    def fill(replica, target):
        @pl.loop(0, rows // block)
        def _(i):
            start = pl.multiple_of(replica * rows + i * block, block)
            total = None
            for n in range(count):
                part = dot(cots[n, pl.ds(start, block), :], gateds[place_ref[n]])
                total = part if total is None else total + part
            target[pl.ds(pl.multiple_of(i * block, block), block), :] = total.astype(target.dtype)

    me = place_ref[count]
    fill(1 - me, others)
    outs[0].start()
    fill(me, owns)
    outs[1].start()
    for copy in outs:
        copy.wait()


def lag_kernel(
    table,
    synth,
    own_ref,
    other_ref,
    state_ref,
    query_ref,
    prior_ref,
    key_ref,
    value_ref,
    place_ref,
    grad_ref,
    signal_ref,
    head_ref,
    sent_lag_ref,
    own_lag_ref,
):
    length, taps, share = signal_ref.shape[0], prior_ref.shape[0], own_lag_ref.shape[0]
    grad_gated = own_ref[...] + other_ref[...].astype(f32)
    grad_ref[...] = (grad_gated * state_ref[...]).astype(bf16)
    signal = (grad_gated * query_ref[...].astype(f32)).astype(bf16)
    signal_ref[...] = signal
    head_ref[...] = signal[:taps]
    spec = mixed_spectrum(table, prior_ref, key_ref, value_ref)
    product = spectrum_product(forward_transform(table, signal, 0), spec, True)
    lags = -inverse_transform(synth, product, length, taps)
    first = place_ref[...] == 0.0
    own_lag_ref[...] = jnp.where(first, lags[:share], lags[share:])
    sent_lag_ref[...] = jnp.where(first, lags[share:], lags[:share]).astype(bf16)


def back_kernel(
    scale, table, synth, signal_ref, later_ref, taps_ref, skip_ref, key_ref, value_ref, grad_key_ref, grad_value_ref
):
    length = key_ref.shape[0]
    spec = forward_transform(table, signal_ref[...], 0) + forward_transform(table, later_ref[...], length)
    product = spectrum_product(spec, filter_spectrum(scale, table, taps_ref, skip_ref), True)
    back = inverse_transform(synth, product, 0, length)
    grad_key_ref[...] = (back * value_ref[...].astype(f32)).astype(bf16)
    grad_value_ref[...] = (back * key_ref[...].astype(f32)).astype(bf16)


def estimate(flops, arrays):
    moved = sum(a.size * jnp.dtype(a.dtype).itemsize for a in arrays)
    return pl.CostEstimate(flops=flops // 64, bytes_accessed=moved // 64, transcendentals=0)


def by_channel(body, tables, args, outs, channels, flops):
    steps = channels // lanes
    flat_outs = [o for group in outs for o in group]
    n_tables, n_args, n_outs = len(tables), len(args), len(outs)

    def part(ref, i, count):
        start = i * lanes
        if ref.shape[1] == count * lanes:
            return ref.at[:, pl.ds(start, lanes)]
        return ref.at[pl.ds(start, lanes), :]

    def kernel(*refs):
        refs = list(refs)
        take = lambda count: [refs.pop(0) for _ in range(count)]
        table_in, arg_in, outs_to = take(n_tables), take(n_args), take(len(flat_outs))
        table_held, arg_held, out_held = take(n_tables), take(n_args), take(n_outs)
        table_sem, arg_sem, out_sem = refs
        groups = [[outs_to.pop(0) for _ in group] for group in outs]

        def table_copy(k):
            return pltpu.make_async_copy(table_in[k], table_held[k], table_sem.at[k])

        def arg_copy(k):
            return pltpu.make_async_copy(arg_in[k], arg_held[k], arg_sem.at[k])

        def out_copy(k, n, i):
            per = steps // len(groups[k])
            place = part(groups[k][n], i - n * per, per)
            return pltpu.make_async_copy(out_held[k].at[i], place, out_sem.at[k, i])

        for k in range(n_tables):
            table_copy(k).start()
        for k in range(n_args):
            arg_copy(k).start()
        for k in range(n_tables):
            table_copy(k).wait()
        for k in range(n_args):
            arg_copy(k).wait()

        for i in range(steps):
            body(*table_held, *[part(ref, i, steps) for ref in arg_held], *[held.at[i] for held in out_held])
            for k in range(n_outs):
                out_copy(k, i * len(groups[k]) // steps, i).start()

        for i in range(steps):
            for k in range(n_outs):
                out_copy(k, i * len(groups[k]) // steps, i).wait()

    return pl.pallas_call(
        kernel,
        in_specs=[pl.BlockSpec(memory_space=pl.ANY)] * (n_tables + n_args),
        out_specs=[pl.BlockSpec(memory_space=pl.ANY)] * len(flat_outs),
        out_shape=flat_outs,
        scratch_shapes=[
            *[pltpu.VMEM(t.shape, bf16) for t in tables],
            *[pltpu.VMEM(a.shape, a.dtype) for a in args],
            *[pltpu.VMEM((steps, group[0].shape[0], lanes), group[0].dtype) for group in outs],
            pltpu.SemaphoreType.DMA((n_tables,)),
            pltpu.SemaphoreType.DMA((n_args,)),
            pltpu.SemaphoreType.DMA((n_outs, steps)),
        ],
        compiler_params=pltpu.CompilerParams(vmem_limit_bytes=vmem_bytes),
        cost_estimate=estimate(flops, [*args, *flat_outs]),
    )(*[jnp.asarray(t) for t in tables], *args)


def local_call(kernel, places, args, outs, scratch, flops):
    return pl.pallas_call(
        kernel,
        in_specs=[pl.BlockSpec(memory_space=pltpu.SMEM)] + [pl.BlockSpec(memory_space=pl.ANY)] * len(args),
        out_specs=[pl.BlockSpec(memory_space=pl.ANY)] * len(outs),
        out_shape=outs,
        scratch_shapes=scratch,
        compiler_params=pltpu.CompilerParams(vmem_limit_bytes=vmem_bytes),
        cost_estimate=estimate(flops, [*args, *outs]),
    )(places, *args)


def project(places, firsts, seconds, out_weight):
    length, width = firsts[0].shape
    channels, total_width = out_weight.shape
    steps = channels // lanes
    return local_call(
        project_kernel,
        places,
        [firsts[0], seconds[0], firsts[1], seconds[1], out_weight],
        [jax.ShapeDtypeStruct((length, channels), dtype) for dtype in (bf16, f32)],
        [
            pltpu.VMEM((2 * length, total_width), bf16),
            pltpu.VMEM((steps, lanes, total_width), bf16),
            pltpu.VMEM((steps, length, lanes), bf16),
            pltpu.VMEM((steps, length, lanes), f32),
            pltpu.SemaphoreType.DMA((2, 2)),
            pltpu.SemaphoreType.DMA((steps,)),
            pltpu.SemaphoreType.DMA((2, steps)),
        ],
        4 * length * out_weight.size,
    )


def weight_sum(places, cot_pieces, gated_pieces, rows):
    count = len(gated_pieces)
    length, width = gated_pieces[0].shape
    outs = [jax.ShapeDtypeStruct((rows, width), dtype) for dtype in (bf16, f32)]
    return local_call(
        functools.partial(weight_kernel, count),
        places,
        [*cot_pieces, *gated_pieces],
        outs,
        [
            pltpu.VMEM((count, *cot_pieces[0].shape), bf16),
            pltpu.VMEM((count, length, width), bf16),
            *[pltpu.VMEM(o.shape, o.dtype) for o in outs],
            pltpu.SemaphoreType.DMA((2, count)),
            pltpu.SemaphoreType.DMA((2,)),
        ],
        4 * count * length * rows * width,
    )


def transpose_kernel(rows_in, out, rows, turned, sems):
    copy = pltpu.make_async_copy(rows_in, rows, sems.at[0])
    copy.start()
    copy.wait()
    for i in range(rows.shape[1] // turn):
        turned[pl.ds(i * turn, turn), :] = rows[:, pl.ds(i * turn, turn)].T
    copy = pltpu.make_async_copy(turned, out, sems.at[1])
    copy.start()
    copy.wait()


def transposed(rows):
    return pl.pallas_call(
        transpose_kernel,
        in_specs=[pl.BlockSpec(memory_space=pl.ANY)],
        out_specs=pl.BlockSpec(memory_space=pl.ANY),
        out_shape=jax.ShapeDtypeStruct(rows.shape[::-1], rows.dtype),
        scratch_shapes=[
            pltpu.VMEM(rows.shape, rows.dtype),
            pltpu.VMEM(rows.shape[::-1], rows.dtype),
            pltpu.SemaphoreType.DMA((2,)),
        ],
        compiler_params=pltpu.CompilerParams(vmem_limit_bytes=vmem_bytes),
        cost_estimate=estimate(0, [rows, rows]),
    )(rows)


def swap_pairs(value, axis, distance):
    count = lax.axis_size(axis)
    return lax.ppermute(value, axis, [(i, i ^ distance) for i in range(count)])


def after(value, *earlier):
    return lax.optimization_barrier((value, *earlier))[0]


def per_device(query_gate, key_gate, value_input, filter_taps, skip_gain, out_weight, cotangent):
    queries, key_rows, value_rows, cot = (
        query_gate[0],
        key_gate[0],
        value_input[0],
        cotangent[0],
    )
    length, channels = queries.shape
    taps = filter_taps.shape[1]
    n_seq, n_tp, n_dp = lax.axis_size("seq"), lax.axis_size("tp"), lax.axis_size("dp")
    subs = n_tp // n_dp
    me_tp, me_dp = lax.axis_index("tp"), lax.axis_index("dp")
    me_half, me_sub = me_tp // subs, me_tp % subs
    size = length + taps
    norm_factor = 1.0 / math.sqrt(length * n_seq * n_dp)

    whole = analysis_table(size, np.arange(size))
    scale = 2.0 / size
    tables = [split_table(whole), np.ascontiguousarray(split_table(whole.T))]
    rows16 = jax.ShapeDtypeStruct((length, channels), bf16)
    rows32 = jax.ShapeDtypeStruct((length, channels), f32)
    half16 = jax.ShapeDtypeStruct((length, channels // 2), bf16)
    unit = 2 * size * channels

    tail = (
        key_rows[length - taps :].astype(f32) * value_rows[length - taps :].astype(f32)
    ).astype(bf16)
    tail, cot = lax.optimization_barrier((tail, cot))
    prior = lax.ppermute(tail, "seq", [(i, i + 1) for i in range(n_seq - 1)])

    def tp_dp(half, sub, replica):
        return (half * subs + sub) * n_dp + replica

    places = [(h, c, d) for h in range(n_dp) for c in range(subs) for d in range(n_dp)]
    rounds = []
    for turn in range(2):
        route = [(tp_dp(h, c, d), tp_dp(d ^ turn, c, h)) for h, c, d in places]
        rounds.append(lax.ppermute(after(cot, prior) if turn else cot, ("tp", "dp"), route))
    square = n_seq == n_tp == 4 and subs == 2
    if square:

        def holder(s, block):
            return (s + block) % 2 * subs + s // 2

        crossed = {0: (1, 2), 1: (0, 3)}
        route = [
            (s * n_tp + t, s * n_tp + sum(crossed[s % 2]) - t)
            for s in range(n_seq)
            for t in crossed[s % 2]
        ]
        swapped = lax.ppermute(cot, ("seq", "tp"), route)
        moves_now = sum(
            jnp.logical_and(lax.axis_index("seq") % 2 == parity, me_tp == t)
            for parity in crossed
            for t in crossed[parity]
        )
        held = jnp.where(moves_now > 0, swapped, cot)
        route = []
        for s in range(n_seq):
            for t in range(n_tp):
                block = sum(crossed[s % 2]) - t if t in crossed[s % 2] else t
                route.append((s * n_tp + t, block * n_tp + holder(s, block)))
        moved = lax.ppermute(held, ("seq", "tp"), route)
    else:
        moved = cot

    same = (me_half == me_dp).astype(jnp.int32)
    subs_of = [me_sub, (me_sub + 1) % subs]
    place = jnp.stack([same, *subs_of]).astype(jnp.int32)
    dp_row = jnp.broadcast_to(me_dp.astype(f32), (1, channels))
    if square:
        order = [*range(0, n_seq, 2), *reversed(range(1, n_seq, 2))]
        ring = [(order[k], order[(k + 1) % n_seq]) for k in range(n_seq)]
        table = np.zeros((n_seq, n_tp, n_tp), np.int32)
        for k, s in enumerate(order):
            for r in range(n_seq):
                for t in range(n_tp):
                    table[s, t, t ^ holder(order[k - r], s)] = r
        sources = jnp.asarray(table)[lax.axis_index("seq"), me_tp]
        weight_place = jnp.concatenate([sources, me_dp[None].astype(jnp.int32)])
        prior, place, weight_place, dp_row = lax.optimization_barrier(
            (prior, place, weight_place, dp_row)
        )
    state, *gated = by_channel(
        functools.partial(state_kernel, scale),
        tables,
        [prior, key_rows, value_rows, filter_taps, skip_gain[None], queries],
        [[rows32], [half16, half16]],
        channels,
        unit * (4 * taps + 5 * length),
    )
    if square:
        halves = [[half] for half in gated]

        def ring_step(pieces):
            pieces.append(lax.ppermute(pieces[-1], "seq", ring))

        ring_step(halves[0])
        halves[1][0], *rounds = lax.optimization_barrier((halves[1][0], *rounds))
    else:
        gated[0], *rounds = lax.optimization_barrier((gated[0], *rounds))

    route = [(tp_dp(h, c, d), tp_dp(h, (c + 1) % subs, d)) for h, c, d in places]
    theirs = [lax.ppermute(r, ("tp", "dp"), route) for r in rounds]
    firsts, seconds = zip(rounds, theirs)
    rows = n_tp * channels // (n_seq * n_dp)
    if square:
        moved = transposed(after(moved, *rounds))
        moved, place = lax.optimization_barrier((moved, place))
    other_sent, own_part = project(place, firsts, seconds, out_weight)
    other_part = swap_pairs(other_sent, "dp", 1)
    if square:
        halves[0][1], halves[1][0], _ = lax.optimization_barrier(
            (halves[0][1], halves[1][0], other_sent)
        )
        ring_step(halves[0])
        ring_step(halves[1])

    if square:
        sent_by = lambda value, flip: lax.ppermute(value, "tp", [(t, t ^ flip) for t in range(n_tp)])
        across = sent_by(moved, subs)
        cot_pieces = [moved, sent_by(moved, 1), across, sent_by(after(across, halves[0][2]), 1)]
        halves[0][2], halves[1][1], own_part = lax.optimization_barrier(
            (halves[0][2], halves[1][1], own_part)
        )
        ring_step(halves[0])
        ring_step(halves[1])
    else:
        full = lax.all_gather(cot, "tp", axis=1, tiled=True)
        cot_all = lax.all_to_all(full, "seq", 1, 0, tiled=True)
        gated_all = [lax.all_gather(half, "seq", axis=0, tiled=True) for half in gated]

        def part(replica, piece):
            block = lax.dynamic_slice_in_dim(cot_all, replica * rows, rows, axis=1)
            return lax.dot_general(
                block, piece, (((0,), (0,)), ((), ())), preferred_element_type=f32
            )

        def weight_one(piece):
            return part(me_dp, piece), swap_pairs(part(1 - me_dp, piece).astype(bf16), "dp", 1)

    share = taps // n_dp
    grad_query, signal, head, sent_lag, own_lag = by_channel(
        lag_kernel,
        tables,
        [own_part, other_part, state, queries, prior, key_rows, value_rows, dp_row],
        [
            [rows16],
            [rows16],
            [jax.ShapeDtypeStruct((taps, channels), bf16)],
            [jax.ShapeDtypeStruct((share, channels), bf16)],
            [jax.ShapeDtypeStruct((share, channels), f32)],
        ],
        channels,
        unit * (2 * taps + 4 * length + 3 * taps),
    )
    later = lax.ppermute(head, "seq", [(i + 1, i) for i in range(n_seq - 1)])

    def run_back(later):
        return by_channel(
            functools.partial(back_kernel, scale),
            tables,
            [signal, later, filter_taps, skip_gain[None], key_rows, value_rows],
            [[rows16], [rows16]],
            channels,
            256 * unit * (4 * taps + 5 * length),
        )

    received = swap_pairs(sent_lag, "dp", 1)
    if square:
        weight_place, halves[1][2], signal = lax.optimization_barrier((weight_place, halves[1][2], signal))
        ring_step(halves[1])
        first_sent, first_own = weight_sum(weight_place, cot_pieces, halves[0], rows)
        first_received = swap_pairs(first_sent, "dp", 1)
        received, first_own = lax.optimization_barrier((received, first_own))
    lag_sum = own_lag + received.astype(f32)
    distance = 1
    while distance < n_seq:
        rounded = lag_sum.astype(bf16)
        received = swap_pairs(rounded, "seq", distance)
        if square and distance == 1:
            second_sent, second_own = weight_sum(weight_place, cot_pieces, halves[1], rows)
            second_received = swap_pairs(second_sent, "dp", 1)
            received, second_own = lax.optimization_barrier((received, second_own))
        lag_sum = rounded.astype(f32) + received.astype(f32)
        distance *= 2
    if square:
        first_received, lag_sum = lax.optimization_barrier((first_received, lag_sum))
    mine = lag_sum.astype(bf16)
    theirs = swap_pairs(mine, "dp", 1)
    grad_key, grad_value = run_back(after(later, second_own) if square else later)
    first = me_dp == 0
    lag_sum = jnp.concatenate([jnp.where(first, mine, theirs), jnp.where(first, theirs, mine)], axis=0)
    grad_filter = lag_sum.astype(f32).T * (norm_factor * scale)

    if square:
        parts = [(first_own, first_received), (second_own, second_received)]
    else:
        parts = [weight_one(half) for half in gated_all]
    grad_weight = jnp.concatenate(
        [(mine + theirs.astype(f32)) * norm_factor for mine, theirs in parts], axis=1
    )
    return (
        grad_query[None],
        grad_key[None],
        grad_value[None],
        grad_filter,
        grad_filter[:, 0],
        grad_weight,
    )


def solution(mesh):
    tokens = P("dp", "seq", "tp")
    return jax.shard_map(
        per_device,
        mesh=mesh,
        in_specs=(tokens, tokens, tokens, P("tp", None), P("tp"), P("tp", "dp"), tokens),
        out_specs=(tokens, tokens, tokens, P("tp", None), P("tp"), P(("seq", "dp"), "tp")),
        check_vma=False,
    )
```

```python
import functools
import math

import jax
import jax.numpy as jnp
import ml_dtypes
import numpy as np
from jax import lax
from jax.experimental import pallas as pl
from jax.experimental.pallas import tpu as pltpu
from jax.sharding import PartitionSpec as P

f32, bf16 = jnp.float32, jnp.bfloat16
lanes = 512
turn = 256
vmem_bytes = 46 * 1024 * 1024


def analysis_table(size, positions):
    half = size // 2
    omega = 2.0 * np.pi * (np.arange(half) + 0.5) / size
    angle = omega[:, None] * np.asarray(positions)[None, :]
    return np.concatenate([np.cos(angle), -np.sin(angle)], axis=0)


def split_table(table):
    high = table.astype(ml_dtypes.bfloat16)
    low = (table - high.astype(np.float64)).astype(ml_dtypes.bfloat16)
    return np.concatenate([high, low])


def split_rows(rows):
    high = rows.astype(bf16)
    return high, (rows - high.astype(f32)).astype(bf16)


def dot(left, right):
    return jnp.dot(left, right, preferred_element_type=f32)


def dot_nt(left, right):
    return lax.dot_general(left, right, (((1,), (1,)), ((), ())), preferred_element_type=f32)


def add_halves(both):
    half = both.shape[0] // 2
    return both[:half] + both[half:]


def forward_transform(table, rows, start):
    return add_halves(dot(table[:, pl.ds(start, rows.shape[0])], rows))


def inverse_transform(table, spectrum, start, count):
    high, low = split_rows(spectrum)
    upper = table[pl.ds(start, count)]
    lower = table[pl.ds(table.shape[0] // 2 + start, count)]
    return dot(upper, high) + dot(upper, low) + dot(lower, high)


def spectrum_product(left, right, conjugate_right):
    half = left.shape[0] // 2
    left_re, left_im = left[:half], left[half:]
    right_re, right_im = right[:half], right[half:]
    if conjugate_right:
        right_im = -right_im
    return jnp.concatenate(
        [left_re * right_re - left_im * right_im, left_re * right_im + left_im * right_re], axis=0
    )


def mixed_spectrum(table, prior_ref, key_ref, value_ref):
    mixed = (key_ref[...].astype(f32) * value_ref[...].astype(f32)).astype(bf16)
    prior = prior_ref[...]
    return forward_transform(table, prior, 0) + forward_transform(table, mixed, prior.shape[0])


def filter_spectrum(scale, table, taps_ref, skip_ref):
    taps = taps_ref.shape[1]
    filt = add_halves(dot_nt(table[:, :taps], taps_ref[...]))
    half = filt.shape[0] // 2
    return jnp.concatenate([(filt[:half] + skip_ref[...]) * scale, filt[half:] * scale], axis=0)


def state_kernel(
    scale, table, synth, prior_ref, key_ref, value_ref, taps_ref, skip_ref, query_ref, state_ref, gated_ref
):
    spec = mixed_spectrum(table, prior_ref, key_ref, value_ref)
    product = spectrum_product(spec, filter_spectrum(scale, table, taps_ref, skip_ref), False)
    state = inverse_transform(synth, product, prior_ref.shape[0], query_ref.shape[0])
    state_ref[...] = state
    gated_ref[...] = (query_ref[...].astype(f32) * state).astype(bf16)


def project_kernel(
    place_ref, first_mine, second_mine, first_theirs, second_theirs, weight, other, own, pieces, blocks, others, owns, piece_sem, block_sem, out_sem
):
    steps, _, total_width = blocks.shape
    length, width = first_mine.shape

    def piece_copy(n, sub, source):
        rows = pl.ds(n * length, length)
        columns = pl.ds(pl.multiple_of(place_ref[1 + sub] * width, width), width)
        return pltpu.make_async_copy(source, pieces.at[rows, columns], piece_sem.at[n, sub])

    def block_copy(i):
        return pltpu.make_async_copy(weight.at[pl.ds(i * lanes, lanes)], blocks.at[i], block_sem.at[i])

    def out_copies(i):
        columns = pl.ds(pl.multiple_of(i * lanes, lanes), lanes)
        return [
            pltpu.make_async_copy(others.at[i], other.at[:, columns], out_sem.at[0, i]),
            pltpu.make_async_copy(owns.at[i], own.at[:, columns], out_sem.at[1, i]),
        ]

    for i in range(steps):
        block_copy(i).start()

    def fetch(own_first):
        for sub, (first, second) in enumerate([(first_mine, second_mine), (first_theirs, second_theirs)]):
            piece_copy(0, sub, second if own_first else first).start()
            piece_copy(1, sub, first if own_first else second).start()

    pl.when(place_ref[0] != 0)(lambda: fetch(True))
    pl.when(place_ref[0] == 0)(lambda: fetch(False))
    for n in range(2):
        for sub in range(2):
            piece_copy(n, sub, first_mine).wait()

    @pl.loop(0, steps)
    def _(i):
        block_copy(i).wait()
        total = dot_nt(pieces[...], blocks[i])
        others[i] = total[:length].astype(bf16)
        owns[i] = total[length:]
        for copy in out_copies(i):
            copy.start()

    for i in range(steps):
        for copy in out_copies(i):
            copy.wait()


def weight_kernel(count, place_ref, *refs):
    cot_in, gated_in = refs[: 2 * count], list(refs[2 * count : 4 * count - 1])
    other, own, cots, gateds, others, owns, cot_sem, gated_sem, out_sem = refs[4 * count - 1 :]
    gated_in[-1:] = [gated_in[-1].at[0], gated_in[-1].at[1]]
    rows = other.shape[0]
    block = min(rows, turn)
    copies = [pltpu.make_async_copy(gated_in[n], gateds.at[n], gated_sem.at[n]) for n in range(2 * count)]
    copies += [pltpu.make_async_copy(cot_in[n], cots.at[n], cot_sem.at[n]) for n in range(2 * count)]
    for copy in copies:
        copy.start()
    for copy in copies:
        copy.wait()
    outs = [
        pltpu.make_async_copy(others, other, out_sem.at[0]),
        pltpu.make_async_copy(owns, own, out_sem.at[1]),
    ]

    def fill(replica, target):
        @pl.loop(0, rows // block)
        def _(i):
            start = pl.multiple_of(replica * rows + i * block, block)
            total = None
            for n in range(2 * count):
                gated = gateds[2 * place_ref[n % count] + n // count]
                part = dot(cots[n, pl.ds(start, block), :], gated)
                total = part if total is None else total + part
            target[pl.ds(pl.multiple_of(i * block, block), block), :] = total.astype(target.dtype)

    me = place_ref[count]
    fill(1 - me, others)
    outs[0].start()
    fill(me, owns)
    outs[1].start()
    for copy in outs:
        copy.wait()


def lag_kernel(
    table,
    synth,
    own_ref,
    other_ref,
    state_ref,
    query_ref,
    prior_ref,
    key_ref,
    value_ref,
    place_ref,
    grad_ref,
    signal_ref,
    head_ref,
    sent_lag_ref,
    own_lag_ref,
):
    length, taps, share = signal_ref.shape[0], prior_ref.shape[0], own_lag_ref.shape[0]
    grad_gated = own_ref[...] + other_ref[...].astype(f32)
    grad_ref[...] = (grad_gated * state_ref[...]).astype(bf16)
    signal = (grad_gated * query_ref[...].astype(f32)).astype(bf16)
    signal_ref[...] = signal
    head_ref[...] = signal[:taps]
    spec = mixed_spectrum(table, prior_ref, key_ref, value_ref)
    product = spectrum_product(forward_transform(table, signal, 0), spec, True)
    lags = -inverse_transform(synth, product, length, taps)
    first = place_ref[...] == 0.0
    own_lag_ref[...] = jnp.where(first, lags[:share], lags[share:])
    sent_lag_ref[...] = jnp.where(first, lags[share:], lags[:share]).astype(bf16)


def back_kernel(
    scale, table, synth, signal_ref, later_ref, taps_ref, skip_ref, key_ref, value_ref, grad_key_ref, grad_value_ref
):
    length = key_ref.shape[0]
    spec = forward_transform(table, signal_ref[...], 0) + forward_transform(table, later_ref[...], length)
    product = spectrum_product(spec, filter_spectrum(scale, table, taps_ref, skip_ref), True)
    back = inverse_transform(synth, product, 0, length)
    grad_key_ref[...] = (back * value_ref[...].astype(f32)).astype(bf16)
    grad_value_ref[...] = (back * key_ref[...].astype(f32)).astype(bf16)


def estimate(flops, arrays):
    moved = sum(a.size * jnp.dtype(a.dtype).itemsize for a in arrays)
    return pl.CostEstimate(flops=flops // 64, bytes_accessed=moved // 64, transcendentals=0)


def by_channel(body, tables, args, outs, channels, flops, swap=None):
    steps = channels // lanes
    flat_outs = [o for group in outs for o in group]
    n_tables, n_args, n_outs = len(tables), len(args), len(outs)

    def part(ref, i, count):
        start = i * lanes
        if ref.shape[1] == count * lanes:
            return ref.at[:, pl.ds(start, lanes)]
        return ref.at[pl.ds(start, lanes), :]

    def kernel(*refs):
        refs = list(refs)
        take = lambda count: [refs.pop(0) for _ in range(count)]
        swap_ref = None if swap is None else refs.pop(0)
        table_in, arg_in, outs_to = take(n_tables), take(n_args), take(len(flat_outs))
        table_held, arg_held, out_held = take(n_tables), take(n_args), take(n_outs)
        table_sem, arg_sem, out_sem = refs
        groups = [[outs_to.pop(0) for _ in group] for group in outs]

        def table_copy(k):
            return pltpu.make_async_copy(table_in[k], table_held[k], table_sem.at[k])

        def arg_copy(k):
            return pltpu.make_async_copy(arg_in[k], arg_held[k], arg_sem.at[k])

        def out_copy(k, n, i):
            place = groups[k][n] if len(groups[k]) > 1 else part(groups[k][n], i, steps)
            return pltpu.make_async_copy(out_held[k].at[i], place, out_sem.at[k, i])

        for k in range(n_tables):
            table_copy(k).start()
        for k in range(n_args):
            arg_copy(k).start()
        for k in range(n_tables):
            table_copy(k).wait()
        for k in range(n_args):
            arg_copy(k).wait()

        for i in range(steps):
            body(*table_held, *[part(ref, i, steps) for ref in arg_held], *[held.at[i] for held in out_held])
            for k in range(n_outs):
                count = len(groups[k])
                if count == 1:
                    out_copy(k, 0, i).start()
                else:
                    pl.when(swap_ref[0] == 0)(out_copy(k, i, i).start)
                    pl.when(swap_ref[0] != 0)(out_copy(k, count - 1 - i, i).start)

        for i in range(steps):
            for k in range(n_outs):
                out_copy(k, 0 if len(groups[k]) == 1 else i, i).wait()

    return pl.pallas_call(
        kernel,
        in_specs=[pl.BlockSpec(memory_space=pltpu.SMEM)] * (swap is not None)
        + [pl.BlockSpec(memory_space=pl.ANY)] * (n_tables + n_args),
        out_specs=[pl.BlockSpec(memory_space=pl.ANY)] * len(flat_outs),
        out_shape=flat_outs,
        scratch_shapes=[
            *[pltpu.VMEM(t.shape, bf16) for t in tables],
            *[pltpu.VMEM(a.shape, a.dtype) for a in args],
            *[pltpu.VMEM((steps, group[0].shape[0], lanes), group[0].dtype) for group in outs],
            pltpu.SemaphoreType.DMA((n_tables,)),
            pltpu.SemaphoreType.DMA((n_args,)),
            pltpu.SemaphoreType.DMA((n_outs, steps)),
        ],
        compiler_params=pltpu.CompilerParams(vmem_limit_bytes=vmem_bytes),
        cost_estimate=estimate(flops, [*args, *flat_outs]),
    )(*([] if swap is None else [swap]), *[jnp.asarray(t) for t in tables], *args)


def local_call(kernel, places, args, outs, scratch, flops):
    return pl.pallas_call(
        kernel,
        in_specs=[pl.BlockSpec(memory_space=pltpu.SMEM)] + [pl.BlockSpec(memory_space=pl.ANY)] * len(args),
        out_specs=[pl.BlockSpec(memory_space=pl.ANY)] * len(outs),
        out_shape=outs,
        scratch_shapes=scratch,
        compiler_params=pltpu.CompilerParams(vmem_limit_bytes=vmem_bytes),
        cost_estimate=estimate(flops, [*args, *outs]),
    )(places, *args)


def project(places, firsts, seconds, out_weight):
    length, width = firsts[0].shape
    channels, total_width = out_weight.shape
    steps = channels // lanes
    return local_call(
        project_kernel,
        places,
        [firsts[0], seconds[0], firsts[1], seconds[1], out_weight],
        [jax.ShapeDtypeStruct((length, channels), dtype) for dtype in (bf16, f32)],
        [
            pltpu.VMEM((2 * length, total_width), bf16),
            pltpu.VMEM((steps, lanes, total_width), bf16),
            pltpu.VMEM((steps, length, lanes), bf16),
            pltpu.VMEM((steps, length, lanes), f32),
            pltpu.SemaphoreType.DMA((2, 2)),
            pltpu.SemaphoreType.DMA((steps,)),
            pltpu.SemaphoreType.DMA((2, steps)),
        ],
        4 * length * out_weight.size,
    )


def weight_sum(places, cot_pieces, gated_pieces, rows):
    count = (len(gated_pieces) + 1) // 2
    length, width = gated_pieces[0].shape
    outs = [jax.ShapeDtypeStruct((rows, width), dtype) for dtype in (bf16, f32)]
    return local_call(
        functools.partial(weight_kernel, count),
        places,
        [*cot_pieces, *gated_pieces],
        outs,
        [
            pltpu.VMEM((2 * count, *cot_pieces[0].shape), bf16),
            pltpu.VMEM((2 * count, *gated_pieces[0].shape), bf16),
            *[pltpu.VMEM(o.shape, o.dtype) for o in outs],
            pltpu.SemaphoreType.DMA((2 * count,)),
            pltpu.SemaphoreType.DMA((2 * count,)),
            pltpu.SemaphoreType.DMA((2,)),
        ],
        8 * count * length * rows * width,
    )


def transpose_kernel(rows_in, out, rows, turned, sems):
    copy = pltpu.make_async_copy(rows_in, rows, sems.at[0])
    copy.start()
    copy.wait()
    for i in range(rows.shape[1] // turn):
        turned[pl.ds(i * turn, turn), :] = rows[:, pl.ds(i * turn, turn)].T
    copy = pltpu.make_async_copy(turned, out, sems.at[1])
    copy.start()
    copy.wait()


def transposed(rows):
    return pl.pallas_call(
        transpose_kernel,
        in_specs=[pl.BlockSpec(memory_space=pl.ANY)],
        out_specs=pl.BlockSpec(memory_space=pl.ANY),
        out_shape=jax.ShapeDtypeStruct(rows.shape[::-1], rows.dtype),
        scratch_shapes=[
            pltpu.VMEM(rows.shape, rows.dtype),
            pltpu.VMEM(rows.shape[::-1], rows.dtype),
            pltpu.SemaphoreType.DMA((2,)),
        ],
        compiler_params=pltpu.CompilerParams(vmem_limit_bytes=vmem_bytes),
        cost_estimate=estimate(0, [rows, rows]),
    )(rows)


def swap_pairs(value, axis, distance):
    count = lax.axis_size(axis)
    return lax.ppermute(value, axis, [(i, i ^ distance) for i in range(count)])


def after(value, *earlier):
    return lax.optimization_barrier((value, *earlier))[0]


def per_device(query_gate, key_gate, value_input, filter_taps, skip_gain, out_weight, cotangent):
    queries, key_rows, value_rows, cot = (
        query_gate[0],
        key_gate[0],
        value_input[0],
        cotangent[0],
    )
    length, channels = queries.shape
    taps = filter_taps.shape[1]
    n_seq, n_tp, n_dp = lax.axis_size("seq"), lax.axis_size("tp"), lax.axis_size("dp")
    subs = n_tp // n_dp
    me_tp, me_dp = lax.axis_index("tp"), lax.axis_index("dp")
    me_half, me_sub = me_tp // subs, me_tp % subs
    size = length + taps
    norm_factor = 1.0 / math.sqrt(length * n_seq * n_dp)

    whole = analysis_table(size, np.arange(size))
    scale = 2.0 / size
    tables = [split_table(whole), np.ascontiguousarray(split_table(whole.T))]
    rows16 = jax.ShapeDtypeStruct((length, channels), bf16)
    rows32 = jax.ShapeDtypeStruct((length, channels), f32)
    half16 = jax.ShapeDtypeStruct((length, channels // 2), bf16)
    unit = 2 * size * channels

    tail = (
        key_rows[length - taps :].astype(f32) * value_rows[length - taps :].astype(f32)
    ).astype(bf16)
    tail, cot = lax.optimization_barrier((tail, cot))
    prior = lax.ppermute(tail, "seq", [(i, i + 1) for i in range(n_seq - 1)])

    def tp_dp(half, sub, replica):
        return (half * subs + sub) * n_dp + replica

    places = [(h, c, d) for h in range(n_dp) for c in range(subs) for d in range(n_dp)]
    rounds = []
    for turn in range(2):
        route = [(tp_dp(h, c, d), tp_dp(d ^ turn, c, h)) for h, c, d in places]
        rounds.append(lax.ppermute(after(cot, prior) if turn else cot, ("tp", "dp"), route))
    square = n_seq == n_tp == 4 and subs == 2
    if square:

        def holder(s, block):
            return (s + block) % 2 * subs + s // 2

        crossed = {0: (1, 2), 1: (0, 3)}
        route = [
            (s * n_tp + t, s * n_tp + sum(crossed[s % 2]) - t)
            for s in range(n_seq)
            for t in crossed[s % 2]
        ]
        swapped = lax.ppermute(cot, ("seq", "tp"), route)
        moves_now = sum(
            jnp.logical_and(lax.axis_index("seq") % 2 == parity, me_tp == t)
            for parity in crossed
            for t in crossed[parity]
        )
        held = jnp.where(moves_now > 0, swapped, cot)
        route = []
        for s in range(n_seq):
            for t in range(n_tp):
                block = sum(crossed[s % 2]) - t if t in crossed[s % 2] else t
                route.append((s * n_tp + t, block * n_tp + holder(s, block)))
        moved = lax.ppermute(held, ("seq", "tp"), route)
    else:
        moved = cot

    same = (me_half == me_dp).astype(jnp.int32)
    subs_of = [me_sub, (me_sub + 1) % subs]
    place = jnp.stack([same, *subs_of]).astype(jnp.int32)
    dp_row = jnp.broadcast_to(me_dp.astype(f32), (1, channels))
    if square:
        order = [*range(0, n_seq, 2), *reversed(range(1, n_seq, 2))]
        ring = [(order[k], order[(k + 1) % n_seq]) for k in range(n_seq)]
        table = np.zeros((n_seq, n_tp, n_tp), np.int32)
        for k, s in enumerate(order):
            for r in range(n_seq):
                for t in range(n_tp):
                    table[s, t, t ^ holder(order[k - r], s)] = r
        sources = jnp.asarray(table)[lax.axis_index("seq"), me_tp]
        weight_place = jnp.concatenate([sources, me_dp[None].astype(jnp.int32)])
        prior, place, weight_place, dp_row = lax.optimization_barrier(
            (prior, place, weight_place, dp_row)
        )
    state, *gated = by_channel(
        functools.partial(state_kernel, scale),
        tables,
        [prior, key_rows, value_rows, filter_taps, skip_gain[None], queries],
        [[rows32], [half16, half16]],
        channels,
        unit * (4 * taps + 5 * length),
        jnp.reshape(me_dp if square else 0 * me_dp, (1,)).astype(jnp.int32),
    )
    if square:
        ring_pieces = [gated[0], swap_pairs(gated[1], "dp", 1)]
        ring_pieces[0], ring_pieces[1], moved = lax.optimization_barrier((*ring_pieces, moved))

        def ring_step():
            for _ in range(2):
                ring_pieces.append(lax.ppermute(ring_pieces[-2], "seq", ring))

        ring_step()
    gated[0], *rounds = lax.optimization_barrier((gated[0], *rounds))

    route = [(tp_dp(h, c, d), tp_dp(h, (c + 1) % subs, d)) for h, c, d in places]
    theirs = [lax.ppermute(r, ("tp", "dp"), route) for r in rounds]
    firsts, seconds = zip(rounds, theirs)
    rows = n_tp * channels // (n_seq * n_dp)
    if square:
        moved = after(moved, *rounds)
        moved_other = swap_pairs(moved, "dp", 1)
        moved = transposed(moved)
        moved, place = lax.optimization_barrier((moved, place))
    other_sent, own_part = project(place, firsts, seconds, out_weight)
    if square:
        other_sent, moved_other = lax.optimization_barrier((other_sent, moved_other))
    other_part = swap_pairs(other_sent, "dp", 1)
    if square:

        def spread(piece, across, gate):
            near = [(t, t ^ 1) for t in range(n_tp)]
            return [
                piece,
                lax.ppermute(piece, "tp", near),
                across,
                lax.ppermute(after(across, gate), "tp", near),
            ]

        opposite = [(t, t ^ subs) for t in range(n_tp)]
        across = lax.ppermute(moved, "tp", opposite)
        ring_pieces[2], ring_pieces[3], _ = lax.optimization_barrier((*ring_pieces[2:4], other_sent))
        ring_step()
        *last, own_part, other_part = lax.optimization_barrier((*ring_pieces[4:6], own_part, other_part))
        last = lax.ppermute(jnp.stack(last), "seq", ring)
        moved_other = transposed(after(moved_other, ring_pieces[2]))
        across_other = lax.ppermute(moved_other, "tp", opposite)
        cot_pieces = spread(moved, across, other_part) + spread(moved_other, across_other, own_part)
    else:
        full = lax.all_gather(cot, "tp", axis=1, tiled=True)
        cot_all = lax.all_to_all(full, "seq", 1, 0, tiled=True)
        gated_all = [lax.all_gather(half, "seq", axis=0, tiled=True) for half in gated]

        def part(replica, piece):
            block = lax.dynamic_slice_in_dim(cot_all, replica * rows, rows, axis=1)
            return lax.dot_general(
                block, piece, (((0,), (0,)), ((), ())), preferred_element_type=f32
            )

        def weight_one(piece):
            return part(me_dp, piece), swap_pairs(part(1 - me_dp, piece).astype(bf16), "dp", 1)

    share = taps // n_dp
    grad_query, signal, head, sent_lag, own_lag = by_channel(
        lag_kernel,
        tables,
        [own_part, other_part, state, queries, prior, key_rows, value_rows, dp_row],
        [
            [rows16],
            [rows16],
            [jax.ShapeDtypeStruct((taps, channels), bf16)],
            [jax.ShapeDtypeStruct((share, channels), bf16)],
            [jax.ShapeDtypeStruct((share, channels), f32)],
        ],
        channels,
        unit * (2 * taps + 4 * length + 3 * taps),
    )
    later = lax.ppermute(head, "seq", [(i + 1, i) for i in range(n_seq - 1)])

    def run_back(later):
        return by_channel(
            functools.partial(back_kernel, scale),
            tables,
            [signal, later, filter_taps, skip_gain[None], key_rows, value_rows],
            [[rows16], [rows16]],
            channels,
            256 * unit * (4 * taps + 5 * length),
        )

    received = swap_pairs(sent_lag, "dp", 1)
    if square:
        last, received = lax.optimization_barrier((last, received))
        ring_pieces.append(last)
    lag_sum = own_lag + received.astype(f32)
    distance = 1
    while distance < n_seq:
        rounded = lag_sum.astype(bf16)
        received = swap_pairs(rounded, "seq", distance)
        if square and distance == 1:
            weight_place, rounded = lax.optimization_barrier((weight_place, rounded))
            weight_sent, weight_own = weight_sum(weight_place, cot_pieces, ring_pieces, rows)
            weight_received = swap_pairs(weight_sent, "dp", 1)
            received, weight_own = lax.optimization_barrier((received, weight_own))
        if square and distance == 2:
            grad_key, grad_value = run_back(after(later, weight_own))
            received, grad_key = lax.optimization_barrier((received, grad_key))
        lag_sum = rounded.astype(f32) + received.astype(f32)
        distance *= 2
    mine = lag_sum.astype(bf16)
    if not square:
        grad_key, grad_value = run_back(later)
    theirs = swap_pairs(mine, "dp", 1)
    first = me_dp == 0
    lag_sum = jnp.concatenate([jnp.where(first, mine, theirs), jnp.where(first, theirs, mine)], axis=0)
    grad_filter = lag_sum.astype(f32).T * (norm_factor * scale)

    if square:
        weight_own, weight_received = weight_own * norm_factor, weight_received.astype(f32) * norm_factor
        grad_weight = jnp.concatenate(
            [
                jnp.where(first, weight_own, weight_received),
                jnp.where(first, weight_received, weight_own),
            ],
            axis=1,
        )
    else:
        parts = [weight_one(half) for half in gated_all]
        grad_weight = jnp.concatenate(
            [(mine + theirs.astype(f32)) * norm_factor for mine, theirs in parts], axis=1
        )
    return (
        grad_query[None],
        grad_key[None],
        grad_value[None],
        grad_filter,
        grad_filter[:, 0],
        grad_weight,
    )


def solution(mesh):
    tokens = P("dp", "seq", "tp")
    return jax.shard_map(
        per_device,
        mesh=mesh,
        in_specs=(tokens, tokens, tokens, P("tp", None), P("tp"), P("tp", "dp"), tokens),
        out_specs=(tokens, tokens, tokens, P("tp", None), P("tp"), P(("seq", "dp"), "tp")),
        check_vma=False,
    )
```

```python
import functools
import math

import jax
import jax.numpy as jnp
import ml_dtypes
import numpy as np
from jax import lax
from jax.experimental import pallas as pl
from jax.experimental.pallas import tpu as pltpu
from jax.sharding import PartitionSpec as P

f32, bf16 = jnp.float32, jnp.bfloat16
lanes = 512
turn = 256
vmem_bytes = 46 * 1024 * 1024


def analysis_table(size, positions):
    half = size // 2
    omega = 2.0 * np.pi * (np.arange(half) + 0.5) / size
    angle = omega[:, None] * np.asarray(positions)[None, :]
    return np.concatenate([np.cos(angle), -np.sin(angle)], axis=0)


def split_table(table):
    high = table.astype(ml_dtypes.bfloat16)
    low = (table - high.astype(np.float64)).astype(ml_dtypes.bfloat16)
    return np.concatenate([high, low])


def split_rows(rows):
    high = rows.astype(bf16)
    return high, (rows - high.astype(f32)).astype(bf16)


def dot(left, right):
    return jnp.dot(left, right, preferred_element_type=f32)


def dot_nt(left, right):
    return lax.dot_general(left, right, (((1,), (1,)), ((), ())), preferred_element_type=f32)


def add_halves(both):
    half = both.shape[0] // 2
    return both[:half] + both[half:]


def forward_transform(table, rows, start):
    return add_halves(dot(table[:, pl.ds(start, rows.shape[0])], rows))


def inverse_transform(table, spectrum, start, count):
    high, low = split_rows(spectrum)
    upper = table[pl.ds(start, count)]
    lower = table[pl.ds(table.shape[0] // 2 + start, count)]
    return dot(upper, high) + dot(upper, low) + dot(lower, high)


def spectrum_product(left, right, conjugate_right):
    half = left.shape[0] // 2
    left_re, left_im = left[:half], left[half:]
    right_re, right_im = right[:half], right[half:]
    if conjugate_right:
        right_im = -right_im
    return jnp.concatenate(
        [left_re * right_re - left_im * right_im, left_re * right_im + left_im * right_re], axis=0
    )


def mixed_spectrum(table, prior_ref, key_ref, value_ref):
    mixed = (key_ref[...].astype(f32) * value_ref[...].astype(f32)).astype(bf16)
    prior = prior_ref[...]
    return forward_transform(table, prior, 0) + forward_transform(table, mixed, prior.shape[0])


def filter_spectrum(scale, table, taps_ref, skip_ref):
    taps = taps_ref.shape[1]
    filt = add_halves(dot_nt(table[:, :taps], taps_ref[...]))
    half = filt.shape[0] // 2
    return jnp.concatenate([(filt[:half] + skip_ref[...]) * scale, filt[half:] * scale], axis=0)


def state_kernel(
    scale, table, synth, prior_ref, key_ref, value_ref, taps_ref, skip_ref, query_ref, state_ref, gated_ref
):
    spec = mixed_spectrum(table, prior_ref, key_ref, value_ref)
    product = spectrum_product(spec, filter_spectrum(scale, table, taps_ref, skip_ref), False)
    state = inverse_transform(synth, product, prior_ref.shape[0], query_ref.shape[0])
    state_ref[...] = state
    gated_ref[...] = (query_ref[...].astype(f32) * state).astype(bf16)


def project_kernel(
    place_ref, first_mine, second_mine, first_theirs, second_theirs, weight, other, own, pieces, blocks, others, owns, piece_sem, block_sem, out_sem
):
    steps, _, total_width = blocks.shape
    length, width = first_mine.shape

    def piece_copy(n, sub, source):
        rows = pl.ds(n * length, length)
        columns = pl.ds(pl.multiple_of(place_ref[1 + sub] * width, width), width)
        return pltpu.make_async_copy(source, pieces.at[rows, columns], piece_sem.at[n, sub])

    def block_copy(i):
        return pltpu.make_async_copy(weight.at[pl.ds(i * lanes, lanes)], blocks.at[i], block_sem.at[i])

    def out_copies(i):
        columns = pl.ds(pl.multiple_of(i * lanes, lanes), lanes)
        return [
            pltpu.make_async_copy(others.at[i], other.at[:, columns], out_sem.at[0, i]),
            pltpu.make_async_copy(owns.at[i], own.at[:, columns], out_sem.at[1, i]),
        ]

    for i in range(steps):
        block_copy(i).start()

    def fetch(own_first):
        for sub, (first, second) in enumerate([(first_mine, second_mine), (first_theirs, second_theirs)]):
            piece_copy(0, sub, second if own_first else first).start()
            piece_copy(1, sub, first if own_first else second).start()

    pl.when(place_ref[0] != 0)(lambda: fetch(True))
    pl.when(place_ref[0] == 0)(lambda: fetch(False))
    for n in range(2):
        for sub in range(2):
            piece_copy(n, sub, first_mine).wait()

    @pl.loop(0, steps)
    def _(i):
        block_copy(i).wait()
        total = dot_nt(pieces[...], blocks[i])
        others[i] = total[:length].astype(bf16)
        owns[i] = total[length:]
        for copy in out_copies(i):
            copy.start()

    for i in range(steps):
        for copy in out_copies(i):
            copy.wait()


def weight_kernel(count, place_ref, *refs):
    cot_in, gated_in = refs[:count], refs[count : 2 * count]
    other, own, cots, gateds, others, owns, in_sem, out_sem = refs[2 * count :]
    length = gateds.shape[1]
    rows = other.shape[0]
    block = min(rows, lanes)
    copies = [pltpu.make_async_copy(cot_in[n], cots.at[n], in_sem.at[0, n]) for n in range(count)]
    copies += [pltpu.make_async_copy(gated_in[n], gateds.at[n], in_sem.at[1, n]) for n in range(count)]
    for copy in copies:
        copy.start()
    for copy in copies:
        copy.wait()
    outs = [
        pltpu.make_async_copy(others, other, out_sem.at[0]),
        pltpu.make_async_copy(owns, own, out_sem.at[1]),
    ]

    def fill(replica, target):
        @pl.loop(0, rows // block)
        def _(i):
            start = pl.multiple_of(replica * rows + i * block, block)
            total = None
            for n in range(count):
                part = dot(cots[n, pl.ds(start, block), :], gateds[place_ref[n]])
                total = part if total is None else total + part
            target[pl.ds(pl.multiple_of(i * block, block), block), :] = total.astype(target.dtype)

    me = place_ref[count]
    fill(1 - me, others)
    outs[0].start()
    fill(me, owns)
    outs[1].start()
    for copy in outs:
        copy.wait()


def lag_kernel(
    table,
    synth,
    own_ref,
    other_ref,
    state_ref,
    query_ref,
    prior_ref,
    key_ref,
    value_ref,
    place_ref,
    grad_ref,
    signal_ref,
    head_ref,
    sent_lag_ref,
    own_lag_ref,
):
    length, taps, share = signal_ref.shape[0], prior_ref.shape[0], own_lag_ref.shape[0]
    grad_gated = own_ref[...] + other_ref[...].astype(f32)
    grad_ref[...] = (grad_gated * state_ref[...]).astype(bf16)
    signal = (grad_gated * query_ref[...].astype(f32)).astype(bf16)
    signal_ref[...] = signal
    head_ref[...] = signal[:taps]
    spec = mixed_spectrum(table, prior_ref, key_ref, value_ref)
    product = spectrum_product(forward_transform(table, signal, 0), spec, True)
    lags = -inverse_transform(synth, product, length, taps)
    first = place_ref[...] == 0.0
    own_lag_ref[...] = jnp.where(first, lags[:share], lags[share:])
    sent_lag_ref[...] = jnp.where(first, lags[share:], lags[:share]).astype(bf16)


def back_kernel(
    scale, table, synth, signal_ref, later_ref, taps_ref, skip_ref, key_ref, value_ref, grad_key_ref, grad_value_ref
):
    length = key_ref.shape[0]
    spec = forward_transform(table, signal_ref[...], 0) + forward_transform(table, later_ref[...], length)
    product = spectrum_product(spec, filter_spectrum(scale, table, taps_ref, skip_ref), True)
    back = inverse_transform(synth, product, 0, length)
    grad_key_ref[...] = (back * value_ref[...].astype(f32)).astype(bf16)
    grad_value_ref[...] = (back * key_ref[...].astype(f32)).astype(bf16)


def estimate(flops, arrays):
    moved = sum(a.size * jnp.dtype(a.dtype).itemsize for a in arrays)
    return pl.CostEstimate(flops=flops // 64, bytes_accessed=moved // 64, transcendentals=0)


def by_channel(body, tables, args, outs, channels, flops):
    steps = channels // lanes
    flat_outs = [o for group in outs for o in group]
    n_tables, n_args, n_outs = len(tables), len(args), len(outs)

    def part(ref, i, count):
        start = i * lanes
        if ref.shape[1] == count * lanes:
            return ref.at[:, pl.ds(start, lanes)]
        return ref.at[pl.ds(start, lanes), :]

    def kernel(*refs):
        refs = list(refs)
        take = lambda count: [refs.pop(0) for _ in range(count)]
        table_in, arg_in, outs_to = take(n_tables), take(n_args), take(len(flat_outs))
        table_held, arg_held, out_held = take(n_tables), take(n_args), take(n_outs)
        table_sem, arg_sem, out_sem = refs
        groups = [[outs_to.pop(0) for _ in group] for group in outs]

        def table_copy(k):
            return pltpu.make_async_copy(table_in[k], table_held[k], table_sem.at[k])

        def arg_copy(k):
            return pltpu.make_async_copy(arg_in[k], arg_held[k], arg_sem.at[k])

        def out_copy(k, n, i):
            per = steps // len(groups[k])
            place = part(groups[k][n], i - n * per, per)
            return pltpu.make_async_copy(out_held[k].at[i], place, out_sem.at[k, i])

        for k in range(n_tables):
            table_copy(k).start()
        for k in range(n_args):
            arg_copy(k).start()
        for k in range(n_tables):
            table_copy(k).wait()
        for k in range(n_args):
            arg_copy(k).wait()

        for i in range(steps):
            body(*table_held, *[part(ref, i, steps) for ref in arg_held], *[held.at[i] for held in out_held])
            for k in range(n_outs):
                out_copy(k, i * len(groups[k]) // steps, i).start()

        for i in range(steps):
            for k in range(n_outs):
                out_copy(k, i * len(groups[k]) // steps, i).wait()

    return pl.pallas_call(
        kernel,
        in_specs=[pl.BlockSpec(memory_space=pl.ANY)] * (n_tables + n_args),
        out_specs=[pl.BlockSpec(memory_space=pl.ANY)] * len(flat_outs),
        out_shape=flat_outs,
        scratch_shapes=[
            *[pltpu.VMEM(t.shape, bf16) for t in tables],
            *[pltpu.VMEM(a.shape, a.dtype) for a in args],
            *[pltpu.VMEM((steps, group[0].shape[0], lanes), group[0].dtype) for group in outs],
            pltpu.SemaphoreType.DMA((n_tables,)),
            pltpu.SemaphoreType.DMA((n_args,)),
            pltpu.SemaphoreType.DMA((n_outs, steps)),
        ],
        compiler_params=pltpu.CompilerParams(vmem_limit_bytes=vmem_bytes),
        cost_estimate=estimate(flops, [*args, *flat_outs]),
    )(*[jnp.asarray(t) for t in tables], *args)


def local_call(kernel, places, args, outs, scratch, flops):
    return pl.pallas_call(
        kernel,
        in_specs=[pl.BlockSpec(memory_space=pltpu.SMEM)] + [pl.BlockSpec(memory_space=pl.ANY)] * len(args),
        out_specs=[pl.BlockSpec(memory_space=pl.ANY)] * len(outs),
        out_shape=outs,
        scratch_shapes=scratch,
        compiler_params=pltpu.CompilerParams(vmem_limit_bytes=vmem_bytes),
        cost_estimate=estimate(flops, [*args, *outs]),
    )(places, *args)


def project(places, firsts, seconds, out_weight):
    length, width = firsts[0].shape
    channels, total_width = out_weight.shape
    steps = channels // lanes
    return local_call(
        project_kernel,
        places,
        [firsts[0], seconds[0], firsts[1], seconds[1], out_weight],
        [jax.ShapeDtypeStruct((length, channels), dtype) for dtype in (bf16, f32)],
        [
            pltpu.VMEM((2 * length, total_width), bf16),
            pltpu.VMEM((steps, lanes, total_width), bf16),
            pltpu.VMEM((steps, length, lanes), bf16),
            pltpu.VMEM((steps, length, lanes), f32),
            pltpu.SemaphoreType.DMA((2, 2)),
            pltpu.SemaphoreType.DMA((steps,)),
            pltpu.SemaphoreType.DMA((2, steps)),
        ],
        4 * length * out_weight.size,
    )


def weight_sum(places, cot_pieces, gated_pieces, rows):
    count = len(gated_pieces)
    length, width = gated_pieces[0].shape
    outs = [jax.ShapeDtypeStruct((rows, width), dtype) for dtype in (bf16, f32)]
    return local_call(
        functools.partial(weight_kernel, count),
        places,
        [*cot_pieces, *gated_pieces],
        outs,
        [
            pltpu.VMEM((count, *cot_pieces[0].shape), bf16),
            pltpu.VMEM((count, length, width), bf16),
            *[pltpu.VMEM(o.shape, o.dtype) for o in outs],
            pltpu.SemaphoreType.DMA((2, count)),
            pltpu.SemaphoreType.DMA((2,)),
        ],
        4 * count * length * rows * width,
    )


def transpose_kernel(rows_in, out, rows, turned, sems):
    copy = pltpu.make_async_copy(rows_in, rows, sems.at[0])
    copy.start()
    copy.wait()
    for i in range(rows.shape[1] // turn):
        turned[pl.ds(i * turn, turn), :] = rows[:, pl.ds(i * turn, turn)].T
    copy = pltpu.make_async_copy(turned, out, sems.at[1])
    copy.start()
    copy.wait()


def transposed(rows):
    return pl.pallas_call(
        transpose_kernel,
        in_specs=[pl.BlockSpec(memory_space=pl.ANY)],
        out_specs=pl.BlockSpec(memory_space=pl.ANY),
        out_shape=jax.ShapeDtypeStruct(rows.shape[::-1], rows.dtype),
        scratch_shapes=[
            pltpu.VMEM(rows.shape, rows.dtype),
            pltpu.VMEM(rows.shape[::-1], rows.dtype),
            pltpu.SemaphoreType.DMA((2,)),
        ],
        compiler_params=pltpu.CompilerParams(vmem_limit_bytes=vmem_bytes),
        cost_estimate=estimate(0, [rows, rows]),
    )(rows)


def swap_pairs(value, axis, distance):
    count = lax.axis_size(axis)
    return lax.ppermute(value, axis, [(i, i ^ distance) for i in range(count)])


def after(value, *earlier):
    return lax.optimization_barrier((value, *earlier))[0]


def per_device(query_gate, key_gate, value_input, filter_taps, skip_gain, out_weight, cotangent):
    queries, key_rows, value_rows, cot = (
        query_gate[0],
        key_gate[0],
        value_input[0],
        cotangent[0],
    )
    length, channels = queries.shape
    taps = filter_taps.shape[1]
    n_seq, n_tp, n_dp = lax.axis_size("seq"), lax.axis_size("tp"), lax.axis_size("dp")
    subs = n_tp // n_dp
    me_tp, me_dp = lax.axis_index("tp"), lax.axis_index("dp")
    me_half, me_sub = me_tp // subs, me_tp % subs
    size = length + taps
    norm_factor = 1.0 / math.sqrt(length * n_seq * n_dp)

    whole = analysis_table(size, np.arange(size))
    scale = 2.0 / size
    tables = [split_table(whole), np.ascontiguousarray(split_table(whole.T))]
    rows16 = jax.ShapeDtypeStruct((length, channels), bf16)
    rows32 = jax.ShapeDtypeStruct((length, channels), f32)
    half16 = jax.ShapeDtypeStruct((length, channels // 2), bf16)
    unit = 2 * size * channels

    tail = (
        key_rows[length - taps :].astype(f32) * value_rows[length - taps :].astype(f32)
    ).astype(bf16)
    tail, cot = lax.optimization_barrier((tail, cot))
    prior = lax.ppermute(tail, "seq", [(i, i + 1) for i in range(n_seq - 1)])

    def tp_dp(half, sub, replica):
        return (half * subs + sub) * n_dp + replica

    places = [(h, c, d) for h in range(n_dp) for c in range(subs) for d in range(n_dp)]
    rounds = []
    for turn in range(2):
        route = [(tp_dp(h, c, d), tp_dp(d ^ turn, c, h)) for h, c, d in places]
        rounds.append(lax.ppermute(after(cot, prior) if turn else cot, ("tp", "dp"), route))
    square = n_seq == n_tp == 4 and subs == 2
    if square:

        def holder(s, block):
            return (s + block) % 2 * subs + s // 2

        crossed = {0: (1, 2), 1: (0, 3)}
        route = [
            (s * n_tp + t, s * n_tp + sum(crossed[s % 2]) - t)
            for s in range(n_seq)
            for t in crossed[s % 2]
        ]
        swapped = lax.ppermute(cot, ("seq", "tp"), route)
        moves_now = sum(
            jnp.logical_and(lax.axis_index("seq") % 2 == parity, me_tp == t)
            for parity in crossed
            for t in crossed[parity]
        )
        held = jnp.where(moves_now > 0, swapped, cot)
        route = []
        for s in range(n_seq):
            for t in range(n_tp):
                block = sum(crossed[s % 2]) - t if t in crossed[s % 2] else t
                route.append((s * n_tp + t, block * n_tp + holder(s, block)))
        moved = lax.ppermute(held, ("seq", "tp"), route)
    else:
        moved = cot

    same = (me_half == me_dp).astype(jnp.int32)
    subs_of = [me_sub, (me_sub + 1) % subs]
    place = jnp.stack([same, *subs_of]).astype(jnp.int32)
    dp_row = jnp.broadcast_to(me_dp.astype(f32), (1, channels))
    if square:
        order = [*range(0, n_seq, 2), *reversed(range(1, n_seq, 2))]
        ring = [(order[k], order[(k + 1) % n_seq]) for k in range(n_seq)]
        table = np.zeros((n_seq, n_tp, n_tp), np.int32)
        for k, s in enumerate(order):
            for r in range(n_seq):
                for t in range(n_tp):
                    table[s, t, t ^ holder(order[k - r], s)] = r
        sources = jnp.asarray(table)[lax.axis_index("seq"), me_tp]
        weight_place = jnp.concatenate([sources, me_dp[None].astype(jnp.int32)])
        prior, place, weight_place, dp_row = lax.optimization_barrier(
            (prior, place, weight_place, dp_row)
        )
    state, *gated = by_channel(
        functools.partial(state_kernel, scale),
        tables,
        [prior, key_rows, value_rows, filter_taps, skip_gain[None], queries],
        [[rows32], [half16, half16]],
        channels,
        unit * (4 * taps + 5 * length),
    )
    if square:
        halves = [[half] for half in gated]

        def ring_step(pieces):
            pieces.append(lax.ppermute(pieces[-1], "seq", ring))

        halves[0][0], moved = lax.optimization_barrier((halves[0][0], moved))
        ring_step(halves[0])
        halves[1][0], *rounds = lax.optimization_barrier((halves[1][0], *rounds))
    else:
        gated[0], *rounds = lax.optimization_barrier((gated[0], *rounds))

    route = [(tp_dp(h, c, d), tp_dp(h, (c + 1) % subs, d)) for h, c, d in places]
    theirs = [lax.ppermute(r, ("tp", "dp"), route) for r in rounds]
    firsts, seconds = zip(rounds, theirs)
    rows = n_tp * channels // (n_seq * n_dp)
    if square:
        moved = transposed(after(moved, *rounds))
        moved, place = lax.optimization_barrier((moved, place))
    other_sent, own_part = project(place, firsts, seconds, out_weight)
    other_part = swap_pairs(other_sent, "dp", 1)
    if square:
        halves[0][1], halves[1][0], _ = lax.optimization_barrier(
            (halves[0][1], halves[1][0], other_sent)
        )
        ring_step(halves[0])
        ring_step(halves[1])

    if square:
        sent_by = lambda value, flip: lax.ppermute(value, "tp", [(t, t ^ flip) for t in range(n_tp)])
        across = sent_by(moved, subs)
        cot_pieces = [moved, sent_by(moved, 1), across, sent_by(after(across, halves[0][2]), 1)]
        halves[0][2], halves[1][1], own_part = lax.optimization_barrier(
            (halves[0][2], halves[1][1], own_part)
        )
        ring_step(halves[0])
        ring_step(halves[1])
    else:
        full = lax.all_gather(cot, "tp", axis=1, tiled=True)
        cot_all = lax.all_to_all(full, "seq", 1, 0, tiled=True)
        gated_all = [lax.all_gather(half, "seq", axis=0, tiled=True) for half in gated]

        def part(replica, piece):
            block = lax.dynamic_slice_in_dim(cot_all, replica * rows, rows, axis=1)
            return lax.dot_general(
                block, piece, (((0,), (0,)), ((), ())), preferred_element_type=f32
            )

        def weight_one(piece):
            return part(me_dp, piece), swap_pairs(part(1 - me_dp, piece).astype(bf16), "dp", 1)

    share = taps // n_dp
    grad_query, signal, head, sent_lag, own_lag = by_channel(
        lag_kernel,
        tables,
        [own_part, other_part, state, queries, prior, key_rows, value_rows, dp_row],
        [
            [rows16],
            [rows16],
            [jax.ShapeDtypeStruct((taps, channels), bf16)],
            [jax.ShapeDtypeStruct((share, channels), bf16)],
            [jax.ShapeDtypeStruct((share, channels), f32)],
        ],
        channels,
        unit * (2 * taps + 4 * length + 3 * taps),
    )
    def run_back(later):
        return by_channel(
            functools.partial(back_kernel, scale),
            tables,
            [signal, later, filter_taps, skip_gain[None], key_rows, value_rows],
            [[rows16], [rows16]],
            channels,
            256 * unit * (4 * taps + 5 * length),
        )

    received = swap_pairs(sent_lag, "dp", 1)
    if square:
        weight_place, halves[1][2], signal = lax.optimization_barrier((weight_place, halves[1][2], signal))
        ring_step(halves[1])
        first_sent, first_own = weight_sum(weight_place, cot_pieces, halves[0], rows)
        first_received = swap_pairs(first_sent, "dp", 1)
        received, first_own, head = lax.optimization_barrier((received, first_own, head))
    later = lax.ppermute(head, "seq", [(i + 1, i) for i in range(n_seq - 1)])
    lag_sum = own_lag + received.astype(f32)
    distance = 1
    while distance < n_seq:
        rounded = lag_sum.astype(bf16)
        received = swap_pairs(rounded, "seq", distance)
        if square and distance == 1:
            second_sent, second_own = weight_sum(weight_place, cot_pieces, halves[1], rows)
            second_received = swap_pairs(second_sent, "dp", 1)
            received, second_own = lax.optimization_barrier((received, second_own))
        lag_sum = rounded.astype(f32) + received.astype(f32)
        distance *= 2
    if square:
        first_received, lag_sum = lax.optimization_barrier((first_received, lag_sum))
    mine = lag_sum.astype(bf16)
    theirs = swap_pairs(mine, "dp", 1)
    grad_key, grad_value = run_back(after(later, second_own) if square else later)
    first = me_dp == 0
    lag_sum = jnp.concatenate([jnp.where(first, mine, theirs), jnp.where(first, theirs, mine)], axis=0)
    grad_filter = lag_sum.astype(f32).T * (norm_factor * scale)

    if square:
        parts = [(first_own, first_received), (second_own, second_received)]
    else:
        parts = [weight_one(half) for half in gated_all]
    grad_weight = jnp.concatenate(
        [(mine + theirs.astype(f32)) * norm_factor for mine, theirs in parts], axis=1
    )
    return (
        grad_query[None],
        grad_key[None],
        grad_value[None],
        grad_filter,
        grad_filter[:, 0],
        grad_weight,
    )


def solution(mesh):
    tokens = P("dp", "seq", "tp")
    return jax.shard_map(
        per_device,
        mesh=mesh,
        in_specs=(tokens, tokens, tokens, P("tp", None), P("tp"), P("tp", "dp"), tokens),
        out_specs=(tokens, tokens, tokens, P("tp", None), P("tp"), P(("seq", "dp"), "tp")),
        check_vma=False,
    )
```
